32 devices in a mesh: dp: 8 (over z, y), seq: 4 (over x, core).
Axes of the slice: x: 2, y: 2, z: 4, core: 2. Of those that a mesh axis runs over, the one named last changes fastest.
Arguments:
- tokens: bfloat16 [16, 1024, 768], P('dp', 'seq'), may hold values from -6 to 6
- lengths: int32 [16, 2], P('dp'), may hold values from 8 to 992, as said below
- first_gain: float32 [768], P('dp'), may hold values from 0.1 to 1.9
- first_shift: float32 [768], P('dp'), may hold values from -3 to 3
- triple_weight: float32 [768, 2304], P('dp'), may hold values from -0.21875 to 0.21875
- triple_bias: float32 [1536], P('dp'), may hold values from -3 to 3
- attend_weight: float32 [768, 768], P('dp'), may hold values from -0.875 to 0.875
- attend_bias: float32 [768], P('dp'), may hold values from -3 to 3
- second_gain: float32 [768], P('dp'), may hold values from 0.1 to 1.9
- second_shift: float32 [768], P('dp'), may hold values from -3 to 3
- expand_weight: float32 [768, 3072], P('dp'), may hold values from -0.21875 to 0.21875
- expand_bias: float32 [3072], P('dp'), may hold values from -3 to 3
- shrink_weight: float32 [3072, 768], P('dp'), may hold values from -0.109375 to 0.109375
- shrink_bias: float32 [768], P('dp'), may hold values from -3 to 3
- upstream: bfloat16 [16, 1024, 768], P('dp', 'seq'), may hold values from -6 to 6
Outputs:
- result: bfloat16 [16, 1024, 768], P('dp', 'seq')
- tokens_grad: bfloat16 [16, 1024, 768], P('dp', 'seq')
- first_gain_grad: float32 [768], P('dp')
- first_shift_grad: float32 [768], P('dp')
- triple_weight_grad: float32 [768, 2304], P('dp')
- triple_bias_grad: float32 [1536], P('dp')
- attend_weight_grad: float32 [768, 768], P('dp')
- attend_bias_grad: float32 [768], P('dp')
- second_gain_grad: float32 [768], P('dp')
- second_shift_grad: float32 [768], P('dp')
- expand_weight_grad: float32 [768, 3072], P('dp')
- expand_bias_grad: float32 [3072], P('dp')
- shrink_weight_grad: float32 [3072, 768], P('dp')
- shrink_bias_grad: float32 [768], P('dp')
The draws below stay inside these ranges and needn't reach their ends.
Inputs may be any that keep to these rules, and one draw needn't show every extreme that they name: Prompt and response lengths are 8 or more each; their sum is at most 1000, and in every aligned block of 2 rows one row's sum is exactly 1000.
All inputs are finite; a program needn't handle non-finite values.
Results may differ from the reference program's by a relative error of at most 0.014.
Values may be sent and summed in bfloat16 or wider, within the bound.
A program may use at most 192 MiB of HBM per device.

```python
import jax
import jax.numpy as jnp
from jax import lax

D = 768
H = 12
HD = 64
FF = 3072
SLOTS = 1024
ROWS_DEV = 2
ROWS = 16
MAXLEN = 1000


def draw_lengths(key, part):
    key = jax.random.fold_in(key, 7)
    key_total, key_split, key_pick = jax.random.split(key, 3)
    cubed_draw = jax.random.randint(key_total, (ROWS,), 0, 1024)
    tail_part = cubed_draw * cubed_draw // 1024 * cubed_draw // 1024
    totals = 16 + tail_part * (MAXLEN - 16) // 1023
    group_pick = jax.random.randint(key_pick, (ROWS // ROWS_DEV,), 0, ROWS_DEV)
    slot_in_group = jnp.arange(ROWS) % ROWS_DEV
    full_row = slot_in_group == jnp.repeat(group_pick, ROWS_DEV)
    totals = jnp.where(full_row, MAXLEN, totals)
    split_draw = jax.random.randint(key_split, (ROWS,), 0, 1024)
    prompt = 8 + split_draw * (totals - 15) // 1024
    return jnp.stack([prompt, totals - prompt], axis=1).astype(jnp.int32)


def spiked(drawn, rng, source, target, blocks, factor):
    owner, partner = [(jnp.arange(drawn.shape[dim]) // (drawn.shape[dim] // blocks)).reshape([-1 if axis == dim else 1 for axis in range(drawn.ndim)]) for dim in (source, target)]
    chosen = jax.random.permutation(rng, blocks)[partner]
    strong = (owner == chosen) | (owner == (partner + blocks // 2) % blocks)
    return jnp.where(strong, factor * drawn, drawn)


def shard_levels(own_key, dims, cuts, low, high):
    factor_of, own = 1.0, jax.random.fold_in(own_key, 6)
    for axis_at, parts in cuts:
        draws = jnp.exp(jax.random.uniform(jax.random.fold_in(own, axis_at), (parts,), jnp.float32, low / len(cuts), high / len(cuts)))
        factor_of = factor_of * jnp.repeat(draws, dims[axis_at] // parts).reshape([-1 if axis == axis_at else 1 for axis in range(len(dims))])
    return factor_of


def bell_draw(own_key, extent, width, bound, pieces=(), kind=jnp.bfloat16):
    drawn = width * jax.random.normal(own_key, extent, jnp.float32)
    if pieces:
        drawn = drawn * shard_levels(own_key, extent, pieces, -0.22, 0.18)
    return jnp.clip(drawn, -bound, bound).astype(kind)


def heavy_noise(key, shape, deviation, reach, cuts, heavy, kind=jnp.bfloat16):
    values = deviation * jax.random.normal(key, shape, jnp.float32)
    if cuts:
        values = values * shard_levels(key, shape, cuts, -0.22, 0.18)
    return jnp.clip(spiked(values, jax.random.fold_in(key, 3), *heavy), -reach, reach).astype(kind)


def setup_inputs(seed: int = 0) -> dict:
    splits = jax.random.split(jax.random.key(seed), 16)
    return {
        "tokens": bell_draw(splits[0], (ROWS, SLOTS, D), 1.0, 6.0, ((0, 8), (1, 4))),
        "lengths": draw_lengths(jax.random.fold_in(splits[15], 71), 0),
        "first_gain": jnp.clip(1.0 + 0.18 * jax.random.normal(splits[2], (D,), jnp.float32), 0.1, 1.9),
        "first_shift": bell_draw(splits[3], (D,), 0.3, 3.0, ((0, 8),), jnp.float32),
        "triple_weight": bell_draw(splits[4], (D, 3 * D), D ** -0.5, 0.21875, ((0, 8),), jnp.float32),
        "triple_bias": bell_draw(splits[5], (2 * D,), 0.3, 3.0, ((0, 8),), jnp.float32),
        "attend_weight": bell_draw(splits[6], (D, D), (D // 16) ** -0.5, 0.875, ((0, 8),), jnp.float32),
        "attend_bias": bell_draw(splits[7], (D,), 0.3, 3.0, ((0, 8),), jnp.float32),
        "second_gain": jnp.clip(1.0 + 0.18 * jax.random.normal(splits[8], (D,), jnp.float32), 0.1, 1.9),
        "second_shift": bell_draw(splits[9], (D,), 0.3, 3.0, ((0, 8),), jnp.float32),
        "expand_weight": bell_draw(splits[10], (D, FF), D ** -0.5, 0.21875, ((0, 8),), jnp.float32),
        "expand_bias": bell_draw(splits[11], (FF,), 0.3, 3.0, ((0, 8),), jnp.float32),
        "shrink_weight": bell_draw(splits[12], (FF, D), FF ** -0.5, 0.109375, ((0, 8),), jnp.float32),
        "shrink_bias": bell_draw(splits[13], (D,), 0.3, 3.0, ((0, 8),), jnp.float32),
        "upstream": heavy_noise(splits[14], (ROWS, SLOTS, D), 1.0, 6.0, ((0, 8), (1, 4)), (0, 2, 8, 2.0)),
    }


@jax.custom_vjp
def low(v):
    return lax.optimization_barrier(v.astype(jnp.bfloat16)).astype(jnp.float32)

@jax.custom_vjp
def low_back(v):
    return v

def low_keep(v):
    return (low(v), None)

def low_pass(kept, grad):
    return (grad,)

def back_keep(v):
    return (v, None)

def back_low(kept, grad):
    return (low(grad),)
low.defvjp(low_keep, low_pass)
low_back.defvjp(back_keep, back_low)
EPSILON = 1e-05
NEG_FILL = -1e+30
HIGHEST = lax.Precision.HIGHEST

def layer_norm(values, norm_gain, norm_shift):
    center = values - lax.optimization_barrier(jnp.mean(values, axis=-1, keepdims=True))
    spread = lax.optimization_barrier(jnp.mean(center * center, axis=-1, keepdims=True))
    return center * lax.rsqrt(spread + EPSILON) * norm_gain + norm_shift

def gelu_tanh(values):
    inside = 0.7978845608028654 * (values + 0.044715 * values * values * values)
    return 0.5 * values * (1.0 + jnp.tanh(inside))

def forward(values, row_lengths, weights):
    norm_gain, norm_shift, triple_weight, triple_bias, attend_weight, attend_bias, second_gain, second_shift, expand_weight, expand_bias, shrink_weight, shrink_bias = [low(member) for member in weights]
    group_rows = values.shape[0]
    normed = low(layer_norm(values, norm_gain, norm_shift))
    bias_full = jnp.concatenate([triple_bias[:D], jnp.zeros((D,), values.dtype), triple_bias[D:]])
    triple = jnp.einsum('rsd,de->rse', normed, triple_weight, precision=HIGHEST) + bias_full
    triple = low_back(low(triple))
    query = triple[..., :D].reshape(group_rows, SLOTS, H, HD)
    key_heads = triple[..., D:2 * D].reshape(group_rows, SLOTS, H, HD)
    value_heads = triple[..., 2 * D:].reshape(group_rows, SLOTS, H, HD)
    scores = jnp.einsum('rqhe,rkhe->rhqk', query, key_heads, precision=HIGHEST) * HD ** (-0.5)
    scores = low_back(scores)
    position = jnp.arange(SLOTS)
    totals = row_lengths[:, 0] + row_lengths[:, 1]
    allowed = (position[None, None, :] <= position[None, :, None]) & (position[None, None, :] < totals[:, None, None])
    scores = jnp.where(allowed[:, None], scores, NEG_FILL)
    probs = low(jax.nn.softmax(scores, axis=-1))
    mixed = jnp.einsum('rhqk,rkhe->rqhe', probs, value_heads, precision=HIGHEST).reshape(group_rows, SLOTS, D)
    mixed = low_back(low(mixed))
    branch = low_back(jnp.einsum('rsd,de->rse', mixed, attend_weight, precision=HIGHEST) + attend_bias)
    resid = values + branch
    normed_two = low(layer_norm(resid, second_gain, second_shift))
    pre_act = low_back(jnp.einsum('rsd,de->rse', normed_two, expand_weight, precision=HIGHEST) + expand_bias)
    activated = low(gelu_tanh(pre_act))
    return resid + jnp.einsum('rsf,fd->rsd', activated, shrink_weight, precision=HIGHEST) + shrink_bias

def reference(tokens, lengths, first_gain, first_shift, triple_weight, triple_bias, attend_weight, attend_bias, second_gain, second_shift, expand_weight, expand_bias, shrink_weight, shrink_bias, upstream):
    params = tuple((member.astype(jnp.float32) for member in (first_gain, first_shift, triple_weight, triple_bias, attend_weight, attend_bias, second_gain, second_shift, expand_weight, expand_bias, shrink_weight, shrink_bias)))
    group_rows = 4 if ROWS % 4 == 0 else 1
    block_count = ROWS // group_rows
    token_blocks = tokens.astype(jnp.float32).reshape(block_count, group_rows, SLOTS, D)
    length_blocks = lengths.reshape(block_count, group_rows, 2)
    seed_blocks = upstream.astype(jnp.float32).reshape(block_count, group_rows, SLOTS, D)

    def scan_step(running, block_item):
        block_tokens, block_lengths, block_seed = block_item
        output, pullback = jax.vjp(lambda values, weights: forward(values, block_lengths, weights), block_tokens, params)
        grad_values, grad_weights = pullback(block_seed)
        running = jax.tree.map(lambda total, addend: total + addend, running, grad_weights)
        return (running, (output.astype(jnp.bfloat16), grad_values.astype(jnp.bfloat16)))
    zeros_start = tuple((jnp.zeros_like(member) for member in params))
    grads, (outputs, input_grads) = lax.scan(scan_step, zeros_start, (token_blocks, length_blocks, seed_blocks))
    result = outputs.reshape(ROWS, SLOTS, D)
    tokens_grad = input_grads.reshape(ROWS, SLOTS, D)
    return (result, tokens_grad, grads[0], grads[1], grads[2], grads[3], grads[4], grads[5], grads[6], grads[7], grads[8], grads[9], grads[10], grads[11])
```

```python
import functools

import jax
import jax.numpy as jnp
from jax import lax
from jax.experimental import pallas as pl
from jax.experimental.pallas import tpu as pltpu
from jax.sharding import PartitionSpec as P

H = 12
HD = 64

EPSILON = 1e-05
NEG_FILL = -1e30
MESH = pl.DeviceIdType.MESH
MIB = 1024 * 1024
BF16 = jnp.bfloat16
F32 = jnp.float32


def layer_norm(values, norm_gain, norm_shift):
    center = values - jnp.mean(values, axis=-1, keepdims=True)
    spread = jnp.mean(center * center, axis=-1, keepdims=True)
    return center * lax.rsqrt(spread + EPSILON) * norm_gain + norm_shift


def gelu_tanh(values):
    inside = 0.7978845608028654 * (values + 0.044715 * values * values * values)
    return 0.5 * values * (1.0 + jnp.tanh(inside))


def product(operand, other):
    return jnp.dot(operand, other, preferred_element_type=F32)


def product_across(operand, other):
    return lax.dot_general(operand, other, (((0,), (0,)), ((), ())), preferred_element_type=F32)


def product_back(operand, other):
    return lax.dot_general(operand, other, (((1,), (1,)), ((), ())), preferred_element_type=F32)


def own_place():
    d, s = lax.axis_index("dp"), lax.axis_index("seq")
    return d, s, d // 2, d % 2, s // 2, s % 2


def flip(index, step):
    return index + step * (1 - 2 * ((index // step) % 2))


def remote(src, dst, send, recv, d, s):
    return pltpu.make_async_remote_copy(
        src_ref=src, dst_ref=dst, send_sem=send, recv_sem=recv, device_id=(d, s), device_id_type=MESH
    )


def greet(depth, steps):
    d, s, z, y, x, c = own_place()
    barrier = pltpu.get_barrier_semaphore()

    def signal(d_to, s_to):
        pl.semaphore_signal(barrier, inc=1, device_id=(d_to, s_to), device_id_type=MESH)

    @pl.when(z > 0)
    def _():
        signal(d - 2, s)

    @pl.when(z < depth - 1)
    def _():
        signal(d + 2, s)

    for step in steps:
        signal(flip(d, step), s)
    signal(d, flip(s, 2))
    signal(d, flip(s, 1))
    ends = jnp.where(z > 0, 1, 0) + jnp.where(z < depth - 1, 1, 0)
    pl.semaphore_wait(barrier, ends + len(steps) + 2)


def doubling_steps(count):
    return [1 << k for k in range(count.bit_length() - 1)]


def spread_kernel(dp, rows, *refs):
    count = len(rows)
    depth = dp // 2
    shard, small = refs[:count], refs[count]
    full, small_full = refs[count + 1 : 2 * count + 1], refs[2 * count + 1]
    low = refs[2 * count + 2 : 3 * count + 2]
    (local, up_s, down_s, y_s, x_s, ca_s, cb_s, yz_r, x_r, ca_r, cb_r, small_s, small_r) = refs[3 * count + 2 :]
    d, s, z, y, x, c = own_place()
    steps = doubling_steps(dp)

    greet(depth, steps)

    def yz_rows(g, at):
        m = rows[g] // 6
        return pl.ds(pl.multiple_of(at * rows[g] + 3 * m * c + m * x, 16), 2 * m)

    def third(g, at, plane):
        m = rows[g] // 6
        return pl.ds(pl.multiple_of(at * rows[g] + 3 * m * c + 2 * m * plane, 16), m)

    def move(g, window, send, recv, d_to, s_to, src=None):
        view = full[g].at[window, :]
        return remote(view if src is None else src, view, send, recv, d_to, s_to)

    def own_piece(g):
        m = rows[g] // 6
        return low[g].at[pl.ds(pl.multiple_of(3 * m * c + m * x, 16), 2 * m), :]

    def up(g, at, src=None):
        return move(g, yz_rows(g, at), up_s.at[g, at], yz_r.at[g, at], d + 2, s, src)

    def down(g, at, src=None):
        return move(g, yz_rows(g, at), down_s.at[g, at], yz_r.at[g, at], d - 2, s, src)

    def over_y(g, at, src=None):
        return move(g, yz_rows(g, at), y_s.at[g, at], yz_r.at[g, at], flip(d, 1), s, src)

    def over_x(g, at):
        return move(g, third(g, at, x), x_s.at[g, at], x_r.at[g, at], d, flip(s, 2))

    def from_x(g, at):
        return move(g, third(g, at, 1 - x), x_s.at[g, at], x_r.at[g, at], d, flip(s, 2))

    def core_a(g, at):
        return move(g, yz_rows(g, at), ca_s.at[g, at], ca_r.at[g, at], d, flip(s, 1))

    def core_b(g, at):
        return move(g, third(g, at, 1 - x), cb_s.at[g, at], cb_r.at[g, at], d, flip(s, 1))

    def small_copy(k):
        size = 16 << k
        base = (d // (1 << k)) * size
        view = small_full.at[pl.ds(pl.multiple_of(base, 16), size), :]
        return remote(view, view, small_s.at[k], small_r.at[k], flip(d, 1 << k), s)

    def own_local(g):
        return pltpu.make_async_copy(
            low[g], full[g].at[pl.ds(pl.multiple_of(d * rows[g], 16), rows[g]), :], local.at[g]
        )

    own_small = pltpu.make_async_copy(small, small_full.at[pl.ds(pl.multiple_of(d * 16, 16), 16), :], local.at[count])
    own_small.start()

    for g in range(count):
        low[g][...] = shard[g][...].astype(BF16)
        src = own_piece(g)

        @pl.when(z < depth - 1)
        def _():
            up(g, d, src).start()

        @pl.when(z > 0)
        def _():
            down(g, d, src).start()

        over_y(g, d, src).start()
        own_local(g).start()

    own_small.wait()
    for k in range(len(steps)):
        small_copy(k).start()
        small_copy(k).wait()

    def z_arrival(g, r):
        @pl.when(z >= r)
        def _():
            at = d - 2 * r
            up(g, at).wait_recv()

            @pl.when(z < depth - 1)
            def _():
                up(g, at).start()

            over_y(g, at).start()
            over_x(g, at).start()
            core_a(g, at).start()

        @pl.when(z + r < depth)
        def _():
            at = d + 2 * r
            down(g, at).wait_recv()

            @pl.when(z > 0)
            def _():
                down(g, at).start()

            over_y(g, at).start()
            over_x(g, at).start()
            core_a(g, at).start()

    other = flip(d, 1)

    def y_one(g, at):
        over_y(g, at).wait_recv()
        over_x(g, at).start()
        core_a(g, at).start()

    def on_shards(r, base, action):
        if r == 0:
            action(base)
        else:

            @pl.when(z >= r)
            def _():
                action(base - 2 * r)

            @pl.when(z + r < depth)
            def _():
                action(base + 2 * r)

    def x_one(g, at):
        from_x(g, at).wait_recv()
        core_b(g, at).start()

    for r in range(depth + 2):
        for g in range(count):
            if 1 <= r < depth:
                z_arrival(g, r)
            if r < depth:
                on_shards(r, other, functools.partial(y_one, g))
            if 1 <= r - 1 < depth:
                on_shards(r - 1, d, functools.partial(x_one, g))
            if 0 <= r - 2 < depth:
                on_shards(r - 2, other, functools.partial(x_one, g))

    for g in range(count):
        own_local(g).wait()

        @pl.when(z < depth - 1)
        def _():
            up(g, d, own_piece(g)).wait_send()

        @pl.when(z > 0)
        def _():
            down(g, d, own_piece(g)).wait_send()

        over_y(g, d, own_piece(g)).wait_send()

        def finish(g, at, own_column):
            if own_column:
                over_y(g, at).wait_send()
            over_x(g, at).wait_send()
            core_a(g, at).wait_send()
            core_b(g, at).wait_send()
            core_a(g, at).wait_recv()
            core_b(g, at).wait_recv()

        for r in range(depth):
            on_shards(r, other, functools.partial(finish, g, own_column=False))
            if r:
                on_shards(r, d, functools.partial(finish, g, own_column=True))

                @pl.when((z >= r) & (z < depth - 1))
                def _():
                    up(g, d - 2 * r).wait_send()

                @pl.when((z + r < depth) & (z > 0))
                def _():
                    down(g, d + 2 * r).wait_send()


def spread(dp, shards, small):
    rows = [member.shape[0] for member in shards]
    count = len(rows)
    dma = pltpu.SemaphoreType.DMA
    any_space = pl.BlockSpec(memory_space=pl.ANY)
    vmem = pl.BlockSpec(memory_space=pltpu.VMEM)
    return pl.pallas_call(
        functools.partial(spread_kernel, dp, rows),
        out_shape=[jax.ShapeDtypeStruct((dp * m.shape[0], m.shape[1]), BF16) for m in shards]
        + [jax.ShapeDtypeStruct((dp * 16, 128), BF16)],
        in_specs=[vmem] * count + [any_space],
        out_specs=[any_space] * (count + 1),
        scratch_shapes=[pltpu.VMEM(m.shape, BF16) for m in shards]
        + [dma((count + 1,))]
        + [dma((count, dp))] * 10
        + [dma((len(doubling_steps(dp)),))] * 2,
        compiler_params=pltpu.CompilerParams(
            collective_id=1, has_side_effects=True, vmem_limit_bytes=40 * MIB
        ),
        name="spread_weights",
    )(*shards, small)


def fold_kernel(dp, rows, *refs):
    count = len(rows)
    depth = dp // 2
    grads, small = refs[:count], refs[count]
    outs, small_out = refs[count + 1 : 2 * count + 1], refs[2 * count + 1]
    at_ref = 2 * count + 2
    acc, c_buf, x_buf, y_buf, u_buf, n_buf, b_buf = [refs[at_ref + k * count : at_ref + (k + 1) * count] for k in range(7)]
    small_buf = refs[at_ref + 7 * count]
    (
        load, c_s, c_r, x_s, x_r, y_s, y_r, u_s, u_r, n_s, n_r, f_s, f_r, small_s, small_r,
    ) = refs[at_ref + 7 * count + 1 :]
    d, s, z, y, x, c = own_place()
    dp_steps = doubling_steps(dp)

    greet(depth, dp_steps)

    order = sorted(range(depth), key=lambda k: -abs(2 * k - depth + 1))
    items = [(g, k, own) for g in range(count) for own in (False, True) for k in order]

    def shard_of(k, own):
        return 2 * k + (y if own else 1 - y)

    def m_of(g):
        return rows[g] // 6

    def fetch(g, at):
        return pltpu.make_async_copy(grads[g].at[at, c], acc[g].at[at], load.at[g, at])

    def core(g, at):
        return remote(grads[g].at[at, 1 - c], c_buf[g].at[at], c_s.at[g, at], c_r.at[g, at], d, flip(s, 1))

    def rows_at(g, units, n):
        m = m_of(g)
        return pl.ds(pl.multiple_of(units * m, 16), n * m)

    def over_x(g, at):
        return remote(
            acc[g].at[at, rows_at(g, 2 * (1 - x), 1), :], x_buf[g].at[at], x_s.at[g, at], x_r.at[g, at], d, flip(s, 2)
        )

    def over_y(g, k):
        return remote(
            acc[g].at[2 * k + 1 - y, rows_at(g, x, 2), :], y_buf[g].at[k], y_s.at[g, k], y_r.at[g, k], flip(d, 1), s
        )

    def up(g, k):
        return remote(acc[g].at[2 * k + y, rows_at(g, x, 2), :], u_buf[g].at[k], u_s.at[g, k], u_r.at[g, k], d + 2, s)

    def down(g, k):
        return remote(acc[g].at[2 * k + y, rows_at(g, x, 2), :], n_buf[g].at[k], n_s.at[g, k], n_r.at[g, k], d - 2, s)

    def add(target, window, extra):
        target[window] = target[window] + extra

    def stage_b(g, k, own):
        at = shard_of(k, own)
        fetch(g, at).wait()
        core(g, at).wait_recv()
        acc[g][at] = acc[g][at] + c_buf[g][at]
        over_x(g, at).start()

    def stage_c(g, k, own):
        at = shard_of(k, own)
        over_x(g, at).wait_recv()
        window = (at, rows_at(g, 2 * x, 1), slice(None))
        acc[g][window] = acc[g][window] + x_buf[g][at]
        if not own:
            over_y(g, k).start()
        else:
            over_y(g, k).wait_recv()
            pair = (at, rows_at(g, x, 2), slice(None))
            acc[g][pair] = acc[g][pair] + y_buf[g][k]

    def stage_e(g, k, hop):
        pair = (2 * k + y, rows_at(g, x, 2), slice(None))

        if k > hop:

            @pl.when(z == hop)
            def _():
                if hop:
                    up(g, k).wait_recv()
                    acc[g][pair] = acc[g][pair] + u_buf[g][k]
                up(g, k).start()

        if k < depth - 1 - hop:

            @pl.when(z == depth - 1 - hop)
            def _():
                if hop:
                    down(g, k).wait_recv()
                    acc[g][pair] = acc[g][pair] + n_buf[g][k]
                down(g, k).start()

    def final_share(g):
        m = m_of(g)
        return remote(
            acc[g].at[d, rows_at(g, 2 * x, 1), :],
            outs[g].at[pl.ds(pl.multiple_of(3 * m * c + 2 * m * x, 16), m), :],
            f_s.at[g, 0], f_r.at[g, 0], d, flip(s, 2),
        )

    def final_swap(g):
        return remote(acc[g].at[d, rows_at(g, 1, 1), :], b_buf[g], f_s.at[g, 1], f_r.at[g, 1], d, flip(s, 2))

    def final_core(g):
        view = outs[g].at[pl.ds(pl.multiple_of(3 * m_of(g) * c, 16), 3 * m_of(g)), :]
        return remote(view, view, f_s.at[g, 2], f_r.at[g, 2], d, flip(s, 1))

    def finish_one(g):
        pair = (d, rows_at(g, x, 2), slice(None))

        @pl.when(z > 0)
        def _():
            up(g, z).wait_recv()
            acc[g][pair] = acc[g][pair] + u_buf[g][z]

        @pl.when(z < depth - 1)
        def _():
            down(g, z).wait_recv()
            acc[g][pair] = acc[g][pair] + n_buf[g][z]

        final_share(g).start()
        final_swap(g).start()
        m = m_of(g)
        outs[g][pl.ds(pl.multiple_of(3 * m * c + 2 * m * x, 16), m), :] = acc[g][d, rows_at(g, 2 * x, 1), :]

    def finish_two(g):
        m = m_of(g)
        final_swap(g).wait_recv()
        outs[g][pl.ds(pl.multiple_of(3 * m * c + m, 16), m), :] = acc[g][d, rows_at(g, 1, 1), :] + b_buf[g][...]
        final_share(g).wait_recv()
        final_core(g).start()

    small_out[...] = small[...]
    small_partners = [(flip(d, step), s) for step in dp_steps] + [(d, flip(s, 1)), (d, flip(s, 2))]

    def small_copy(k):
        d_to, s_to = small_partners[k]
        return remote(small_out, small_buf.at[k], small_s.at[k], small_r.at[k], d_to, s_to)

    def small_finish(k):
        small_copy(k).wait()
        small_out[...] = small_out[...] + small_buf[k]

    for g, k, own in items:
        core(g, shard_of(k, own)).start()
        fetch(g, shard_of(k, own)).start()

    timeline = {}

    def plan(at, action, *args):
        timeline.setdefault(at, []).append((action, args))

    per = 2 * depth
    for i, (g, k, own) in enumerate(items):
        plan(i, stage_b, g, k, own)
        plan(i + 2, stage_c, g, k, own)
        if own:
            for hop in range(depth - 1):
                plan(i + 3 + 2 * hop, stage_e, g, k, hop)
    for g in range(count):
        last = (g + 1) * per + 2 + 2 * depth
        plan(last, finish_one, g)
        plan(last + 2, finish_two, g)
    for k in range(len(small_partners)):
        plan(2 * k, lambda k: small_copy(k).start(), k)
        plan(2 * k + 1, small_finish, k)
    for at in sorted(timeline):
        for action, args in reversed(timeline[at]):
            action(*args)

    for g in range(count):
        final_share(g).wait_send()
        final_swap(g).wait_send()
        final_core(g).wait()
        for k in range(depth):
            for own in (False, True):
                core(g, shard_of(k, own)).wait_send()
                over_x(g, shard_of(k, own)).wait_send()
            over_y(g, k).wait_send()

            @pl.when(k > z)
            def _():
                up(g, k).wait_send()

            @pl.when(k < z)
            def _():
                down(g, k).wait_send()


def fold(dp, grads, small):
    rows = [member.shape[0] // dp for member in grads]
    count, depth = len(rows), dp // 2
    views = [member.reshape(dp, 2, r // 2, member.shape[1]) for member, r in zip(grads, rows)]
    dma = pltpu.SemaphoreType.DMA
    any_space = pl.BlockSpec(memory_space=pl.ANY)
    vmem = pl.BlockSpec(memory_space=pltpu.VMEM)

    def buffers(lead, part):
        return [pltpu.VMEM((*lead, r // part, m.shape[1]), BF16) for r, m in zip(rows, grads)]

    partners = len(doubling_steps(dp)) + 2
    return pl.pallas_call(
        functools.partial(fold_kernel, dp, rows),
        out_shape=[jax.ShapeDtypeStruct((r, m.shape[1]), BF16) for r, m in zip(rows, grads)]
        + [jax.ShapeDtypeStruct(small.shape, F32)],
        in_specs=[any_space] * count + [vmem],
        out_specs=[vmem] * (count + 1),
        scratch_shapes=buffers((dp,), 2)
        + buffers((dp,), 2)
        + buffers((dp,), 6)
        + buffers((depth,), 3)
        + buffers((depth,), 3)
        + buffers((depth,), 3)
        + buffers((), 6)
        + [pltpu.VMEM((partners, *small.shape), F32)]
        + [dma((count, dp))] * 5
        + [dma((count, depth))] * 6
        + [dma((count, 3))] * 2
        + [dma((partners,))] * 2,
        compiler_params=pltpu.CompilerParams(
            collective_id=2, has_side_effects=True, vmem_limit_bytes=50 * MIB
        ),
        name="fold_gradients",
    )(*views, small)


def head_mask():
    return lax.broadcasted_iota(jnp.int32, (1, 2 * HD), 1) < HD


def stack_keys(mine, other, target, quarter):
    target[0:quarter] = mine[0:quarter]
    target[quarter : 2 * quarter] = other[0:quarter]
    target[2 * quarter : 3 * quarter] = mine[quarter:]
    target[3 * quarter :] = other[quarter:]


def attend_kernel(quarter, place, q_ref, k_ref, v_ref, ok_ref, ov_ref, mixed_ref, probs_ref, keys, values):
    stack_keys(k_ref, ok_ref, keys, quarter)
    stack_keys(v_ref, ov_ref, values, quarter)
    first = head_mask()
    row = lax.broadcasted_iota(jnp.int32, (4 * quarter, 1), 0)
    block = row // quarter
    base = jnp.where(block == 0, place[1], jnp.where(block == 1, place[2], jnp.where(block == 2, place[3], place[4])))
    key_pos = row - block * quarter + base * quarter
    key_pos = jnp.where(key_pos < place[0], key_pos, 1 << 20)
    lane = lax.broadcasted_iota(jnp.int32, (1, quarter), 1)
    for part in range(2):
        length = 2 * quarter * (part + 1)
        query_pos = lane + place[1 + 2 * part] * quarter
        allowed = key_pos[:length] <= query_pos
        query = q_ref[part * quarter : (part + 1) * quarter] * jnp.asarray(HD**-0.5, BF16)
        sums = []
        for head in range(2):
            mask = first if head == 0 else ~first
            scores = product_back(keys[:length], jnp.where(mask, query, jnp.zeros_like(query)))
            scores = jnp.where(allowed, scores, NEG_FILL)
            exponent = jnp.exp(scores - jnp.max(scores, axis=0, keepdims=True))
            probs = (exponent * (1.0 / jnp.sum(exponent, axis=0, keepdims=True))).astype(BF16)
            probs_ref[0, head, 2 * quarter * part : 2 * quarter * part + length] = probs
            sums.append(product_across(probs, values[:length]))
        mixed_ref[part * quarter : (part + 1) * quarter] = jnp.where(first, sums[0], sums[1]).astype(BF16)


def attend(triple, other, place, width):
    tokens = triple.shape[0]
    quarter = tokens // 2
    pairs = width // (2 * HD)

    def block(shift):
        return pl.BlockSpec((tokens, 2 * HD), lambda p, _: (0, p + shift))

    return pl.pallas_call(
        functools.partial(attend_kernel, quarter),
        grid_spec=pltpu.PrefetchScalarGridSpec(
            num_scalar_prefetch=1,
            grid=(pairs,),
            in_specs=[block(0), block(pairs), block(2 * pairs), block(0), block(pairs)],
            out_specs=[block(0), pl.BlockSpec((1, 2, 6 * quarter, quarter), lambda p, _: (p, 0, 0, 0))],
            scratch_shapes=[pltpu.VMEM((4 * quarter, 2 * HD), BF16)] * 2,
        ),
        out_shape=[
            jax.ShapeDtypeStruct((tokens, width), BF16),
            jax.ShapeDtypeStruct((pairs, 2, 6 * quarter, quarter), BF16),
        ],
        compiler_params=pltpu.CompilerParams(vmem_limit_bytes=50 * MIB),
        name="attend",
    )(place, triple, triple, triple, other, other)


def attend_back_kernel(
    quarter, q_ref, k_ref, v_ref, ok_ref, ov_ref, g_ref, probs_ref, dq_ref, dk_ref, dv_ref, odk_ref, odv_ref,
    keys, values, dkeys, dvalues,
):
    stack_keys(k_ref, ok_ref, keys, quarter)
    stack_keys(v_ref, ov_ref, values, quarter)
    first = head_mask()
    for part in range(2):
        length = 2 * quarter * (part + 1)
        rows = slice(part * quarter, (part + 1) * quarter)
        query = q_ref[rows] * jnp.asarray(HD**-0.5, BF16)
        grad = g_ref[rows]
        dq = []
        for head in range(2):
            mask = first if head == 0 else ~first
            own_query = jnp.where(mask, query, jnp.zeros_like(query))
            own_grad = jnp.where(mask, grad, jnp.zeros_like(grad))
            probs = probs_ref[0, head, 2 * quarter * part : 2 * quarter * part + length]
            wide = probs.astype(F32)
            grad_probs = product_back(values[:length], own_grad)
            delta = jnp.sum(wide * grad_probs, axis=0, keepdims=True)
            grad_scores = (wide * (grad_probs - delta)).astype(BF16)
            dv = product(probs, own_grad)
            dk = product(grad_scores, own_query)
            if part == 0 and head == 0:
                dvalues[:length] = dv
                dkeys[:length] = dk
            elif part == 1 and head == 0:
                dvalues[: length // 2] += dv[: length // 2]
                dkeys[: length // 2] += dk[: length // 2]
                dvalues[length // 2 :] = dv[length // 2 :]
                dkeys[length // 2 :] = dk[length // 2 :]
            else:
                dvalues[:length] += dv
                dkeys[:length] += dk
            dq.append(product_across(grad_scores, keys[:length]))
        dq_ref[rows] = (jnp.where(first, dq[0], dq[1]) * HD**-0.5).astype(BF16)
    for source, mine, other in ((dkeys, dk_ref, odk_ref), (dvalues, dv_ref, odv_ref)):
        mine[:quarter] = source[:quarter].astype(BF16)
        mine[quarter:] = source[2 * quarter : 3 * quarter].astype(BF16)
        other[:quarter] = source[quarter : 2 * quarter].astype(BF16)
        other[quarter:] = source[3 * quarter :].astype(BF16)


def attend_back(triple, other, grad, probs, width):
    tokens = triple.shape[0]
    quarter = tokens // 2
    pairs = width // (2 * HD)

    def block(shift):
        return pl.BlockSpec((tokens, 2 * HD), lambda p: (0, p + shift))

    return pl.pallas_call(
        functools.partial(attend_back_kernel, quarter),
        grid=(pairs,),
        in_specs=[block(0), block(pairs), block(2 * pairs), block(0), block(pairs), block(0)]
        + [pl.BlockSpec((1, 2, 6 * quarter, quarter), lambda p: (p, 0, 0, 0))],
        out_specs=[block(0)] * 5,
        out_shape=[jax.ShapeDtypeStruct((tokens, width), BF16)] * 5,
        scratch_shapes=[pltpu.VMEM((4 * quarter, 2 * HD), BF16)] * 2 + [pltpu.VMEM((4 * quarter, 2 * HD), F32)] * 2,
        compiler_params=pltpu.CompilerParams(vmem_limit_bytes=50 * MIB),
        name="attend_back",
    )(triple, triple, triple, other, other, grad, probs)


def body(
    dp,
    tokens,
    lengths,
    first_gain,
    first_shift,
    triple_weight,
    triple_bias,
    attend_weight,
    attend_bias,
    second_gain,
    second_shift,
    expand_weight,
    expand_bias,
    shrink_weight,
    shrink_bias,
    upstream,
):
    row_count, quarter, width = tokens.shape
    matrices = (triple_weight, attend_weight, expand_weight, shrink_weight)
    vectors = (first_gain, first_shift, triple_bias, attend_bias, second_gain, second_shift, expand_bias, shrink_bias)
    sizes = [member.shape[0] for member in vectors]
    total_small = sum(sizes)
    by_kernel = dp & (dp - 1) == 0 and dp > 1 and all(m.shape[0] % 96 == 0 for m in matrices)
    by_kernel = by_kernel and total_small <= 16 * 128
    place = lax.axis_index("seq")
    x_place = place // 2

    small = jnp.concatenate([member.astype(BF16) for member in vectors])
    if by_kernel:
        small = jnp.pad(small, (0, 16 * 128 - total_small)).reshape(16, 128)
        *weights, small_full = spread(dp, matrices, small)
        small_full = small_full.reshape(dp, 16 * 128)[:, :total_small]
    else:
        weights = [lax.all_gather(m.astype(BF16), "dp", axis=0, tiled=True) for m in matrices]
        small_full = lax.all_gather(small, "dp", axis=0)
    floats, at = [], 0
    for size in sizes:
        floats.append(small_full[:, at : at + size].reshape(-1).astype(F32))
        at += size
    gain_one, shift_one, bias_triple, bias_attend, gain_two, shift_two, bias_expand, bias_shrink = floats
    triple_low, attend_low, expand_low, shrink_low = weights

    swap = [(k, 3 - k) for k in range(4)]
    twin = [(k, k + 1 - 2 * (k % 2)) for k in range(4)]
    upper = x_place == 1

    def exchange(array):
        mine = jnp.where(upper, array[1], array[0])
        theirs = lax.ppermute(jnp.where(upper, array[0], array[1]), "seq", swap)
        return jnp.concatenate([jnp.where(upper, theirs, mine), jnp.where(upper, mine, theirs)], axis=0)

    def give_back(array):
        low_part, high_part = array[:quarter], array[quarter:]
        mine = jnp.where(upper, high_part, low_part)
        theirs = lax.ppermute(jnp.where(upper, low_part, high_part), "seq", swap)
        return jnp.stack([jnp.where(upper, theirs, mine), jnp.where(upper, mine, theirs)])

    low_quarter = jnp.minimum(place, 3 - place)
    totals = lengths[:, 0] + lengths[:, 1]
    total = jnp.where(upper, totals[1], totals[0])
    spots = jnp.stack([total, low_quarter, 1 - low_quarter, 3 - low_quarter, 2 + low_quarter]).astype(jnp.int32)

    flat_tokens = exchange(tokens).astype(F32)
    seed_low = exchange(upstream)
    bias_full = jnp.concatenate([bias_triple[:width], jnp.zeros((width,), F32), bias_triple[width:]])

    normed, first_pull = jax.vjp(layer_norm, flat_tokens, gain_one, shift_one)
    normed_low = normed.astype(BF16)
    triple = (product(normed_low, triple_low) + bias_full).astype(BF16)
    other_keyval = lax.ppermute(triple[:, width:], "seq", twin)
    mixed_low, probs = attend(triple, other_keyval, spots, width)
    resid = flat_tokens + product(mixed_low, attend_low) + bias_attend
    normed_two, second_pull = jax.vjp(layer_norm, resid, gain_two, shift_two)
    normed_two_low = normed_two.astype(BF16)
    activated, gelu_pull = jax.vjp(gelu_tanh, product(normed_two_low, expand_low) + bias_expand)
    act_low = activated.astype(BF16)
    result = give_back((resid + product(act_low, shrink_low) + bias_shrink).astype(BF16))

    seed = seed_low.astype(F32)
    shrink_grad = product_across(act_low, seed_low)
    shrink_bias_grad = jnp.sum(seed, axis=0)
    grad_pre = gelu_pull(product_back(seed_low, shrink_low))[0].astype(BF16)
    expand_grad = product_across(normed_two_low, grad_pre)
    expand_bias_grad = jnp.sum(grad_pre.astype(F32), axis=0)
    resid_part, second_gain_grad, second_shift_grad = second_pull(product_back(grad_pre, expand_low))
    grad_resid = seed + resid_part
    grad_branch = grad_resid.astype(BF16)
    attend_grad = product_across(mixed_low, grad_branch)
    attend_bias_grad = jnp.sum(grad_branch.astype(F32), axis=0)
    grad_mixed = product_back(grad_branch, attend_low).astype(BF16)

    dq, dk, dv, other_dk, other_dv = attend_back(triple, other_keyval, grad_mixed, probs, width)
    got_dk = lax.ppermute(other_dk, "seq", twin)
    got_dv = lax.ppermute(other_dv, "seq", twin)
    dk = (dk.astype(F32) + got_dk.astype(F32)).astype(BF16)
    dv = (dv.astype(F32) + got_dv.astype(F32)).astype(BF16)
    grad_triple = jnp.concatenate([dq, dk, dv], axis=1)
    triple_grad = product_across(normed_low, grad_triple)
    triple_sums = jnp.sum(grad_triple.astype(F32), axis=0)
    triple_bias_grad = jnp.concatenate([triple_sums[:width], triple_sums[2 * width :]])
    flat_grad, first_gain_grad, first_shift_grad = first_pull(product_back(grad_triple, triple_low))
    tokens_grad = give_back((grad_resid + flat_grad).astype(BF16))

    big = [member.astype(BF16) for member in (triple_grad, attend_grad, expand_grad, shrink_grad)]
    small_grads = (
        first_gain_grad, first_shift_grad, triple_bias_grad, attend_bias_grad,
        second_gain_grad, second_shift_grad, expand_bias_grad, shrink_bias_grad,
    )
    flat_small = jnp.concatenate([g.reshape(dp, -1) for g in small_grads], axis=1)
    if by_kernel:
        *sums, small_sum = fold(dp, big, flat_small.reshape(-1, 128))
        own_small = lax.dynamic_index_in_dim(small_sum.reshape(dp, -1), lax.axis_index("dp"), 0, keepdims=False)
        sums = [member.astype(F32) for member in sums]
    else:
        sums = [lax.psum_scatter(member, "dp", scatter_dimension=0, tiled=True) for member in big]
        sums = [lax.psum(member, "seq").astype(F32) for member in sums]
        own_small = lax.psum(lax.psum_scatter(flat_small, "dp", scatter_dimension=0, tiled=True), "seq").reshape(-1)
    small_out, at = [], 0
    for size in sizes:
        small_out.append(own_small[at : at + size])
        at += size
    return (
        result,
        tokens_grad,
        small_out[0],
        small_out[1],
        sums[0],
        small_out[2],
        sums[1],
        small_out[3],
        small_out[4],
        small_out[5],
        sums[2],
        small_out[6],
        sums[3],
        small_out[7],
    )


def solution(mesh):
    return jax.shard_map(
        functools.partial(body, mesh.shape["dp"]),
        mesh=mesh,
        in_specs=(
            P("dp", "seq", None),
            P("dp", None),
            P("dp"),
            P("dp"),
            P("dp", None),
            P("dp"),
            P("dp", None),
            P("dp"),
            P("dp"),
            P("dp"),
            P("dp", None),
            P("dp"),
            P("dp", None),
            P("dp"),
            P("dp", "seq", None),
        ),
        out_specs=(
            P("dp", "seq", None),
            P("dp", "seq", None),
            P("dp"),
            P("dp"),
            P("dp", None),
            P("dp"),
            P("dp", None),
            P("dp"),
            P("dp"),
            P("dp"),
            P("dp", None),
            P("dp"),
            P("dp", None),
            P("dp"),
        ),
        check_vma=False,
    )
```

```python
import functools

import jax
import jax.numpy as jnp
from jax import lax
from jax.experimental import pallas as pl
from jax.experimental.pallas import tpu as pltpu
from jax.sharding import PartitionSpec as P

H = 12
HD = 64

EPSILON = 1e-05
NEG_FILL = -1e30
MESH = pl.DeviceIdType.MESH
MIB = 1024 * 1024
BF16 = jnp.bfloat16
F32 = jnp.float32


def layer_norm(values, norm_gain, norm_shift):
    center = values - jnp.mean(values, axis=-1, keepdims=True)
    spread = jnp.mean(center * center, axis=-1, keepdims=True)
    return center * lax.rsqrt(spread + EPSILON) * norm_gain + norm_shift


def gelu_tanh(values):
    inside = 0.7978845608028654 * (values + 0.044715 * values * values * values)
    return 0.5 * values * (1.0 + jnp.tanh(inside))


def product(operand, other):
    return jnp.dot(operand, other, preferred_element_type=F32)


def product_across(operand, other):
    return lax.dot_general(operand, other, (((0,), (0,)), ((), ())), preferred_element_type=F32)


def product_back(operand, other):
    return lax.dot_general(operand, other, (((1,), (1,)), ((), ())), preferred_element_type=F32)


def own_place():
    d, s = lax.axis_index("dp"), lax.axis_index("seq")
    return d, s, d // 2, d % 2, s // 2, s % 2


def flip(index, step):
    return index + step * (1 - 2 * ((index // step) % 2))


def remote(src, dst, send, recv, d, s):
    return pltpu.make_async_remote_copy(
        src_ref=src, dst_ref=dst, send_sem=send, recv_sem=recv, device_id=(d, s), device_id_type=MESH
    )


def greet(depth, steps):
    d, s, z, y, x, c = own_place()
    barrier = pltpu.get_barrier_semaphore()

    def signal(d_to, s_to):
        pl.semaphore_signal(barrier, inc=1, device_id=(d_to, s_to), device_id_type=MESH)

    @pl.when(z > 0)
    def _():
        signal(d - 2, s)

    @pl.when(z < depth - 1)
    def _():
        signal(d + 2, s)

    for step in steps:
        signal(flip(d, step), s)
    signal(d, flip(s, 2))
    signal(d, flip(s, 1))
    ends = jnp.where(z > 0, 1, 0) + jnp.where(z < depth - 1, 1, 0)
    pl.semaphore_wait(barrier, ends + len(steps) + 2)


def doubling_steps(count):
    return [1 << k for k in range(count.bit_length() - 1)]


def spread_kernel(dp, kinds, rows, quarter, *refs):
    count = len(rows)
    depth, half = dp // 2, dp // 2
    shard, (small, tokens, upstream) = refs[:count], refs[count : count + 3]
    at_ref = count + 3
    full, (small_full, row, seed) = refs[at_ref : at_ref + count], refs[at_ref + count : at_ref + count + 3]
    at_ref += count + 3
    wide, low = refs[at_ref : at_ref + count], refs[at_ref + count : at_ref + 2 * count]
    (
        load, local, up_s, down_s, y_s, x_s, ca_s, cb_s, yz_r, x_r, ca_r, cb_r, small_s, small_r, tok_l, tok_s, tok_r,
    ) = refs[at_ref + 2 * count :]
    d, s, z, y, x, c = own_place()
    steps = doubling_steps(dp)

    def parts(g):
        if kinds[g] != "cols":
            return [(slice(None), slice(None))]
        n = wide[g].shape[1]
        thirds = 3 if shard[g].shape[1] == 3 * shard[g].shape[0] * dp else 1
        n = n // thirds
        return [
            (pl.ds(pl.multiple_of((2 * t + c) * n, 128), n), slice(t * n, (t + 1) * n)) for t in range(thirds)
        ]

    def active(g, at):
        return True if kinds[g] != "shards" else at // half == c

    def fetches(g):
        return [
            pltpu.make_async_copy(shard[g].at[:, source], wide[g].at[:, target], load.at[g, t])
            for t, (source, target) in enumerate(parts(g))
        ]

    def when(condition, action):
        if condition is True:
            action()
        else:
            pl.when(condition)(action)

    for g in range(count):

        def fetch():
            for copy in fetches(g):
                copy.start()

        when(active(g, d), fetch)

    greet(depth, steps)

    def columns(g):
        if kinds[g] != "share":
            return slice(None)
        n = full[g].shape[1] // 2
        return pl.ds(pl.multiple_of(c * n, 128), n)

    def window(g, at, offset, n):
        m = rows[g] // 3
        place = at if kinds[g] != "shards" else at % half
        return full[g].at[pl.ds(pl.multiple_of(place * rows[g] + offset * m, 16), n * m), columns(g)]

    def own_piece(g):
        m = rows[g] // 3
        return low[g].at[pl.ds(pl.multiple_of(x * m, 16), 2 * m), columns(g)]

    def move(view, send, recv, d_to, s_to, src=None):
        return remote(view if src is None else src, view, send, recv, d_to, s_to)

    def up(g, at, src=None):
        return move(window(g, at, x, 2), up_s.at[g, at], yz_r.at[g, at], d + 2, s, src)

    def down(g, at, src=None):
        return move(window(g, at, x, 2), down_s.at[g, at], yz_r.at[g, at], d - 2, s, src)

    def over_y(g, at, src=None):
        return move(window(g, at, x, 2), y_s.at[g, at], yz_r.at[g, at], flip(d, 1), s, src)

    def over_x(g, at):
        return move(window(g, at, 2 * x, 1), x_s.at[g, at], x_r.at[g, at], d, flip(s, 2))

    def from_x(g, at):
        return move(window(g, at, 2 * (1 - x), 1), x_s.at[g, at], x_r.at[g, at], d, flip(s, 2))

    def core_a(g, at):
        return move(window(g, at, x, 2), ca_s.at[at], ca_r.at[at], d, flip(s, 1))

    def core_b(g, at):
        return move(window(g, at, 2 * (1 - x), 1), cb_s.at[at], cb_r.at[at], d, flip(s, 1))

    def small_copy(k):
        size = 16 << k
        view = small_full.at[pl.ds(pl.multiple_of((d // (1 << k)) * size, 16), size), :]
        return remote(view, view, small_s.at[k], small_r.at[k], flip(d, 1 << k), s)

    def own_local(g):
        place = d if kinds[g] != "shards" else d % half
        view = full[g].at[pl.ds(pl.multiple_of(place * rows[g], 16), rows[g]), :]
        return pltpu.make_async_copy(low[g], view, local.at[g])

    def spot(array, index):
        return array.at[pl.ds(pl.multiple_of(index * quarter, 16), quarter), :]

    def token_copies(t):
        source, target = (tokens, row) if t == 0 else (upstream, seed)
        mine, theirs = spot(target, 2 * x + c), spot(target, 2 * (1 - x) + c)
        return (
            pltpu.make_async_copy(source.at[x], mine, tok_l.at[t]),
            remote(source.at[1 - x], mine, tok_s.at[t, 0], tok_r.at[t, 0], d, flip(s, 2)),
            remote(source.at[x], mine, tok_s.at[t, 1], tok_r.at[t, 1], d, flip(s, 1)),
            remote(theirs, theirs, tok_s.at[t, 2], tok_r.at[t, 2], d, flip(s, 1)),
        )

    def tokens_start(t):
        for copy in token_copies(t)[:3]:
            copy.start()

    def tokens_pass(t):
        token_copies(t)[1].wait_recv()
        token_copies(t)[3].start()

    own_small = pltpu.make_async_copy(small, small_full.at[pl.ds(pl.multiple_of(d * 16, 16), 16), :], local.at[count])
    own_small.start()
    tokens_start(0)

    for g in range(count):

        def begin():
            for copy in fetches(g):
                copy.wait()
            low[g][...] = wide[g][...].astype(BF16)
            src = own_piece(g)

            @pl.when(z < depth - 1)
            def _():
                up(g, d, src).start()

            @pl.when(z > 0)
            def _():
                down(g, d, src).start()

            over_y(g, d, src).start()
            own_local(g).start()

        when(active(g, d), begin)

    own_small.wait()
    tokens_start(1)

    def small_step(k):
        if k:
            small_copy(k - 1).wait()
        if k < len(steps):
            small_copy(k).start()

    def arrived(g, at):
        over_x(g, at).start()
        if kinds[g] == "share":
            core_a(g, at).start()

    def z_arrival(g, r):
        def low_side():
            at = d - 2 * r
            up(g, at).wait_recv()

            @pl.when(z < depth - 1)
            def _():
                up(g, at).start()

            over_y(g, at).start()
            arrived(g, at)

        def high_side():
            at = d + 2 * r
            down(g, at).wait_recv()

            @pl.when(z > 0)
            def _():
                down(g, at).start()

            over_y(g, at).start()
            arrived(g, at)

        pl.when((z >= r) & active(g, d - 2 * r))(low_side)
        pl.when((z + r < depth) & active(g, d + 2 * r))(high_side)

    other = flip(d, 1)

    def y_one(g, at):
        over_y(g, at).wait_recv()
        arrived(g, at)

    def on_shards(g, r, base, action):
        if r == 0:
            when(active(g, base), lambda: action(base))
        else:
            pl.when((z >= r) & active(g, base - 2 * r))(lambda: action(base - 2 * r))
            pl.when((z + r < depth) & active(g, base + 2 * r))(lambda: action(base + 2 * r))

    def x_one(g, at):
        from_x(g, at).wait_recv()
        if kinds[g] == "share":
            core_b(g, at).start()

    for r in range(max(depth + 2, len(steps) + 1)):
        if r <= len(steps):
            small_step(r)
        if r in (1, 2):
            tokens_pass(r - 1)
        for g in range(count):
            if 1 <= r < depth:
                z_arrival(g, r)
            if r < depth:
                on_shards(g, r, other, functools.partial(y_one, g))
            if 1 <= r - 1 < depth:
                on_shards(g, r - 1, d, functools.partial(x_one, g))
            if 0 <= r - 2 < depth:
                on_shards(g, r - 2, other, functools.partial(x_one, g))

    for t in range(2):
        own, to_x, to_core, passed = token_copies(t)
        own.wait()
        to_x.wait_send()
        to_core.wait()
        passed.wait()

    for g in range(count):

        def end():
            own_local(g).wait()

            @pl.when(z < depth - 1)
            def _():
                up(g, d, own_piece(g)).wait_send()

            @pl.when(z > 0)
            def _():
                down(g, d, own_piece(g)).wait_send()

            over_y(g, d, own_piece(g)).wait_send()

        when(active(g, d), end)

        def finish(g, own_column, at):
            if own_column:
                over_y(g, at).wait_send()
            over_x(g, at).wait_send()
            if kinds[g] == "share":
                core_a(g, at).wait()
                core_b(g, at).wait()

        for r in range(depth):
            on_shards(g, r, other, functools.partial(finish, g, False))
            if r:
                on_shards(g, r, d, functools.partial(finish, g, True))
                pl.when((z >= r) & (z < depth - 1) & active(g, d - 2 * r))(lambda: up(g, d - 2 * r).wait_send())
                pl.when((z + r < depth) & (z > 0) & active(g, d + 2 * r))(lambda: down(g, d + 2 * r).wait_send())


def spread(dp, shards, small, tokens, upstream):
    kinds = ["cols", "share", "cols", "shards"]
    rows = [member.shape[0] for member in shards]
    count = len(rows)
    quarter, width = tokens.shape[1:]
    dma = pltpu.SemaphoreType.DMA
    any_space = pl.BlockSpec(memory_space=pl.ANY)
    held = [(m.shape[0], m.shape[1] // 2 if kind == "cols" else m.shape[1]) for m, kind in zip(shards, kinds)]
    whole = [(dp * r // 2 if kind == "shards" else dp * r, n) for (r, n), kind in zip(held, kinds)]
    return pl.pallas_call(
        functools.partial(spread_kernel, dp, kinds, rows, quarter),
        out_shape=[jax.ShapeDtypeStruct(shape, BF16) for shape in whole]
        + [jax.ShapeDtypeStruct((dp * 16, 128), BF16)]
        + [jax.ShapeDtypeStruct((4 * quarter, width), BF16)] * 2,
        in_specs=[any_space] * (count + 3),
        out_specs=[any_space] * (count + 3),
        scratch_shapes=[pltpu.VMEM(shape, F32) for shape in held]
        + [pltpu.VMEM(shape, BF16) for shape in held]
        + [dma((count, 3)), dma((count + 1,))]
        + [dma((count, dp))] * 4
        + [dma((dp,))] * 2
        + [dma((count, dp))] * 2
        + [dma((dp,))] * 2
        + [dma((len(doubling_steps(dp)),))] * 2
        + [dma((2,)), dma((2, 3)), dma((2, 3))],
        compiler_params=pltpu.CompilerParams(
            collective_id=1, has_side_effects=True, vmem_limit_bytes=40 * MIB
        ),
        name="spread_weights",
    )(*shards, small, tokens, upstream)


def fold_kernel(dp, kinds, rows, *refs):
    count = len(rows)
    depth = dp // 2
    grads, small = refs[:count], refs[count]
    outs, small_out = refs[count + 1 : 2 * count + 1], refs[2 * count + 1]
    at_ref = 2 * count + 2
    acc, x_buf, y_buf, u_buf, n_buf, b_buf = [refs[at_ref + k * count : at_ref + (k + 1) * count] for k in range(6)]
    small_buf = refs[at_ref + 6 * count]
    (
        load, x_s, x_r, y_s, y_r, u_s, u_r, n_s, n_r, f_s, f_r, small_s, small_r,
    ) = refs[at_ref + 6 * count + 1 :]
    d, s, z, y, x, c = own_place()
    dp_steps = doubling_steps(dp)

    def layers(g):
        return depth if kinds[g] != "shards" else depth // 2

    def first_layer(g):
        return 0 if kinds[g] != "shards" else c * (depth // 2)

    def layer(g, n):
        if kinds[g] != "shards":
            return sorted(range(depth), key=lambda k: -abs(2 * k - depth + 1))[n]
        return n + c * (depth // 2 - 1 - 2 * n)

    def of(j, own):
        return 2 * j + (y if own else 1 - y)

    def fetch(g, at):
        return pltpu.make_async_copy(grads[g].at[at], acc[g].at[at], load.at[g, at])

    items = [(g, n, own) for g in range(count) for own in (False, True) for n in range(layers(g))]
    for g, n, own in items:
        fetch(g, of(layer(g, n), own)).start()

    greet(depth, dp_steps)

    def span(g, units, n):
        m = rows[g] // 3
        return pl.ds(pl.multiple_of(units * m, 16), n * m)

    def over_x(g, at):
        return remote(
            acc[g].at[at, span(g, 2 * (1 - x), 1), :], x_buf[g].at[at], x_s.at[g, at], x_r.at[g, at], d, flip(s, 2)
        )

    def over_y(g, j):
        return remote(acc[g].at[of(j, False), span(g, x, 2), :], y_buf[g].at[j], y_s.at[g, j], y_r.at[g, j], flip(d, 1), s)

    def up(g, j):
        return remote(acc[g].at[of(j, True), span(g, x, 2), :], u_buf[g].at[j], u_s.at[g, j], u_r.at[g, j], d + 2, s)

    def down(g, j):
        return remote(acc[g].at[of(j, True), span(g, x, 2), :], n_buf[g].at[j], n_s.at[g, j], n_r.at[g, j], d - 2, s)

    def stage_a(g, n, own):
        at = of(layer(g, n), own)
        fetch(g, at).wait()
        over_x(g, at).start()

    def stage_c(g, n, own):
        j = layer(g, n)
        at = of(j, own)
        over_x(g, at).wait_recv()
        third = (at, span(g, 2 * x, 1), slice(None))
        acc[g][third] = acc[g][third] + x_buf[g][at]
        if not own:
            over_y(g, j).start()
        else:
            over_y(g, j).wait_recv()
            pair = (at, span(g, x, 2), slice(None))
            acc[g][pair] = acc[g][pair] + y_buf[g][j]

    def stage_e(g, n, hop):
        j = layer(g, n)
        k = j + first_layer(g)
        pair = (of(j, True), span(g, x, 2), slice(None))

        @pl.when((z == hop) & (k > hop))
        def _():
            if hop:
                up(g, j).wait_recv()
                acc[g][pair] = acc[g][pair] + u_buf[g][j]
            up(g, j).start()

        @pl.when((z == depth - 1 - hop) & (k < depth - 1 - hop))
        def _():
            if hop:
                down(g, j).wait_recv()
                acc[g][pair] = acc[g][pair] + n_buf[g][j]
            down(g, j).start()

    def own_layer(g):
        return z - first_layer(g)

    def ours(g, action):
        if kinds[g] != "shards":
            action()
        else:
            pl.when((z >= first_layer(g)) & (z < first_layer(g) + layers(g)))(action)

    def out_rows(g, units, n):
        return outs[g].at[c, span(g, units, n), :] if kinds[g] != "shards" else outs[g].at[span(g, units, n), :]

    def final_share(g):
        return remote(
            acc[g].at[of(own_layer(g), True), span(g, 2 * x, 1), :], out_rows(g, 2 * x, 1),
            f_s.at[g, 0], f_r.at[g, 0], d, flip(s, 2),
        )

    def final_swap(g):
        return remote(
            acc[g].at[of(own_layer(g), True), span(g, 1, 1), :], b_buf[g], f_s.at[g, 1], f_r.at[g, 1], d, flip(s, 2)
        )

    def final_core(g):
        view = out_rows(g, 0, 3)
        return remote(view, view, f_s.at[g, 2], f_r.at[g, 2], d, flip(s, 1))

    def finish_one(g):
        def run():
            j = own_layer(g)
            at = of(j, True)
            pair = (at, span(g, x, 2), slice(None))

            @pl.when(z > 0)
            def _():
                up(g, j).wait_recv()
                acc[g][pair] = acc[g][pair] + u_buf[g][j]

            @pl.when(z < depth - 1)
            def _():
                down(g, j).wait_recv()
                acc[g][pair] = acc[g][pair] + n_buf[g][j]

            final_share(g).start()
            final_swap(g).start()
            out_rows(g, 2 * x, 1)[...] = acc[g][at, span(g, 2 * x, 1), :]

        ours(g, run)

    def finish_two(g):
        def run():
            final_swap(g).wait_recv()
            out_rows(g, 1, 1)[...] = acc[g][of(own_layer(g), True), span(g, 1, 1), :] + b_buf[g][...]
            final_share(g).wait_recv()
            final_core(g).start()

        ours(g, run)

    small_out[...] = small[...]
    small_partners = [(flip(d, step), s) for step in dp_steps] + [(d, flip(s, 1)), (d, flip(s, 2))]

    def small_copy(k):
        d_to, s_to = small_partners[k]
        return remote(small_out, small_buf.at[k], small_s.at[k], small_r.at[k], d_to, s_to)

    def small_finish(k):
        small_copy(k).wait()
        small_out[...] = small_out[...] + small_buf[k]

    timeline = {}

    def plan(at, action, *args):
        timeline.setdefault(at, []).append((action, args))

    for k in range(len(small_partners)):
        plan(2 * k, lambda k: small_copy(k).start(), k)
        plan(2 * k + 1, small_finish, k)
    for i, (g, n, own) in enumerate(items):
        plan(-1, stage_a, g, n, own)
        plan(i, stage_c, g, n, own)
        if own:
            for hop in range(depth - 1):
                plan(i + 1 + 2 * hop, stage_e, g, n, hop)
            if n == layers(g) - 1:
                plan(i + 2 * depth, finish_one, g)
                plan(i + 2 * depth + 2, finish_two, g)
    for at in sorted(timeline):
        for action, args in timeline[at]:
            action(*args)

    for g in range(count):

        def drain():
            final_share(g).wait_send()
            final_swap(g).wait_send()
            if kinds[g] == "shards":
                final_core(g).wait_send()

        ours(g, drain)
        if kinds[g] == "shards":
            pl.when((z < first_layer(g)) | (z >= first_layer(g) + layers(g)))(lambda: final_core(g).wait_recv())
        else:
            final_core(g).wait()
        for j in range(layers(g)):
            over_x(g, of(j, False)).wait_send()
            over_x(g, of(j, True)).wait_send()
            over_y(g, j).wait_send()
            pl.when(j + first_layer(g) > z)(lambda: up(g, j).wait_send())
            pl.when(j + first_layer(g) < z)(lambda: down(g, j).wait_send())


def fold(dp, grads, small):
    kinds = ["shards", "cols", "cols", "cols"]
    owners = [dp // 2 if kind == "shards" else dp for kind in kinds]
    rows = [m.shape[0] // n for m, n in zip(grads, owners)]
    count, depth = len(rows), dp // 2
    views = [m.reshape(n, r, m.shape[1]) for m, r, n in zip(grads, rows, owners)]
    dma = pltpu.SemaphoreType.DMA
    any_space = pl.BlockSpec(memory_space=pl.ANY)
    vmem = pl.BlockSpec(memory_space=pltpu.VMEM)

    def buffers(lead, part):
        slots = [() if lead is None else (n // lead,) for n in owners]
        return [pltpu.VMEM((*slot, r // 3 * part, m.shape[1]), BF16) for slot, r, m in zip(slots, rows, grads)]

    partners = len(doubling_steps(dp)) + 2
    return pl.pallas_call(
        functools.partial(fold_kernel, dp, kinds, rows),
        out_shape=[
            jax.ShapeDtypeStruct((r, m.shape[1]) if kind == "shards" else (2, r, m.shape[1]), BF16)
            for r, m, kind in zip(rows, grads, kinds)
        ]
        + [jax.ShapeDtypeStruct(small.shape, F32)],
        in_specs=[any_space] * count + [vmem],
        out_specs=[vmem] * (count + 1),
        scratch_shapes=buffers(1, 3)
        + buffers(1, 1)
        + buffers(2, 2)
        + buffers(2, 2)
        + buffers(2, 2)
        + buffers(None, 1)
        + [pltpu.VMEM((partners, *small.shape), F32)]
        + [dma((count, dp))] * 3
        + [dma((count, depth))] * 6
        + [dma((count, 3))] * 2
        + [dma((partners,))] * 2,
        compiler_params=pltpu.CompilerParams(
            collective_id=2, has_side_effects=True, vmem_limit_bytes=50 * MIB
        ),
        name="fold_gradients",
    )(*views, small)


def head_mask():
    return lax.broadcasted_iota(jnp.int32, (1, 2 * HD), 1) < HD


def part_start(part, quarter):
    return quarter * (part * (part + 1) // 2)


def attend_kernel(quarter, total, q_ref, k_ref, v_ref, mixed_ref, probs_ref):
    first = head_mask()
    key_pos = lax.broadcasted_iota(jnp.int32, (4 * quarter, 1), 0)
    key_pos = jnp.where(key_pos < total[0], key_pos, 1 << 20)
    lane = lax.broadcasted_iota(jnp.int32, (1, quarter), 1)
    for part in range(4):
        length = quarter * (part + 1)
        allowed = key_pos[:length] <= lane + part * quarter
        query = q_ref[part * quarter : (part + 1) * quarter] * jnp.asarray(HD**-0.5, BF16)
        sums = []
        for head in range(2):
            mask = first if head == 0 else ~first
            scores = product_back(k_ref[:length], jnp.where(mask, query, jnp.zeros_like(query)))
            scores = jnp.where(allowed, scores, NEG_FILL)
            exponent = jnp.exp(scores - jnp.max(scores, axis=0, keepdims=True))
            probs = (exponent * (1.0 / jnp.sum(exponent, axis=0, keepdims=True))).astype(BF16)
            probs_ref[0, head, part_start(part, quarter) : part_start(part + 1, quarter)] = probs
            sums.append(product_across(probs, v_ref[:length]))
        mixed_ref[part * quarter : (part + 1) * quarter] = jnp.where(first, sums[0], sums[1]).astype(BF16)


def attend(triple, total):
    tokens, width = triple.shape[0], triple.shape[1] // 3
    quarter = tokens // 4
    pairs = width // (2 * HD)
    kept = part_start(4, quarter)

    def block(shift):
        return pl.BlockSpec((tokens, 2 * HD), lambda p, _: (0, p + shift))

    return pl.pallas_call(
        functools.partial(attend_kernel, quarter),
        grid_spec=pltpu.PrefetchScalarGridSpec(
            num_scalar_prefetch=1,
            grid=(pairs,),
            in_specs=[block(0), block(pairs), block(2 * pairs)],
            out_specs=[block(0), pl.BlockSpec((1, 2, kept, quarter), lambda p, _: (p, 0, 0, 0))],
        ),
        out_shape=[
            jax.ShapeDtypeStruct((tokens, width), BF16),
            jax.ShapeDtypeStruct((pairs, 2, kept, quarter), BF16),
        ],
        compiler_params=pltpu.CompilerParams(vmem_limit_bytes=50 * MIB),
        name="attend",
    )(total, triple, triple, triple)


def attend_back_kernel(quarter, q_ref, k_ref, v_ref, g_ref, probs_ref, dq_ref, dk_ref, dv_ref, dkeys, dvalues):
    first = head_mask()
    for part in reversed(range(4)):
        length = quarter * (part + 1)
        rows = slice(part * quarter, (part + 1) * quarter)
        query = q_ref[rows] * jnp.asarray(HD**-0.5, BF16)
        grad = g_ref[rows]
        dq = []
        for head in range(2):
            mask = first if head == 0 else ~first
            own_query = jnp.where(mask, query, jnp.zeros_like(query))
            own_grad = jnp.where(mask, grad, jnp.zeros_like(grad))
            probs = probs_ref[0, head, part_start(part, quarter) : part_start(part + 1, quarter)]
            wide = probs.astype(F32)
            grad_probs = product_back(v_ref[:length], own_grad)
            delta = jnp.sum(wide * grad_probs, axis=0, keepdims=True)
            grad_scores = (wide * (grad_probs - delta)).astype(BF16)
            dv = product(probs, own_grad)
            dk = product(grad_scores, own_query)
            if part == 3 and head == 0:
                dvalues[...] = dv
                dkeys[...] = dk
            else:
                dvalues[:length] += dv
                dkeys[:length] += dk
            dq.append(product_across(grad_scores, k_ref[:length]))
        dq_ref[rows] = (jnp.where(first, dq[0], dq[1]) * HD**-0.5).astype(BF16)
    dk_ref[...] = dkeys[...].astype(BF16)
    dv_ref[...] = dvalues[...].astype(BF16)


def attend_back(triple, grad, probs):
    tokens, width = triple.shape[0], triple.shape[1] // 3
    quarter = tokens // 4
    pairs = width // (2 * HD)

    def block(shift):
        return pl.BlockSpec((tokens, 2 * HD), lambda p: (0, p + shift))

    return pl.pallas_call(
        functools.partial(attend_back_kernel, quarter),
        grid=(pairs,),
        in_specs=[block(0), block(pairs), block(2 * pairs), block(0)]
        + [pl.BlockSpec((1, 2, part_start(4, quarter), quarter), lambda p: (p, 0, 0, 0))],
        out_specs=[block(0)] * 3,
        out_shape=[jax.ShapeDtypeStruct((tokens, width), BF16)] * 3,
        scratch_shapes=[pltpu.VMEM((tokens, 2 * HD), F32)] * 2,
        compiler_params=pltpu.CompilerParams(vmem_limit_bytes=50 * MIB),
        name="attend_back",
    )(triple, triple, triple, grad, probs)


def take(array, index, size, axis):
    return lax.dynamic_slice_in_dim(array, index * size, size, axis)


def gather_plain(matrices, small, tokens, upstream, core, upper):
    triple, attend_full, expand, shrink = [
        lax.all_gather(m.astype(BF16), "dp", axis=0, tiled=True) for m in matrices
    ]
    width = triple.shape[0]
    thirds = triple.reshape(width, 3, width)
    row, seed = [
        jnp.where(upper, m[1], m[0])
        for m in [lax.all_gather(array, "seq", axis=1, tiled=True) for array in (tokens, upstream)]
    ]
    return (
        take(thirds, core, width // 2, 2).reshape(width, -1),
        attend_full,
        take(expand, core, expand.shape[1] // 2, 1),
        take(shrink, core, shrink.shape[0] // 2, 0),
        lax.all_gather(small, "dp", axis=0),
        row,
        seed,
    )


def fold_plain(grads, small, core):
    def by_core(array):
        empty = jnp.zeros_like(array)
        return jnp.stack([jnp.where(core == 0, array, empty), jnp.where(core == 1, array, empty)], axis=1)

    shrink, *others = grads
    wide = jnp.swapaxes(by_core(shrink), 0, 1).reshape(-1, shrink.shape[1])
    arrays = [wide] + [by_core(m) for m in others]
    sums = [lax.psum(lax.psum_scatter(m, "dp", scatter_dimension=0, tiled=True), "seq") for m in arrays]
    sums = [sums[0]] + [jnp.swapaxes(m, 0, 1) for m in sums[1:]]
    return sums, lax.psum(lax.psum_scatter(small, "dp", scatter_dimension=0, tiled=True), "seq").reshape(-1)


def body(
    dp,
    tokens,
    lengths,
    first_gain,
    first_shift,
    triple_weight,
    triple_bias,
    attend_weight,
    attend_bias,
    second_gain,
    second_shift,
    expand_weight,
    expand_bias,
    shrink_weight,
    shrink_bias,
    upstream,
):
    row_count, quarter, width = tokens.shape
    matrices = (triple_weight, attend_weight, expand_weight, shrink_weight)
    vectors = (first_gain, first_shift, triple_bias, attend_bias, second_gain, second_shift, expand_bias, shrink_bias)
    sizes = [member.shape[0] for member in vectors]
    total_small = sum(sizes)
    by_kernel = dp & (dp - 1) == 0 and dp > 2 and all(m.shape[0] % 48 == 0 for m in matrices)
    by_kernel = by_kernel and total_small <= 16 * 128
    place = lax.axis_index("seq")
    upper, core = place // 2 == 1, place % 2
    hidden = expand_weight.shape[1] // 2

    small = jnp.concatenate([member.astype(BF16) for member in vectors])
    if by_kernel:
        small = jnp.pad(small, (0, 16 * 128 - total_small)).reshape(16, 128)
        *weights, small_full, row, seed_low = spread(dp, matrices, small, tokens, upstream)
        small_full = small_full.reshape(dp, 16 * 128)[:, :total_small]
    else:
        *weights, small_full, row, seed_low = gather_plain(matrices, small, tokens, upstream, core, upper)
    floats, at = [], 0
    for size in sizes:
        floats.append(small_full[:, at : at + size].reshape(-1).astype(F32))
        at += size
    gain_one, shift_one, bias_triple, bias_attend, gain_two, shift_two, bias_expand, bias_shrink = floats
    triple_low, attend_low, expand_low, shrink_low = weights

    across = [(k, (k + 2) % 4) for k in range(4)]
    twin = [(k, k + 1 - 2 * (k % 2)) for k in range(4)]

    def halves(partial):
        view = partial.reshape(2, 2, quarter, width)
        mine = jnp.where(core == 0, view[:, 0], view[:, 1])
        theirs = jnp.where(core == 0, view[:, 1], view[:, 0]).astype(BF16)
        return mine + lax.ppermute(theirs, "seq", twin).astype(F32)

    def own_half(array):
        view = array.reshape(2, 2, quarter, width)
        return jnp.where(core == 0, view[:, 0], view[:, 1])

    def give_back(array):
        mine = jnp.where(upper, array[1], array[0])
        theirs = lax.ppermute(jnp.where(upper, array[0], array[1]), "seq", across)
        return jnp.stack([jnp.where(upper, theirs, mine), jnp.where(upper, mine, theirs)])

    def of_core(vector):
        return take(vector, core, vector.shape[0] // 2, 0)

    def spread_out(part):
        empty = jnp.zeros_like(part)
        return jnp.concatenate([jnp.where(core == 0, part, empty), jnp.where(core == 1, part, empty)])

    totals = lengths[:, 0] + lengths[:, 1]
    total = jnp.where(upper, totals[1], totals[0]).reshape(1)

    flat_tokens = row.astype(F32)
    seed = seed_low.astype(F32)
    bias_core = jnp.concatenate(
        [of_core(bias_triple[:width]), jnp.zeros((width // 2,), F32), of_core(bias_triple[width:])]
    )

    normed = layer_norm(flat_tokens, gain_one, shift_one)
    normed_low = normed.astype(BF16)
    triple = (product(normed_low, triple_low) + bias_core).astype(BF16)
    mixed_core, probs = attend(triple, total)
    mixed_other = lax.ppermute(mixed_core, "seq", twin)
    mixed_low = jnp.concatenate(
        [jnp.where(core == 0, mixed_core, mixed_other), jnp.where(core == 0, mixed_other, mixed_core)], axis=1
    )
    resid = flat_tokens + product(mixed_low, attend_low) + bias_attend
    normed_two, second_pull = jax.vjp(layer_norm, resid, gain_two, shift_two)
    normed_two_low = normed_two.astype(BF16)
    activated, gelu_pull = jax.vjp(gelu_tanh, product(normed_two_low, expand_low) + of_core(bias_expand))
    act_low = activated.astype(BF16)

    grad_pre = gelu_pull(product_back(seed_low, shrink_low))[0].astype(BF16)
    partial = product_back(grad_pre, expand_low).astype(BF16)
    other_partial = lax.ppermute(partial, "seq", twin)
    shrink_grad = product_across(act_low, seed_low)
    expand_grad = product_across(normed_two_low, grad_pre)
    result = own_half(resid) + halves(product(act_low, shrink_low)) + bias_shrink
    result = give_back(result.astype(BF16))
    shrink_bias_grad = 0.5 * jnp.sum(seed, axis=0)
    expand_bias_grad = spread_out(jnp.sum(grad_pre.astype(F32), axis=0))
    resid_part, second_gain_grad, second_shift_grad = second_pull(partial.astype(F32) + other_partial.astype(F32))
    grad_resid = seed + resid_part
    grad_branch = grad_resid.astype(BF16)
    attend_grad = product_across(mixed_low, take(grad_branch, core, width // 2, 1))
    attend_bias_grad = 0.5 * jnp.sum(grad_branch.astype(F32), axis=0)
    grad_mixed = product_back(grad_branch, take(attend_low, core, width // 2, 0)).astype(BF16)

    grad_triple = jnp.concatenate(attend_back(triple, grad_mixed, probs), axis=1)
    n_one = halves(product_back(grad_triple, triple_low))
    triple_grad = product_across(normed_low, grad_triple)
    triple_sums = jnp.sum(grad_triple.astype(F32), axis=0)
    triple_bias_grad = jnp.concatenate([spread_out(triple_sums[: width // 2]), spread_out(triple_sums[width:])])
    _, first_pull = jax.vjp(layer_norm, own_half(flat_tokens), gain_one, shift_one)
    flat_grad, first_gain_grad, first_shift_grad = first_pull(n_one)
    tokens_grad = give_back((own_half(grad_resid) + flat_grad).astype(BF16))

    big = [member.astype(BF16) for member in (shrink_grad, expand_grad, attend_grad, triple_grad)]
    small_grads = (
        first_gain_grad, first_shift_grad, triple_bias_grad, attend_bias_grad,
        0.5 * second_gain_grad, 0.5 * second_shift_grad, expand_bias_grad, shrink_bias_grad,
    )
    flat_small = jnp.concatenate([g.reshape(dp, -1) for g in small_grads], axis=1)
    if by_kernel:
        *sums, small_sum = fold(dp, big, flat_small.reshape(-1, 128))
        own_small = lax.dynamic_index_in_dim(small_sum.reshape(dp, -1), lax.axis_index("dp"), 0, keepdims=False)
    else:
        sums, own_small = fold_plain(big, flat_small, core)
    shrink_sum, expand_sum, attend_sum, triple_sum = [member.astype(F32) for member in sums]
    triple_sum = triple_sum.reshape(2, -1, 3, width // 2).transpose(1, 2, 0, 3).reshape(-1, 3 * width)
    expand_sum, attend_sum = [m.transpose(1, 0, 2).reshape(m.shape[1], -1) for m in (expand_sum, attend_sum)]
    small_out, at = [], 0
    for size in sizes:
        small_out.append(own_small[at : at + size])
        at += size
    return (
        result,
        tokens_grad,
        small_out[0],
        small_out[1],
        triple_sum,
        small_out[2],
        attend_sum,
        small_out[3],
        small_out[4],
        small_out[5],
        expand_sum,
        small_out[6],
        shrink_sum,
        small_out[7],
    )


def solution(mesh):
    return jax.shard_map(
        functools.partial(body, mesh.shape["dp"]),
        mesh=mesh,
        in_specs=(
            P("dp", "seq", None),
            P("dp", None),
            P("dp"),
            P("dp"),
            P("dp", None),
            P("dp"),
            P("dp", None),
            P("dp"),
            P("dp"),
            P("dp"),
            P("dp", None),
            P("dp"),
            P("dp", None),
            P("dp"),
            P("dp", "seq", None),
        ),
        out_specs=(
            P("dp", "seq", None),
            P("dp", "seq", None),
            P("dp"),
            P("dp"),
            P("dp", None),
            P("dp"),
            P("dp", None),
            P("dp"),
            P("dp"),
            P("dp"),
            P("dp", None),
            P("dp"),
            P("dp", None),
            P("dp"),
        ),
        check_vma=False,
    )
```

```python
import functools

import jax
import jax.numpy as jnp
from jax import lax
from jax.experimental import pallas as pl
from jax.experimental.pallas import tpu as pltpu
from jax.sharding import PartitionSpec as P

H = 12
HD = 64

EPSILON = 1e-05
NEG_FILL = -1e30
MESH = pl.DeviceIdType.MESH
MIB = 1024 * 1024
BF16 = jnp.bfloat16
F32 = jnp.float32


def layer_norm(values, norm_gain, norm_shift):
    center = values - jnp.mean(values, axis=-1, keepdims=True)
    spread = jnp.mean(center * center, axis=-1, keepdims=True)
    return center * lax.rsqrt(spread + EPSILON) * norm_gain + norm_shift


def gelu_tanh(values):
    inside = 0.7978845608028654 * (values + 0.044715 * values * values * values)
    return 0.5 * values * (1.0 + jnp.tanh(inside))


def product(operand, other):
    return jnp.dot(operand, other, preferred_element_type=F32)


def product_across(operand, other):
    return lax.dot_general(operand, other, (((0,), (0,)), ((), ())), preferred_element_type=F32)


def product_back(operand, other):
    return lax.dot_general(operand, other, (((1,), (1,)), ((), ())), preferred_element_type=F32)


def own_place():
    d, s = lax.axis_index("dp"), lax.axis_index("seq")
    return d, s, d // 2, d % 2, s // 2, s % 2


def flip(index, step):
    return index + step * (1 - 2 * ((index // step) % 2))


def remote(src, dst, send, recv, d, s):
    return pltpu.make_async_remote_copy(
        src_ref=src, dst_ref=dst, send_sem=send, recv_sem=recv, device_id=(d, s), device_id_type=MESH
    )


def greet(depth, steps):
    d, s, z, y, x, c = own_place()
    barrier = pltpu.get_barrier_semaphore()

    def signal(d_to, s_to):
        pl.semaphore_signal(barrier, inc=1, device_id=(d_to, s_to), device_id_type=MESH)

    @pl.when(z > 0)
    def _():
        signal(d - 2, s)

    @pl.when(z < depth - 1)
    def _():
        signal(d + 2, s)

    for step in steps:
        signal(flip(d, step), s)
    signal(d, flip(s, 2))
    signal(d, flip(s, 1))
    ends = jnp.where(z > 0, 1, 0) + jnp.where(z < depth - 1, 1, 0)
    pl.semaphore_wait(barrier, ends + len(steps) + 2)


def doubling_steps(count):
    return [1 << k for k in range(count.bit_length() - 1)]


class Plan:
    def __init__(self):
        self.steps = []

    def add(self, at, action, *args):
        self.steps.append((at, len(self.steps), action, args))

    def run(self):
        for _, _, action, args in sorted(self.steps, key=lambda step: step[:2]):
            action(*args)


def spread_kernel(dp, kinds, rows, quarter, *refs):
    count = len(rows)
    depth, half = dp // 2, dp // 2
    shard, (small, tokens) = refs[:count], refs[count : count + 2]
    at_ref = count + 2
    full, (small_full, row) = refs[at_ref : at_ref + count], refs[at_ref + count : at_ref + count + 2]
    at_ref += count + 2
    wide, low = refs[at_ref : at_ref + count], refs[at_ref + count : at_ref + 2 * count]
    (
        load, local, up_s, down_s, y_s, x_s, ca_s, cb_s, yz_r, x_r, ca_r, cb_r, small_s, small_r, tok_l, tok_s, tok_r,
    ) = refs[at_ref + 2 * count :]
    d, s, z, y, x, c = own_place()
    steps = doubling_steps(dp)

    def parts(g):
        if kinds[g] != "cols":
            return [(slice(None), slice(None))]
        n = wide[g].shape[1]
        thirds = 3 if shard[g].shape[1] == 3 * shard[g].shape[0] * dp else 1
        n = n // thirds
        return [
            (pl.ds(pl.multiple_of((2 * t + c) * n, 128), n), slice(t * n, (t + 1) * n)) for t in range(thirds)
        ]

    def active(g, at):
        return True if kinds[g] != "shards" else at // half == c

    def fetches(g):
        return [
            pltpu.make_async_copy(shard[g].at[:, source], wide[g].at[:, target], load.at[g, t])
            for t, (source, target) in enumerate(parts(g))
        ]

    def when(condition, action):
        if condition is True:
            action()
        else:
            pl.when(condition)(action)

    for g in range(count):

        def fetch():
            for copy in fetches(g):
                copy.start()

        when(active(g, d), fetch)

    greet(depth, steps)

    def columns(g):
        if kinds[g] != "share":
            return slice(None)
        n = full[g].shape[1] // 2
        return pl.ds(pl.multiple_of(c * n, 128), n)

    def window(g, at, offset, n):
        m = rows[g] // 3
        place = at if kinds[g] != "shards" else at % half
        return full[g].at[pl.ds(pl.multiple_of(place * rows[g] + offset * m, 16), n * m), columns(g)]

    def own_piece(g):
        m = rows[g] // 3
        return low[g].at[pl.ds(pl.multiple_of(x * m, 16), 2 * m), columns(g)]

    def move(view, send, recv, d_to, s_to, src=None):
        return remote(view if src is None else src, view, send, recv, d_to, s_to)

    def up(g, at, src=None):
        return move(window(g, at, x, 2), up_s.at[g, at], yz_r.at[g, at], d + 2, s, src)

    def down(g, at, src=None):
        return move(window(g, at, x, 2), down_s.at[g, at], yz_r.at[g, at], d - 2, s, src)

    def over_y(g, at, src=None):
        return move(window(g, at, x, 2), y_s.at[g, at], yz_r.at[g, at], flip(d, 1), s, src)

    def over_x(g, at):
        return move(window(g, at, 2 * x, 1), x_s.at[g, at], x_r.at[g, at], d, flip(s, 2))

    def from_x(g, at):
        return move(window(g, at, 2 * (1 - x), 1), x_s.at[g, at], x_r.at[g, at], d, flip(s, 2))

    def core_a(g, at):
        return move(window(g, at, x, 2), ca_s.at[at], ca_r.at[at], d, flip(s, 1))

    def core_b(g, at):
        return move(window(g, at, 2 * (1 - x), 1), cb_s.at[at], cb_r.at[at], d, flip(s, 1))

    def small_copy(k):
        size = 16 << k
        view = small_full.at[pl.ds(pl.multiple_of((d // (1 << k)) * size, 16), size), :]
        return remote(view, view, small_s.at[k], small_r.at[k], flip(d, 1 << k), s)

    def own_local(g):
        place = d if kinds[g] != "shards" else d % half
        view = full[g].at[pl.ds(pl.multiple_of(place * rows[g], 16), rows[g]), :]
        return pltpu.make_async_copy(low[g], view, local.at[g])

    def spot(array, index):
        return array.at[pl.ds(pl.multiple_of(index * quarter, 16), quarter), :]

    mine, theirs = spot(row, 2 * x + c), spot(row, 2 * (1 - x) + c)
    own_tokens = pltpu.make_async_copy(tokens.at[x], mine, tok_l.at[0])
    tokens_over_x = remote(tokens.at[1 - x], mine, tok_s.at[0], tok_r.at[0], d, flip(s, 2))
    tokens_to_core = remote(tokens.at[x], mine, tok_s.at[1], tok_r.at[1], d, flip(s, 1))
    tokens_passed = remote(theirs, theirs, tok_s.at[2], tok_r.at[2], d, flip(s, 1))

    def tokens_pass():
        tokens_over_x.wait_recv()
        tokens_passed.start()

    own_small = pltpu.make_async_copy(small, small_full.at[pl.ds(pl.multiple_of(d * 16, 16), 16), :], local.at[count])
    own_small.start()
    own_tokens.start()
    tokens_over_x.start()
    tokens_to_core.start()

    def begin(g):
        for copy in fetches(g):
            copy.wait()
        low[g][...] = wide[g][...].astype(BF16)
        src = own_piece(g)
        pl.when(z < depth - 1)(lambda: up(g, d, src).start())
        pl.when(z > 0)(lambda: down(g, d, src).start())
        over_y(g, d, src).start()
        own_local(g).start()

    def small_step(k):
        if k == 0:
            own_small.wait()
        else:
            small_copy(k - 1).wait()
        if k < len(steps):
            small_copy(k).start()

    def arrived(g, at):
        over_x(g, at).start()
        if kinds[g] == "share":
            core_a(g, at).start()

    def z_arrival(g, r):
        def low_side():
            at = d - 2 * r
            up(g, at).wait_recv()

            @pl.when(z < depth - 1)
            def _():
                up(g, at).start()

            over_y(g, at).start()
            arrived(g, at)

        def high_side():
            at = d + 2 * r
            down(g, at).wait_recv()

            @pl.when(z > 0)
            def _():
                down(g, at).start()

            over_y(g, at).start()
            arrived(g, at)

        pl.when((z >= r) & active(g, d - 2 * r))(low_side)
        pl.when((z + r < depth) & active(g, d + 2 * r))(high_side)

    other = flip(d, 1)

    def y_one(g, at):
        over_y(g, at).wait_recv()
        arrived(g, at)

    def on_shards(g, r, base, action):
        if r == 0:
            when(active(g, base), lambda: action(base))
        else:
            pl.when((z >= r) & active(g, base - 2 * r))(lambda: action(base - 2 * r))
            pl.when((z + r < depth) & active(g, base + 2 * r))(lambda: action(base + 2 * r))

    def x_one(g, at):
        from_x(g, at).wait_recv()
        if kinds[g] == "share":
            core_b(g, at).start()

    plan = Plan()
    for k in range(len(steps) + 1):
        plan.add(2 * k, small_step, k)
    plan.add(8, tokens_pass)
    first = 0.0
    for g in range(count):
        piece = rows[g] * wide[g].shape[1] * 2 / 50e3 * 2 / 3
        if kinds[g] != "cols":
            piece /= 2
        hop = piece + 1.5
        plan.add(first, when, active(g, d), functools.partial(begin, g))
        for r in range(depth):
            if r:
                plan.add(first + hop * r, z_arrival, g, r)
                plan.add(first + hop * r + 0.5 * piece + 1.5, on_shards, g, r, d, functools.partial(x_one, g))
            plan.add(first + hop * (r + 1), on_shards, g, r, other, functools.partial(y_one, g))
            plan.add(
                first + hop * (r + 1) + 0.5 * piece + 1.5, on_shards, g, r, other, functools.partial(x_one, g)
            )
        first += 4 * piece if g == count - 1 else 3 * piece
    plan.run()

    own_tokens.wait()
    tokens_over_x.wait_send()
    tokens_to_core.wait()
    tokens_passed.wait()

    for g in range(count):

        def end():
            own_local(g).wait()

            @pl.when(z < depth - 1)
            def _():
                up(g, d, own_piece(g)).wait_send()

            @pl.when(z > 0)
            def _():
                down(g, d, own_piece(g)).wait_send()

            over_y(g, d, own_piece(g)).wait_send()

        when(active(g, d), end)

        def finish(g, own_column, at):
            if own_column:
                over_y(g, at).wait_send()
            over_x(g, at).wait_send()
            if kinds[g] == "share":
                core_a(g, at).wait()
                core_b(g, at).wait()

        for r in range(depth):
            on_shards(g, r, other, functools.partial(finish, g, False))
            if r:
                on_shards(g, r, d, functools.partial(finish, g, True))
                pl.when((z >= r) & (z < depth - 1) & active(g, d - 2 * r))(lambda: up(g, d - 2 * r).wait_send())
                pl.when((z + r < depth) & (z > 0) & active(g, d + 2 * r))(lambda: down(g, d + 2 * r).wait_send())


def spread(dp, shards, small, tokens):
    kinds = ["cols", "share", "cols", "shards"]
    rows = [member.shape[0] for member in shards]
    count = len(rows)
    quarter, width = tokens.shape[1:]
    dma = pltpu.SemaphoreType.DMA
    any_space = pl.BlockSpec(memory_space=pl.ANY)
    held = [(m.shape[0], m.shape[1] // 2 if kind == "cols" else m.shape[1]) for m, kind in zip(shards, kinds)]
    whole = [(dp * r // 2 if kind == "shards" else dp * r, n) for (r, n), kind in zip(held, kinds)]
    return pl.pallas_call(
        functools.partial(spread_kernel, dp, kinds, rows, quarter),
        out_shape=[jax.ShapeDtypeStruct(shape, BF16) for shape in whole]
        + [jax.ShapeDtypeStruct((dp * 16, 128), F32), jax.ShapeDtypeStruct((4 * quarter, width), BF16)],
        in_specs=[any_space] * (count + 2),
        out_specs=[any_space] * (count + 2),
        scratch_shapes=[pltpu.VMEM(shape, F32) for shape in held]
        + [pltpu.VMEM(shape, BF16) for shape in held]
        + [dma((count, 3)), dma((count + 1,))]
        + [dma((count, dp))] * 4
        + [dma((dp,))] * 2
        + [dma((count, dp))] * 2
        + [dma((dp,))] * 2
        + [dma((len(doubling_steps(dp)),))] * 2
        + [dma((1,)), dma((3,)), dma((3,))],
        compiler_params=pltpu.CompilerParams(
            collective_id=1, has_side_effects=True, vmem_limit_bytes=60 * MIB
        ),
        name="spread_weights",
    )(*shards, small, tokens)


def fold_kernel(dp, kinds, rows, *refs):
    count = len(rows)
    depth = dp // 2
    grads, small = refs[:count], refs[count]
    outs, small_out = refs[count + 1 : 2 * count + 1], refs[2 * count + 1]
    at_ref = 2 * count + 2
    acc, x_buf, y_buf, u_buf, n_buf, b_buf = [refs[at_ref + k * count : at_ref + (k + 1) * count] for k in range(6)]
    small_buf = refs[at_ref + 6 * count]
    (
        load, x_s, x_r, y_s, y_r, u_s, u_r, n_s, n_r, f_s, f_r, small_s, small_r,
    ) = refs[at_ref + 6 * count + 1 :]
    d, s, z, y, x, c = own_place()
    dp_steps = doubling_steps(dp)

    def layers(g):
        return depth if kinds[g] != "shards" else depth // 2

    def first_layer(g):
        return 0 if kinds[g] != "shards" else c * (depth // 2)

    def layer(g, n):
        if kinds[g] != "shards":
            return sorted(range(depth), key=lambda k: -abs(2 * k - depth + 1))[n]
        return n + c * (depth // 2 - 1 - 2 * n)

    def of(j, own):
        return 2 * j + (y if own else 1 - y)

    def fetch(g, at):
        return pltpu.make_async_copy(grads[g].at[at], acc[g].at[at], load.at[g, at])

    items = [(g, n, own) for g in range(count) for own in (False, True) for n in range(layers(g))]
    for g, n, own in items:
        fetch(g, of(layer(g, n), own)).start()

    greet(depth, dp_steps)

    def span(g, units, n):
        m = rows[g] // 3
        return pl.ds(pl.multiple_of(units * m, 16), n * m)

    def over_x(g, at):
        return remote(
            acc[g].at[at, span(g, 2 * (1 - x), 1), :], x_buf[g].at[at], x_s.at[g, at], x_r.at[g, at], d, flip(s, 2)
        )

    def over_y(g, j):
        return remote(acc[g].at[of(j, False), span(g, x, 2), :], y_buf[g].at[j], y_s.at[g, j], y_r.at[g, j], flip(d, 1), s)

    def up(g, j):
        return remote(acc[g].at[of(j, True), span(g, x, 2), :], u_buf[g].at[j], u_s.at[g, j], u_r.at[g, j], d + 2, s)

    def down(g, j):
        return remote(acc[g].at[of(j, True), span(g, x, 2), :], n_buf[g].at[j], n_s.at[g, j], n_r.at[g, j], d - 2, s)

    def stage_a(g, n, own):
        at = of(layer(g, n), own)
        fetch(g, at).wait()
        over_x(g, at).start()

    def stage_c(g, n, own):
        j = layer(g, n)
        at = of(j, own)
        over_x(g, at).wait_recv()
        third = (at, span(g, 2 * x, 1), slice(None))
        acc[g][third] = acc[g][third] + x_buf[g][at]
        if not own:
            over_y(g, j).start()
        else:
            over_y(g, j).wait_recv()
            pair = (at, span(g, x, 2), slice(None))
            acc[g][pair] = acc[g][pair] + y_buf[g][j]

    def stage_e(g, n, hop):
        j = layer(g, n)
        k = j + first_layer(g)
        pair = (of(j, True), span(g, x, 2), slice(None))

        @pl.when((z == hop) & (k > hop))
        def _():
            if hop:
                up(g, j).wait_recv()
                acc[g][pair] = acc[g][pair] + u_buf[g][j]
            up(g, j).start()

        @pl.when((z == depth - 1 - hop) & (k < depth - 1 - hop))
        def _():
            if hop:
                down(g, j).wait_recv()
                acc[g][pair] = acc[g][pair] + n_buf[g][j]
            down(g, j).start()

    def own_layer(g):
        return z - first_layer(g)

    def ours(g, action):
        if kinds[g] != "shards":
            action()
        else:
            pl.when((z >= first_layer(g)) & (z < first_layer(g) + layers(g)))(action)

    def out_rows(g, units, n):
        return outs[g].at[c, span(g, units, n), :] if kinds[g] != "shards" else outs[g].at[span(g, units, n), :]

    def final_share(g):
        return remote(
            acc[g].at[of(own_layer(g), True), span(g, 2 * x, 1), :], out_rows(g, 2 * x, 1),
            f_s.at[g, 0], f_r.at[g, 0], d, flip(s, 2),
        )

    def final_swap(g):
        return remote(
            acc[g].at[of(own_layer(g), True), span(g, 1, 1), :], b_buf[g], f_s.at[g, 1], f_r.at[g, 1], d, flip(s, 2)
        )

    def final_core(g):
        view = out_rows(g, 0, 3)
        return remote(view, view, f_s.at[g, 2], f_r.at[g, 2], d, flip(s, 1))

    def finish_one(g):
        def run():
            j = own_layer(g)
            at = of(j, True)
            pair = (at, span(g, x, 2), slice(None))

            @pl.when(z > 0)
            def _():
                up(g, j).wait_recv()
                acc[g][pair] = acc[g][pair] + u_buf[g][j]

            @pl.when(z < depth - 1)
            def _():
                down(g, j).wait_recv()
                acc[g][pair] = acc[g][pair] + n_buf[g][j]

            final_share(g).start()
            final_swap(g).start()
            out_rows(g, 2 * x, 1)[...] = acc[g][at, span(g, 2 * x, 1), :]

        ours(g, run)

    def finish_two(g):
        def run():
            final_swap(g).wait_recv()
            out_rows(g, 1, 1)[...] = acc[g][of(own_layer(g), True), span(g, 1, 1), :] + b_buf[g][...]
            final_share(g).wait_recv()
            final_core(g).start()

        ours(g, run)

    small_out[...] = small[...]
    small_partners = [(flip(d, step), s) for step in dp_steps] + [(d, flip(s, 1)), (d, flip(s, 2))]

    def small_copy(k):
        d_to, s_to = small_partners[k]
        return remote(small_out, small_buf.at[k], small_s.at[k], small_r.at[k], d_to, s_to)

    def small_finish(k):
        small_copy(k).wait()
        small_out[...] = small_out[...] + small_buf[k]

    plan = Plan()
    for k in range(len(small_partners)):
        plan.add(4 * k, lambda k: small_copy(k).start(), k)
        plan.add(4 * k + 4, small_finish, k)
    done = 0.0
    for g, n, own in items:
        unit = rows[g] * grads[g].shape[2] * 2 / 50e3 / 3
        plan.add(done - 4.0, stage_a, g, n, own)
        done += unit
        plan.add(done, stage_c, g, n, own)
        if own:
            for hop in range(depth - 1):
                plan.add(done + 0.5 + (2 * unit + 1.5) * hop, stage_e, g, n, hop)
            if n == layers(g) - 1:
                plan.add(done + 0.5 + (2 * unit + 1.5) * (depth - 1), finish_one, g)
                plan.add(done + 2.5 + (2 * unit + 1.5) * (depth - 1) + unit, finish_two, g)
    plan.run()

    for g in range(count):

        def drain():
            final_share(g).wait_send()
            final_swap(g).wait_send()
            if kinds[g] == "shards":
                final_core(g).wait_send()

        ours(g, drain)
        if kinds[g] == "shards":
            pl.when((z < first_layer(g)) | (z >= first_layer(g) + layers(g)))(lambda: final_core(g).wait_recv())
        else:
            final_core(g).wait()
        for j in range(layers(g)):
            over_x(g, of(j, False)).wait_send()
            over_x(g, of(j, True)).wait_send()
            over_y(g, j).wait_send()
            pl.when(j + first_layer(g) > z)(lambda: up(g, j).wait_send())
            pl.when(j + first_layer(g) < z)(lambda: down(g, j).wait_send())


def fold(dp, grads, small):
    kinds = ["shards", "cols", "cols", "cols"]
    owners = [dp // 2 if kind == "shards" else dp for kind in kinds]
    rows = [m.shape[0] // n for m, n in zip(grads, owners)]
    count, depth = len(rows), dp // 2
    views = [m.reshape(n, r, m.shape[1]) for m, r, n in zip(grads, rows, owners)]
    dma = pltpu.SemaphoreType.DMA
    any_space = pl.BlockSpec(memory_space=pl.ANY)
    vmem = pl.BlockSpec(memory_space=pltpu.VMEM)

    def buffers(lead, part):
        slots = [() if lead is None else (n // lead,) for n in owners]
        return [pltpu.VMEM((*slot, r // 3 * part, m.shape[1]), BF16) for slot, r, m in zip(slots, rows, grads)]

    partners = len(doubling_steps(dp)) + 2
    return pl.pallas_call(
        functools.partial(fold_kernel, dp, kinds, rows),
        out_shape=[
            jax.ShapeDtypeStruct((r, m.shape[1]) if kind == "shards" else (2, r, m.shape[1]), BF16)
            for r, m, kind in zip(rows, grads, kinds)
        ]
        + [jax.ShapeDtypeStruct(small.shape, F32)],
        in_specs=[any_space] * count + [vmem],
        out_specs=[vmem] * (count + 1),
        scratch_shapes=buffers(1, 3)
        + buffers(1, 1)
        + buffers(2, 2)
        + buffers(2, 2)
        + buffers(2, 2)
        + buffers(None, 1)
        + [pltpu.VMEM((partners, *small.shape), F32)]
        + [dma((count, dp))] * 3
        + [dma((count, depth))] * 6
        + [dma((count, 3))] * 2
        + [dma((partners,))] * 2,
        compiler_params=pltpu.CompilerParams(
            collective_id=2, has_side_effects=True, vmem_limit_bytes=60 * MIB
        ),
        name="fold_gradients",
    )(*views, small)


def head_mask():
    return lax.broadcasted_iota(jnp.int32, (1, 2 * HD), 1) < HD


def part_start(part, quarter):
    return quarter * (part * (part + 1) // 2)


def attend_kernel(quarter, total, q_ref, k_ref, v_ref, mixed_ref, probs_ref):
    first = head_mask()
    key_pos = lax.broadcasted_iota(jnp.int32, (4 * quarter, 1), 0)
    key_pos = jnp.where(key_pos < total[0], key_pos, 1 << 20)
    lane = lax.broadcasted_iota(jnp.int32, (1, quarter), 1)
    for part in range(4):
        length = quarter * (part + 1)
        allowed = key_pos[:length] <= lane + part * quarter
        query = q_ref[part * quarter : (part + 1) * quarter] * jnp.asarray(HD**-0.5, BF16)
        sums = []
        for head in range(2):
            mask = first if head == 0 else ~first
            scores = product_back(k_ref[:length], jnp.where(mask, query, jnp.zeros_like(query)))
            scores = jnp.where(allowed, scores, NEG_FILL)
            exponent = jnp.exp(scores - jnp.max(scores, axis=0, keepdims=True))
            probs = (exponent * (1.0 / jnp.sum(exponent, axis=0, keepdims=True))).astype(BF16)
            probs_ref[0, head, part_start(part, quarter) : part_start(part + 1, quarter)] = probs
            sums.append(product_across(probs, v_ref[:length]))
        mixed_ref[part * quarter : (part + 1) * quarter] = jnp.where(first, sums[0], sums[1]).astype(BF16)


def attend(triple, total):
    tokens, width = triple.shape[0], triple.shape[1] // 3
    quarter = tokens // 4
    pairs = width // (2 * HD)
    kept = part_start(4, quarter)

    def block(shift):
        return pl.BlockSpec((tokens, 2 * HD), lambda p, _: (0, p + shift))

    return pl.pallas_call(
        functools.partial(attend_kernel, quarter),
        grid_spec=pltpu.PrefetchScalarGridSpec(
            num_scalar_prefetch=1,
            grid=(pairs,),
            in_specs=[block(0), block(pairs), block(2 * pairs)],
            out_specs=[block(0), pl.BlockSpec((1, 2, kept, quarter), lambda p, _: (p, 0, 0, 0))],
        ),
        out_shape=[
            jax.ShapeDtypeStruct((tokens, width), BF16),
            jax.ShapeDtypeStruct((pairs, 2, kept, quarter), BF16),
        ],
        compiler_params=pltpu.CompilerParams(vmem_limit_bytes=50 * MIB),
        name="attend",
    )(total, triple, triple, triple)


def attend_back_kernel(quarter, q_ref, k_ref, v_ref, g_ref, probs_ref, dq_ref, dk_ref, dv_ref, dkeys, dvalues):
    first = head_mask()
    for part in reversed(range(4)):
        length = quarter * (part + 1)
        rows = slice(part * quarter, (part + 1) * quarter)
        query = q_ref[rows] * jnp.asarray(HD**-0.5, BF16)
        grad = g_ref[rows]
        dq = []
        for head in range(2):
            mask = first if head == 0 else ~first
            own_query = jnp.where(mask, query, jnp.zeros_like(query))
            own_grad = jnp.where(mask, grad, jnp.zeros_like(grad))
            probs = probs_ref[0, head, part_start(part, quarter) : part_start(part + 1, quarter)]
            wide = probs.astype(F32)
            grad_probs = product_back(v_ref[:length], own_grad)
            delta = jnp.sum(wide * grad_probs, axis=0, keepdims=True)
            grad_scores = (wide * (grad_probs - delta)).astype(BF16)
            dv = product(probs, own_grad)
            dk = product(grad_scores, own_query)
            if part == 3 and head == 0:
                dvalues[...] = dv
                dkeys[...] = dk
            else:
                dvalues[:length] += dv
                dkeys[:length] += dk
            dq.append(product_across(grad_scores, k_ref[:length]))
        dq_ref[rows] = (jnp.where(first, dq[0], dq[1]) * HD**-0.5).astype(BF16)
    dk_ref[...] = dkeys[...].astype(BF16)
    dv_ref[...] = dvalues[...].astype(BF16)


def attend_back(triple, grad, probs):
    tokens, width = triple.shape[0], triple.shape[1] // 3
    quarter = tokens // 4
    pairs = width // (2 * HD)

    def block(shift):
        return pl.BlockSpec((tokens, 2 * HD), lambda p: (0, p + shift))

    return pl.pallas_call(
        functools.partial(attend_back_kernel, quarter),
        grid=(pairs,),
        in_specs=[block(0), block(pairs), block(2 * pairs), block(0)]
        + [pl.BlockSpec((1, 2, part_start(4, quarter), quarter), lambda p: (p, 0, 0, 0))],
        out_specs=[block(0)] * 3,
        out_shape=[jax.ShapeDtypeStruct((tokens, width), BF16)] * 3,
        scratch_shapes=[pltpu.VMEM((tokens, 2 * HD), F32)] * 2,
        compiler_params=pltpu.CompilerParams(vmem_limit_bytes=50 * MIB),
        name="attend_back",
    )(triple, triple, triple, grad, probs)


def take(array, index, size, axis):
    return lax.dynamic_slice_in_dim(array, index * size, size, axis)


def gather_plain(matrices, small, tokens, core, upper):
    triple, attend_full, expand, shrink = [
        lax.all_gather(m.astype(BF16), "dp", axis=0, tiled=True) for m in matrices
    ]
    width = triple.shape[0]
    thirds = triple.reshape(width, 3, width)
    row = lax.all_gather(tokens, "seq", axis=1, tiled=True)
    return (
        take(thirds, core, width // 2, 2).reshape(width, -1),
        attend_full,
        take(expand, core, expand.shape[1] // 2, 1),
        take(shrink, core, shrink.shape[0] // 2, 0),
        lax.all_gather(small, "dp", axis=0),
        jnp.where(upper, row[1], row[0]),
    )


def fold_plain(grads, small, core):
    def by_core(array):
        empty = jnp.zeros_like(array)
        return jnp.stack([jnp.where(core == 0, array, empty), jnp.where(core == 1, array, empty)], axis=1)

    shrink, *others = grads
    wide = jnp.swapaxes(by_core(shrink), 0, 1).reshape(-1, shrink.shape[1])
    arrays = [wide] + [by_core(m) for m in others]
    sums = [lax.psum(lax.psum_scatter(m, "dp", scatter_dimension=0, tiled=True), "seq") for m in arrays]
    sums = [sums[0]] + [jnp.swapaxes(m, 0, 1) for m in sums[1:]]
    return sums, lax.psum(lax.psum_scatter(small, "dp", scatter_dimension=0, tiled=True), "seq").reshape(-1)


def body(
    dp,
    tokens,
    lengths,
    first_gain,
    first_shift,
    triple_weight,
    triple_bias,
    attend_weight,
    attend_bias,
    second_gain,
    second_shift,
    expand_weight,
    expand_bias,
    shrink_weight,
    shrink_bias,
    upstream,
):
    row_count, quarter, width = tokens.shape
    matrices = (triple_weight, attend_weight, expand_weight, shrink_weight)
    vectors = (first_gain, first_shift, triple_bias, attend_bias, second_gain, second_shift, expand_bias, shrink_bias)
    sizes = [member.shape[0] for member in vectors]
    total_small = sum(sizes)
    by_kernel = dp & (dp - 1) == 0 and dp > 2 and all(m.shape[0] % 48 == 0 for m in matrices)
    by_kernel = by_kernel and total_small <= 16 * 128
    place = lax.axis_index("seq")
    upper, core = place // 2 == 1, place % 2
    hidden = expand_weight.shape[1] // 2

    small = jnp.concatenate(vectors)
    if by_kernel:
        small = jnp.pad(small, (0, 16 * 128 - total_small)).reshape(16, 128)
        *weights, small_full, row = spread(dp, matrices, small, tokens)
        small_full = small_full.reshape(dp, 16 * 128)[:, :total_small]
        upstream, small_full = lax.optimization_barrier((upstream, small_full))
    else:
        *weights, small_full, row = gather_plain(matrices, small, tokens, core, upper)
    floats, at = [], 0
    for size in sizes:
        floats.append(small_full[:, at : at + size].reshape(-1).astype(BF16).astype(F32))
        at += size
    gain_one, shift_one, bias_triple, bias_attend, gain_two, shift_two, bias_expand, bias_shrink = floats
    triple_low, attend_low, expand_low, shrink_low = weights

    across = [(k, (k + 2) % 4) for k in range(4)]
    twin = [(k, k + 1 - 2 * (k % 2)) for k in range(4)]

    def halves(partial):
        view = partial.reshape(2, 2, quarter, width)
        mine = jnp.where(core == 0, view[:, 0], view[:, 1])
        theirs = jnp.where(core == 0, view[:, 1], view[:, 0]).astype(BF16)
        return mine + lax.ppermute(theirs, "seq", twin).astype(F32)

    def own_half(array):
        view = array.reshape(2, 2, quarter, width)
        return jnp.where(core == 0, view[:, 0], view[:, 1])

    def give_back(array):
        mine = jnp.where(upper, array[1], array[0])
        theirs = lax.ppermute(jnp.where(upper, array[0], array[1]), "seq", across)
        return jnp.stack([jnp.where(upper, theirs, mine), jnp.where(upper, mine, theirs)])

    def of_core(vector):
        return take(vector, core, vector.shape[0] // 2, 0)

    def spread_out(part):
        empty = jnp.zeros_like(part)
        return jnp.concatenate([jnp.where(core == 0, part, empty), jnp.where(core == 1, part, empty)])

    def whole_row(array):
        mine = jnp.where(upper, array[1], array[0])
        theirs = lax.ppermute(jnp.where(upper, array[0], array[1]), "seq", across)
        pair = jnp.stack([jnp.where(upper, theirs, mine), jnp.where(upper, mine, theirs)])
        others = lax.ppermute(pair, "seq", twin)
        return jnp.stack(
            [jnp.where(core == 0, pair, others), jnp.where(core == 0, others, pair)], axis=1
        ).reshape(-1, width)

    seed_low = whole_row(upstream)
    totals = lengths[:, 0] + lengths[:, 1]
    total = jnp.where(upper, totals[1], totals[0]).reshape(1)

    flat_tokens = row.astype(F32)
    seed = seed_low.astype(F32)
    bias_core = jnp.concatenate(
        [of_core(bias_triple[:width]), jnp.zeros((width // 2,), F32), of_core(bias_triple[width:])]
    )

    normed = layer_norm(flat_tokens, gain_one, shift_one)
    normed_low = normed.astype(BF16)
    triple = (product(normed_low, triple_low) + bias_core).astype(BF16)
    mixed_core, probs = attend(triple, total)
    mixed_other = lax.ppermute(mixed_core, "seq", twin)
    mixed_low = jnp.concatenate(
        [jnp.where(core == 0, mixed_core, mixed_other), jnp.where(core == 0, mixed_other, mixed_core)], axis=1
    )
    resid = flat_tokens + product(mixed_low, attend_low) + bias_attend
    normed_two, second_pull = jax.vjp(layer_norm, resid, gain_two, shift_two)
    normed_two_low = normed_two.astype(BF16)
    activated, gelu_pull = jax.vjp(gelu_tanh, product(normed_two_low, expand_low) + of_core(bias_expand))
    act_low = activated.astype(BF16)

    grad_pre = gelu_pull(product_back(seed_low, shrink_low))[0].astype(BF16)
    partial = product_back(grad_pre, expand_low).astype(BF16)
    other_partial = lax.ppermute(partial, "seq", twin)
    shrink_grad = product_across(act_low, seed_low)
    expand_grad = product_across(normed_two_low, grad_pre)
    result = own_half(resid) + halves(product(act_low, shrink_low)) + bias_shrink
    result = give_back(result.astype(BF16))
    shrink_bias_grad = 0.5 * jnp.sum(seed, axis=0)
    expand_bias_grad = spread_out(jnp.sum(grad_pre.astype(F32), axis=0))
    resid_part, second_gain_grad, second_shift_grad = second_pull(partial.astype(F32) + other_partial.astype(F32))
    grad_resid = seed + resid_part
    grad_branch = grad_resid.astype(BF16)
    attend_grad = product_across(mixed_low, take(grad_branch, core, width // 2, 1))
    attend_bias_grad = 0.5 * jnp.sum(grad_branch.astype(F32), axis=0)
    grad_mixed = product_back(grad_branch, take(attend_low, core, width // 2, 0)).astype(BF16)

    grad_triple = jnp.concatenate(attend_back(triple, grad_mixed, probs), axis=1)
    n_one = halves(product_back(grad_triple, triple_low))
    triple_grad = product_across(normed_low, grad_triple)
    triple_sums = jnp.sum(grad_triple.astype(F32), axis=0)
    triple_bias_grad = jnp.concatenate([spread_out(triple_sums[: width // 2]), spread_out(triple_sums[width:])])
    _, first_pull = jax.vjp(layer_norm, own_half(flat_tokens), gain_one, shift_one)
    flat_grad, first_gain_grad, first_shift_grad = first_pull(n_one)
    tokens_grad = give_back((own_half(grad_resid) + flat_grad).astype(BF16))

    big = [member.astype(BF16) for member in (shrink_grad, expand_grad, attend_grad, triple_grad)]
    small_grads = (
        first_gain_grad, first_shift_grad, triple_bias_grad, attend_bias_grad,
        0.5 * second_gain_grad, 0.5 * second_shift_grad, expand_bias_grad, shrink_bias_grad,
    )
    flat_small = jnp.concatenate([g.reshape(dp, -1) for g in small_grads], axis=1)
    if by_kernel:
        *sums, small_sum = fold(dp, big, flat_small.reshape(-1, 128))
        own_small = lax.dynamic_index_in_dim(small_sum.reshape(dp, -1), lax.axis_index("dp"), 0, keepdims=False)
    else:
        sums, own_small = fold_plain(big, flat_small, core)
    shrink_sum, expand_sum, attend_sum, triple_sum = [member.astype(F32) for member in sums]
    triple_sum = triple_sum.reshape(2, -1, 3, width // 2).transpose(1, 2, 0, 3).reshape(-1, 3 * width)
    expand_sum, attend_sum = [m.transpose(1, 0, 2).reshape(m.shape[1], -1) for m in (expand_sum, attend_sum)]
    small_out, at = [], 0
    for size in sizes:
        small_out.append(own_small[at : at + size])
        at += size
    return (
        result,
        tokens_grad,
        small_out[0],
        small_out[1],
        triple_sum,
        small_out[2],
        attend_sum,
        small_out[3],
        small_out[4],
        small_out[5],
        expand_sum,
        small_out[6],
        shrink_sum,
        small_out[7],
    )


def solution(mesh):
    return jax.shard_map(
        functools.partial(body, mesh.shape["dp"]),
        mesh=mesh,
        in_specs=(
            P("dp", "seq", None),
            P("dp", None),
            P("dp"),
            P("dp"),
            P("dp", None),
            P("dp"),
            P("dp", None),
            P("dp"),
            P("dp"),
            P("dp"),
            P("dp", None),
            P("dp"),
            P("dp", None),
            P("dp"),
            P("dp", "seq", None),
        ),
        out_specs=(
            P("dp", "seq", None),
            P("dp", "seq", None),
            P("dp"),
            P("dp"),
            P("dp", None),
            P("dp"),
            P("dp", None),
            P("dp"),
            P("dp"),
            P("dp"),
            P("dp", None),
            P("dp"),
            P("dp", None),
            P("dp"),
        ),
        check_vma=False,
    )
```

```python
import functools

import jax
import jax.numpy as jnp
from jax import lax
from jax.experimental import pallas as pl
from jax.experimental.pallas import tpu as pltpu
from jax.sharding import PartitionSpec as P

H = 12
HD = 64

EPSILON = 1e-05
NEG_FILL = -1e30
MESH = pl.DeviceIdType.MESH
MIB = 1024 * 1024
BF16 = jnp.bfloat16
F32 = jnp.float32


def layer_norm(values, norm_gain, norm_shift):
    center = values - jnp.mean(values, axis=-1, keepdims=True)
    spread = jnp.mean(center * center, axis=-1, keepdims=True)
    return center * lax.rsqrt(spread + EPSILON) * norm_gain + norm_shift


def gelu_tanh(values):
    inside = 0.7978845608028654 * (values + 0.044715 * values * values * values)
    return 0.5 * values * (1.0 + jnp.tanh(inside))


def product(operand, other):
    return jnp.dot(operand, other, preferred_element_type=F32)


def product_across(operand, other):
    return lax.dot_general(operand, other, (((0,), (0,)), ((), ())), preferred_element_type=F32)


def product_back(operand, other):
    return lax.dot_general(operand, other, (((1,), (1,)), ((), ())), preferred_element_type=F32)


def own_place():
    d, s = lax.axis_index("dp"), lax.axis_index("seq")
    return d, s, d // 2, d % 2, s // 2, s % 2


def flip(index, step):
    return index + step * (1 - 2 * ((index // step) % 2))


def remote(src, dst, send, recv, d, s):
    return pltpu.make_async_remote_copy(
        src_ref=src, dst_ref=dst, send_sem=send, recv_sem=recv, device_id=(d, s), device_id_type=MESH
    )


def greet(depth, steps):
    d, s, z, y, x, c = own_place()
    barrier = pltpu.get_barrier_semaphore()

    def signal(d_to, s_to):
        pl.semaphore_signal(barrier, inc=1, device_id=(d_to, s_to), device_id_type=MESH)

    @pl.when(z > 0)
    def _():
        signal(d - 2, s)

    @pl.when(z < depth - 1)
    def _():
        signal(d + 2, s)

    for step in steps:
        signal(flip(d, step), s)
    signal(d, flip(s, 2))
    signal(d, flip(s, 1))
    ends = jnp.where(z > 0, 1, 0) + jnp.where(z < depth - 1, 1, 0)
    pl.semaphore_wait(barrier, ends + len(steps) + 2)


def doubling_steps(count):
    return [1 << k for k in range(count.bit_length() - 1)]


class Plan:
    def __init__(self):
        self.steps = []

    def add(self, at, action, *args):
        self.steps.append((at, len(self.steps), action, args))

    def run(self):
        for _, _, action, args in sorted(self.steps, key=lambda step: step[:2]):
            action(*args)


def spread_kernel(dp, kinds, rows, quarter, seg, *refs):
    count = len(rows)
    depth, half = dp // 2, dp // 2
    shard, (small, tokens, total) = refs[:count], refs[count : count + 3]
    at_ref = count + 3
    full = refs[at_ref : at_ref + count]
    at_ref += count
    (
        small_full, row, normed_out, triple_out, probs_out, mixed_out, resid_out, second_out, act_out, slope_out,
    ) = refs[at_ref : at_ref + 10]
    at_ref += 10
    wide, low = refs[at_ref : at_ref + count], refs[at_ref + count : at_ref + 2 * count]
    (
        row_v, normed, triple, probs, mixed, resid, second, act, slope, triple_w, attend_w, expand_w,
        load, local, up_s, down_s, y_s, x_s, ca_s, cb_s, yz_r, x_r, ca_r, cb_r, small_s, small_r, tok_l, tok_s, tok_r,
        weight_l, out_l, probs_l, mixed_s, mixed_r,
    ) = refs[at_ref + 2 * count :]
    d, s, z, y, x, c = own_place()
    steps = doubling_steps(dp)

    def parts(g):
        if kinds[g] != "cols":
            return [(slice(None), slice(None))]
        n = wide[g].shape[1]
        thirds = 3 if shard[g].shape[1] == 3 * shard[g].shape[0] * dp else 1
        n = n // thirds
        return [
            (pl.ds(pl.multiple_of((2 * t + c) * n, 128), n), slice(t * n, (t + 1) * n)) for t in range(thirds)
        ]

    def active(g, at):
        return True if kinds[g] != "shards" else at // half == c

    def fetches(g):
        return [
            pltpu.make_async_copy(shard[g].at[:, source], wide[g].at[:, target], load.at[g, t])
            for t, (source, target) in enumerate(parts(g))
        ]

    def when(condition, action):
        if condition is True:
            action()
        else:
            pl.when(condition)(action)

    for g in range(count):

        def fetch():
            for copy in fetches(g):
                copy.start()

        when(active(g, d), fetch)

    greet(depth, steps)

    def columns(g):
        if kinds[g] != "share":
            return slice(None)
        n = full[g].shape[1] // 2
        return pl.ds(pl.multiple_of(c * n, 128), n)

    def window(g, at, offset, n):
        m = rows[g] // 3
        place = at if kinds[g] != "shards" else at % half
        return full[g].at[pl.ds(pl.multiple_of(place * rows[g] + offset * m, 16), n * m), columns(g)]

    def own_piece(g):
        m = rows[g] // 3
        return low[g].at[pl.ds(pl.multiple_of(x * m, 16), 2 * m), columns(g)]

    def move(view, send, recv, d_to, s_to, src=None):
        return remote(view if src is None else src, view, send, recv, d_to, s_to)

    def up(g, at, src=None):
        return move(window(g, at, x, 2), up_s.at[g, at], yz_r.at[g, at], d + 2, s, src)

    def down(g, at, src=None):
        return move(window(g, at, x, 2), down_s.at[g, at], yz_r.at[g, at], d - 2, s, src)

    def over_y(g, at, src=None):
        return move(window(g, at, x, 2), y_s.at[g, at], yz_r.at[g, at], flip(d, 1), s, src)

    def over_x(g, at):
        return move(window(g, at, 2 * x, 1), x_s.at[g, at], x_r.at[g, at], d, flip(s, 2))

    def from_x(g, at):
        return move(window(g, at, 2 * (1 - x), 1), x_s.at[g, at], x_r.at[g, at], d, flip(s, 2))

    def core_a(g, at):
        return move(window(g, at, x, 2), ca_s.at[at], ca_r.at[at], d, flip(s, 1))

    def core_b(g, at):
        return move(window(g, at, 2 * (1 - x), 1), cb_s.at[at], cb_r.at[at], d, flip(s, 1))

    def small_copy(k):
        size = 16 << k
        view = small_full.at[pl.ds(pl.multiple_of((d // (1 << k)) * size, 16), size), :]
        return remote(view, view, small_s.at[k], small_r.at[k], flip(d, 1 << k), s)

    def own_local(g):
        place = d if kinds[g] != "shards" else d % half
        view = full[g].at[pl.ds(pl.multiple_of(place * rows[g], 16), rows[g]), :]
        return pltpu.make_async_copy(low[g], view, local.at[g])

    def spot(array, index):
        return array.at[pl.ds(pl.multiple_of(index * quarter, 16), quarter), :]

    mine, theirs = spot(row, 2 * x + c), spot(row, 2 * (1 - x) + c)
    own_tokens = pltpu.make_async_copy(tokens.at[x], mine, tok_l.at[0])
    tokens_over_x = remote(tokens.at[1 - x], mine, tok_s.at[0], tok_r.at[0], d, flip(s, 2))
    tokens_to_core = remote(tokens.at[x], mine, tok_s.at[1], tok_r.at[1], d, flip(s, 1))
    tokens_passed = remote(theirs, theirs, tok_s.at[2], tok_r.at[2], d, flip(s, 1))

    def tokens_pass():
        tokens_over_x.wait_recv()
        tokens_passed.start()

    own_small = pltpu.make_async_copy(small, small_full.at[pl.ds(pl.multiple_of(d * 16, 16), 16), :], local.at[count])
    own_small.start()
    own_tokens.start()
    tokens_over_x.start()
    tokens_to_core.start()

    def begin(g):
        for copy in fetches(g):
            copy.wait()
        low[g][...] = wide[g][...].astype(BF16)
        src = own_piece(g)
        pl.when(z < depth - 1)(lambda: up(g, d, src).start())
        pl.when(z > 0)(lambda: down(g, d, src).start())
        over_y(g, d, src).start()
        own_local(g).start()

    def small_step(k):
        if k == 0:
            own_small.wait()
        else:
            small_copy(k - 1).wait()
        if k < len(steps):
            small_copy(k).start()

    def arrived(g, at):
        over_x(g, at).start()
        if kinds[g] == "share":
            core_a(g, at).start()

    def z_arrival(g, r):
        def low_side():
            at = d - 2 * r
            up(g, at).wait_recv()

            @pl.when(z < depth - 1)
            def _():
                up(g, at).start()

            over_y(g, at).start()
            arrived(g, at)

        def high_side():
            at = d + 2 * r
            down(g, at).wait_recv()

            @pl.when(z > 0)
            def _():
                down(g, at).start()

            over_y(g, at).start()
            arrived(g, at)

        pl.when((z >= r) & active(g, d - 2 * r))(low_side)
        pl.when((z + r < depth) & active(g, d + 2 * r))(high_side)

    other = flip(d, 1)

    def y_one(g, at):
        over_y(g, at).wait_recv()
        arrived(g, at)

    def on_shards(g, r, base, action):
        if r == 0:
            when(active(g, base), lambda: action(base))
        else:
            pl.when((z >= r) & active(g, base - 2 * r))(lambda: action(base - 2 * r))
            pl.when((z + r < depth) & active(g, base + 2 * r))(lambda: action(base + 2 * r))

    def x_one(g, at):
        from_x(g, at).wait_recv()
        if kinds[g] == "share":
            core_b(g, at).start()


    width, pairs = row.shape[1], triple.shape[1] // (6 * HD)
    half_width = width // 2
    segs = 16

    def small_row(at, index):
        return small_full[pl.ds(at * segs + index, 1), :].astype(BF16).astype(F32)

    lane = lax.broadcasted_iota(jnp.int32, (1, 128), 1)

    def join(pieces):
        blocks = []
        for b in range(len(pieces) * seg // 128):
            block = jnp.zeros((1, 128), F32)
            for n, piece in enumerate(pieces):
                low_lane = n * seg - 128 * b
                if low_lane < 128 and low_lane + seg > 0:
                    turned = piece if low_lane % 128 == 0 else pltpu.roll(piece, low_lane % 128, 1)
                    block = jnp.where((lane >= low_lane) & (lane < low_lane + seg), turned, block)
            blocks.append(block)
        return jnp.concatenate(blocks, axis=1)

    def vector(index):
        return join([small_row(at, index) for at in range(dp)])

    def tile(i, n=quarter):
        return slice(i * n, (i + 1) * n)

    weight_loads = [
        pltpu.make_async_copy(full[g], target, weight_l.at[g]) for g, target in enumerate((triple_w, attend_w, expand_w))
    ]
    row_load = pltpu.make_async_copy(row, row_v, weight_l.at[3])

    def row_ready():
        own_tokens.wait()
        tokens_to_core.wait_recv()
        tokens_passed.wait_recv()
        row_load.start()

    def every_shard(g, action):
        for r in range(depth):
            on_shards(g, r, other, action)
            if r:
                on_shards(g, r, d, action)

    def weight_ready(g):
        own_local(g).wait()
        if kinds[g] == "share":

            def passed_on(at):
                core_a(g, at).wait_recv()
                core_b(g, at).wait_recv()

            every_shard(g, passed_on)
        weight_loads[g].start()

    def normalize(values, gain, shift):
        center = values - jnp.mean(values, axis=-1, keepdims=True)
        spread_of = jnp.mean(center * center, axis=-1, keepdims=True)
        return (center * lax.rsqrt(spread_of + EPSILON) * gain + shift).astype(BF16)

    def norm_tile(i):
        if i == 0:
            row_load.wait()
        normed[tile(i)] = normalize(row_v[tile(i)].astype(F32), vector(0), vector(1))

    def triple_tile(i):
        if i == 0:
            weight_loads[0].wait()
        n = half_width // seg
        ends = [
            join([small_row((first + c * n + k) // 2, 2 + (first + c * n + k) % 2) for k in range(n)])
            for first in (0, width // seg)
        ]
        bias = jnp.concatenate([ends[0], jnp.zeros((1, half_width), F32), ends[1]], axis=1)
        triple[tile(i)] = (product(normed[tile(i)], triple_w[...]) + bias).astype(BF16)

    def probs_copy(p):
        return pltpu.make_async_copy(probs.at[p % 2], probs_out.at[p], probs_l.at[p % 2])

    def mixed_window(p, core):
        return pl.ds(pl.multiple_of(core * half_width + 2 * HD * p, 2 * HD), 2 * HD)

    def mixed_copy(p):
        view = mixed.at[:, mixed_window(p, c)]
        return remote(view, view, mixed_s.at[p], mixed_r.at[p], d, flip(s, 1))

    def attend_part(p, part):
        if p > 1 and part == 0:
            probs_copy(p - 2).wait()
        columns = [slice(k * half_width + 2 * HD * p, k * half_width + 2 * HD * (p + 1)) for k in range(3)]
        mixed[tile(part), mixed_window(p, c)] = attend_block(
            part, quarter, total[0], triple[tile(part), columns[0]], triple.at[:, columns[1]], triple.at[:, columns[2]],
            probs.at[p % 2],
        )
        if part == 3:
            probs_copy(p).start()
            mixed_copy(p).start()

    out_copies = [
        pltpu.make_async_copy(source, target, out_l.at[k])
        for k, (source, target) in enumerate(
            (
                (normed, normed_out), (triple, triple_out), (mixed, mixed_out), (resid, resid_out),
                (second, second_out), (act, act_out), (slope, slope_out),
            )
        )
    ]

    def resid_tile(i):
        if i == 0:
            weight_loads[1].wait()
            out_copies[0].start()
            out_copies[1].start()
            for p in range(pairs):
                mixed_copy(p).wait()
            out_copies[2].start()
        values = row_v[tile(i)].astype(F32) + product(mixed[tile(i)], attend_w[...]) + vector(4)
        resid[tile(i)] = values
        second[tile(i)] = normalize(values, vector(5), vector(6))

    def expand_tile(i):
        if i == 0:
            weight_loads[2].wait()
            out_copies[3].start()
            out_copies[4].start()
        n = expand_w.shape[1] // seg
        bias = join([small_row((c * n + k) // 4, 7 + (c * n + k) % 4) for k in range(n)])
        for k in range(expand_w.shape[1] // 256):
            part = tile(k, 256)
            value = product(second[tile(i)], expand_w[:, part]) + bias[:, part]
            square = value * value
            bend = jnp.tanh(0.7978845608028654 * value * (1.0 + 0.044715 * square))
            raised = 0.5 * (1.0 + bend)
            act[tile(i), part] = (value * raised).astype(BF16)
            inner = 0.7978845608028654 + (3 * 0.7978845608028654 * 0.044715) * square
            slope[tile(i), part] = (raised + 0.5 * value * (1.0 - bend * bend) * inner).astype(BF16)

    plan = Plan()
    for k in range(len(steps) + 1):
        plan.add(2 * k, small_step, k)
    plan.add(8, tokens_pass)
    plan.add(11, row_ready)
    first = 0.0
    ready = []
    for g in range(count):
        piece = rows[g] * wide[g].shape[1] * 2 / 50e3 * 2 / 3
        if kinds[g] != "cols":
            piece /= 2
        hop = piece + 1.5
        plan.add(first, when, active(g, d), functools.partial(begin, g))
        for r in range(depth):
            if r:
                plan.add(first + hop * r, z_arrival, g, r)
                plan.add(first + hop * r + 0.5 * piece + 1.5, on_shards, g, r, d, functools.partial(x_one, g))
            plan.add(first + hop * (r + 1), on_shards, g, r, other, functools.partial(y_one, g))
            plan.add(
                first + hop * (r + 1) + 0.5 * piece + 1.5, on_shards, g, r, other, functools.partial(x_one, g)
            )
        ready.append(first + hop * depth + 0.5 * piece + 1.6)
        if kinds[g] != "shards":
            plan.add(ready[g] + (2 if kinds[g] == "share" else 0), weight_ready, g)
        first += 4 * piece if g == count - 1 else 3 * piece
    for i in range(4):
        plan.add(12.5 + 0.7 * i, norm_tile, i)
    at = ready[0] + 1.5
    for i in range(4):
        plan.add(at, triple_tile, i)
        at += 1.3
    for p in range(pairs):
        for part in range(4):
            plan.add(at, attend_part, p, part)
            at += 0.4 * (part + 1)
    at = max(at, ready[1] + 3.5) + 2.0
    for i in range(4):
        plan.add(at, resid_tile, i)
        at += 1.3
    at = max(at, ready[2] + 1.5)
    for i in range(4):
        plan.add(at, expand_tile, i)
        at += 1.5
    plan.run()

    out_copies[5].start()
    out_copies[6].start()
    for copy in out_copies:
        copy.wait()
    for p in range(max(pairs - 2, 0), pairs):
        probs_copy(p).wait()
    tokens_over_x.wait_send()
    tokens_to_core.wait_send()
    tokens_passed.wait_send()

    for g in range(count):

        def end():
            if kinds[g] == "shards":
                own_local(g).wait()

            @pl.when(z < depth - 1)
            def _():
                up(g, d, own_piece(g)).wait_send()

            @pl.when(z > 0)
            def _():
                down(g, d, own_piece(g)).wait_send()

            over_y(g, d, own_piece(g)).wait_send()

        when(active(g, d), end)

        def finish(g, own_column, at):
            if own_column:
                over_y(g, at).wait_send()
            over_x(g, at).wait_send()
            if kinds[g] == "share":
                core_a(g, at).wait_send()
                core_b(g, at).wait_send()

        for r in range(depth):
            on_shards(g, r, other, functools.partial(finish, g, False))
            if r:
                on_shards(g, r, d, functools.partial(finish, g, True))
                pl.when((z >= r) & (z < depth - 1) & active(g, d - 2 * r))(lambda: up(g, d - 2 * r).wait_send())
                pl.when((z + r < depth) & (z > 0) & active(g, d + 2 * r))(lambda: down(g, d + 2 * r).wait_send())


def spread(dp, shards, small, tokens, total):
    kinds = ["cols", "share", "cols", "shards"]
    rows = [member.shape[0] for member in shards]
    count = len(rows)
    quarter, width = tokens.shape[1:]
    length = 4 * quarter
    dma = pltpu.SemaphoreType.DMA
    any_space = pl.BlockSpec(memory_space=pl.ANY)
    vmem = pl.BlockSpec(memory_space=pltpu.VMEM)
    held = [(m.shape[0], m.shape[1] // 2 if kind == "cols" else m.shape[1]) for m, kind in zip(shards, kinds)]
    whole = [(dp * r // 2 if kind == "shards" else dp * r, n) for (r, n), kind in zip(held, kinds)]
    kept = part_start(4, quarter)
    pairs = width // (4 * HD)
    hidden = whole[2][1]
    states = [
        ((length, width), BF16), ((length, 3 * width // 2), BF16), ((pairs, 2, kept, quarter), BF16),
        ((length, width), BF16), ((length, width), F32), ((length, width), BF16),
        ((length, hidden), BF16), ((length, hidden), BF16),
    ]
    slots = [(shape if k != 2 else (2, *shape[1:]), kind) for k, (shape, kind) in enumerate(states)]
    return pl.pallas_call(
        functools.partial(spread_kernel, dp, kinds, rows, quarter, width // dp),
        out_shape=[jax.ShapeDtypeStruct(shape, BF16) for shape in whole]
        + [jax.ShapeDtypeStruct((dp * 16, 128), F32), jax.ShapeDtypeStruct((length, width), BF16)]
        + [jax.ShapeDtypeStruct(*state) for state in states],
        in_specs=[any_space] * (count + 2) + [pl.BlockSpec(memory_space=pltpu.SMEM)],
        out_specs=[any_space] * count + [vmem] + [any_space] * (1 + len(states)),
        scratch_shapes=[pltpu.VMEM(shape, F32) for shape in held]
        + [pltpu.VMEM(shape, BF16) for shape in held]
        + [pltpu.VMEM((length, width), BF16)]
        + [pltpu.VMEM(*slot) for slot in slots]
        + [pltpu.VMEM(shape, BF16) for shape in whole[:3]]
        + [dma((count, 3)), dma((count + 1,))]
        + [dma((count, dp))] * 4
        + [dma((dp,))] * 2
        + [dma((count, dp))] * 2
        + [dma((dp,))] * 2
        + [dma((len(doubling_steps(dp)),))] * 2
        + [dma((1,)), dma((3,)), dma((3,))]
        + [dma((4,)), dma((7,)), dma((2,)), dma((pairs,)), dma((pairs,))],
        compiler_params=pltpu.CompilerParams(
            collective_id=1, has_side_effects=True, vmem_limit_bytes=60 * MIB
        ),
        name="spread_weights",
    )(*shards, small, tokens, total)


def fold_kernel(dp, kinds, rows, *refs):
    count = len(rows)
    depth = dp // 2
    grads, small = refs[:count], refs[count]
    outs, small_out = refs[count + 1 : 2 * count + 1], refs[2 * count + 1]
    at_ref = 2 * count + 2
    acc, x_buf, y_buf, u_buf, n_buf, b_buf = [refs[at_ref + k * count : at_ref + (k + 1) * count] for k in range(6)]
    small_buf = refs[at_ref + 6 * count]
    (
        load, x_s, x_r, y_s, y_r, u_s, u_r, n_s, n_r, f_s, f_r, small_s, small_r,
    ) = refs[at_ref + 6 * count + 1 :]
    d, s, z, y, x, c = own_place()
    dp_steps = doubling_steps(dp)

    def layers(g):
        return depth if kinds[g] != "shards" else depth // 2

    def first_layer(g):
        return 0 if kinds[g] != "shards" else c * (depth // 2)

    def layer(g, n):
        if kinds[g] != "shards":
            return sorted(range(depth), key=lambda k: -abs(2 * k - depth + 1))[n]
        return n + c * (depth // 2 - 1 - 2 * n)

    def of(j, own):
        return 2 * j + (y if own else 1 - y)

    def fetch(g, at):
        return pltpu.make_async_copy(grads[g].at[at], acc[g].at[at], load.at[g, at])

    items = [(g, n, own) for g in range(count) for own in (False, True) for n in range(layers(g))]
    for g, n, own in items:
        fetch(g, of(layer(g, n), own)).start()

    greet(depth, dp_steps)

    def span(g, units, n):
        m = rows[g] // 3
        return pl.ds(pl.multiple_of(units * m, 16), n * m)

    def over_x(g, at):
        return remote(
            acc[g].at[at, span(g, 2 * (1 - x), 1), :], x_buf[g].at[at], x_s.at[g, at], x_r.at[g, at], d, flip(s, 2)
        )

    def over_y(g, j):
        return remote(acc[g].at[of(j, False), span(g, x, 2), :], y_buf[g].at[j], y_s.at[g, j], y_r.at[g, j], flip(d, 1), s)

    def up(g, j):
        return remote(acc[g].at[of(j, True), span(g, x, 2), :], u_buf[g].at[j], u_s.at[g, j], u_r.at[g, j], d + 2, s)

    def down(g, j):
        return remote(acc[g].at[of(j, True), span(g, x, 2), :], n_buf[g].at[j], n_s.at[g, j], n_r.at[g, j], d - 2, s)

    def stage_a(g, n, own):
        at = of(layer(g, n), own)
        fetch(g, at).wait()
        over_x(g, at).start()

    def stage_c(g, n, own):
        j = layer(g, n)
        at = of(j, own)
        over_x(g, at).wait_recv()
        third = (at, span(g, 2 * x, 1), slice(None))
        acc[g][third] = acc[g][third] + x_buf[g][at]
        if not own:
            over_y(g, j).start()
        else:
            over_y(g, j).wait_recv()
            pair = (at, span(g, x, 2), slice(None))
            acc[g][pair] = acc[g][pair] + y_buf[g][j]

    def stage_e(g, n, hop):
        j = layer(g, n)
        k = j + first_layer(g)
        pair = (of(j, True), span(g, x, 2), slice(None))

        @pl.when((z == hop) & (k > hop))
        def _():
            if hop:
                up(g, j).wait_recv()
                acc[g][pair] = acc[g][pair] + u_buf[g][j]
            up(g, j).start()

        @pl.when((z == depth - 1 - hop) & (k < depth - 1 - hop))
        def _():
            if hop:
                down(g, j).wait_recv()
                acc[g][pair] = acc[g][pair] + n_buf[g][j]
            down(g, j).start()

    def own_layer(g):
        return z - first_layer(g)

    def ours(g, action):
        if kinds[g] != "shards":
            action()
        else:
            pl.when((z >= first_layer(g)) & (z < first_layer(g) + layers(g)))(action)

    def out_rows(g, units, n):
        return outs[g].at[c, span(g, units, n), :] if kinds[g] != "shards" else outs[g].at[span(g, units, n), :]

    def final_share(g):
        return remote(
            acc[g].at[of(own_layer(g), True), span(g, 2 * x, 1), :], out_rows(g, 2 * x, 1),
            f_s.at[g, 0], f_r.at[g, 0], d, flip(s, 2),
        )

    def final_swap(g):
        return remote(
            acc[g].at[of(own_layer(g), True), span(g, 1, 1), :], b_buf[g], f_s.at[g, 1], f_r.at[g, 1], d, flip(s, 2)
        )

    def final_core(g):
        view = out_rows(g, 0, 3)
        return remote(view, view, f_s.at[g, 2], f_r.at[g, 2], d, flip(s, 1))

    def finish_one(g):
        def run():
            j = own_layer(g)
            at = of(j, True)
            pair = (at, span(g, x, 2), slice(None))

            @pl.when(z > 0)
            def _():
                up(g, j).wait_recv()
                acc[g][pair] = acc[g][pair] + u_buf[g][j]

            @pl.when(z < depth - 1)
            def _():
                down(g, j).wait_recv()
                acc[g][pair] = acc[g][pair] + n_buf[g][j]

            final_share(g).start()
            final_swap(g).start()
            out_rows(g, 2 * x, 1)[...] = acc[g][at, span(g, 2 * x, 1), :]

        ours(g, run)

    def finish_two(g):
        def run():
            final_swap(g).wait_recv()
            out_rows(g, 1, 1)[...] = acc[g][of(own_layer(g), True), span(g, 1, 1), :] + b_buf[g][...]
            final_share(g).wait_recv()
            final_core(g).start()

        ours(g, run)

    small_out[...] = small[...]
    small_partners = [(flip(d, step), s) for step in dp_steps] + [(d, flip(s, 1)), (d, flip(s, 2))]

    def small_copy(k):
        d_to, s_to = small_partners[k]
        return remote(small_out, small_buf.at[k], small_s.at[k], small_r.at[k], d_to, s_to)

    def small_finish(k):
        small_copy(k).wait()
        small_out[...] = small_out[...] + small_buf[k]

    plan = Plan()
    for k in range(len(small_partners)):
        plan.add(4 * k, lambda k: small_copy(k).start(), k)
        plan.add(4 * k + 4, small_finish, k)
    done = 0.0
    for g, n, own in items:
        unit = rows[g] * grads[g].shape[2] * 2 / 50e3 / 3
        plan.add(done - 4.0, stage_a, g, n, own)
        done += unit
        plan.add(done, stage_c, g, n, own)
        if own:
            for hop in range(depth - 1):
                plan.add(done + 0.5 + (2 * unit + 1.5) * hop, stage_e, g, n, hop)
            if n == layers(g) - 1:
                plan.add(done + 0.5 + (2 * unit + 1.5) * (depth - 1), finish_one, g)
                plan.add(done + 2.5 + (2 * unit + 1.5) * (depth - 1) + unit, finish_two, g)
    plan.run()

    for g in range(count):

        def drain():
            final_share(g).wait_send()
            final_swap(g).wait_send()
            if kinds[g] == "shards":
                final_core(g).wait_send()

        ours(g, drain)
        if kinds[g] == "shards":
            pl.when((z < first_layer(g)) | (z >= first_layer(g) + layers(g)))(lambda: final_core(g).wait_recv())
        else:
            final_core(g).wait()
        for j in range(layers(g)):
            over_x(g, of(j, False)).wait_send()
            over_x(g, of(j, True)).wait_send()
            over_y(g, j).wait_send()
            pl.when(j + first_layer(g) > z)(lambda: up(g, j).wait_send())
            pl.when(j + first_layer(g) < z)(lambda: down(g, j).wait_send())


def fold(dp, grads, small):
    kinds = ["shards", "cols", "cols", "cols"]
    owners = [dp // 2 if kind == "shards" else dp for kind in kinds]
    rows = [m.shape[0] // n for m, n in zip(grads, owners)]
    count, depth = len(rows), dp // 2
    views = [m.reshape(n, r, m.shape[1]) for m, r, n in zip(grads, rows, owners)]
    dma = pltpu.SemaphoreType.DMA
    any_space = pl.BlockSpec(memory_space=pl.ANY)
    vmem = pl.BlockSpec(memory_space=pltpu.VMEM)

    def buffers(lead, part):
        slots = [() if lead is None else (n // lead,) for n in owners]
        return [pltpu.VMEM((*slot, r // 3 * part, m.shape[1]), BF16) for slot, r, m in zip(slots, rows, grads)]

    partners = len(doubling_steps(dp)) + 2
    return pl.pallas_call(
        functools.partial(fold_kernel, dp, kinds, rows),
        out_shape=[
            jax.ShapeDtypeStruct((r, m.shape[1]) if kind == "shards" else (2, r, m.shape[1]), BF16)
            for r, m, kind in zip(rows, grads, kinds)
        ]
        + [jax.ShapeDtypeStruct(small.shape, F32)],
        in_specs=[any_space] * count + [vmem],
        out_specs=[vmem] * (count + 1),
        scratch_shapes=buffers(1, 3)
        + buffers(1, 1)
        + buffers(2, 2)
        + buffers(2, 2)
        + buffers(2, 2)
        + buffers(None, 1)
        + [pltpu.VMEM((partners, *small.shape), F32)]
        + [dma((count, dp))] * 3
        + [dma((count, depth))] * 6
        + [dma((count, 3))] * 2
        + [dma((partners,))] * 2,
        compiler_params=pltpu.CompilerParams(
            collective_id=2, has_side_effects=True, vmem_limit_bytes=60 * MIB
        ),
        name="fold_gradients",
    )(*views, small)


def head_mask():
    return lax.broadcasted_iota(jnp.int32, (1, 2 * HD), 1) < HD


def part_start(part, quarter):
    return quarter * (part * (part + 1) // 2)


def attend_block(part, quarter, total, query, k_ref, v_ref, probs_ref):
    first = head_mask()
    length = quarter * (part + 1)
    key_pos = lax.broadcasted_iota(jnp.int32, (length, 1), 0)
    key_pos = jnp.where(key_pos < total, key_pos, 1 << 20)
    allowed = key_pos <= lax.broadcasted_iota(jnp.int32, (1, quarter), 1) + part * quarter
    query = query * jnp.asarray(HD**-0.5, BF16)
    sums = []
    for head in range(2):
        mask = first if head == 0 else ~first
        scores = product_back(k_ref[:length], jnp.where(mask, query, jnp.zeros_like(query)))
        scores = jnp.where(allowed, scores, NEG_FILL)
        exponent = jnp.exp(scores - jnp.max(scores, axis=0, keepdims=True))
        probs = (exponent * (1.0 / jnp.sum(exponent, axis=0, keepdims=True))).astype(BF16)
        probs_ref[head, part_start(part, quarter) : part_start(part + 1, quarter)] = probs
        sums.append(product_across(probs, v_ref[:length]))
    return jnp.where(first, sums[0], sums[1]).astype(BF16)


def attend_kernel(quarter, total, q_ref, k_ref, v_ref, mixed_ref, probs_ref):
    for part in range(4):
        rows = slice(part * quarter, (part + 1) * quarter)
        mixed_ref[rows] = attend_block(part, quarter, total[0], q_ref[rows], k_ref, v_ref, probs_ref.at[0])


def attend(triple, total):
    tokens, width = triple.shape[0], triple.shape[1] // 3
    quarter = tokens // 4
    pairs = width // (2 * HD)
    kept = part_start(4, quarter)

    def block(shift):
        return pl.BlockSpec((tokens, 2 * HD), lambda p, _: (0, p + shift))

    return pl.pallas_call(
        functools.partial(attend_kernel, quarter),
        grid_spec=pltpu.PrefetchScalarGridSpec(
            num_scalar_prefetch=1,
            grid=(pairs,),
            in_specs=[block(0), block(pairs), block(2 * pairs)],
            out_specs=[block(0), pl.BlockSpec((1, 2, kept, quarter), lambda p, _: (p, 0, 0, 0))],
        ),
        out_shape=[
            jax.ShapeDtypeStruct((tokens, width), BF16),
            jax.ShapeDtypeStruct((pairs, 2, kept, quarter), BF16),
        ],
        compiler_params=pltpu.CompilerParams(vmem_limit_bytes=50 * MIB),
        name="attend",
    )(total, triple, triple, triple)


def attend_back_kernel(quarter, q_ref, k_ref, v_ref, g_ref, probs_ref, dq_ref, dk_ref, dv_ref, dkeys, dvalues):
    first = head_mask()
    for part in reversed(range(4)):
        length = quarter * (part + 1)
        rows = slice(part * quarter, (part + 1) * quarter)
        query = q_ref[rows] * jnp.asarray(HD**-0.5, BF16)
        grad = g_ref[rows]
        dq = []
        for head in range(2):
            mask = first if head == 0 else ~first
            own_query = jnp.where(mask, query, jnp.zeros_like(query))
            own_grad = jnp.where(mask, grad, jnp.zeros_like(grad))
            probs = probs_ref[0, head, part_start(part, quarter) : part_start(part + 1, quarter)]
            wide = probs.astype(F32)
            grad_probs = product_back(v_ref[:length], own_grad)
            delta = jnp.sum(wide * grad_probs, axis=0, keepdims=True)
            grad_scores = (wide * (grad_probs - delta)).astype(BF16)
            dv = product(probs, own_grad)
            dk = product(grad_scores, own_query)
            if part == 3 and head == 0:
                dvalues[...] = dv
                dkeys[...] = dk
            else:
                dvalues[:length] += dv
                dkeys[:length] += dk
            dq.append(product_across(grad_scores, k_ref[:length]))
        dq_ref[rows] = (jnp.where(first, dq[0], dq[1]) * HD**-0.5).astype(BF16)
    dk_ref[...] = dkeys[...].astype(BF16)
    dv_ref[...] = dvalues[...].astype(BF16)


def attend_back(triple, grad, probs):
    tokens, width = triple.shape[0], triple.shape[1] // 3
    quarter = tokens // 4
    pairs = width // (2 * HD)

    def block(shift):
        return pl.BlockSpec((tokens, 2 * HD), lambda p: (0, p + shift))

    return pl.pallas_call(
        functools.partial(attend_back_kernel, quarter),
        grid=(pairs,),
        in_specs=[block(0), block(pairs), block(2 * pairs), block(0)]
        + [pl.BlockSpec((1, 2, part_start(4, quarter), quarter), lambda p: (p, 0, 0, 0))],
        out_specs=[block(0)] * 3,
        out_shape=[jax.ShapeDtypeStruct((tokens, width), BF16)] * 3,
        scratch_shapes=[pltpu.VMEM((tokens, 2 * HD), F32)] * 2,
        compiler_params=pltpu.CompilerParams(vmem_limit_bytes=50 * MIB),
        name="attend_back",
    )(triple, triple, triple, grad, probs)


def take(array, index, size, axis):
    return lax.dynamic_slice_in_dim(array, index * size, size, axis)


def gather_plain(matrices, small, tokens, core, upper):
    triple, attend_full, expand, shrink = [
        lax.all_gather(m.astype(BF16), "dp", axis=0, tiled=True) for m in matrices
    ]
    width = triple.shape[0]
    thirds = triple.reshape(width, 3, width)
    row = lax.all_gather(tokens, "seq", axis=1, tiled=True)
    return (
        take(thirds, core, width // 2, 2).reshape(width, -1),
        attend_full,
        take(expand, core, expand.shape[1] // 2, 1),
        take(shrink, core, shrink.shape[0] // 2, 0),
        lax.all_gather(small, "dp", axis=0),
        jnp.where(upper, row[1], row[0]),
    )


def fold_plain(grads, small, core):
    def by_core(array):
        empty = jnp.zeros_like(array)
        return jnp.stack([jnp.where(core == 0, array, empty), jnp.where(core == 1, array, empty)], axis=1)

    shrink, *others = grads
    wide = jnp.swapaxes(by_core(shrink), 0, 1).reshape(-1, shrink.shape[1])
    arrays = [wide] + [by_core(m) for m in others]
    sums = [lax.psum(lax.psum_scatter(m, "dp", scatter_dimension=0, tiled=True), "seq") for m in arrays]
    sums = [sums[0]] + [jnp.swapaxes(m, 0, 1) for m in sums[1:]]
    return sums, lax.psum(lax.psum_scatter(small, "dp", scatter_dimension=0, tiled=True), "seq").reshape(-1)


def body(
    dp,
    tokens,
    lengths,
    first_gain,
    first_shift,
    triple_weight,
    triple_bias,
    attend_weight,
    attend_bias,
    second_gain,
    second_shift,
    expand_weight,
    expand_bias,
    shrink_weight,
    shrink_bias,
    upstream,
):
    row_count, quarter, width = tokens.shape
    matrices = (triple_weight, attend_weight, expand_weight, shrink_weight)
    vectors = (first_gain, first_shift, triple_bias, attend_bias, second_gain, second_shift, expand_bias, shrink_bias)
    sizes = [member.shape[0] for member in vectors]
    total_small = sum(sizes)
    by_kernel = dp & (dp - 1) == 0 and dp > 2 and all(m.shape[0] % 48 == 0 for m in matrices)
    segs = total_small * dp // width
    by_kernel = by_kernel and segs <= 16 and width // dp <= 128
    place = lax.axis_index("seq")
    upper, core = place // 2 == 1, place % 2

    totals = lengths[:, 0] + lengths[:, 1]
    total = jnp.where(upper, totals[1], totals[0]).reshape(1)

    across = [(k, (k + 2) % 4) for k in range(4)]
    twin = [(k, k + 1 - 2 * (k % 2)) for k in range(4)]

    def halves(partial):
        view = partial.reshape(2, 2, quarter, width)
        mine = jnp.where(core == 0, view[:, 0], view[:, 1])
        theirs = jnp.where(core == 0, view[:, 1], view[:, 0]).astype(BF16)
        return mine + lax.ppermute(theirs, "seq", twin).astype(F32)

    def own_half(array):
        view = array.reshape(2, 2, quarter, width)
        return jnp.where(core == 0, view[:, 0], view[:, 1])

    def give_back(array):
        mine = jnp.where(upper, array[1], array[0])
        theirs = lax.ppermute(jnp.where(upper, array[0], array[1]), "seq", across)
        return jnp.stack([jnp.where(upper, theirs, mine), jnp.where(upper, mine, theirs)])

    def of_core(vector):
        return take(vector, core, vector.shape[0] // 2, 0)

    def spread_out(part):
        empty = jnp.zeros_like(part)
        return jnp.concatenate([jnp.where(core == 0, part, empty), jnp.where(core == 1, part, empty)])

    def whole_row(array):
        mine = jnp.where(upper, array[1], array[0])
        theirs = lax.ppermute(jnp.where(upper, array[0], array[1]), "seq", across)
        pair = jnp.stack([jnp.where(upper, theirs, mine), jnp.where(upper, mine, theirs)])
        others = lax.ppermute(pair, "seq", twin)
        return jnp.stack(
            [jnp.where(core == 0, pair, others), jnp.where(core == 0, others, pair)], axis=1
        ).reshape(-1, width)

    small = jnp.concatenate(vectors)
    if by_kernel:
        small = jnp.pad(small.reshape(segs, -1), ((0, 16 - segs), (0, 128 - width // dp)))
        *weights, small_full, row, normed_low, triple, probs, mixed_low, resid, normed_two_low, act_low, slope = spread(
            dp, matrices, small, tokens, total
        )
        small_full = small_full.reshape(dp, 16, 128)[:, :segs, : width // dp].reshape(dp, -1)
        upstream, small_full = lax.optimization_barrier((upstream, small_full))
    else:
        *weights, small_full, row = gather_plain(matrices, small, tokens, core, upper)
    floats, at = [], 0
    for size in sizes:
        floats.append(small_full[:, at : at + size].reshape(-1).astype(BF16).astype(F32))
        at += size
    gain_one, shift_one, bias_triple, bias_attend, gain_two, shift_two, bias_expand, bias_shrink = floats
    triple_low, attend_low, expand_low, shrink_low = weights
    seed_low = whole_row(upstream)
    flat_tokens = row.astype(F32)
    seed = seed_low.astype(F32)

    if not by_kernel:
        bias_core = jnp.concatenate(
            [of_core(bias_triple[:width]), jnp.zeros((width // 2,), F32), of_core(bias_triple[width:])]
        )
        normed_low = layer_norm(flat_tokens, gain_one, shift_one).astype(BF16)
        triple = (product(normed_low, triple_low) + bias_core).astype(BF16)
        mixed_core, probs = attend(triple, total)
        mixed_other = lax.ppermute(mixed_core, "seq", twin)
        mixed_low = jnp.concatenate(
            [jnp.where(core == 0, mixed_core, mixed_other), jnp.where(core == 0, mixed_other, mixed_core)], axis=1
        )
        resid = flat_tokens + product(mixed_low, attend_low) + bias_attend
        normed_two_low = layer_norm(resid, gain_two, shift_two).astype(BF16)
        activated, gelu_pull = jax.vjp(gelu_tanh, product(normed_two_low, expand_low) + of_core(bias_expand))
        act_low, slope = activated.astype(BF16), gelu_pull(jnp.ones_like(activated))[0]
    _, second_pull = jax.vjp(layer_norm, resid, gain_two, shift_two)

    grad_pre = (product_back(seed_low, shrink_low) * slope.astype(F32)).astype(BF16)
    partial = product_back(grad_pre, expand_low).astype(BF16)
    other_partial = lax.ppermute(partial, "seq", twin)
    shrink_grad = product_across(act_low, seed_low)
    expand_grad = product_across(normed_two_low, grad_pre)
    result = own_half(resid) + halves(product(act_low, shrink_low)) + bias_shrink
    result = give_back(result.astype(BF16))
    shrink_bias_grad = 0.5 * jnp.sum(seed, axis=0)
    expand_bias_grad = spread_out(jnp.sum(grad_pre.astype(F32), axis=0))
    resid_part, second_gain_grad, second_shift_grad = second_pull(partial.astype(F32) + other_partial.astype(F32))
    grad_resid = seed + resid_part
    grad_branch = grad_resid.astype(BF16)
    attend_grad = product_across(mixed_low, take(grad_branch, core, width // 2, 1))
    attend_bias_grad = 0.5 * jnp.sum(grad_branch.astype(F32), axis=0)
    grad_mixed = product_back(grad_branch, take(attend_low, core, width // 2, 0)).astype(BF16)

    grad_triple = jnp.concatenate(attend_back(triple, grad_mixed, probs), axis=1)
    n_one = halves(product_back(grad_triple, triple_low))
    triple_grad = product_across(normed_low, grad_triple)
    triple_sums = jnp.sum(grad_triple.astype(F32), axis=0)
    triple_bias_grad = jnp.concatenate([spread_out(triple_sums[: width // 2]), spread_out(triple_sums[width:])])
    _, first_pull = jax.vjp(layer_norm, own_half(flat_tokens), gain_one, shift_one)
    flat_grad, first_gain_grad, first_shift_grad = first_pull(n_one)
    tokens_grad = give_back((own_half(grad_resid) + flat_grad).astype(BF16))

    big = [member.astype(BF16) for member in (shrink_grad, expand_grad, attend_grad, triple_grad)]
    small_grads = (
        first_gain_grad, first_shift_grad, triple_bias_grad, attend_bias_grad,
        0.5 * second_gain_grad, 0.5 * second_shift_grad, expand_bias_grad, shrink_bias_grad,
    )
    flat_small = jnp.concatenate([g.reshape(dp, -1) for g in small_grads], axis=1)
    if by_kernel:
        *sums, small_sum = fold(dp, big, flat_small.reshape(-1, 128))
        own_small = lax.dynamic_index_in_dim(small_sum.reshape(dp, -1), lax.axis_index("dp"), 0, keepdims=False)
    else:
        sums, own_small = fold_plain(big, flat_small, core)
    shrink_sum, expand_sum, attend_sum, triple_sum = [member.astype(F32) for member in sums]
    triple_sum = triple_sum.reshape(2, -1, 3, width // 2).transpose(1, 2, 0, 3).reshape(-1, 3 * width)
    expand_sum, attend_sum = [m.transpose(1, 0, 2).reshape(m.shape[1], -1) for m in (expand_sum, attend_sum)]
    small_out, at = [], 0
    for size in sizes:
        small_out.append(own_small[at : at + size])
        at += size
    return (
        result,
        tokens_grad,
        small_out[0],
        small_out[1],
        triple_sum,
        small_out[2],
        attend_sum,
        small_out[3],
        small_out[4],
        small_out[5],
        expand_sum,
        small_out[6],
        shrink_sum,
        small_out[7],
    )


def solution(mesh):
    return jax.shard_map(
        functools.partial(body, mesh.shape["dp"]),
        mesh=mesh,
        in_specs=(
            P("dp", "seq", None),
            P("dp", None),
            P("dp"),
            P("dp"),
            P("dp", None),
            P("dp"),
            P("dp", None),
            P("dp"),
            P("dp"),
            P("dp"),
            P("dp", None),
            P("dp"),
            P("dp", None),
            P("dp"),
            P("dp", "seq", None),
        ),
        out_specs=(
            P("dp", "seq", None),
            P("dp", "seq", None),
            P("dp"),
            P("dp"),
            P("dp", None),
            P("dp"),
            P("dp", None),
            P("dp"),
            P("dp"),
            P("dp"),
            P("dp", None),
            P("dp"),
            P("dp", None),
            P("dp"),
        ),
        check_vma=False,
    )
```

```python
import functools

import jax
import jax.numpy as jnp
from jax import lax
from jax.experimental import pallas as pl
from jax.experimental.pallas import tpu as pltpu
from jax.sharding import PartitionSpec as P

H = 12
HD = 64

EPSILON = 1e-05
NEG_FILL = -1e30
MESH = pl.DeviceIdType.MESH
MIB = 1024 * 1024
BF16 = jnp.bfloat16
F32 = jnp.float32


def layer_norm(values, norm_gain, norm_shift):
    center = values - jnp.mean(values, axis=-1, keepdims=True)
    spread = jnp.mean(center * center, axis=-1, keepdims=True)
    return center * lax.rsqrt(spread + EPSILON) * norm_gain + norm_shift


def gelu_tanh(values):
    inside = 0.7978845608028654 * (values + 0.044715 * values * values * values)
    return 0.5 * values * (1.0 + jnp.tanh(inside))


def product(operand, other):
    return jnp.dot(operand, other, preferred_element_type=F32)


def product_across(operand, other):
    return lax.dot_general(operand, other, (((0,), (0,)), ((), ())), preferred_element_type=F32)


def product_back(operand, other):
    return lax.dot_general(operand, other, (((1,), (1,)), ((), ())), preferred_element_type=F32)


def own_place():
    d, s = lax.axis_index("dp"), lax.axis_index("seq")
    return d, s, d // 2, d % 2, s // 2, s % 2


def flip(index, step):
    return index + step * (1 - 2 * ((index // step) % 2))


def remote(src, dst, send, recv, d, s):
    return pltpu.make_async_remote_copy(
        src_ref=src, dst_ref=dst, send_sem=send, recv_sem=recv, device_id=(d, s), device_id_type=MESH
    )


def greet(depth, steps):
    d, s, z, y, x, c = own_place()
    barrier = pltpu.get_barrier_semaphore()

    def signal(d_to, s_to):
        pl.semaphore_signal(barrier, inc=1, device_id=(d_to, s_to), device_id_type=MESH)

    @pl.when(z > 0)
    def _():
        signal(d - 2, s)

    @pl.when(z < depth - 1)
    def _():
        signal(d + 2, s)

    for step in steps:
        signal(flip(d, step), s)
    signal(d, flip(s, 2))
    signal(d, flip(s, 1))
    ends = jnp.where(z > 0, 1, 0) + jnp.where(z < depth - 1, 1, 0)
    pl.semaphore_wait(barrier, ends + len(steps) + 2)


def doubling_steps(count):
    return [1 << k for k in range(count.bit_length() - 1)]


class Plan:
    def __init__(self):
        self.steps = []

    def add(self, at, action, *args):
        self.steps.append((at, len(self.steps), action, args))

    def run(self):
        for _, _, action, args in sorted(self.steps, key=lambda step: step[:2]):
            action(*args)


def small_segment(ref, at, index):
    return ref[pl.ds(at * 16 + index, 1), :].astype(BF16).astype(F32)


def join_rows(seg, pieces):
    lane = lax.broadcasted_iota(jnp.int32, (1, 128), 1)
    blocks = []
    for b in range(len(pieces) * seg // 128):
        block = jnp.zeros((1, 128), F32)
        for n, piece in enumerate(pieces):
            low_lane = n * seg - 128 * b
            if low_lane < 128 and low_lane + seg > 0:
                turned = piece if low_lane % 128 == 0 else pltpu.roll(piece, low_lane % 128, 1)
                block = jnp.where((lane >= low_lane) & (lane < low_lane + seg), turned, block)
        blocks.append(block)
    return jnp.concatenate(blocks, axis=1)


def small_vector(ref, seg, dp, index):
    return join_rows(seg, [small_segment(ref, at, index) for at in range(dp)])


def spread_kernel(dp, kinds, rows, quarter, seg, *refs):
    count = len(rows)
    depth, half = dp // 2, dp // 2
    shard, (small, tokens, upstream, total) = refs[:count], refs[count : count + 4]
    at_ref = count + 4
    full = refs[at_ref : at_ref + count]
    at_ref += count
    (
        small_full, row, seed, normed_out, triple_out, probs_out, mixed_out, resid_out, second_out, act_out, slope_out,
    ) = refs[at_ref : at_ref + 11]
    at_ref += 11
    wide, low = refs[at_ref : at_ref + count], refs[at_ref + count : at_ref + 2 * count]
    (
        row_v, normed, triple, probs, mixed, resid, second, act, slope, triple_w, attend_w, expand_w,
        load, local, up_s, down_s, y_s, x_s, ca_s, cb_s, yz_r, x_r, ca_r, cb_r, small_s, small_r, tok_l, tok_s, tok_r,
        weight_l, out_l, probs_l, mixed_s, mixed_r,
    ) = refs[at_ref + 2 * count :]
    d, s, z, y, x, c = own_place()
    steps = doubling_steps(dp)

    def parts(g):
        if kinds[g] != "cols":
            return [(slice(None), slice(None))]
        n = wide[g].shape[1]
        thirds = 3 if shard[g].shape[1] == 3 * shard[g].shape[0] * dp else 1
        n = n // thirds
        return [
            (pl.ds(pl.multiple_of((2 * t + c) * n, 128), n), slice(t * n, (t + 1) * n)) for t in range(thirds)
        ]

    def active(g, at):
        return True if kinds[g] != "shards" else at // half == c

    def fetches(g):
        return [
            pltpu.make_async_copy(shard[g].at[:, source], wide[g].at[:, target], load.at[g, t])
            for t, (source, target) in enumerate(parts(g))
        ]

    def when(condition, action):
        if condition is True:
            action()
        else:
            pl.when(condition)(action)

    for g in range(count):

        def fetch():
            for copy in fetches(g):
                copy.start()

        when(active(g, d), fetch)

    greet(depth, steps)

    def columns(g):
        if kinds[g] != "share":
            return slice(None)
        n = full[g].shape[1] // 2
        return pl.ds(pl.multiple_of(c * n, 128), n)

    def window(g, at, offset, n):
        m = rows[g] // 3
        place = at if kinds[g] != "shards" else at % half
        return full[g].at[pl.ds(pl.multiple_of(place * rows[g] + offset * m, 16), n * m), columns(g)]

    def own_piece(g):
        m = rows[g] // 3
        return low[g].at[pl.ds(pl.multiple_of(x * m, 16), 2 * m), columns(g)]

    def move(view, send, recv, d_to, s_to, src=None):
        return remote(view if src is None else src, view, send, recv, d_to, s_to)

    def up(g, at, src=None):
        return move(window(g, at, x, 2), up_s.at[g, at], yz_r.at[g, at], d + 2, s, src)

    def down(g, at, src=None):
        return move(window(g, at, x, 2), down_s.at[g, at], yz_r.at[g, at], d - 2, s, src)

    def over_y(g, at, src=None):
        return move(window(g, at, x, 2), y_s.at[g, at], yz_r.at[g, at], flip(d, 1), s, src)

    def over_x(g, at):
        return move(window(g, at, 2 * x, 1), x_s.at[g, at], x_r.at[g, at], d, flip(s, 2))

    def from_x(g, at):
        return move(window(g, at, 2 * (1 - x), 1), x_s.at[g, at], x_r.at[g, at], d, flip(s, 2))

    def core_a(g, at):
        return move(window(g, at, x, 2), ca_s.at[at], ca_r.at[at], d, flip(s, 1))

    def core_b(g, at):
        return move(window(g, at, 2 * (1 - x), 1), cb_s.at[at], cb_r.at[at], d, flip(s, 1))

    def small_copy(k):
        size = 16 << k
        view = small_full.at[pl.ds(pl.multiple_of((d // (1 << k)) * size, 16), size), :]
        return remote(view, view, small_s.at[k], small_r.at[k], flip(d, 1 << k), s)

    def own_local(g):
        place = d if kinds[g] != "shards" else d % half
        view = full[g].at[pl.ds(pl.multiple_of(place * rows[g], 16), rows[g]), :]
        return pltpu.make_async_copy(low[g], view, local.at[g])

    def spot(array, index):
        return array.at[pl.ds(pl.multiple_of(index * quarter, 16), quarter), :]

    def row_copies(t, source, target):
        mine, theirs = spot(target, 2 * x + c), spot(target, 2 * (1 - x) + c)
        return (
            pltpu.make_async_copy(source.at[x], mine, tok_l.at[t]),
            remote(source.at[1 - x], mine, tok_s.at[t, 0], tok_r.at[t, 0], d, flip(s, 2)),
            remote(source.at[x], mine, tok_s.at[t, 1], tok_r.at[t, 1], d, flip(s, 1)),
            remote(theirs, theirs, tok_s.at[t, 2], tok_r.at[t, 2], d, flip(s, 1)),
        )

    moves = [row_copies(0, tokens, row), row_copies(1, upstream, seed)]

    def row_begin(t):
        for copy in moves[t][:3]:
            copy.start()

    def row_pass(t):
        moves[t][1].wait_recv()
        moves[t][3].start()

    def row_arrived(t):
        own, _, to_core, passed = moves[t]
        own.wait()
        to_core.wait_recv()
        passed.wait_recv()

    own_small = pltpu.make_async_copy(small, small_full.at[pl.ds(pl.multiple_of(d * 16, 16), 16), :], local.at[count])
    own_small.start()
    row_begin(0)

    def begin(g):
        for copy in fetches(g):
            copy.wait()
        low[g][...] = wide[g][...].astype(BF16)
        src = own_piece(g)
        pl.when(z < depth - 1)(lambda: up(g, d, src).start())
        pl.when(z > 0)(lambda: down(g, d, src).start())
        over_y(g, d, src).start()
        own_local(g).start()

    def small_step(k):
        if k == 0:
            own_small.wait()
        else:
            small_copy(k - 1).wait()
        if k < len(steps):
            small_copy(k).start()

    def arrived(g, at):
        over_x(g, at).start()
        if kinds[g] == "share":
            core_a(g, at).start()

    def z_arrival(g, r):
        def low_side():
            at = d - 2 * r
            up(g, at).wait_recv()

            @pl.when(z < depth - 1)
            def _():
                up(g, at).start()

            over_y(g, at).start()
            arrived(g, at)

        def high_side():
            at = d + 2 * r
            down(g, at).wait_recv()

            @pl.when(z > 0)
            def _():
                down(g, at).start()

            over_y(g, at).start()
            arrived(g, at)

        pl.when((z >= r) & active(g, d - 2 * r))(low_side)
        pl.when((z + r < depth) & active(g, d + 2 * r))(high_side)

    other = flip(d, 1)

    def y_one(g, at):
        over_y(g, at).wait_recv()
        arrived(g, at)

    def on_shards(g, r, base, action):
        if r == 0:
            when(active(g, base), lambda: action(base))
        else:
            pl.when((z >= r) & active(g, base - 2 * r))(lambda: action(base - 2 * r))
            pl.when((z + r < depth) & active(g, base + 2 * r))(lambda: action(base + 2 * r))

    def x_one(g, at):
        from_x(g, at).wait_recv()
        if kinds[g] == "share":
            core_b(g, at).start()


    width, pairs = row.shape[1], triple.shape[1] // (6 * HD)
    half_width = width // 2

    def small_row(at, index):
        return small_segment(small_full, at, index)

    def join(pieces):
        return join_rows(seg, pieces)

    def vector(index):
        return small_vector(small_full, seg, dp, index)

    def tile(i, n=quarter):
        return slice(i * n, (i + 1) * n)

    weight_loads = [
        pltpu.make_async_copy(full[g], target, weight_l.at[g]) for g, target in enumerate((triple_w, attend_w, expand_w))
    ]
    row_load = pltpu.make_async_copy(row, row_v, weight_l.at[3])

    def row_ready():
        row_arrived(0)
        row_load.start()

    def every_shard(g, action):
        for r in range(depth):
            on_shards(g, r, other, action)
            if r:
                on_shards(g, r, d, action)

    def weight_ready(g):
        own_local(g).wait()
        if kinds[g] == "share":

            def passed_on(at):
                core_a(g, at).wait_recv()
                core_b(g, at).wait_recv()

            every_shard(g, passed_on)
        weight_loads[g].start()

    def normalize(values, gain, shift):
        center = values - jnp.mean(values, axis=-1, keepdims=True)
        spread_of = jnp.mean(center * center, axis=-1, keepdims=True)
        return (center * lax.rsqrt(spread_of + EPSILON) * gain + shift).astype(BF16)

    def norm_tile(i):
        if i == 0:
            row_load.wait()
        normed[tile(i)] = normalize(row_v[tile(i)].astype(F32), vector(0), vector(1))

    def triple_tile(i):
        if i == 0:
            weight_loads[0].wait()
        n = half_width // seg
        ends = [
            join([small_row((first + c * n + k) // 2, 2 + (first + c * n + k) % 2) for k in range(n)])
            for first in (0, width // seg)
        ]
        bias = jnp.concatenate([ends[0], jnp.zeros((1, half_width), F32), ends[1]], axis=1)
        triple[tile(i)] = (product(normed[tile(i)], triple_w[...]) + bias).astype(BF16)

    def probs_copy(p):
        return pltpu.make_async_copy(probs.at[p % 2], probs_out.at[p], probs_l.at[p % 2])

    def mixed_window(p, core):
        return pl.ds(pl.multiple_of(core * half_width + 2 * HD * p, 2 * HD), 2 * HD)

    def mixed_copy(p):
        view = mixed.at[:, mixed_window(p, c)]
        return remote(view, view, mixed_s.at[p], mixed_r.at[p], d, flip(s, 1))

    def attend_part(p, part):
        if p > 1 and part == 0:
            probs_copy(p - 2).wait()
        columns = [slice(k * half_width + 2 * HD * p, k * half_width + 2 * HD * (p + 1)) for k in range(3)]
        mixed[tile(part), mixed_window(p, c)] = attend_block(
            part, quarter, total[0], triple[tile(part), columns[0]], triple.at[:, columns[1]], triple.at[:, columns[2]],
            probs.at[p % 2],
        )
        if part == 3:
            probs_copy(p).start()
            mixed_copy(p).start()

    out_copies = [
        pltpu.make_async_copy(source, target, out_l.at[k])
        for k, (source, target) in enumerate(
            (
                (normed, normed_out), (triple, triple_out), (mixed, mixed_out), (resid, resid_out),
                (second, second_out), (act, act_out), (slope, slope_out),
            )
        )
    ]

    def resid_tile(i):
        if i == 0:
            weight_loads[1].wait()
            out_copies[0].start()
            out_copies[1].start()
            for p in range(pairs):
                mixed_copy(p).wait()
            out_copies[2].start()
        values = row_v[tile(i)].astype(F32) + product(mixed[tile(i)], attend_w[...]) + vector(4)
        resid[tile(i)] = values
        second[tile(i)] = normalize(values, vector(5), vector(6))

    def expand_tile(i):
        if i == 0:
            weight_loads[2].wait()
            out_copies[3].start()
            out_copies[4].start()
        n = expand_w.shape[1] // seg
        bias = join([small_row((c * n + k) // 4, 7 + (c * n + k) % 4) for k in range(n)])
        for k in range(expand_w.shape[1] // 256):
            part = tile(k, 256)
            value = product(second[tile(i)], expand_w[:, part]) + bias[:, part]
            square = value * value
            bend = jnp.tanh(0.7978845608028654 * value * (1.0 + 0.044715 * square))
            raised = 0.5 * (1.0 + bend)
            act[tile(i), part] = (value * raised).astype(BF16)
            inner = 0.7978845608028654 + (3 * 0.7978845608028654 * 0.044715) * square
            slope[tile(i), part] = (raised + 0.5 * value * (1.0 - bend * bend) * inner).astype(BF16)

    plan = Plan()
    for k in range(len(steps) + 1):
        plan.add(2 * k, small_step, k)
    plan.add(8, row_pass, 0)
    plan.add(11, row_ready)
    plan.add(42, row_begin, 1)
    plan.add(55, row_pass, 1)
    first = 0.0
    ready = []
    for g in range(count):
        piece = rows[g] * wide[g].shape[1] * 2 / 50e3 * 2 / 3
        if kinds[g] != "cols":
            piece /= 2
        hop = piece + 1.5
        plan.add(first, when, active(g, d), functools.partial(begin, g))
        for r in range(depth):
            if r:
                plan.add(first + hop * r, z_arrival, g, r)
                plan.add(first + hop * r + 0.5 * piece + 1.5, on_shards, g, r, d, functools.partial(x_one, g))
            plan.add(first + hop * (r + 1), on_shards, g, r, other, functools.partial(y_one, g))
            plan.add(
                first + hop * (r + 1) + 0.5 * piece + 1.5, on_shards, g, r, other, functools.partial(x_one, g)
            )
        ready.append(first + hop * depth + 0.5 * piece + 1.6)
        if kinds[g] != "shards":
            plan.add(ready[g] + (2 if kinds[g] == "share" else 0), weight_ready, g)
        first += 4 * piece if g == count - 1 else 3 * piece
    for i in range(4):
        plan.add(12.5 + 0.7 * i, norm_tile, i)
    at = ready[0] + 1.5
    for i in range(4):
        plan.add(at, triple_tile, i)
        at += 1.3
    for p in range(pairs):
        for part in range(4):
            plan.add(at, attend_part, p, part)
            at += 0.4 * (part + 1)
    at = max(at, ready[1] + 3.5) + 2.0
    for i in range(4):
        plan.add(at, resid_tile, i)
        at += 1.3
    at = max(at, ready[2] + 1.5)
    for i in range(4):
        plan.add(at, expand_tile, i)
        at += 1.5
    plan.run()

    out_copies[5].start()
    out_copies[6].start()
    for copy in out_copies:
        copy.wait()
    for p in range(max(pairs - 2, 0), pairs):
        probs_copy(p).wait()
    row_arrived(1)
    for move_of in moves:
        for copy in move_of[1:]:
            copy.wait_send()

    for g in range(count):

        def end():
            if kinds[g] == "shards":
                own_local(g).wait()

            @pl.when(z < depth - 1)
            def _():
                up(g, d, own_piece(g)).wait_send()

            @pl.when(z > 0)
            def _():
                down(g, d, own_piece(g)).wait_send()

            over_y(g, d, own_piece(g)).wait_send()

        when(active(g, d), end)

        def finish(g, own_column, at):
            if own_column:
                over_y(g, at).wait_send()
            over_x(g, at).wait_send()
            if kinds[g] == "share":
                core_a(g, at).wait_send()
                core_b(g, at).wait_send()

        for r in range(depth):
            on_shards(g, r, other, functools.partial(finish, g, False))
            if r:
                on_shards(g, r, d, functools.partial(finish, g, True))
                pl.when((z >= r) & (z < depth - 1) & active(g, d - 2 * r))(lambda: up(g, d - 2 * r).wait_send())
                pl.when((z + r < depth) & (z > 0) & active(g, d + 2 * r))(lambda: down(g, d + 2 * r).wait_send())


def spread(dp, shards, small, tokens, upstream, total):
    kinds = ["cols", "share", "cols", "shards"]
    rows = [member.shape[0] for member in shards]
    count = len(rows)
    quarter, width = tokens.shape[1:]
    length = 4 * quarter
    dma = pltpu.SemaphoreType.DMA
    any_space = pl.BlockSpec(memory_space=pl.ANY)
    vmem = pl.BlockSpec(memory_space=pltpu.VMEM)
    held = [(m.shape[0], m.shape[1] // 2 if kind == "cols" else m.shape[1]) for m, kind in zip(shards, kinds)]
    whole = [(dp * r // 2 if kind == "shards" else dp * r, n) for (r, n), kind in zip(held, kinds)]
    kept = part_start(4, quarter)
    pairs = width // (4 * HD)
    hidden = whole[2][1]
    states = [
        ((length, width), BF16), ((length, 3 * width // 2), BF16), ((pairs, 2, kept, quarter), BF16),
        ((length, width), BF16), ((length, width), F32), ((length, width), BF16),
        ((length, hidden), BF16), ((length, hidden), BF16),
    ]
    slots = [(shape if k != 2 else (2, *shape[1:]), kind) for k, (shape, kind) in enumerate(states)]
    return pl.pallas_call(
        functools.partial(spread_kernel, dp, kinds, rows, quarter, width // dp),
        out_shape=[jax.ShapeDtypeStruct(shape, BF16) for shape in whole]
        + [jax.ShapeDtypeStruct((dp * 16, 128), F32)]
        + [jax.ShapeDtypeStruct((length, width), BF16)] * 2
        + [jax.ShapeDtypeStruct(*state) for state in states],
        in_specs=[any_space] * (count + 3) + [pl.BlockSpec(memory_space=pltpu.SMEM)],
        out_specs=[any_space] * count + [vmem] + [any_space] * (2 + len(states)),
        scratch_shapes=[pltpu.VMEM(shape, F32) for shape in held]
        + [pltpu.VMEM(shape, BF16) for shape in held]
        + [pltpu.VMEM((length, width), BF16)]
        + [pltpu.VMEM(*slot) for slot in slots]
        + [pltpu.VMEM(shape, BF16) for shape in whole[:3]]
        + [dma((count, 3)), dma((count + 1,))]
        + [dma((count, dp))] * 4
        + [dma((dp,))] * 2
        + [dma((count, dp))] * 2
        + [dma((dp,))] * 2
        + [dma((len(doubling_steps(dp)),))] * 2
        + [dma((2,)), dma((2, 3)), dma((2, 3))]
        + [dma((4,)), dma((7,)), dma((2,)), dma((pairs,)), dma((pairs,))],
        compiler_params=pltpu.CompilerParams(
            collective_id=1, has_side_effects=True, vmem_limit_bytes=60 * MIB
        ),
        name="spread_weights",
    )(*shards, small, tokens, upstream, total)


def back_kernel(dp, kinds, rows, quarter, seg, *refs):
    count = len(rows)
    depth, half = dp // 2, dp // 2
    (
        shrink_in, expand_in, attend_in, triple_w_in, small_full, row_in, seed_in, normed_in, triple_in, probs_in, mixed_in,
        resid_in, second_in, act_in, slope_in,
    ) = refs[:15]
    outs, (small_out, result_out, tokens_out) = refs[15 : 15 + count], refs[15 + count : 18 + count]
    at_ref = 18 + count
    acc, x_buf, y_buf, z_buf, b_buf = [refs[at_ref + k * count : at_ref + (k + 1) * count] for k in range(5)]
    (
        act, slope, seed, shrink_w, second, expand_w, partial, other, resid, mixed, attend_w, grad_own, grad_mixed, probs,
        dkeys, dvalues, row_own, send_own, sum_recv, n_recv, stage, small_buf,
        load, resid_l, probs_l, x_s, x_r, y_s, y_r, u_s, u_r, n_s, n_r, f_s, f_r, small_s, small_r,
        part_s, part_r, sum_s, sum_r, one_s, one_r, give_s, give_r,
    ) = refs[at_ref + 5 * count :]
    d, s, z, y, x, c = own_place()
    dp_steps = doubling_steps(dp)
    twin = flip(s, 1)
    length, width = seed.shape
    hidden, half_width = act.shape[1], width // 2
    pairs = half_width // (2 * HD)
    normed, grad_pre, branch = second, slope, partial
    triple = slope.at[:, pl.ds(0, 3 * half_width)]
    grad_triple = act.at[:, pl.ds(0, 3 * half_width)]
    triple_w = expand_w.at[:, pl.ds(0, 3 * half_width)]

    sources = [
        (act_in, act), (seed_in, seed), (shrink_in, shrink_w), (slope_in, slope), (expand_in, expand_w),
        (second_in, second), (mixed_in, mixed), (attend_in, attend_w),
        (normed_in, normed), (triple_in, triple), (triple_w_in, triple_w),
    ]
    loads = [pltpu.make_async_copy(source, target, load.at[k]) for k, (source, target) in enumerate(sources)]
    row_loads = [
        pltpu.make_async_copy(
            row_in.at[pl.ds(pl.multiple_of((2 * h + c) * quarter, 16), quarter), :], row_own.at[h], load.at[len(sources) + h]
        )
        for h in range(2)
    ]

    def resid_load(i):
        return pltpu.make_async_copy(resid_in.at[pl.ds(i * quarter, quarter), :], resid.at[i % 2], resid_l.at[i % 2])

    def probs_load(k):
        return pltpu.make_async_copy(probs_in.at[k // 2, k % 2], probs.at[k % 2], probs_l.at[k % 2])

    for copy in loads[:8]:
        copy.start()
    resid_load(0).start()
    resid_load(1).start()
    for copy in row_loads:
        copy.start()
    probs_load(0).start()
    probs_load(1).start()

    greet(depth, dp_steps)

    small_out[...] = jnp.zeros_like(small_out)


    def layers(g):
        return depth if kinds[g] != "shards" else depth // 2

    def first_layer(g):
        return 0 if kinds[g] != "shards" else c * (depth // 2)

    def layer(g, n):
        if kinds[g] != "shards":
            return sorted(range(depth), key=lambda k: -abs(2 * k - depth + 1))[n]
        return n + c * (depth // 2 - 1 - 2 * n)

    def of(j, own):
        return 2 * j + (y if own else 1 - y)

    def place(g, at, units, n):
        m = rows[g] // 3
        return pl.ds(pl.multiple_of(at * rows[g] + units * m, 16), n * m)

    def span(g, units, n):
        return place(g, 0, units, n)

    def add(g, window, extra):
        acc[g][window, :] = acc[g][window, :] + extra

    def over_x(g, at):
        return remote(
            acc[g].at[place(g, at, 2 * (1 - x), 1), :], x_buf[g].at[at], x_s.at[g, at], x_r.at[g, at], d, flip(s, 2)
        )

    def over_y(g, j):
        source = acc[g].at[place(g, of(j, False), x, 2), :]
        return remote(source, y_buf[g].at[j], y_s.at[g, j], y_r.at[g, j], flip(d, 1), s)

    def up(g, j):
        source = acc[g].at[place(g, of(j, True), x, 2), :]
        return remote(source, z_buf[g].at[j], u_s.at[g, j], u_r.at[g, j], d + 2, s)

    def down_slot(g, j, at_z):
        return jnp.where(j + first_layer(g) == at_z, layers(g), j)

    def down(g, j):
        source = acc[g].at[place(g, of(j, True), x, 2), :]
        return remote(source, z_buf[g].at[down_slot(g, j, z - 1)], n_s.at[g, j], n_r.at[g, j], d - 2, s)

    def stage_a(g, n, own):
        over_x(g, of(layer(g, n), own)).start()

    def stage_c(g, n, own):
        j = layer(g, n)
        at = of(j, own)
        over_x(g, at).wait_recv()
        add(g, place(g, at, 2 * x, 1), x_buf[g][at])
        if not own:
            over_y(g, j).start()

    def stage_d(g, n):
        j = layer(g, n)
        over_y(g, j).wait_recv()
        add(g, place(g, of(j, True), x, 2), y_buf[g][j])

    def stage_e(g, n, hop):
        j = layer(g, n)
        k = j + first_layer(g)
        window = place(g, of(j, True), x, 2)

        @pl.when((z == hop) & (k > hop))
        def _():
            if hop:
                up(g, j).wait_recv()
                add(g, window, z_buf[g][j])
            up(g, j).start()

        @pl.when((z == depth - 1 - hop) & (k < depth - 1 - hop))
        def _():
            if hop:
                down(g, j).wait_recv()
                add(g, window, z_buf[g][down_slot(g, j, z)])
            down(g, j).start()

    def own_layer(g):
        return z - first_layer(g)

    def ours(g, action):
        if kinds[g] != "shards":
            action()
        else:
            pl.when((z >= first_layer(g)) & (z < first_layer(g) + layers(g)))(action)

    def out_rows(g, units, n):
        return outs[g].at[c, span(g, units, n), :] if kinds[g] != "shards" else outs[g].at[span(g, units, n), :]

    def final_share(g):
        source = acc[g].at[place(g, of(own_layer(g), True), 2 * x, 1), :]
        return remote(source, out_rows(g, 2 * x, 1), f_s.at[g, 0], f_r.at[g, 0], d, flip(s, 2))

    def final_swap(g):
        source = acc[g].at[place(g, of(own_layer(g), True), 1, 1), :]
        return remote(source, b_buf[g], f_s.at[g, 1], f_r.at[g, 1], d, flip(s, 2))

    def final_core(g):
        view = out_rows(g, 0, 3)
        return remote(view, view, f_s.at[g, 2], f_r.at[g, 2], d, twin)

    def finish_one(g):
        def run():
            j = own_layer(g)
            at = of(j, True)
            window = place(g, at, x, 2)

            @pl.when(z > 0)
            def _():
                up(g, j).wait_recv()
                add(g, window, z_buf[g][j])

            @pl.when(z < depth - 1)
            def _():
                down(g, j).wait_recv()
                add(g, window, z_buf[g][layers(g)])

            final_share(g).start()
            final_swap(g).start()
            out_rows(g, 2 * x, 1)[...] = acc[g][place(g, at, 2 * x, 1), :]

        ours(g, run)

    def finish_two(g):
        def run():
            final_swap(g).wait_recv()
            out_rows(g, 1, 1)[...] = acc[g][place(g, of(own_layer(g), True), 1, 1), :] + b_buf[g][...]
            final_share(g).wait_recv()
            final_core(g).start()

        ours(g, run)

    small_partners = [(flip(d, step), s) for step in dp_steps] + [(d, twin), (d, flip(s, 2))]

    def small_copy(k):
        d_to, s_to = small_partners[k]
        return remote(small_out, small_buf.at[k], small_s.at[k], small_r.at[k], d_to, s_to)

    def small_finish(k):
        small_copy(k).wait()
        small_out[...] = small_out[...] + small_buf[k]


    def tile(i, n=quarter):
        return slice(i * n, (i + 1) * n)

    def own_tile(h):
        return pl.ds(pl.multiple_of((2 * h + c) * quarter, 16), quarter)

    def twin_tile(h):
        return pl.ds(pl.multiple_of((2 * h + 1 - c) * quarter, 16), quarter)

    def vector(index):
        return small_vector(small_full, seg, dp, index)

    def sums(index, values, columns=slice(None)):
        small_out[index : index + 1, columns] += jnp.sum(values, axis=0, keepdims=True)

    def shrink_grad(k):
        if k == 0:
            loads[0].wait()
            loads[1].wait()
        acc[0][tile(k, 256), :] = product_across(act[:, tile(k, 256)], seed[...]).astype(BF16)

    def sum_copy(h):
        return remote(send_own.at[h], sum_recv.at[h], sum_s.at[h], sum_r.at[h], d, twin)

    def result_partial(h):
        if h == 0:
            loads[2].wait()
        send_own[h] = product(act[twin_tile(h), :], shrink_w[...]).astype(BF16)
        sum_copy(h).start()

    def grad_pre_tile(i):
        if i == 0:
            loads[3].wait()
        for k in range(hidden // 256):
            columns = tile(k, 256)
            value = product_back(seed[tile(i)], shrink_w[columns, :]) * slope[tile(i), columns].astype(F32)
            low_value = value.astype(BF16)
            grad_pre[tile(i), columns] = low_value
            total = jnp.sum(low_value.astype(F32), axis=0, keepdims=True)
            spot = (pl.ds(7 + (hidden // width) * c + k * 256 // width, 1), slice(k * 256 % width, k * 256 % width + 256))
            small_out[spot] = small_out[spot] + total
        sums(11, 0.5 * seed[tile(i)].astype(F32))

    def part_copy(i):
        return remote(partial.at[tile(i)], other.at[tile(i)], part_s.at[i], part_r.at[i], d, twin)

    def n_two_tile(i):
        if i == 0:
            loads[4].wait()
        partial[tile(i)] = product_back(grad_pre[tile(i)], expand_w[...]).astype(BF16)
        part_copy(i).start()

    def expand_grad(k):
        if k == 0:
            loads[5].wait()
        acc[1][tile(k, 256), :] = product_across(second[:, tile(k, 256)], grad_pre[...]).astype(BF16)

    def later_loads():
        for copy in loads[8:]:
            copy.start()

    def back_norm(n, values, gain, index, scale):
        center = values - jnp.mean(values, axis=-1, keepdims=True)
        r = lax.rsqrt(jnp.mean(center * center, axis=-1, keepdims=True) + EPSILON)
        hat = center * r
        sums(index, scale * n * hat)
        sums(index + 1, scale * n)
        e = n * gain
        return r * (e - jnp.mean(e, axis=-1, keepdims=True) - hat * jnp.mean(e * hat, axis=-1, keepdims=True))

    def resid_tile(i):
        resid_load(i).wait()
        part_copy(i).wait()
        n = partial[tile(i)].astype(F32) + other[tile(i)].astype(F32)
        grad = seed[tile(i)].astype(F32) + back_norm(n, resid[i % 2], vector(5), 5, 0.5)
        low_grad = grad.astype(BF16)
        branch[tile(i)] = low_grad
        sums(4, 0.5 * low_grad.astype(F32))

        @pl.when(c == i % 2)
        def _():
            h = i // 2
            grad_own[h] = grad
            sum_copy(h).wait_recv()
            value = resid[i % 2] + product(act[tile(i)], shrink_w[...]) + sum_recv[h].astype(F32) + vector(11)
            stage[h] = value.astype(BF16)

        if i + 2 < 4:
            resid_load(i + 2).start()

    def give_copy(t):
        return remote(stage.at[1 - x], (result_out, tokens_out)[t].at[x], give_s.at[t], give_r.at[t], d, flip(s, 2))

    def give_back(t):
        (result_out, tokens_out)[t][x] = stage[x]
        give_copy(t).start()

    def attend_grad(k):
        if k == 0:
            loads[6].wait()
        columns = pl.ds(pl.multiple_of(c * half_width, 128), half_width)
        acc[2][tile(k, 256), :] = product_across(mixed[:, tile(k, 256)], branch[:, columns]).astype(BF16)

    def mixed_tile(i):
        if i == 0:
            loads[7].wait()
        rows_c = pl.ds(pl.multiple_of(c * half_width, 16), half_width)
        grad_mixed[tile(i)] = product_back(branch[tile(i)], attend_w[rows_c, :]).astype(BF16)

    def attend_back_step(k, part):
        p, head = k // 2, k % 2
        if part == 3:
            probs_load(k).wait()
        if k == 0 and part == 3:
            loads[9].wait()
        columns = [slice(n * half_width + 2 * HD * p, n * half_width + 2 * HD * (p + 1)) for n in range(3)]
        grad_query = attend_back_block(
            head, part, quarter, triple[tile(part), columns[0]], triple.at[:, columns[1]], triple.at[:, columns[2]],
            grad_mixed[tile(part), 2 * HD * p : 2 * HD * (p + 1)],
            probs[k % 2, part_start(part, quarter) : part_start(part + 1, quarter)], dkeys, dvalues,
            part == 3 and head == 0,
        )
        if head:
            grad_query = jnp.where(head_mask(), grad_triple[tile(part), columns[0]], grad_query)
            place_q = pl.ds(pl.multiple_of(c * half_width + 2 * HD * p, 128), 2 * HD)
            small_out[2:3, place_q] += jnp.sum(grad_query.astype(F32), axis=0, keepdims=True)
        grad_triple[tile(part), columns[0]] = grad_query
        if part == 0:
            if k + 2 < 2 * pairs:
                probs_load(k + 2).start()
            if head:
                grad_triple[:, columns[1]] = dkeys[...].astype(BF16)
                low_values = dvalues[...].astype(BF16)
                grad_triple[:, columns[2]] = low_values
                small_out[3:4, place_q] += jnp.sum(low_values.astype(F32), axis=0, keepdims=True)

    def triple_grad(k):
        if k == 0:
            loads[8].wait()
        acc[3][tile(k, 256), :] = product_across(normed[:, tile(k, 256)], grad_triple[...]).astype(BF16)

    def one_copy(h):
        return remote(send_own.at[h], n_recv.at[h], one_s.at[h], one_r.at[h], d, twin)

    def n_one_partial(h):
        if h == 0:
            loads[10].wait()
        sum_copy(h).wait_send()
        send_own[h] = product_back(grad_triple[twin_tile(h), :], triple_w[...]).astype(BF16)
        one_copy(h).start()

    def first_tile(h):
        if h == 0:
            give_copy(0).wait_send()
        row_loads[h].wait()
        n = product_back(grad_triple[own_tile(h), :], triple_w[...])
        one_copy(h).wait_recv()
        n = n + n_recv[h].astype(F32)
        grad = grad_own[h] + back_norm(n, row_own[h].astype(F32), vector(0), 0, 1.0)
        stage[h] = grad.astype(BF16)


    plan = Plan()
    clock = [2.0]

    def compute(micros, action, *args):
        plan.add(clock[0], action, *args)
        clock[0] += micros

    made = []

    def group_made():
        made.append(clock[0] - 0.01)

    for k in range(hidden // 256):
        compute(0.5, shrink_grad, k)
    group_made()
    for h in range(2):
        compute(0.8, result_partial, h)
    for i in range(4):
        compute(0.9, grad_pre_tile, i)
    for i in range(4):
        compute(0.8, n_two_tile, i)
    for k in range(width // 256):
        compute(1.0, expand_grad, k)
    group_made()
    compute(0.0, later_loads)
    for i in range(4):
        compute(1.5, resid_tile, i)
    compute(0.2, give_back, 0)
    for k in range(width // 256):
        compute(0.4, attend_grad, k)
    group_made()
    for i in range(4):
        compute(0.3, mixed_tile, i)
    for k in range(2 * pairs):
        for part in reversed(range(4)):
            compute(0.25 * (part + 1), attend_back_step, k, part)
    for k in range(width // 256):
        compute(0.8, triple_grad, k)
    group_made()
    for h in range(2):
        compute(0.6, n_one_partial, h)
    compute(1.0, lambda: None)
    for h in range(2):
        compute(1.8, first_tile, h)
    compute(0.2, give_back, 1)
    for k in range(len(small_partners)):
        compute(0.0, lambda k: small_copy(k).start(), k)
        compute(3.0, lambda: None)
        compute(0.1, small_finish, k)

    done = 0.0
    for g in range(count):
        unit = rows[g] * acc[g].shape[1] * 2 / 50e3 / 3
        done = max(done, made[g])
        for own in (False, True):
            for n in range(layers(g)):
                plan.add(max(done - 4.0, made[g]), stage_a, g, n, own)
                done += unit
                plan.add(done + 1.5, stage_c, g, n, own)
                if own:
                    plan.add(done + 3.5, stage_d, g, n)
                    for hop in range(depth - 1):
                        plan.add(done + 4.0 + (2 * unit + 1.5) * hop, stage_e, g, n, hop)
        last = done + 4.0 + (2 * unit + 1.5) * (depth - 1)
        plan.add(last, finish_one, g)
        plan.add(last + unit + 2.0, finish_two, g)
    plan.run()

    for g in range(count):

        def drain():
            final_share(g).wait_send()
            final_swap(g).wait_send()
            if kinds[g] == "shards":
                final_core(g).wait_send()

        ours(g, drain)
        if kinds[g] == "shards":
            pl.when((z < first_layer(g)) | (z >= first_layer(g) + layers(g)))(lambda: final_core(g).wait_recv())
        else:
            final_core(g).wait()
        for j in range(layers(g)):
            over_x(g, of(j, False)).wait_send()
            over_x(g, of(j, True)).wait_send()
            over_y(g, j).wait_send()
            pl.when(j + first_layer(g) > z)(lambda: up(g, j).wait_send())
            pl.when(j + first_layer(g) < z)(lambda: down(g, j).wait_send())
    for h in range(2):
        one_copy(h).wait_send()
    give_copy(0).wait_recv()
    give_copy(1).wait()


def back(dp, weights, small_full, row, seed, normed, triple, probs, mixed, resid, second, act, slope):
    triple_w, attend_w, expand_w, shrink_w = weights
    kinds = ["shards", "cols", "cols", "cols"]
    length, width = row.shape
    quarter, hidden = length // 4, act.shape[1]
    shapes = [(hidden, width), (width, hidden), (width, width // 2), (width, 3 * width // 2)]
    owners = [dp // 2 if kind == "shards" else dp for kind in kinds]
    rows = [m[0] // n for m, n in zip(shapes, owners)]
    count, depth = len(rows), dp // 2
    pairs = width // (4 * HD)
    dma = pltpu.SemaphoreType.DMA
    any_space = pl.BlockSpec(memory_space=pl.ANY)
    vmem = pl.BlockSpec(memory_space=pltpu.VMEM)

    def buffers(lead, part, extra=0):
        slots = [() if lead is None else (n // lead + extra,) for n in owners]
        return [pltpu.VMEM((*slot, r // 3 * part, m[1]), BF16) for slot, r, m in zip(slots, rows, shapes)]

    partners = len(doubling_steps(dp)) + 2
    halves = (2, quarter, width)
    working = [
        (act.shape, BF16), (act.shape, BF16), (row.shape, BF16), (shrink_w.shape, BF16), (row.shape, BF16),
        (expand_w.shape, BF16), (row.shape, BF16), (row.shape, BF16), (halves, F32), (row.shape, BF16),
        (attend_w.shape, BF16), (halves, F32), ((length, width // 2), BF16), ((2, *probs.shape[2:]), BF16),
        ((length, 2 * HD), F32), ((length, 2 * HD), F32), (halves, BF16), (halves, BF16), (halves, BF16), (halves, BF16),
        (halves, BF16), ((partners, 16, width), F32),
    ]
    return pl.pallas_call(
        functools.partial(back_kernel, dp, kinds, rows, quarter, width // dp),
        out_shape=[
            jax.ShapeDtypeStruct((r, m[1]) if kind == "shards" else (2, r, m[1]), BF16)
            for r, m, kind in zip(rows, shapes, kinds)
        ]
        + [jax.ShapeDtypeStruct((16, width), F32)]
        + [jax.ShapeDtypeStruct(halves, BF16)] * 2,
        in_specs=[any_space] * 4 + [vmem] + [any_space] * 10,
        out_specs=[vmem] * (count + 3),
        scratch_shapes=[pltpu.VMEM(m, BF16) for m in shapes]
        + buffers(1, 1)
        + buffers(2, 2)
        + buffers(2, 2, 1)
        + buffers(None, 1)
        + [pltpu.VMEM(*item) for item in working]
        + [dma((13,)), dma((2,)), dma((2,))]
        + [dma((count, dp))] * 2
        + [dma((count, depth))] * 6
        + [dma((count, 3))] * 2
        + [dma((partners,))] * 2
        + [dma((4,))] * 2
        + [dma((2,))] * 6,
        compiler_params=pltpu.CompilerParams(
            collective_id=2, has_side_effects=True, vmem_limit_bytes=60 * MIB
        ),
        name="back_and_fold",
    )(shrink_w, expand_w, attend_w, triple_w, small_full, row, seed, normed, triple, probs, mixed, resid, second, act, slope)


def head_mask():
    return lax.broadcasted_iota(jnp.int32, (1, 2 * HD), 1) < HD


def part_start(part, quarter):
    return quarter * (part * (part + 1) // 2)


def attend_block(part, quarter, total, query, k_ref, v_ref, probs_ref):
    first = head_mask()
    length = quarter * (part + 1)
    key_pos = lax.broadcasted_iota(jnp.int32, (length, 1), 0)
    key_pos = jnp.where(key_pos < total, key_pos, 1 << 20)
    allowed = key_pos <= lax.broadcasted_iota(jnp.int32, (1, quarter), 1) + part * quarter
    query = query * jnp.asarray(HD**-0.5, BF16)
    sums = []
    for head in range(2):
        mask = first if head == 0 else ~first
        scores = product_back(k_ref[:length], jnp.where(mask, query, jnp.zeros_like(query)))
        scores = jnp.where(allowed, scores, NEG_FILL)
        exponent = jnp.exp(scores - jnp.max(scores, axis=0, keepdims=True))
        probs = (exponent * (1.0 / jnp.sum(exponent, axis=0, keepdims=True))).astype(BF16)
        probs_ref[head, part_start(part, quarter) : part_start(part + 1, quarter)] = probs
        sums.append(product_across(probs, v_ref[:length]))
    return jnp.where(first, sums[0], sums[1]).astype(BF16)


def attend_kernel(quarter, total, q_ref, k_ref, v_ref, mixed_ref, probs_ref):
    for part in range(4):
        rows = slice(part * quarter, (part + 1) * quarter)
        mixed_ref[rows] = attend_block(part, quarter, total[0], q_ref[rows], k_ref, v_ref, probs_ref.at[0])


def attend(triple, total):
    tokens, width = triple.shape[0], triple.shape[1] // 3
    quarter = tokens // 4
    pairs = width // (2 * HD)
    kept = part_start(4, quarter)

    def block(shift):
        return pl.BlockSpec((tokens, 2 * HD), lambda p, _: (0, p + shift))

    return pl.pallas_call(
        functools.partial(attend_kernel, quarter),
        grid_spec=pltpu.PrefetchScalarGridSpec(
            num_scalar_prefetch=1,
            grid=(pairs,),
            in_specs=[block(0), block(pairs), block(2 * pairs)],
            out_specs=[block(0), pl.BlockSpec((1, 2, kept, quarter), lambda p, _: (p, 0, 0, 0))],
        ),
        out_shape=[
            jax.ShapeDtypeStruct((tokens, width), BF16),
            jax.ShapeDtypeStruct((pairs, 2, kept, quarter), BF16),
        ],
        compiler_params=pltpu.CompilerParams(vmem_limit_bytes=50 * MIB),
        name="attend",
    )(total, triple, triple, triple)


def attend_back_block(head, part, quarter, query, k_ref, v_ref, grad, probs, dkeys, dvalues, fresh):
    length = quarter * (part + 1)
    mask = head_mask() if head == 0 else ~head_mask()
    own_query = jnp.where(mask, query * jnp.asarray(HD**-0.5, BF16), jnp.zeros_like(query))
    own_grad = jnp.where(mask, grad, jnp.zeros_like(grad))
    wide = probs.astype(F32)
    grad_probs = product_back(v_ref[:length], own_grad)
    delta = jnp.sum(wide * grad_probs, axis=0, keepdims=True)
    grad_scores = (wide * (grad_probs - delta)).astype(BF16)
    dv = product(probs, own_grad)
    dk = product(grad_scores, own_query)
    if fresh:
        dvalues[:length] = dv
        dkeys[:length] = dk
    else:
        dvalues[:length] += dv
        dkeys[:length] += dk
    return (product_across(grad_scores, k_ref[:length]) * HD**-0.5).astype(BF16)


def attend_back_kernel(quarter, q_ref, k_ref, v_ref, g_ref, probs_ref, dq_ref, dk_ref, dv_ref, dkeys, dvalues):
    for part in reversed(range(4)):
        rows = slice(part * quarter, (part + 1) * quarter)
        kept = slice(part_start(part, quarter), part_start(part + 1, quarter))
        dq = [
            attend_back_block(
                head, part, quarter, q_ref[rows], k_ref, v_ref, g_ref[rows], probs_ref[0, head, kept], dkeys, dvalues,
                part == 3 and head == 0,
            )
            for head in range(2)
        ]
        dq_ref[rows] = jnp.where(head_mask(), dq[0], dq[1])
    dk_ref[...] = dkeys[...].astype(BF16)
    dv_ref[...] = dvalues[...].astype(BF16)


def attend_back(triple, grad, probs):
    tokens, width = triple.shape[0], triple.shape[1] // 3
    quarter = tokens // 4
    pairs = width // (2 * HD)

    def block(shift):
        return pl.BlockSpec((tokens, 2 * HD), lambda p: (0, p + shift))

    return pl.pallas_call(
        functools.partial(attend_back_kernel, quarter),
        grid=(pairs,),
        in_specs=[block(0), block(pairs), block(2 * pairs), block(0)]
        + [pl.BlockSpec((1, 2, part_start(4, quarter), quarter), lambda p: (p, 0, 0, 0))],
        out_specs=[block(0)] * 3,
        out_shape=[jax.ShapeDtypeStruct((tokens, width), BF16)] * 3,
        scratch_shapes=[pltpu.VMEM((tokens, 2 * HD), F32)] * 2,
        compiler_params=pltpu.CompilerParams(vmem_limit_bytes=50 * MIB),
        name="attend_back",
    )(triple, triple, triple, grad, probs)


def take(array, index, size, axis):
    return lax.dynamic_slice_in_dim(array, index * size, size, axis)


def gather_plain(matrices, small, tokens, core, upper):
    triple, attend_full, expand, shrink = [
        lax.all_gather(m.astype(BF16), "dp", axis=0, tiled=True) for m in matrices
    ]
    width = triple.shape[0]
    thirds = triple.reshape(width, 3, width)
    row = lax.all_gather(tokens, "seq", axis=1, tiled=True)
    return (
        take(thirds, core, width // 2, 2).reshape(width, -1),
        attend_full,
        take(expand, core, expand.shape[1] // 2, 1),
        take(shrink, core, shrink.shape[0] // 2, 0),
        lax.all_gather(small, "dp", axis=0),
        jnp.where(upper, row[1], row[0]),
    )


def fold_plain(grads, small, core):
    def by_core(array):
        empty = jnp.zeros_like(array)
        return jnp.stack([jnp.where(core == 0, array, empty), jnp.where(core == 1, array, empty)], axis=1)

    shrink, *others = grads
    wide = jnp.swapaxes(by_core(shrink), 0, 1).reshape(-1, shrink.shape[1])
    arrays = [wide] + [by_core(m) for m in others]
    sums = [lax.psum(lax.psum_scatter(m, "dp", scatter_dimension=0, tiled=True), "seq") for m in arrays]
    sums = [sums[0]] + [jnp.swapaxes(m, 0, 1) for m in sums[1:]]
    return sums, lax.psum(lax.psum_scatter(small, "dp", scatter_dimension=0, tiled=True), "seq").reshape(-1)


def outputs(result, tokens_grad, sums, small_out):
    width = result.shape[-1]
    shrink_sum, expand_sum, attend_sum, triple_sum = [member.astype(F32) for member in sums]
    triple_sum = triple_sum.reshape(2, -1, 3, width // 2).transpose(1, 2, 0, 3).reshape(-1, 3 * width)
    expand_sum, attend_sum = [m.transpose(1, 0, 2).reshape(m.shape[1], -1) for m in (expand_sum, attend_sum)]
    return (
        result,
        tokens_grad,
        small_out[0],
        small_out[1],
        triple_sum,
        small_out[2],
        attend_sum,
        small_out[3],
        small_out[4],
        small_out[5],
        expand_sum,
        small_out[6],
        shrink_sum,
        small_out[7],
    )


def body(
    dp,
    tokens,
    lengths,
    first_gain,
    first_shift,
    triple_weight,
    triple_bias,
    attend_weight,
    attend_bias,
    second_gain,
    second_shift,
    expand_weight,
    expand_bias,
    shrink_weight,
    shrink_bias,
    upstream,
):
    row_count, quarter, width = tokens.shape
    matrices = (triple_weight, attend_weight, expand_weight, shrink_weight)
    vectors = (first_gain, first_shift, triple_bias, attend_bias, second_gain, second_shift, expand_bias, shrink_bias)
    sizes = [member.shape[0] for member in vectors]
    total_small = sum(sizes)
    by_kernel = dp & (dp - 1) == 0 and dp > 2 and all(m.shape[0] % 48 == 0 for m in matrices)
    segs = total_small * dp // width
    by_kernel = by_kernel and segs <= 16 and width // dp <= 128
    place = lax.axis_index("seq")
    upper, core = place // 2 == 1, place % 2

    totals = lengths[:, 0] + lengths[:, 1]
    total = jnp.where(upper, totals[1], totals[0]).reshape(1)

    across = [(k, (k + 2) % 4) for k in range(4)]
    twin = [(k, k + 1 - 2 * (k % 2)) for k in range(4)]

    def halves(partial):
        view = partial.reshape(2, 2, quarter, width)
        mine = jnp.where(core == 0, view[:, 0], view[:, 1])
        theirs = jnp.where(core == 0, view[:, 1], view[:, 0]).astype(BF16)
        return mine + lax.ppermute(theirs, "seq", twin).astype(F32)

    def own_half(array):
        view = array.reshape(2, 2, quarter, width)
        return jnp.where(core == 0, view[:, 0], view[:, 1])

    def give_back(array):
        mine = jnp.where(upper, array[1], array[0])
        theirs = lax.ppermute(jnp.where(upper, array[0], array[1]), "seq", across)
        return jnp.stack([jnp.where(upper, theirs, mine), jnp.where(upper, mine, theirs)])

    def of_core(vector):
        return take(vector, core, vector.shape[0] // 2, 0)

    def spread_out(part):
        empty = jnp.zeros_like(part)
        return jnp.concatenate([jnp.where(core == 0, part, empty), jnp.where(core == 1, part, empty)])

    def whole_row(array):
        mine = jnp.where(upper, array[1], array[0])
        theirs = lax.ppermute(jnp.where(upper, array[0], array[1]), "seq", across)
        pair = jnp.stack([jnp.where(upper, theirs, mine), jnp.where(upper, mine, theirs)])
        others = lax.ppermute(pair, "seq", twin)
        return jnp.stack(
            [jnp.where(core == 0, pair, others), jnp.where(core == 0, others, pair)], axis=1
        ).reshape(-1, width)

    small = jnp.concatenate(vectors)
    if by_kernel:
        small = jnp.pad(small.reshape(segs, -1), ((0, 16 - segs), (0, 128 - width // dp)))
        *weights, small_full, row, seed_low, normed, triple, probs, mixed, resid, second, act, slope = spread(
            dp, matrices, small, tokens, upstream, total
        )
        *sums, small_sum, result, tokens_grad = back(
            dp, weights, small_full, row, seed_low, normed, triple, probs, mixed, resid, second, act, slope
        )
        out, at = [], 0
        for size in sizes:
            n = size * dp // width
            out.append(
                lax.dynamic_slice_in_dim(small_sum[at : at + n].reshape(-1), lax.axis_index("dp") * size, size)
            )
            at += n
        return outputs(result, tokens_grad, sums, out)
    *weights, small_full, row = gather_plain(matrices, small, tokens, core, upper)
    floats, at = [], 0
    for size in sizes:
        floats.append(small_full[:, at : at + size].reshape(-1).astype(BF16).astype(F32))
        at += size
    gain_one, shift_one, bias_triple, bias_attend, gain_two, shift_two, bias_expand, bias_shrink = floats
    triple_low, attend_low, expand_low, shrink_low = weights
    seed_low = whole_row(upstream)
    flat_tokens = row.astype(F32)
    seed = seed_low.astype(F32)

    bias_core = jnp.concatenate(
        [of_core(bias_triple[:width]), jnp.zeros((width // 2,), F32), of_core(bias_triple[width:])]
    )
    normed_low = layer_norm(flat_tokens, gain_one, shift_one).astype(BF16)
    triple = (product(normed_low, triple_low) + bias_core).astype(BF16)
    mixed_core, probs = attend(triple, total)
    mixed_other = lax.ppermute(mixed_core, "seq", twin)
    mixed_low = jnp.concatenate(
        [jnp.where(core == 0, mixed_core, mixed_other), jnp.where(core == 0, mixed_other, mixed_core)], axis=1
    )
    resid = flat_tokens + product(mixed_low, attend_low) + bias_attend
    normed_two_low = layer_norm(resid, gain_two, shift_two).astype(BF16)
    activated, gelu_pull = jax.vjp(gelu_tanh, product(normed_two_low, expand_low) + of_core(bias_expand))
    act_low, slope = activated.astype(BF16), gelu_pull(jnp.ones_like(activated))[0]
    _, second_pull = jax.vjp(layer_norm, resid, gain_two, shift_two)

    grad_pre = (product_back(seed_low, shrink_low) * slope.astype(F32)).astype(BF16)
    partial = product_back(grad_pre, expand_low).astype(BF16)
    other_partial = lax.ppermute(partial, "seq", twin)
    shrink_grad = product_across(act_low, seed_low)
    expand_grad = product_across(normed_two_low, grad_pre)
    result = own_half(resid) + halves(product(act_low, shrink_low)) + bias_shrink
    result = give_back(result.astype(BF16))
    shrink_bias_grad = 0.5 * jnp.sum(seed, axis=0)
    expand_bias_grad = spread_out(jnp.sum(grad_pre.astype(F32), axis=0))
    resid_part, second_gain_grad, second_shift_grad = second_pull(partial.astype(F32) + other_partial.astype(F32))
    grad_resid = seed + resid_part
    grad_branch = grad_resid.astype(BF16)
    attend_grad = product_across(mixed_low, take(grad_branch, core, width // 2, 1))
    attend_bias_grad = 0.5 * jnp.sum(grad_branch.astype(F32), axis=0)
    grad_mixed = product_back(grad_branch, take(attend_low, core, width // 2, 0)).astype(BF16)

    grad_triple = jnp.concatenate(attend_back(triple, grad_mixed, probs), axis=1)
    n_one = halves(product_back(grad_triple, triple_low))
    triple_grad = product_across(normed_low, grad_triple)
    triple_sums = jnp.sum(grad_triple.astype(F32), axis=0)
    triple_bias_grad = jnp.concatenate([spread_out(triple_sums[: width // 2]), spread_out(triple_sums[width:])])
    _, first_pull = jax.vjp(layer_norm, own_half(flat_tokens), gain_one, shift_one)
    flat_grad, first_gain_grad, first_shift_grad = first_pull(n_one)
    tokens_grad = give_back((own_half(grad_resid) + flat_grad).astype(BF16))

    big = [member.astype(BF16) for member in (shrink_grad, expand_grad, attend_grad, triple_grad)]
    small_grads = (
        first_gain_grad, first_shift_grad, triple_bias_grad, attend_bias_grad,
        0.5 * second_gain_grad, 0.5 * second_shift_grad, expand_bias_grad, shrink_bias_grad,
    )
    flat_small = jnp.concatenate([g.reshape(dp, -1) for g in small_grads], axis=1)
    sums, own_small = fold_plain(big, flat_small, core)
    small_out, at = [], 0
    for size in sizes:
        small_out.append(own_small[at : at + size])
        at += size
    return outputs(result, tokens_grad, sums, small_out)


def solution(mesh):
    return jax.shard_map(
        functools.partial(body, mesh.shape["dp"]),
        mesh=mesh,
        in_specs=(
            P("dp", "seq", None),
            P("dp", None),
            P("dp"),
            P("dp"),
            P("dp", None),
            P("dp"),
            P("dp", None),
            P("dp"),
            P("dp"),
            P("dp"),
            P("dp", None),
            P("dp"),
            P("dp", None),
            P("dp"),
            P("dp", "seq", None),
        ),
        out_specs=(
            P("dp", "seq", None),
            P("dp", "seq", None),
            P("dp"),
            P("dp"),
            P("dp", None),
            P("dp"),
            P("dp", None),
            P("dp"),
            P("dp"),
            P("dp"),
            P("dp", None),
            P("dp"),
            P("dp", None),
            P("dp"),
        ),
        check_vma=False,
    )
```

```python
import functools

import jax
import jax.numpy as jnp
from jax import lax
from jax.experimental import pallas as pl
from jax.experimental.pallas import tpu as pltpu
from jax.sharding import PartitionSpec as P

H = 12
HD = 64

EPSILON = 1e-05
NEG_FILL = -1e30
MESH = pl.DeviceIdType.MESH
MIB = 1024 * 1024
BF16 = jnp.bfloat16
F32 = jnp.float32


def layer_norm(values, norm_gain, norm_shift):
    center = values - jnp.mean(values, axis=-1, keepdims=True)
    spread = jnp.mean(center * center, axis=-1, keepdims=True)
    return center * lax.rsqrt(spread + EPSILON) * norm_gain + norm_shift


def gelu_tanh(values):
    inside = 0.7978845608028654 * (values + 0.044715 * values * values * values)
    return 0.5 * values * (1.0 + jnp.tanh(inside))


def product(operand, other):
    return jnp.dot(operand, other, preferred_element_type=F32)


def product_across(operand, other):
    return lax.dot_general(operand, other, (((0,), (0,)), ((), ())), preferred_element_type=F32)


def product_back(operand, other):
    return lax.dot_general(operand, other, (((1,), (1,)), ((), ())), preferred_element_type=F32)


def own_place():
    d, s = lax.axis_index("dp"), lax.axis_index("seq")
    return d, s, d // 2, d % 2, s // 2, s % 2


def flip(index, step):
    return index + step * (1 - 2 * ((index // step) % 2))


def remote(src, dst, send, recv, d, s):
    return pltpu.make_async_remote_copy(
        src_ref=src, dst_ref=dst, send_sem=send, recv_sem=recv, device_id=(d, s), device_id_type=MESH
    )


def greet(depth, steps):
    d, s, z, y, x, c = own_place()
    barrier = pltpu.get_barrier_semaphore()

    def signal(d_to, s_to):
        pl.semaphore_signal(barrier, inc=1, device_id=(d_to, s_to), device_id_type=MESH)

    @pl.when(z > 0)
    def _():
        signal(d - 2, s)

    @pl.when(z < depth - 1)
    def _():
        signal(d + 2, s)

    for step in steps:
        signal(flip(d, step), s)
    signal(d, flip(s, 2))
    signal(d, flip(s, 1))
    ends = jnp.where(z > 0, 1, 0) + jnp.where(z < depth - 1, 1, 0)
    pl.semaphore_wait(barrier, ends + len(steps) + 2)


def doubling_steps(count):
    return [1 << k for k in range(count.bit_length() - 1)]


class Plan:
    def __init__(self):
        self.steps = []

    def add(self, at, action, *args):
        self.steps.append((at, len(self.steps), action, args))

    def run(self):
        for _, _, action, args in sorted(self.steps, key=lambda step: step[:2]):
            action(*args)


def small_rows(sizes):
    firsts, at = [], 0
    for size in sizes:
        firsts.append(at)
        at += -(-size // 128)
    return firsts, at


def join_rows(pieces):
    lane = lax.broadcasted_iota(jnp.int32, (1, 128), 1)
    blocks = []
    for b in range(sum(n for _, n in pieces) // 128):
        block, start = jnp.zeros((1, 128), F32), -128 * b
        for piece, n in pieces:
            if start < 128 and start + n > 0:
                turned = piece if start % 128 == 0 else pltpu.roll(piece, start % 128, 1)
                block = jnp.where((lane >= start) & (lane < start + n), turned, block)
            start += n
        blocks.append(block)
    return jnp.concatenate(blocks, axis=1)


def small_vector(ref, sizes, index, shards):
    first, size = small_rows(sizes)[0][index], sizes[index]
    return join_rows(
        [
            (ref[pl.ds(at * 16 + first + k, 1), :].astype(BF16).astype(F32), min(128, size - 128 * k))
            for at in shards
            for k in range(-(-size // 128))
        ]
    )


def spread_kernel(dp, kinds, rows, quarter, sizes, *refs):
    count = len(rows)
    depth, half = dp // 2, dp // 2
    shard, vectors = refs[:count], refs[count : count + len(sizes)]
    at_ref = count + len(sizes)
    tokens, upstream, lengths = refs[at_ref : at_ref + 3]
    at_ref += 3
    full = refs[at_ref : at_ref + count]
    at_ref += count
    (
        small_full, row, seed, normed_out, triple_out, probs_out, mixed_out, resid_out, second_out, act_out, slope_out,
    ) = refs[at_ref : at_ref + 11]
    at_ref += 11
    wide, low = refs[at_ref : at_ref + count], refs[at_ref + count : at_ref + 2 * count]
    (
        row_v, normed, triple, probs, mixed, resid, second, act, slope, triple_w, attend_w, expand_w,
        load, local, up_s, down_s, y_s, x_s, ca_s, cb_s, yz_r, x_r, ca_r, cb_r, small_s, small_r, tok_l, tok_s, tok_r,
        weight_l, out_l, probs_l, mixed_s, mixed_r,
    ) = refs[at_ref + 2 * count :]
    d, s, z, y, x, c = own_place()
    steps = doubling_steps(dp)

    def parts(g):
        if kinds[g] != "cols":
            return [(slice(None), slice(None))]
        n = wide[g].shape[1]
        if g:
            return [(pl.ds(pl.multiple_of(c * n, 128), n), slice(None))]
        n, wide_pair = n // 3, 2 * HD
        return [
            (pl.ds(pl.multiple_of((2 * t + c) * n + wide_pair * p, 128), wide_pair), tile(3 * p + t, wide_pair))
            for p in range(n // wide_pair)
            for t in range(3)
        ]

    def tile(i, n=quarter):
        return slice(i * n, (i + 1) * n)

    def active(g, at):
        return True if kinds[g] != "shards" else at // half == c

    def fetches(g):
        return [
            pltpu.make_async_copy(shard[g].at[:, source], wide[g].at[:, target], load.at[g, t])
            for t, (source, target) in enumerate(parts(g))
        ]

    def when(condition, action):
        if condition is True:
            action()
        else:
            pl.when(condition)(action)

    for g in range(count):

        def fetch():
            for copy in fetches(g):
                copy.start()

        when(active(g, d), fetch)

    greet(depth, steps)

    def columns(g):
        if kinds[g] != "share":
            return slice(None)
        n = full[g].shape[1] // 2
        return pl.ds(pl.multiple_of(c * n, 128), n)

    def window(g, at, offset, n):
        m = rows[g] // 3
        place = at if kinds[g] != "shards" else at % half
        return full[g].at[pl.ds(pl.multiple_of(place * rows[g] + offset * m, 16), n * m), columns(g)]

    def own_piece(g):
        m = rows[g] // 3
        return low[g].at[pl.ds(pl.multiple_of(x * m, 16), 2 * m), columns(g)]

    def move(view, send, recv, d_to, s_to, src=None):
        return remote(view if src is None else src, view, send, recv, d_to, s_to)

    def up(g, at, src=None):
        return move(window(g, at, x, 2), up_s.at[g, at], yz_r.at[g, at], d + 2, s, src)

    def down(g, at, src=None):
        return move(window(g, at, x, 2), down_s.at[g, at], yz_r.at[g, at], d - 2, s, src)

    def over_y(g, at, src=None):
        return move(window(g, at, x, 2), y_s.at[g, at], yz_r.at[g, at], flip(d, 1), s, src)

    def over_x(g, at):
        return move(window(g, at, 2 * x, 1), x_s.at[g, at], x_r.at[g, at], d, flip(s, 2))

    def from_x(g, at):
        return move(window(g, at, 2 * (1 - x), 1), x_s.at[g, at], x_r.at[g, at], d, flip(s, 2))

    def core_a(g, at):
        return move(window(g, at, x, 2), ca_s.at[at], ca_r.at[at], d, flip(s, 1))

    def core_b(g, at):
        return move(window(g, at, 2 * (1 - x), 1), cb_s.at[at], cb_r.at[at], d, flip(s, 1))

    def small_copy(k):
        size = 16 << k
        view = small_full.at[pl.ds(pl.multiple_of((d // (1 << k)) * size, 16), size), :]
        return remote(view, view, small_s.at[k], small_r.at[k], flip(d, 1 << k), s)

    def own_local(g):
        place = d if kinds[g] != "shards" else d % half
        view = full[g].at[pl.ds(pl.multiple_of(place * rows[g], 16), rows[g]), :]
        return pltpu.make_async_copy(low[g], view, local.at[g])

    def spot(array, index):
        return array.at[pl.ds(pl.multiple_of(index * quarter, 16), quarter), :]

    def row_copies(t, source, target):
        mine, theirs = spot(target, 2 * x + c), spot(target, 2 * (1 - x) + c)
        return (
            pltpu.make_async_copy(source.at[x], mine, tok_l.at[t]),
            remote(source.at[1 - x], mine, tok_s.at[t, 0], tok_r.at[t, 0], d, flip(s, 2)),
            remote(source.at[x], mine, tok_s.at[t, 1], tok_r.at[t, 1], d, flip(s, 1)),
            remote(theirs, theirs, tok_s.at[t, 2], tok_r.at[t, 2], d, flip(s, 1)),
        )

    moves = [row_copies(0, tokens, row), row_copies(1, upstream, seed)]

    def row_begin(t):
        for copy in moves[t][:3]:
            copy.start()

    def row_pass(t):
        moves[t][1].wait_recv()
        moves[t][3].start()

    def row_arrived(t):
        own, _, to_core, passed = moves[t]
        own.wait()
        to_core.wait_recv()
        passed.wait_recv()

    small_full[pl.ds(pl.multiple_of(d * 16, 16), 16), :] = jnp.zeros((16, 128), F32)
    for ref, size, first_row in zip(vectors, sizes, small_rows(sizes)[0]):
        for k in range(-(-size // 128)):
            n = min(128, size - 128 * k)
            small_full[pl.ds(d * 16 + first_row + k, 1), 0:n] = ref[128 * k : 128 * k + n].reshape(1, n)
    row_begin(0)

    def begin(g):
        for copy in fetches(g):
            copy.wait()
        low[g][...] = wide[g][...].astype(BF16)
        src = own_piece(g)
        pl.when(z < depth - 1)(lambda: up(g, d, src).start())
        pl.when(z > 0)(lambda: down(g, d, src).start())
        over_y(g, d, src).start()
        own_local(g).start()

    def small_step(k):
        if k:
            small_copy(k - 1).wait()
        if k < len(steps):
            small_copy(k).start()

    def arrived(g, at):
        over_x(g, at).start()
        if kinds[g] == "share":
            core_a(g, at).start()

    def z_arrival(g, r):
        def low_side():
            at = d - 2 * r
            up(g, at).wait_recv()

            @pl.when(z < depth - 1)
            def _():
                up(g, at).start()

            over_y(g, at).start()
            arrived(g, at)

        def high_side():
            at = d + 2 * r
            down(g, at).wait_recv()

            @pl.when(z > 0)
            def _():
                down(g, at).start()

            over_y(g, at).start()
            arrived(g, at)

        pl.when((z >= r) & active(g, d - 2 * r))(low_side)
        pl.when((z + r < depth) & active(g, d + 2 * r))(high_side)

    other = flip(d, 1)

    def y_one(g, at):
        over_y(g, at).wait_recv()
        arrived(g, at)

    def on_shards(g, r, base, action):
        if r == 0:
            when(active(g, base), lambda: action(base))
        else:
            pl.when((z >= r) & active(g, base - 2 * r))(lambda: action(base - 2 * r))
            pl.when((z + r < depth) & active(g, base + 2 * r))(lambda: action(base + 2 * r))

    def x_one(g, at):
        from_x(g, at).wait_recv()
        if kinds[g] == "share":
            core_b(g, at).start()


    width, pairs = row.shape[1], triple.shape[1] // (6 * HD)
    half_width = width // 2

    total = lengths[x, 0] + lengths[x, 1]

    def vector(index, shards=range(dp)):
        return small_vector(small_full, sizes, index, shards)

    weight_loads = [
        pltpu.make_async_copy(full[g], target, weight_l.at[g]) for g, target in enumerate((triple_w, attend_w, expand_w))
    ]
    row_load = pltpu.make_async_copy(row, row_v, weight_l.at[3])

    def row_ready():
        row_arrived(0)
        row_load.start()

    def every_shard(g, action):
        for r in range(depth):
            on_shards(g, r, other, action)
            if r:
                on_shards(g, r, d, action)

    def weight_ready(g):
        own_local(g).wait()
        if kinds[g] == "share":

            def passed_on(at):
                core_a(g, at).wait_recv()
                core_b(g, at).wait_recv()

            every_shard(g, passed_on)
        weight_loads[g].start()

    def normalize(values, gain, shift):
        center = values - jnp.mean(values, axis=-1, keepdims=True)
        spread_of = jnp.mean(center * center, axis=-1, keepdims=True)
        return (center * lax.rsqrt(spread_of + EPSILON) * gain + shift).astype(BF16)

    def norm_tile(i):
        if i == 0:
            row_load.wait()
        normed[tile(i)] = normalize(row_v[tile(i)].astype(F32), vector(0), vector(1))

    def triple_tile(i):
        if i == 0:
            weight_loads[0].wait()
        n = half_width // sizes[2]
        ends = [vector(2, [first + c * n + k for k in range(n)]) for first in (0, dp // 2)]
        wide_pair = 2 * HD
        bias = jnp.concatenate(
            [
                part[:, tile(p, wide_pair)]
                for p in range(pairs)
                for part in (ends[0], jnp.zeros((1, half_width), F32), ends[1])
            ],
            axis=1,
        )
        triple[tile(i)] = (product(normed[tile(i)], triple_w[...]) + bias).astype(BF16)

    def probs_copy(p):
        return pltpu.make_async_copy(probs.at[p % 2], probs_out.at[p], probs_l.at[p % 2])

    def mixed_window(p, core):
        return pl.ds(pl.multiple_of(core * half_width + 2 * HD * p, 2 * HD), 2 * HD)

    def mixed_copy(p):
        view = mixed.at[:, mixed_window(p, c)]
        return remote(view, view, mixed_s.at[p], mixed_r.at[p], d, flip(s, 1))

    def attend_part(p, part):
        if p > 1 and part == 0:
            probs_copy(p - 2).wait()
        columns = [tile(3 * p + k, 2 * HD) for k in range(3)]
        mixed[tile(part), mixed_window(p, c)] = attend_block(
            part, quarter, total, triple[tile(part), columns[0]], triple.at[:, columns[1]], triple.at[:, columns[2]],
            probs.at[p % 2],
        )
        if part == 3:
            probs_copy(p).start()
            mixed_copy(p).start()

    out_copies = [
        pltpu.make_async_copy(source, target, out_l.at[k])
        for k, (source, target) in enumerate(
            (
                (normed, normed_out), (triple, triple_out), (mixed, mixed_out), (resid, resid_out),
                (second, second_out), (act, act_out), (slope, slope_out),
            )
        )
    ]

    def resid_tile(i):
        if i == 0:
            weight_loads[1].wait()
            out_copies[0].start()
            out_copies[1].start()
            for p in range(pairs):
                mixed_copy(p).wait()
            out_copies[2].start()
        values = row_v[tile(i)].astype(F32) + product(mixed[tile(i)], attend_w[...]) + vector(3)
        resid[tile(i)] = values
        second[tile(i)] = normalize(values, vector(4), vector(5))

    def expand_tile(i):
        if i == 0:
            weight_loads[2].wait()
            out_copies[3].start()
            out_copies[4].start()
        bias = vector(6, [c * half + k for k in range(half)])
        for k in range(expand_w.shape[1] // 256):
            part = tile(k, 256)
            value = product(second[tile(i)], expand_w[:, part]) + bias[:, part]
            square = value * value
            bend = jnp.tanh(0.7978845608028654 * value * (1.0 + 0.044715 * square))
            raised = 0.5 * (1.0 + bend)
            act[tile(i), part] = (value * raised).astype(BF16)
            inner = 0.7978845608028654 + (3 * 0.7978845608028654 * 0.044715) * square
            slope[tile(i), part] = (raised + 0.5 * value * (1.0 - bend * bend) * inner).astype(BF16)

    plan = Plan()
    for k in range(len(steps) + 1):
        plan.add(2 * k, small_step, k)
    plan.add(8, row_pass, 0)
    plan.add(11, row_ready)
    plan.add(42, row_begin, 1)
    plan.add(55, row_pass, 1)
    first = 0.0
    ready = []
    for g in range(count):
        piece = rows[g] * wide[g].shape[1] * 2 / 50e3 * 2 / 3
        if kinds[g] != "cols":
            piece /= 2
        hop = piece + 1.5
        plan.add(first, when, active(g, d), functools.partial(begin, g))
        for r in range(depth):
            if r:
                plan.add(first + hop * r, z_arrival, g, r)
                plan.add(first + hop * r + 0.5 * piece + 1.5, on_shards, g, r, d, functools.partial(x_one, g))
            plan.add(first + hop * (r + 1), on_shards, g, r, other, functools.partial(y_one, g))
            plan.add(
                first + hop * (r + 1) + 0.5 * piece + 1.5, on_shards, g, r, other, functools.partial(x_one, g)
            )
        ready.append(first + hop * depth + 0.5 * piece + 1.6)
        if kinds[g] != "shards":
            plan.add(ready[g] + (2 if kinds[g] == "share" else 0), weight_ready, g)
        first += 4 * piece if g == count - 1 else 3 * piece
    for i in range(4):
        plan.add(12.5 + 0.7 * i, norm_tile, i)
    at = ready[0] + 1.5
    for i in range(4):
        plan.add(at, triple_tile, i)
        at += 1.3
    for p in range(pairs):
        for part in range(4):
            plan.add(at, attend_part, p, part)
            at += 0.4 * (part + 1)
    at = max(at, ready[1] + 3.5) + 2.0
    for i in range(4):
        plan.add(at, resid_tile, i)
        at += 1.3
    at = max(at, ready[2] + 1.5)
    for i in range(4):
        plan.add(at, expand_tile, i)
        at += 1.5
    plan.run()

    out_copies[5].start()
    out_copies[6].start()
    for copy in out_copies:
        copy.wait()
    for p in range(max(pairs - 2, 0), pairs):
        probs_copy(p).wait()
    row_arrived(1)
    for move_of in moves:
        for copy in move_of[1:]:
            copy.wait_send()

    for g in range(count):

        def end():
            if kinds[g] == "shards":
                own_local(g).wait()

            @pl.when(z < depth - 1)
            def _():
                up(g, d, own_piece(g)).wait_send()

            @pl.when(z > 0)
            def _():
                down(g, d, own_piece(g)).wait_send()

            over_y(g, d, own_piece(g)).wait_send()

        when(active(g, d), end)

        def finish(g, own_column, at):
            if own_column:
                over_y(g, at).wait_send()
            over_x(g, at).wait_send()
            if kinds[g] == "share":
                core_a(g, at).wait_send()
                core_b(g, at).wait_send()

        for r in range(depth):
            on_shards(g, r, other, functools.partial(finish, g, False))
            if r:
                on_shards(g, r, d, functools.partial(finish, g, True))
                pl.when((z >= r) & (z < depth - 1) & active(g, d - 2 * r))(lambda: up(g, d - 2 * r).wait_send())
                pl.when((z + r < depth) & (z > 0) & active(g, d + 2 * r))(lambda: down(g, d + 2 * r).wait_send())


def spread(dp, shards, vectors, tokens, upstream, lengths):
    kinds = ["cols", "share", "cols", "shards"]
    rows = [member.shape[0] for member in shards]
    count = len(rows)
    quarter, width = tokens.shape[1:]
    length = 4 * quarter
    dma = pltpu.SemaphoreType.DMA
    any_space = pl.BlockSpec(memory_space=pl.ANY)
    vmem = pl.BlockSpec(memory_space=pltpu.VMEM)
    held = [(m.shape[0], m.shape[1] // 2 if kind == "cols" else m.shape[1]) for m, kind in zip(shards, kinds)]
    whole = [(dp * r // 2 if kind == "shards" else dp * r, n) for (r, n), kind in zip(held, kinds)]
    kept = part_start(4, quarter)
    pairs = width // (4 * HD)
    hidden = whole[2][1]
    states = [
        ((length, width), BF16), ((length, 3 * width // 2), BF16), ((pairs, 2, kept, quarter), BF16),
        ((length, width), BF16), ((length, width), F32), ((length, width), BF16),
        ((length, hidden), BF16), ((length, hidden), BF16),
    ]
    slots = [(shape if k != 2 else (2, *shape[1:]), kind) for k, (shape, kind) in enumerate(states)]
    return pl.pallas_call(
        functools.partial(spread_kernel, dp, kinds, rows, quarter, [v.shape[0] for v in vectors]),
        out_shape=[jax.ShapeDtypeStruct(shape, BF16) for shape in whole]
        + [jax.ShapeDtypeStruct((dp * 16, 128), F32)]
        + [jax.ShapeDtypeStruct((length, width), BF16)] * 2
        + [jax.ShapeDtypeStruct(*state) for state in states],
        in_specs=[any_space] * count
        + [vmem] * len(vectors)
        + [any_space] * 2
        + [pl.BlockSpec(memory_space=pltpu.SMEM)],
        out_specs=[any_space] * count + [vmem] + [any_space] * (2 + len(states)),
        scratch_shapes=[pltpu.VMEM(shape, F32) for shape in held]
        + [pltpu.VMEM(shape, BF16) for shape in held]
        + [pltpu.VMEM((length, width), BF16)]
        + [pltpu.VMEM(*slot) for slot in slots]
        + [pltpu.VMEM(shape, BF16) for shape in whole[:3]]
        + [dma((count, 3 * pairs)), dma((count,))]
        + [dma((count, dp))] * 4
        + [dma((dp,))] * 2
        + [dma((count, dp))] * 2
        + [dma((dp,))] * 2
        + [dma((len(doubling_steps(dp)),))] * 2
        + [dma((2,)), dma((2, 3)), dma((2, 3))]
        + [dma((4,)), dma((7,)), dma((2,)), dma((pairs,)), dma((pairs,))],
        compiler_params=pltpu.CompilerParams(
            collective_id=1, has_side_effects=True, vmem_limit_bytes=60 * MIB
        ),
        name="spread_weights",
    )(*shards, *vectors, tokens, upstream, lengths)


ATTEND_ROW, SECOND_ROW, EXPAND_ROW, SHRINK_ROW = (0, 0), (0, 1), 3, (0, 7)
FIRST_ROW, TRIPLE_ROW = (1, 0), (1, 2)


def back_kernel(dp, kinds, rows, quarter, sizes, *refs):
    count = len(rows)
    depth, half = dp // 2, dp // 2
    (
        shrink_in, expand_in, attend_in, triple_w_in, small_full, row_in, seed_in, normed_in, triple_in, probs_in, mixed_in,
        resid_in, second_in, act_in, slope_in,
    ) = refs[:15]
    outs, (small_sum, result_out, tokens_out) = refs[15 : 15 + count], refs[15 + count : 18 + count]
    at_ref = 18 + count
    acc, x_buf, y_buf, z_buf, b_buf = [refs[at_ref + k * count : at_ref + (k + 1) * count] for k in range(5)]
    (
        act, slope, seed, shrink_w, second, expand_w, partial, other, resid, mixed, attend_w, grad_own, grad_mixed, probs,
        dkeys, dvalues, row_own, send_own, sum_recv, n_recv, stage, ring_buf, line_buf,
        load, resid_l, probs_l, x_s, x_r, y_s, y_r, u_s, u_r, n_s, n_r, f_s, f_r, small_s, small_r,
        part_s, part_r, sum_s, sum_r, one_s, one_r, give_s, give_r,
    ) = refs[at_ref + 5 * count :]
    d, s, z, y, x, c = own_place()
    twin = flip(s, 1)
    length, width = seed.shape
    hidden, half_width = act.shape[1], width // 2
    pairs = half_width // (2 * HD)
    normed, grad_pre, branch = second, slope, partial
    triple = slope.at[:, pl.ds(0, 3 * half_width)]
    grad_triple = act.at[:, pl.ds(0, 3 * half_width)]
    triple_w = expand_w.at[:, pl.ds(0, 3 * half_width)]

    sources = [
        (act_in, act), (seed_in, seed), (shrink_in, shrink_w), (slope_in, slope), (expand_in, expand_w),
        (second_in, second), (mixed_in, mixed), (attend_in, attend_w),
        (normed_in, normed), (triple_in, triple), (triple_w_in, triple_w),
    ]
    loads = [pltpu.make_async_copy(source, target, load.at[k]) for k, (source, target) in enumerate(sources)]
    row_loads = [
        pltpu.make_async_copy(
            row_in.at[pl.ds(pl.multiple_of((2 * h + c) * quarter, 16), quarter), :], row_own.at[h], load.at[len(sources) + h]
        )
        for h in range(2)
    ]

    def resid_load(i):
        return pltpu.make_async_copy(resid_in.at[pl.ds(i * quarter, quarter), :], resid.at[i % 2], resid_l.at[i % 2])

    def probs_load(k):
        return pltpu.make_async_copy(probs_in.at[k // 2, k % 2], probs.at[k % 2], probs_l.at[k % 2])

    for copy in loads[:8]:
        copy.start()
    resid_load(0).start()
    resid_load(1).start()
    for copy in row_loads:
        copy.start()
    probs_load(0).start()
    probs_load(1).start()

    def turned(offset):
        s_to = s
        for bit in (1, 2):
            s_to = flip(s_to, bit) if offset & bit else s_to
        return (flip(d, 1) if offset & 4 else d), s_to

    def along(offset):
        d_to = d
        for k in range(depth.bit_length() - 1):
            d_to = flip(d_to, 2 << k) if offset >> k & 1 else d_to
        return d_to, s

    barrier = pltpu.get_barrier_semaphore()
    ring, line = range(1, 8), range(1, depth)
    for to in [turned(offset) for offset in ring] + [along(offset) for offset in line]:
        pl.semaphore_signal(barrier, inc=1, device_id=to, device_id_type=MESH)
    pl.semaphore_wait(barrier, len(ring) + len(line))

    small_sum[...] = jnp.zeros_like(small_sum)


    def layers(g):
        return depth if kinds[g] != "shards" else depth // 2

    def first_layer(g):
        return 0 if kinds[g] != "shards" else c * (depth // 2)

    def layer(g, n):
        if kinds[g] != "shards":
            return sorted(range(depth), key=lambda k: -abs(2 * k - depth + 1))[n]
        return n + c * (depth // 2 - 1 - 2 * n)

    def of(j, own):
        return 2 * j + (y if own else 1 - y)

    def place(g, at, units, n):
        m = rows[g] // 3
        return pl.ds(pl.multiple_of(at * rows[g] + units * m, 16), n * m)

    def span(g, units, n):
        return place(g, 0, units, n)

    def add(g, window, extra):
        acc[g][window, :] = acc[g][window, :] + extra

    def over_x(g, at):
        return remote(
            acc[g].at[place(g, at, 2 * (1 - x), 1), :], x_buf[g].at[at], x_s.at[g, at], x_r.at[g, at], d, flip(s, 2)
        )

    def over_y(g, j):
        source = acc[g].at[place(g, of(j, False), x, 2), :]
        return remote(source, y_buf[g].at[j], y_s.at[g, j], y_r.at[g, j], flip(d, 1), s)

    def up(g, j):
        source = acc[g].at[place(g, of(j, True), x, 2), :]
        return remote(source, z_buf[g].at[j], u_s.at[g, j], u_r.at[g, j], d + 2, s)

    def down_slot(g, j, at_z):
        return jnp.where(j + first_layer(g) == at_z, layers(g), j)

    def down(g, j):
        source = acc[g].at[place(g, of(j, True), x, 2), :]
        return remote(source, z_buf[g].at[down_slot(g, j, z - 1)], n_s.at[g, j], n_r.at[g, j], d - 2, s)

    def stage_a(g, n, own):
        over_x(g, of(layer(g, n), own)).start()

    def stage_c(g, n, own):
        j = layer(g, n)
        at = of(j, own)
        over_x(g, at).wait_recv()
        add(g, place(g, at, 2 * x, 1), x_buf[g][at])
        if not own:
            over_y(g, j).start()

    def stage_d(g, n):
        j = layer(g, n)
        over_y(g, j).wait_recv()
        add(g, place(g, of(j, True), x, 2), y_buf[g][j])

    def stage_e(g, n, hop):
        j = layer(g, n)
        k = j + first_layer(g)
        window = place(g, of(j, True), x, 2)

        @pl.when((z == hop) & (k > hop))
        def _():
            if hop:
                up(g, j).wait_recv()
                add(g, window, z_buf[g][j])
            up(g, j).start()

        @pl.when((z == depth - 1 - hop) & (k < depth - 1 - hop))
        def _():
            if hop:
                down(g, j).wait_recv()
                add(g, window, z_buf[g][down_slot(g, j, z)])
            down(g, j).start()

    def own_layer(g):
        return z - first_layer(g)

    def ours(g, action):
        if kinds[g] != "shards":
            action()
        else:
            pl.when((z >= first_layer(g)) & (z < first_layer(g) + layers(g)))(action)

    def out_rows(g, units, n):
        return outs[g].at[c, span(g, units, n), :] if kinds[g] != "shards" else outs[g].at[span(g, units, n), :]

    def final_share(g):
        source = acc[g].at[place(g, of(own_layer(g), True), 2 * x, 1), :]
        return remote(source, out_rows(g, 2 * x, 1), f_s.at[g, 0], f_r.at[g, 0], d, flip(s, 2))

    def final_swap(g):
        source = acc[g].at[place(g, of(own_layer(g), True), 1, 1), :]
        return remote(source, b_buf[g], f_s.at[g, 1], f_r.at[g, 1], d, flip(s, 2))

    def final_core(g):
        view = out_rows(g, 0, 3)
        return remote(view, view, f_s.at[g, 2], f_r.at[g, 2], d, twin)

    def finish_one(g):
        def run():
            j = own_layer(g)
            at = of(j, True)
            window = place(g, at, x, 2)

            @pl.when(z > 0)
            def _():
                up(g, j).wait_recv()
                add(g, window, z_buf[g][j])

            @pl.when(z < depth - 1)
            def _():
                down(g, j).wait_recv()
                add(g, window, z_buf[g][layers(g)])

            final_share(g).start()
            final_swap(g).start()
            out_rows(g, 2 * x, 1)[...] = acc[g][place(g, at, 2 * x, 1), :]

        ours(g, run)

    def finish_two(g):
        def run():
            final_swap(g).wait_recv()
            out_rows(g, 1, 1)[...] = acc[g][place(g, of(own_layer(g), True), 1, 1), :] + b_buf[g][...]
            final_share(g).wait_recv()
            final_core(g).start()

        ours(g, run)

    ring_place = y * 4 + s

    def ring_copy(t, offset):
        target = turned(offset)
        return remote(
            ring_buf.at[t, ring_place], ring_buf.at[t, ring_place], small_s.at[t, offset], small_r.at[t, offset], *target
        )

    def line_copy(t, offset):
        target = along(offset)
        return remote(
            line_buf.at[t, z], line_buf.at[t, z], small_s.at[t, 7 + offset], small_r.at[t, 7 + offset], *target
        )

    def small_begin(t):
        ring_buf[t, ring_place] = small_sum[t]
        for offset in ring:
            ring_copy(t, offset).start()

    def small_pass(t):
        for offset in ring:
            ring_copy(t, offset).wait()
        total = ring_buf[t, 0]
        for k in range(1, 8):
            total = total + ring_buf[t, k]
        line_buf[t, z] = total
        for offset in line:
            line_copy(t, offset).start()

    def small_end(t):
        for offset in line:
            line_copy(t, offset).wait()
        total = line_buf[t, 0]
        for k in line:
            total = total + line_buf[t, k]
        small_sum[t] = total


    def tile(i, n=quarter):
        return slice(i * n, (i + 1) * n)

    def own_tile(h):
        return pl.ds(pl.multiple_of((2 * h + c) * quarter, 16), quarter)

    def twin_tile(h):
        return pl.ds(pl.multiple_of((2 * h + 1 - c) * quarter, 16), quarter)

    def vector(index):
        return small_vector(small_full, sizes, index, range(dp))

    def sums(row_at, values, columns=slice(None)):
        block, at = row_at
        small_sum[block, at : at + 1, columns] += jnp.sum(values, axis=0, keepdims=True)

    def shrink_grad(k):
        if k == 0:
            loads[0].wait()
            loads[1].wait()
        acc[0][tile(k, 256), :] = product_across(act[:, tile(k, 256)], seed[...]).astype(BF16)

    def sum_copy(h):
        return remote(send_own.at[h], sum_recv.at[h], sum_s.at[h], sum_r.at[h], d, twin)

    def result_partial(h):
        if h == 0:
            loads[2].wait()
        send_own[h] = product(act[twin_tile(h), :], shrink_w[...]).astype(BF16)
        sum_copy(h).start()

    def grad_pre_tile(i):
        if i == 0:
            loads[3].wait()
        for k in range(hidden // 256):
            columns = tile(k, 256)
            value = product_back(seed[tile(i)], shrink_w[columns, :]) * slope[tile(i), columns].astype(F32)
            low_value = value.astype(BF16)
            grad_pre[tile(i), columns] = low_value
            total = jnp.sum(low_value.astype(F32), axis=0, keepdims=True)
            spot = (
                0, pl.ds(EXPAND_ROW + (hidden // width) * c + k * 256 // width, 1),
                slice(k * 256 % width, k * 256 % width + 256),
            )
            small_sum[spot] = small_sum[spot] + total
        sums(SHRINK_ROW, 0.5 * seed[tile(i)].astype(F32))

    def part_copy(i):
        return remote(partial.at[tile(i)], other.at[tile(i)], part_s.at[i], part_r.at[i], d, twin)

    def n_two_tile(i):
        if i == 0:
            loads[4].wait()
        partial[tile(i)] = product_back(grad_pre[tile(i)], expand_w[...]).astype(BF16)
        part_copy(i).start()

    def expand_grad(k):
        if k == 0:
            loads[5].wait()
        acc[1][tile(k, 256), :] = product_across(second[:, tile(k, 256)], grad_pre[...]).astype(BF16)

    def later_loads():
        for copy in loads[8:]:
            copy.start()

    def back_norm(n, values, gain, index, scale):
        center = values - jnp.mean(values, axis=-1, keepdims=True)
        r = lax.rsqrt(jnp.mean(center * center, axis=-1, keepdims=True) + EPSILON)
        hat = center * r
        sums(index, scale * n * hat)
        sums((index[0], index[1] + 1), scale * n)
        e = n * gain
        return r * (e - jnp.mean(e, axis=-1, keepdims=True) - hat * jnp.mean(e * hat, axis=-1, keepdims=True))

    def resid_tile(i):
        resid_load(i).wait()
        part_copy(i).wait()
        n = partial[tile(i)].astype(F32) + other[tile(i)].astype(F32)
        grad = seed[tile(i)].astype(F32) + back_norm(n, resid[i % 2], vector(4), SECOND_ROW, 0.5)
        low_grad = grad.astype(BF16)
        branch[tile(i)] = low_grad
        sums(ATTEND_ROW, 0.5 * low_grad.astype(F32))

        @pl.when(c == i % 2)
        def _():
            h = i // 2
            grad_own[h] = grad
            sum_copy(h).wait_recv()
            value = resid[i % 2] + product(act[tile(i)], shrink_w[...]) + sum_recv[h].astype(F32) + vector(7)
            stage[h] = value.astype(BF16)

        if i + 2 < 4:
            resid_load(i + 2).start()

    def give_copy(t):
        return remote(stage.at[1 - x], (result_out, tokens_out)[t].at[x], give_s.at[t], give_r.at[t], d, flip(s, 2))

    def give_back(t):
        (result_out, tokens_out)[t][x] = stage[x]
        give_copy(t).start()

    def attend_grad(k):
        if k == 0:
            loads[6].wait()
        columns = pl.ds(pl.multiple_of(c * half_width, 128), half_width)
        acc[2][tile(k, 256), :] = product_across(mixed[:, tile(k, 256)], branch[:, columns]).astype(BF16)

    def mixed_tile(i):
        if i == 0:
            loads[7].wait()
        rows_c = pl.ds(pl.multiple_of(c * half_width, 16), half_width)
        grad_mixed[tile(i)] = product_back(branch[tile(i)], attend_w[rows_c, :]).astype(BF16)

    def attend_back_step(k, part):
        p, head = k // 2, k % 2
        if part == 3:
            probs_load(k).wait()
        if k == 0 and part == 3:
            loads[9].wait()
        columns = [tile(3 * p + n, 2 * HD) for n in range(3)]
        grad_query = attend_back_block(
            head, part, quarter, triple[tile(part), columns[0]], triple.at[:, columns[1]], triple.at[:, columns[2]],
            grad_mixed[tile(part), 2 * HD * p : 2 * HD * (p + 1)],
            probs[k % 2, part_start(part, quarter) : part_start(part + 1, quarter)], dkeys, dvalues,
            part == 3 and head == 0,
        )
        if head:
            grad_query = jnp.where(head_mask(), grad_triple[tile(part), columns[0]], grad_query)
            place_q = pl.ds(pl.multiple_of(c * half_width + 2 * HD * p, 128), 2 * HD)
            sums(TRIPLE_ROW, grad_query.astype(F32), place_q)
        grad_triple[tile(part), columns[0]] = grad_query
        if part == 0:
            if k + 2 < 2 * pairs:
                probs_load(k + 2).start()
            if head:
                grad_triple[:, columns[1]] = dkeys[...].astype(BF16)
                low_values = dvalues[...].astype(BF16)
                grad_triple[:, columns[2]] = low_values
                sums((TRIPLE_ROW[0], TRIPLE_ROW[1] + 1), low_values.astype(F32), place_q)

    def triple_grad(p, k):
        if p == 0 and k == 0:
            loads[8].wait()
        columns = tile(p, 6 * HD)
        acc[3 + p][tile(k, 256), :] = product_across(normed[:, tile(k, 256)], grad_triple[:, columns]).astype(BF16)

    def one_copy(h):
        return remote(send_own.at[h], n_recv.at[h], one_s.at[h], one_r.at[h], d, twin)

    def n_one_partial(h):
        if h == 0:
            loads[10].wait()
        sum_copy(h).wait_send()
        send_own[h] = product_back(grad_triple[twin_tile(h), :], triple_w[...]).astype(BF16)
        one_copy(h).start()

    def first_tile(h):
        if h == 0:
            give_copy(0).wait_send()
        row_loads[h].wait()
        n = product_back(grad_triple[own_tile(h), :], triple_w[...])
        one_copy(h).wait_recv()
        n = n + n_recv[h].astype(F32)
        grad = grad_own[h] + back_norm(n, row_own[h].astype(F32), vector(0), FIRST_ROW, 1.0)
        stage[h] = grad.astype(BF16)


    plan = Plan()
    clock = [2.0]

    def compute(micros, action, *args):
        plan.add(clock[0], action, *args)
        clock[0] += micros

    made = []

    def group_made():
        made.append(clock[0] - 0.01)

    for k in range(hidden // 256):
        compute(0.5, shrink_grad, k)
    group_made()
    for h in range(2):
        compute(0.8, result_partial, h)
    for i in range(4):
        compute(0.9, grad_pre_tile, i)
    for i in range(4):
        compute(0.8, n_two_tile, i)
    for k in range(width // 256):
        compute(1.0, expand_grad, k)
    group_made()
    compute(0.0, later_loads)
    for i in range(4):
        compute(1.5, resid_tile, i)
    compute(0.2, give_back, 0)
    for k in range(width // 256):
        compute(0.4, attend_grad, k)
    group_made()
    for i in range(4):
        compute(0.3, mixed_tile, i)
    plan.add(clock[0], small_begin, 0)
    plan.add(clock[0] + 4.0, small_pass, 0)
    plan.add(clock[0] + 8.0, small_end, 0)
    for k in range(2 * pairs):
        for part in reversed(range(4)):
            compute(0.25 * (part + 1), attend_back_step, k, part)
        if k % 2:
            for n in range(width // 256):
                compute(0.3, triple_grad, k // 2, n)
            group_made()
    for h in range(2):
        compute(0.6, n_one_partial, h)
    compute(1.0, lambda: None)
    for h in range(2):
        compute(1.8, first_tile, h)
    compute(0.2, give_back, 1)
    compute(3.0, small_begin, 1)
    compute(3.0, small_pass, 1)
    compute(0.1, small_end, 1)

    done = 0.0
    for g in range(count):
        unit = rows[g] * acc[g].shape[1] * 2 / 50e3 / 3
        done = max(done, made[g])
        for own in (False, True):
            for n in range(layers(g)):
                plan.add(max(done - 4.0, made[g]), stage_a, g, n, own)
                done += unit
                plan.add(done + 1.5, stage_c, g, n, own)
                if own:
                    plan.add(done + 3.5, stage_d, g, n)
                    for hop in range(depth - 1):
                        plan.add(done + 4.0 + (2 * unit + 1.5) * hop, stage_e, g, n, hop)
        last = done + 4.0 + (2 * unit + 1.5) * (depth - 1)
        plan.add(last, finish_one, g)
        plan.add(last + unit + 2.0, finish_two, g)
    plan.run()

    for g in range(count):

        def drain():
            final_share(g).wait_send()
            final_swap(g).wait_send()
            if kinds[g] == "shards":
                final_core(g).wait_send()

        ours(g, drain)
        if kinds[g] == "shards":
            pl.when((z < first_layer(g)) | (z >= first_layer(g) + layers(g)))(lambda: final_core(g).wait_recv())
        else:
            final_core(g).wait()
        for j in range(layers(g)):
            over_x(g, of(j, False)).wait_send()
            over_x(g, of(j, True)).wait_send()
            over_y(g, j).wait_send()
            pl.when(j + first_layer(g) > z)(lambda: up(g, j).wait_send())
            pl.when(j + first_layer(g) < z)(lambda: down(g, j).wait_send())
    for h in range(2):
        one_copy(h).wait_send()
    give_copy(0).wait_recv()
    give_copy(1).wait()


def back(dp, sizes, weights, small_full, row, seed, normed, triple, probs, mixed, resid, second, act, slope):
    triple_w, attend_w, expand_w, shrink_w = weights
    length, width = row.shape
    quarter, hidden = length // 4, act.shape[1]
    pairs = width // (4 * HD)
    kinds = ["shards"] + ["cols"] * (2 + pairs)
    shapes = [(hidden, width), (width, hidden), (width, width // 2)] + [(width, 6 * HD)] * pairs
    owners = [dp // 2 if kind == "shards" else dp for kind in kinds]
    rows = [m[0] // n for m, n in zip(shapes, owners)]
    count, depth = len(rows), dp // 2
    dma = pltpu.SemaphoreType.DMA
    any_space = pl.BlockSpec(memory_space=pl.ANY)
    vmem = pl.BlockSpec(memory_space=pltpu.VMEM)

    def buffers(lead, part, extra=0):
        slots = [() if lead is None else (n // lead + extra,) for n in owners]
        return [pltpu.VMEM((*slot, r // 3 * part, m[1]), BF16) for slot, r, m in zip(slots, rows, shapes)]

    halves = (2, quarter, width)
    working = [
        (act.shape, BF16), (act.shape, BF16), (row.shape, BF16), (shrink_w.shape, BF16), (row.shape, BF16),
        (expand_w.shape, BF16), (row.shape, BF16), (row.shape, BF16), (halves, F32), (row.shape, BF16),
        (attend_w.shape, BF16), (halves, F32), ((length, width // 2), BF16), ((2, *probs.shape[2:]), BF16),
        ((length, 2 * HD), F32), ((length, 2 * HD), F32), (halves, BF16), (halves, BF16), (halves, BF16), (halves, BF16),
        (halves, BF16), ((2, 8, 8, width), F32), ((2, depth, 8, width), F32),
    ]
    return pl.pallas_call(
        functools.partial(back_kernel, dp, kinds, rows, quarter, sizes),
        out_shape=[
            jax.ShapeDtypeStruct((r, m[1]) if kind == "shards" else (2, r, m[1]), BF16)
            for r, m, kind in zip(rows, shapes, kinds)
        ]
        + [jax.ShapeDtypeStruct((2, 8, width), F32)]
        + [jax.ShapeDtypeStruct(halves, BF16)] * 2,
        in_specs=[any_space] * 4 + [vmem] + [any_space] * 10,
        out_specs=[vmem] * (count + 3),
        scratch_shapes=[pltpu.VMEM(m, BF16) for m in shapes]
        + buffers(1, 1)
        + buffers(2, 2)
        + buffers(2, 2, 1)
        + buffers(None, 1)
        + [pltpu.VMEM(*item) for item in working]
        + [dma((13,)), dma((2,)), dma((2,))]
        + [dma((count, dp))] * 2
        + [dma((count, depth))] * 6
        + [dma((count, 3))] * 2
        + [dma((2, 7 + depth))] * 2
        + [dma((4,))] * 2
        + [dma((2,))] * 6,
        compiler_params=pltpu.CompilerParams(
            collective_id=2, has_side_effects=True, vmem_limit_bytes=60 * MIB
        ),
        name="back_and_fold",
    )(shrink_w, expand_w, attend_w, triple_w, small_full, row, seed, normed, triple, probs, mixed, resid, second, act, slope)


def write_kernel(dp, sizes, *refs):
    shrink, expand, attend = refs[:3]
    at_ref = len(refs) - 14 - 3
    triples, (small, result, tokens_grad) = refs[3:at_ref], refs[at_ref : at_ref + 3]
    (
        result_out, tokens_out, gain_one, shift_one, triple_out, bias_triple, attend_out, bias_attend, gain_two, shift_two,
        expand_out, bias_expand, shrink_out, bias_shrink,
    ) = refs[at_ref + 3 :]
    d = lax.axis_index("dp")
    width = small.shape[2]
    result_out[...] = result[...]
    tokens_out[...] = tokens_grad[...]
    shrink_out[...] = shrink[...].astype(F32)
    for core in range(2):
        for source, target in ((expand, expand_out), (attend, attend_out)):
            n = source.shape[2]
            target[:, core * n : (core + 1) * n] = source[core].astype(F32)
        for p, source in enumerate(triples):
            for t in range(3):
                at = t * width + core * (width // 2) + 2 * HD * p
                triple_out[:, at : at + 2 * HD] = source[core, :, 2 * HD * t : 2 * HD * (t + 1)].astype(F32)
    rows = (FIRST_ROW, (1, 1), TRIPLE_ROW, ATTEND_ROW, SECOND_ROW, (0, 2), (0, EXPAND_ROW), SHRINK_ROW)
    targets = (gain_one, shift_one, bias_triple, bias_attend, gain_two, shift_two, bias_expand, bias_shrink)
    for (block, at), size, target in zip(rows, sizes, targets):
        lines = size * dp // width
        whole = jnp.concatenate([small[block, at + k : at + k + 1, :] for k in range(lines)], axis=1)
        target[...] = pltpu.roll(whole, whole.shape[1] - size * d, 1)[0, 0:size]


def write(dp, sizes, sums, small, result, tokens_grad):
    shrink, expand, attend = [member.shape for member in sums[:3]]
    width = attend[2] * 2
    vmem = pl.BlockSpec(memory_space=pltpu.VMEM)
    halves = [jax.ShapeDtypeStruct(result.shape, BF16)] * 2
    whole = [(expand[1], 3 * width), (attend[1], width), (expand[1], 2 * expand[2]), shrink]
    triple_f, attend_f, expand_f, shrink_f = [jax.ShapeDtypeStruct(shape, F32) for shape in whole]
    v = [jax.ShapeDtypeStruct((size,), F32) for size in sizes]
    return pl.pallas_call(
        functools.partial(write_kernel, dp, sizes),
        out_shape=(
            *halves, v[0], v[1], triple_f, v[2], attend_f, v[3], v[4], v[5], expand_f, v[6], shrink_f, v[7],
        ),
        in_specs=[vmem] * (len(sums) + 3),
        out_specs=(vmem,) * 14,
        compiler_params=pltpu.CompilerParams(vmem_limit_bytes=40 * MIB),
        name="write_outputs",
    )(*sums, small, result, tokens_grad)


def head_mask():
    return lax.broadcasted_iota(jnp.int32, (1, 2 * HD), 1) < HD


def part_start(part, quarter):
    return quarter * (part * (part + 1) // 2)


def attend_block(part, quarter, total, query, k_ref, v_ref, probs_ref):
    first = head_mask()
    length = quarter * (part + 1)
    key_pos = lax.broadcasted_iota(jnp.int32, (length, 1), 0)
    key_pos = jnp.where(key_pos < total, key_pos, 1 << 20)
    allowed = key_pos <= lax.broadcasted_iota(jnp.int32, (1, quarter), 1) + part * quarter
    query = query * jnp.asarray(HD**-0.5, BF16)
    sums = []
    for head in range(2):
        mask = first if head == 0 else ~first
        scores = product_back(k_ref[:length], jnp.where(mask, query, jnp.zeros_like(query)))
        scores = jnp.where(allowed, scores, NEG_FILL)
        exponent = jnp.exp(scores - jnp.max(scores, axis=0, keepdims=True))
        probs = (exponent * (1.0 / jnp.sum(exponent, axis=0, keepdims=True))).astype(BF16)
        probs_ref[head, part_start(part, quarter) : part_start(part + 1, quarter)] = probs
        sums.append(product_across(probs, v_ref[:length]))
    return jnp.where(first, sums[0], sums[1]).astype(BF16)


def attend_kernel(quarter, total, q_ref, k_ref, v_ref, mixed_ref, probs_ref):
    for part in range(4):
        rows = slice(part * quarter, (part + 1) * quarter)
        mixed_ref[rows] = attend_block(part, quarter, total[0], q_ref[rows], k_ref, v_ref, probs_ref.at[0])


def attend(triple, total):
    tokens, width = triple.shape[0], triple.shape[1] // 3
    quarter = tokens // 4
    pairs = width // (2 * HD)
    kept = part_start(4, quarter)

    def block(shift):
        return pl.BlockSpec((tokens, 2 * HD), lambda p, _: (0, p + shift))

    return pl.pallas_call(
        functools.partial(attend_kernel, quarter),
        grid_spec=pltpu.PrefetchScalarGridSpec(
            num_scalar_prefetch=1,
            grid=(pairs,),
            in_specs=[block(0), block(pairs), block(2 * pairs)],
            out_specs=[block(0), pl.BlockSpec((1, 2, kept, quarter), lambda p, _: (p, 0, 0, 0))],
        ),
        out_shape=[
            jax.ShapeDtypeStruct((tokens, width), BF16),
            jax.ShapeDtypeStruct((pairs, 2, kept, quarter), BF16),
        ],
        compiler_params=pltpu.CompilerParams(vmem_limit_bytes=50 * MIB),
        name="attend",
    )(total, triple, triple, triple)


def attend_back_block(head, part, quarter, query, k_ref, v_ref, grad, probs, dkeys, dvalues, fresh):
    length = quarter * (part + 1)
    mask = head_mask() if head == 0 else ~head_mask()
    own_query = jnp.where(mask, query * jnp.asarray(HD**-0.5, BF16), jnp.zeros_like(query))
    own_grad = jnp.where(mask, grad, jnp.zeros_like(grad))
    wide = probs.astype(F32)
    grad_probs = product_back(v_ref[:length], own_grad)
    delta = jnp.sum(wide * grad_probs, axis=0, keepdims=True)
    grad_scores = (wide * (grad_probs - delta)).astype(BF16)
    dv = product(probs, own_grad)
    dk = product(grad_scores, own_query)
    if fresh:
        dvalues[:length] = dv
        dkeys[:length] = dk
    else:
        dvalues[:length] += dv
        dkeys[:length] += dk
    return (product_across(grad_scores, k_ref[:length]) * HD**-0.5).astype(BF16)


def attend_back_kernel(quarter, q_ref, k_ref, v_ref, g_ref, probs_ref, dq_ref, dk_ref, dv_ref, dkeys, dvalues):
    for part in reversed(range(4)):
        rows = slice(part * quarter, (part + 1) * quarter)
        kept = slice(part_start(part, quarter), part_start(part + 1, quarter))
        dq = [
            attend_back_block(
                head, part, quarter, q_ref[rows], k_ref, v_ref, g_ref[rows], probs_ref[0, head, kept], dkeys, dvalues,
                part == 3 and head == 0,
            )
            for head in range(2)
        ]
        dq_ref[rows] = jnp.where(head_mask(), dq[0], dq[1])
    dk_ref[...] = dkeys[...].astype(BF16)
    dv_ref[...] = dvalues[...].astype(BF16)


def attend_back(triple, grad, probs):
    tokens, width = triple.shape[0], triple.shape[1] // 3
    quarter = tokens // 4
    pairs = width // (2 * HD)

    def block(shift):
        return pl.BlockSpec((tokens, 2 * HD), lambda p: (0, p + shift))

    return pl.pallas_call(
        functools.partial(attend_back_kernel, quarter),
        grid=(pairs,),
        in_specs=[block(0), block(pairs), block(2 * pairs), block(0)]
        + [pl.BlockSpec((1, 2, part_start(4, quarter), quarter), lambda p: (p, 0, 0, 0))],
        out_specs=[block(0)] * 3,
        out_shape=[jax.ShapeDtypeStruct((tokens, width), BF16)] * 3,
        scratch_shapes=[pltpu.VMEM((tokens, 2 * HD), F32)] * 2,
        compiler_params=pltpu.CompilerParams(vmem_limit_bytes=50 * MIB),
        name="attend_back",
    )(triple, triple, triple, grad, probs)


def take(array, index, size, axis):
    return lax.dynamic_slice_in_dim(array, index * size, size, axis)


def gather_plain(matrices, small, tokens, core, upper):
    triple, attend_full, expand, shrink = [
        lax.all_gather(m.astype(BF16), "dp", axis=0, tiled=True) for m in matrices
    ]
    width = triple.shape[0]
    thirds = triple.reshape(width, 3, width)
    row = lax.all_gather(tokens, "seq", axis=1, tiled=True)
    return (
        take(thirds, core, width // 2, 2).reshape(width, -1),
        attend_full,
        take(expand, core, expand.shape[1] // 2, 1),
        take(shrink, core, shrink.shape[0] // 2, 0),
        lax.all_gather(small, "dp", axis=0),
        jnp.where(upper, row[1], row[0]),
    )


def fold_plain(grads, small, core):
    def by_core(array):
        empty = jnp.zeros_like(array)
        return jnp.stack([jnp.where(core == 0, array, empty), jnp.where(core == 1, array, empty)], axis=1)

    shrink, *others = grads
    wide = jnp.swapaxes(by_core(shrink), 0, 1).reshape(-1, shrink.shape[1])
    arrays = [wide] + [by_core(m) for m in others]
    sums = [lax.psum(lax.psum_scatter(m, "dp", scatter_dimension=0, tiled=True), "seq") for m in arrays]
    sums = [sums[0]] + [jnp.swapaxes(m, 0, 1) for m in sums[1:]]
    return sums, lax.psum(lax.psum_scatter(small, "dp", scatter_dimension=0, tiled=True), "seq").reshape(-1)


def outputs(result, tokens_grad, sums, small_out):
    width = result.shape[-1]
    shrink_sum, expand_sum, attend_sum, triple_sum = [member.astype(F32) for member in sums]
    triple_sum = triple_sum.reshape(2, -1, 3, width // 2).transpose(1, 2, 0, 3).reshape(-1, 3 * width)
    expand_sum, attend_sum = [m.transpose(1, 0, 2).reshape(m.shape[1], -1) for m in (expand_sum, attend_sum)]
    return (
        result,
        tokens_grad,
        small_out[0],
        small_out[1],
        triple_sum,
        small_out[2],
        attend_sum,
        small_out[3],
        small_out[4],
        small_out[5],
        expand_sum,
        small_out[6],
        shrink_sum,
        small_out[7],
    )


def body(
    dp,
    tokens,
    lengths,
    first_gain,
    first_shift,
    triple_weight,
    triple_bias,
    attend_weight,
    attend_bias,
    second_gain,
    second_shift,
    expand_weight,
    expand_bias,
    shrink_weight,
    shrink_bias,
    upstream,
):
    row_count, quarter, width = tokens.shape
    matrices = (triple_weight, attend_weight, expand_weight, shrink_weight)
    vectors = (first_gain, first_shift, triple_bias, attend_bias, second_gain, second_shift, expand_bias, shrink_bias)
    sizes = [member.shape[0] for member in vectors]
    by_kernel = dp & (dp - 1) == 0 and dp > 2 and all(m.shape[0] % 48 == 0 for m in matrices)
    by_kernel = by_kernel and small_rows(sizes)[1] <= 16 and width == matrices[0].shape[0] * dp
    by_kernel = by_kernel and sizes[2] * dp == 2 * width and (width // 2) % sizes[2] == 0
    place = lax.axis_index("seq")
    upper, core = place // 2 == 1, place % 2

    totals = lengths[:, 0] + lengths[:, 1]
    total = jnp.where(upper, totals[1], totals[0]).reshape(1)

    across = [(k, (k + 2) % 4) for k in range(4)]
    twin = [(k, k + 1 - 2 * (k % 2)) for k in range(4)]

    def halves(partial):
        view = partial.reshape(2, 2, quarter, width)
        mine = jnp.where(core == 0, view[:, 0], view[:, 1])
        theirs = jnp.where(core == 0, view[:, 1], view[:, 0]).astype(BF16)
        return mine + lax.ppermute(theirs, "seq", twin).astype(F32)

    def own_half(array):
        view = array.reshape(2, 2, quarter, width)
        return jnp.where(core == 0, view[:, 0], view[:, 1])

    def give_back(array):
        mine = jnp.where(upper, array[1], array[0])
        theirs = lax.ppermute(jnp.where(upper, array[0], array[1]), "seq", across)
        return jnp.stack([jnp.where(upper, theirs, mine), jnp.where(upper, mine, theirs)])

    def of_core(vector):
        return take(vector, core, vector.shape[0] // 2, 0)

    def spread_out(part):
        empty = jnp.zeros_like(part)
        return jnp.concatenate([jnp.where(core == 0, part, empty), jnp.where(core == 1, part, empty)])

    def whole_row(array):
        mine = jnp.where(upper, array[1], array[0])
        theirs = lax.ppermute(jnp.where(upper, array[0], array[1]), "seq", across)
        pair = jnp.stack([jnp.where(upper, theirs, mine), jnp.where(upper, mine, theirs)])
        others = lax.ppermute(pair, "seq", twin)
        return jnp.stack(
            [jnp.where(core == 0, pair, others), jnp.where(core == 0, others, pair)], axis=1
        ).reshape(-1, width)

    if by_kernel:
        *weights, small_full, row, seed_low, normed, triple, probs, mixed, resid, second, act, slope = spread(
            dp, matrices, vectors, tokens, upstream, lengths
        )
        *sums, small_sum, result, tokens_grad = back(
            dp, sizes, weights, small_full, row, seed_low, normed, triple, probs, mixed, resid, second, act, slope
        )
        return write(dp, sizes, sums, small_sum, result, tokens_grad)
    small = jnp.concatenate(vectors)
    *weights, small_full, row = gather_plain(matrices, small, tokens, core, upper)
    floats, at = [], 0
    for size in sizes:
        floats.append(small_full[:, at : at + size].reshape(-1).astype(BF16).astype(F32))
        at += size
    gain_one, shift_one, bias_triple, bias_attend, gain_two, shift_two, bias_expand, bias_shrink = floats
    triple_low, attend_low, expand_low, shrink_low = weights
    seed_low = whole_row(upstream)
    flat_tokens = row.astype(F32)
    seed = seed_low.astype(F32)

    bias_core = jnp.concatenate(
        [of_core(bias_triple[:width]), jnp.zeros((width // 2,), F32), of_core(bias_triple[width:])]
    )
    normed_low = layer_norm(flat_tokens, gain_one, shift_one).astype(BF16)
    triple = (product(normed_low, triple_low) + bias_core).astype(BF16)
    mixed_core, probs = attend(triple, total)
    mixed_other = lax.ppermute(mixed_core, "seq", twin)
    mixed_low = jnp.concatenate(
        [jnp.where(core == 0, mixed_core, mixed_other), jnp.where(core == 0, mixed_other, mixed_core)], axis=1
    )
    resid = flat_tokens + product(mixed_low, attend_low) + bias_attend
    normed_two_low = layer_norm(resid, gain_two, shift_two).astype(BF16)
    activated, gelu_pull = jax.vjp(gelu_tanh, product(normed_two_low, expand_low) + of_core(bias_expand))
    act_low, slope = activated.astype(BF16), gelu_pull(jnp.ones_like(activated))[0]
    _, second_pull = jax.vjp(layer_norm, resid, gain_two, shift_two)

    grad_pre = (product_back(seed_low, shrink_low) * slope.astype(F32)).astype(BF16)
    partial = product_back(grad_pre, expand_low).astype(BF16)
    other_partial = lax.ppermute(partial, "seq", twin)
    shrink_grad = product_across(act_low, seed_low)
    expand_grad = product_across(normed_two_low, grad_pre)
    result = own_half(resid) + halves(product(act_low, shrink_low)) + bias_shrink
    result = give_back(result.astype(BF16))
    shrink_bias_grad = 0.5 * jnp.sum(seed, axis=0)
    expand_bias_grad = spread_out(jnp.sum(grad_pre.astype(F32), axis=0))
    resid_part, second_gain_grad, second_shift_grad = second_pull(partial.astype(F32) + other_partial.astype(F32))
    grad_resid = seed + resid_part
    grad_branch = grad_resid.astype(BF16)
    attend_grad = product_across(mixed_low, take(grad_branch, core, width // 2, 1))
    attend_bias_grad = 0.5 * jnp.sum(grad_branch.astype(F32), axis=0)
    grad_mixed = product_back(grad_branch, take(attend_low, core, width // 2, 0)).astype(BF16)

    grad_triple = jnp.concatenate(attend_back(triple, grad_mixed, probs), axis=1)
    n_one = halves(product_back(grad_triple, triple_low))
    triple_grad = product_across(normed_low, grad_triple)
    triple_sums = jnp.sum(grad_triple.astype(F32), axis=0)
    triple_bias_grad = jnp.concatenate([spread_out(triple_sums[: width // 2]), spread_out(triple_sums[width:])])
    _, first_pull = jax.vjp(layer_norm, own_half(flat_tokens), gain_one, shift_one)
    flat_grad, first_gain_grad, first_shift_grad = first_pull(n_one)
    tokens_grad = give_back((own_half(grad_resid) + flat_grad).astype(BF16))

    big = [member.astype(BF16) for member in (shrink_grad, expand_grad, attend_grad, triple_grad)]
    small_grads = (
        first_gain_grad, first_shift_grad, triple_bias_grad, attend_bias_grad,
        0.5 * second_gain_grad, 0.5 * second_shift_grad, expand_bias_grad, shrink_bias_grad,
    )
    flat_small = jnp.concatenate([g.reshape(dp, -1) for g in small_grads], axis=1)
    sums, own_small = fold_plain(big, flat_small, core)
    small_out, at = [], 0
    for size in sizes:
        small_out.append(own_small[at : at + size])
        at += size
    return outputs(result, tokens_grad, sums, small_out)


def solution(mesh):
    return jax.shard_map(
        functools.partial(body, mesh.shape["dp"]),
        mesh=mesh,
        in_specs=(
            P("dp", "seq", None),
            P("dp", None),
            P("dp"),
            P("dp"),
            P("dp", None),
            P("dp"),
            P("dp", None),
            P("dp"),
            P("dp"),
            P("dp"),
            P("dp", None),
            P("dp"),
            P("dp", None),
            P("dp"),
            P("dp", "seq", None),
        ),
        out_specs=(
            P("dp", "seq", None),
            P("dp", "seq", None),
            P("dp"),
            P("dp"),
            P("dp", None),
            P("dp"),
            P("dp", None),
            P("dp"),
            P("dp"),
            P("dp"),
            P("dp", None),
            P("dp"),
            P("dp", None),
            P("dp"),
        ),
        check_vma=False,
    )
```

```python
import functools

import jax
import jax.numpy as jnp
from jax import lax
from jax.experimental import pallas as pl
from jax.experimental.pallas import tpu as pltpu
from jax.sharding import PartitionSpec as P

H = 12
HD = 64

EPSILON = 1e-05
NEG_FILL = -1e30
MESH = pl.DeviceIdType.MESH
MIB = 1024 * 1024
BF16 = jnp.bfloat16
F32 = jnp.float32


def layer_norm(values, norm_gain, norm_shift):
    center = values - jnp.mean(values, axis=-1, keepdims=True)
    spread = jnp.mean(center * center, axis=-1, keepdims=True)
    return center * lax.rsqrt(spread + EPSILON) * norm_gain + norm_shift


def gelu_tanh(values):
    inside = 0.7978845608028654 * (values + 0.044715 * values * values * values)
    return 0.5 * values * (1.0 + jnp.tanh(inside))


def product(operand, other):
    return jnp.dot(operand, other, preferred_element_type=F32)


def product_across(operand, other):
    return lax.dot_general(operand, other, (((0,), (0,)), ((), ())), preferred_element_type=F32)


def product_back(operand, other):
    return lax.dot_general(operand, other, (((1,), (1,)), ((), ())), preferred_element_type=F32)


def own_place():
    d, s = lax.axis_index("dp"), lax.axis_index("seq")
    return d, s, d // 2, d % 2, s // 2, s % 2


def flip(index, step):
    return index + step * (1 - 2 * ((index // step) % 2))


def remote(src, dst, send, recv, d, s):
    return pltpu.make_async_remote_copy(
        src_ref=src, dst_ref=dst, send_sem=send, recv_sem=recv, device_id=(d, s), device_id_type=MESH
    )


def greet(depth, steps):
    d, s, z, y, x, c = own_place()
    barrier = pltpu.get_barrier_semaphore()

    def signal(d_to, s_to):
        pl.semaphore_signal(barrier, inc=1, device_id=(d_to, s_to), device_id_type=MESH)

    @pl.when(z > 0)
    def _():
        signal(d - 2, s)

    @pl.when(z < depth - 1)
    def _():
        signal(d + 2, s)

    for step in steps:
        signal(flip(d, step), s)
    signal(d, flip(s, 2))
    signal(d, flip(s, 1))
    ends = jnp.where(z > 0, 1, 0) + jnp.where(z < depth - 1, 1, 0)
    pl.semaphore_wait(barrier, ends + len(steps) + 2)


def doubling_steps(count):
    return [1 << k for k in range(count.bit_length() - 1)]


class Plan:
    def __init__(self):
        self.steps = []

    def add(self, at, action, *args):
        self.steps.append((at, len(self.steps), action, args))

    def run(self):
        for _, _, action, args in sorted(self.steps, key=lambda step: step[:2]):
            action(*args)


def small_rows(sizes):
    firsts, at = [], 0
    for size in sizes:
        firsts.append(at)
        at += -(-size // 128)
    return firsts, at


def join_rows(pieces):
    lane = lax.broadcasted_iota(jnp.int32, (1, 128), 1)
    blocks = []
    for b in range(sum(n for _, n in pieces) // 128):
        block, start = jnp.zeros((1, 128), F32), -128 * b
        for piece, n in pieces:
            if start < 128 and start + n > 0:
                turned = piece if start % 128 == 0 else pltpu.roll(piece, start % 128, 1)
                block = jnp.where((lane >= start) & (lane < start + n), turned, block)
            start += n
        blocks.append(block)
    return jnp.concatenate(blocks, axis=1)


def small_vector(ref, sizes, index, shards):
    first, size = small_rows(sizes)[0][index], sizes[index]
    return join_rows(
        [
            (ref[pl.ds(at * 16 + first + k, 1), :].astype(BF16).astype(F32), min(128, size - 128 * k))
            for at in shards
            for k in range(-(-size // 128))
        ]
    )


def spread_kernel(dp, kinds, rows, quarter, sizes, *refs):
    count = len(rows)
    depth, half = dp // 2, dp // 2
    shard, vectors = refs[:count], refs[count : count + len(sizes)]
    at_ref = count + len(sizes)
    tokens, upstream, lengths = refs[at_ref : at_ref + 3]
    at_ref += 3
    full = refs[at_ref : at_ref + count]
    at_ref += count
    (
        small_full, row, seed, normed_out, triple_out, probs_out, mixed_out, resid_out, second_out, act_out, slope_out,
    ) = refs[at_ref : at_ref + 11]
    at_ref += 11
    wide, low = refs[at_ref : at_ref + count], refs[at_ref + count : at_ref + 2 * count]
    (
        row_v, normed, triple, probs, mixed, resid, second, act, slope, triple_w, attend_w, expand_w,
        load, local, up_s, down_s, y_s, x_s, ca_s, cb_s, yz_r, x_r, ca_r, cb_r, small_s, small_r, tok_l, tok_s, tok_r,
        weight_l, out_l, probs_l, mixed_s, mixed_r,
    ) = refs[at_ref + 2 * count :]
    d, s, z, y, x, c = own_place()
    steps = doubling_steps(dp)

    def parts(g):
        if kinds[g] != "cols":
            return [(slice(None), slice(None))]
        n = wide[g].shape[1]
        if g:
            return [(pl.ds(pl.multiple_of(c * n, 128), n), slice(None))]
        n, wide_pair = n // 3, 2 * HD
        return [
            (pl.ds(pl.multiple_of((2 * t + c) * n + wide_pair * p, 128), wide_pair), tile(3 * p + t, wide_pair))
            for p in range(n // wide_pair)
            for t in range(3)
        ]

    def tile(i, n=quarter):
        return slice(i * n, (i + 1) * n)

    def active(g, at):
        return True if kinds[g] != "shards" else at // half == c

    def fetches(g):
        return [
            pltpu.make_async_copy(shard[g].at[:, source], wide[g].at[:, target], load.at[g, t])
            for t, (source, target) in enumerate(parts(g))
        ]

    def when(condition, action):
        if condition is True:
            action()
        else:
            pl.when(condition)(action)

    for g in range(count):

        def fetch():
            for copy in fetches(g):
                copy.start()

        when(active(g, d), fetch)

    greet(depth, steps)

    def columns(g):
        if kinds[g] != "share":
            return slice(None)
        n = full[g].shape[1] // 2
        return pl.ds(pl.multiple_of(c * n, 128), n)

    def window(g, at, offset, n):
        m = rows[g] // 3
        place = at if kinds[g] != "shards" else at % half
        return full[g].at[pl.ds(pl.multiple_of(place * rows[g] + offset * m, 16), n * m), columns(g)]

    def own_piece(g):
        m = rows[g] // 3
        return low[g].at[pl.ds(pl.multiple_of(x * m, 16), 2 * m), columns(g)]

    def move(view, send, recv, d_to, s_to, src=None):
        return remote(view if src is None else src, view, send, recv, d_to, s_to)

    def up(g, at, src=None):
        return move(window(g, at, x, 2), up_s.at[g, at], yz_r.at[g, at], d + 2, s, src)

    def down(g, at, src=None):
        return move(window(g, at, x, 2), down_s.at[g, at], yz_r.at[g, at], d - 2, s, src)

    def over_y(g, at, src=None):
        return move(window(g, at, x, 2), y_s.at[g, at], yz_r.at[g, at], flip(d, 1), s, src)

    def over_x(g, at):
        return move(window(g, at, 2 * x, 1), x_s.at[g, at], x_r.at[g, at], d, flip(s, 2))

    def from_x(g, at):
        return move(window(g, at, 2 * (1 - x), 1), x_s.at[g, at], x_r.at[g, at], d, flip(s, 2))

    def core_a(g, at):
        return move(window(g, at, x, 2), ca_s.at[at], ca_r.at[at], d, flip(s, 1))

    def core_b(g, at):
        return move(window(g, at, 2 * (1 - x), 1), cb_s.at[at], cb_r.at[at], d, flip(s, 1))

    def small_copy(k):
        size = 16 << k
        view = small_full.at[pl.ds(pl.multiple_of((d // (1 << k)) * size, 16), size), :]
        return remote(view, view, small_s.at[k], small_r.at[k], flip(d, 1 << k), s)

    def own_local(g):
        place = d if kinds[g] != "shards" else d % half
        view = full[g].at[pl.ds(pl.multiple_of(place * rows[g], 16), rows[g]), :]
        return pltpu.make_async_copy(low[g], view, local.at[g])

    def spot(array, index):
        return array.at[pl.ds(pl.multiple_of(index * quarter, 16), quarter), :]

    def row_copies(t, source, target):
        mine, theirs = spot(target, 2 * x + c), spot(target, 2 * (1 - x) + c)
        return (
            pltpu.make_async_copy(source.at[x], mine, tok_l.at[t]),
            remote(source.at[1 - x], mine, tok_s.at[t, 0], tok_r.at[t, 0], d, flip(s, 2)),
            remote(source.at[x], mine, tok_s.at[t, 1], tok_r.at[t, 1], d, flip(s, 1)),
            remote(theirs, theirs, tok_s.at[t, 2], tok_r.at[t, 2], d, flip(s, 1)),
        )

    moves = [row_copies(0, tokens, row), row_copies(1, upstream, seed)]

    def row_begin(t):
        for copy in moves[t][:3]:
            copy.start()

    def row_pass(t):
        moves[t][1].wait_recv()
        moves[t][3].start()

    def row_arrived(t):
        own, _, to_core, passed = moves[t]
        own.wait()
        to_core.wait_recv()
        passed.wait_recv()

    small_full[pl.ds(pl.multiple_of(d * 16, 16), 16), :] = jnp.zeros((16, 128), F32)
    for ref, size, first_row in zip(vectors, sizes, small_rows(sizes)[0]):
        for k in range(-(-size // 128)):
            n = min(128, size - 128 * k)
            small_full[pl.ds(d * 16 + first_row + k, 1), 0:n] = ref[128 * k : 128 * k + n].reshape(1, n)
    row_begin(0)

    def begin(g):
        for copy in fetches(g):
            copy.wait()
        low[g][...] = wide[g][...].astype(BF16)
        src = own_piece(g)
        pl.when(z < depth - 1)(lambda: up(g, d, src).start())
        pl.when(z > 0)(lambda: down(g, d, src).start())
        over_y(g, d, src).start()
        own_local(g).start()

    def small_step(k):
        if k:
            small_copy(k - 1).wait()
        if k < len(steps):
            small_copy(k).start()

    def arrived(g, at):
        over_x(g, at).start()
        if kinds[g] == "share":
            core_a(g, at).start()

    def z_arrival(g, r):
        def low_side():
            at = d - 2 * r
            up(g, at).wait_recv()

            @pl.when(z < depth - 1)
            def _():
                up(g, at).start()

            over_y(g, at).start()
            arrived(g, at)

        def high_side():
            at = d + 2 * r
            down(g, at).wait_recv()

            @pl.when(z > 0)
            def _():
                down(g, at).start()

            over_y(g, at).start()
            arrived(g, at)

        pl.when((z >= r) & active(g, d - 2 * r))(low_side)
        pl.when((z + r < depth) & active(g, d + 2 * r))(high_side)

    other = flip(d, 1)

    def y_one(g, at):
        over_y(g, at).wait_recv()
        arrived(g, at)

    def on_shards(g, r, base, action):
        if r == 0:
            when(active(g, base), lambda: action(base))
        else:
            pl.when((z >= r) & active(g, base - 2 * r))(lambda: action(base - 2 * r))
            pl.when((z + r < depth) & active(g, base + 2 * r))(lambda: action(base + 2 * r))

    def x_one(g, at):
        from_x(g, at).wait_recv()
        if kinds[g] == "share":
            core_b(g, at).start()


    width, pairs = row.shape[1], triple.shape[1] // (6 * HD)
    half_width = width // 2

    total = lengths[x, 0] + lengths[x, 1]

    def vector(index, shards=range(dp)):
        return small_vector(small_full, sizes, index, shards)

    weight_loads = [
        pltpu.make_async_copy(full[g], target, weight_l.at[g]) for g, target in enumerate((triple_w, attend_w, expand_w))
    ]
    row_load = pltpu.make_async_copy(row, row_v, weight_l.at[3])

    def row_ready():
        row_arrived(0)
        row_load.start()

    def every_shard(g, action):
        for r in range(depth):
            on_shards(g, r, other, action)
            if r:
                on_shards(g, r, d, action)

    def weight_ready(g):
        own_local(g).wait()
        if kinds[g] == "share":

            def passed_on(at):
                core_a(g, at).wait_recv()
                core_b(g, at).wait_recv()

            every_shard(g, passed_on)
        weight_loads[g].start()

    def normalize(values, gain, shift):
        center = values - jnp.mean(values, axis=-1, keepdims=True)
        spread_of = jnp.mean(center * center, axis=-1, keepdims=True)
        return (center * lax.rsqrt(spread_of + EPSILON) * gain + shift).astype(BF16)

    def norm_tile(i):
        if i == 0:
            row_load.wait()
        normed[tile(i)] = normalize(row_v[tile(i)].astype(F32), vector(0), vector(1))

    def triple_tile(i):
        if i == 0:
            weight_loads[0].wait()
        n = half_width // sizes[2]
        ends = [vector(2, [first + c * n + k for k in range(n)]) for first in (0, dp // 2)]
        wide_pair = 2 * HD
        bias = jnp.concatenate(
            [
                part[:, tile(p, wide_pair)]
                for p in range(pairs)
                for part in (ends[0], jnp.zeros((1, half_width), F32), ends[1])
            ],
            axis=1,
        )
        triple[tile(i)] = (product(normed[tile(i)], triple_w[...]) + bias).astype(BF16)

    def probs_copy(p):
        return pltpu.make_async_copy(probs.at[p % 2], probs_out.at[p], probs_l.at[p % 2])

    def mixed_window(p, core):
        return pl.ds(pl.multiple_of(core * half_width + 2 * HD * p, 2 * HD), 2 * HD)

    def mixed_copy(p):
        view = mixed.at[:, mixed_window(p, c)]
        return remote(view, view, mixed_s.at[p], mixed_r.at[p], d, flip(s, 1))

    def attend_part(p, part):
        if p > 1 and part == 0:
            probs_copy(p - 2).wait()
        columns = [tile(3 * p + k, 2 * HD) for k in range(3)]
        mixed[tile(part), mixed_window(p, c)] = attend_block(
            part, quarter, total, triple[tile(part), columns[0]], triple.at[:, columns[1]], triple.at[:, columns[2]],
            probs.at[p % 2],
        )
        if part == 3:
            probs_copy(p).start()
            mixed_copy(p).start()

    out_copies = [
        pltpu.make_async_copy(source, target, out_l.at[k])
        for k, (source, target) in enumerate(
            (
                (normed, normed_out), (triple, triple_out), (mixed, mixed_out), (resid, resid_out),
                (second, second_out), (act, act_out), (slope, slope_out),
            )
        )
    ]

    def resid_tile(i):
        if i == 0:
            weight_loads[1].wait()
            out_copies[0].start()
            out_copies[1].start()
            for p in range(pairs):
                mixed_copy(p).wait()
            out_copies[2].start()
        values = row_v[tile(i)].astype(F32) + product(mixed[tile(i)], attend_w[...]) + vector(3)
        resid[tile(i)] = values
        second[tile(i)] = normalize(values, vector(4), vector(5))

    def expand_tile(i):
        if i == 0:
            weight_loads[2].wait()
            out_copies[3].start()
            out_copies[4].start()
        bias = vector(6, [c * half + k for k in range(half)])
        for k in range(expand_w.shape[1] // 256):
            part = tile(k, 256)
            value = product(second[tile(i)], expand_w[:, part]) + bias[:, part]
            square = value * value
            bend = jnp.tanh(0.7978845608028654 * value * (1.0 + 0.044715 * square))
            raised = 0.5 * (1.0 + bend)
            act[tile(i), part] = (value * raised).astype(BF16)
            inner = 0.7978845608028654 + (3 * 0.7978845608028654 * 0.044715) * square
            slope[tile(i), part] = (raised + 0.5 * value * (1.0 - bend * bend) * inner).astype(BF16)

    plan = Plan()
    for k in range(len(steps) + 1):
        plan.add(2 * k, small_step, k)
    plan.add(8, row_pass, 0)
    plan.add(11, row_ready)
    plan.add(42, row_begin, 1)
    plan.add(55, row_pass, 1)
    first = 0.0
    ready = []
    for g in range(count):
        piece = rows[g] * wide[g].shape[1] * 2 / 50e3 * 2 / 3
        if kinds[g] != "cols":
            piece /= 2
        hop = piece + 1.5
        plan.add(first, when, active(g, d), functools.partial(begin, g))
        for r in range(depth):
            if r:
                plan.add(first + hop * r, z_arrival, g, r)
                plan.add(first + hop * r + 0.5 * piece + 1.5, on_shards, g, r, d, functools.partial(x_one, g))
            plan.add(first + hop * (r + 1), on_shards, g, r, other, functools.partial(y_one, g))
            plan.add(
                first + hop * (r + 1) + 0.5 * piece + 1.5, on_shards, g, r, other, functools.partial(x_one, g)
            )
        ready.append(first + hop * depth + 0.5 * piece + 1.6)
        if kinds[g] != "shards":
            plan.add(ready[g] + (2 if kinds[g] == "share" else 0), weight_ready, g)
        first += 4 * piece if g == count - 1 else 3 * piece
    for i in range(4):
        plan.add(12.5 + 0.7 * i, norm_tile, i)
    at = ready[0] + 1.5
    for i in range(4):
        plan.add(at, triple_tile, i)
        at += 1.3
    for p in range(pairs):
        for part in range(4):
            plan.add(at, attend_part, p, part)
            at += 0.4 * (part + 1)
    at = max(at, ready[1] + 3.5) + 2.0
    for i in range(4):
        plan.add(at, resid_tile, i)
        at += 1.3
    at = max(at, ready[2] + 1.5)
    for i in range(4):
        plan.add(at, expand_tile, i)
        at += 1.5
    plan.run()

    out_copies[5].start()
    out_copies[6].start()
    for copy in out_copies:
        copy.wait()
    for p in range(max(pairs - 2, 0), pairs):
        probs_copy(p).wait()
    row_arrived(1)
    for move_of in moves:
        for copy in move_of[1:]:
            copy.wait_send()

    for g in range(count):

        def end():
            if kinds[g] == "shards":
                own_local(g).wait()

            @pl.when(z < depth - 1)
            def _():
                up(g, d, own_piece(g)).wait_send()

            @pl.when(z > 0)
            def _():
                down(g, d, own_piece(g)).wait_send()

            over_y(g, d, own_piece(g)).wait_send()

        when(active(g, d), end)

        def finish(g, own_column, at):
            if own_column:
                over_y(g, at).wait_send()
            over_x(g, at).wait_send()
            if kinds[g] == "share":
                core_a(g, at).wait_send()
                core_b(g, at).wait_send()

        for r in range(depth):
            on_shards(g, r, other, functools.partial(finish, g, False))
            if r:
                on_shards(g, r, d, functools.partial(finish, g, True))
                pl.when((z >= r) & (z < depth - 1) & active(g, d - 2 * r))(lambda: up(g, d - 2 * r).wait_send())
                pl.when((z + r < depth) & (z > 0) & active(g, d + 2 * r))(lambda: down(g, d + 2 * r).wait_send())


def spread(dp, shards, vectors, tokens, upstream, lengths):
    kinds = ["cols", "share", "cols", "shards"]
    rows = [member.shape[0] for member in shards]
    count = len(rows)
    quarter, width = tokens.shape[1:]
    length = 4 * quarter
    dma = pltpu.SemaphoreType.DMA
    any_space = pl.BlockSpec(memory_space=pl.ANY)
    vmem = pl.BlockSpec(memory_space=pltpu.VMEM)
    held = [(m.shape[0], m.shape[1] // 2 if kind == "cols" else m.shape[1]) for m, kind in zip(shards, kinds)]
    whole = [(dp * r // 2 if kind == "shards" else dp * r, n) for (r, n), kind in zip(held, kinds)]
    kept = part_start(4, quarter)
    pairs = width // (4 * HD)
    hidden = whole[2][1]
    states = [
        ((length, width), BF16), ((length, 3 * width // 2), BF16), ((pairs, 2, kept, quarter), BF16),
        ((length, width), BF16), ((length, width), F32), ((length, width), BF16),
        ((length, hidden), BF16), ((length, hidden), BF16),
    ]
    slots = [(shape if k != 2 else (2, *shape[1:]), kind) for k, (shape, kind) in enumerate(states)]
    return pl.pallas_call(
        functools.partial(spread_kernel, dp, kinds, rows, quarter, [v.shape[0] for v in vectors]),
        out_shape=[jax.ShapeDtypeStruct(shape, BF16) for shape in whole]
        + [jax.ShapeDtypeStruct((dp * 16, 128), F32)]
        + [jax.ShapeDtypeStruct((length, width), BF16)] * 2
        + [jax.ShapeDtypeStruct(*state) for state in states],
        in_specs=[any_space] * count
        + [vmem] * len(vectors)
        + [any_space] * 2
        + [pl.BlockSpec(memory_space=pltpu.SMEM)],
        out_specs=[any_space] * count + [vmem] + [any_space] * (2 + len(states)),
        scratch_shapes=[pltpu.VMEM(shape, F32) for shape in held]
        + [pltpu.VMEM(shape, BF16) for shape in held]
        + [pltpu.VMEM((length, width), BF16)]
        + [pltpu.VMEM(*slot) for slot in slots]
        + [pltpu.VMEM(shape, BF16) for shape in whole[:3]]
        + [dma((count, 3 * pairs)), dma((count,))]
        + [dma((count, dp))] * 4
        + [dma((dp,))] * 2
        + [dma((count, dp))] * 2
        + [dma((dp,))] * 2
        + [dma((len(doubling_steps(dp)),))] * 2
        + [dma((2,)), dma((2, 3)), dma((2, 3))]
        + [dma((4,)), dma((7,)), dma((2,)), dma((pairs,)), dma((pairs,))],
        compiler_params=pltpu.CompilerParams(
            collective_id=1, has_side_effects=True, vmem_limit_bytes=60 * MIB
        ),
        name="spread_weights",
    )(*shards, *vectors, tokens, upstream, lengths)


ATTEND_ROW, SECOND_ROW, EXPAND_ROW, SHRINK_ROW = (0, 0), (0, 1), 3, (0, 7)
FIRST_ROW, TRIPLE_ROW = (1, 0), (1, 2)


def back_kernel(dp, kinds, rows, quarter, sizes, *refs):
    count = len(rows)
    depth, half = dp // 2, dp // 2
    (
        shrink_in, expand_in, attend_in, triple_w_in, small_full, row_in, seed_in, normed_in, triple_in, probs_in, mixed_in,
        resid_in, second_in, act_in, slope_in,
    ) = refs[:15]
    outs, (small_sum, result_out, tokens_out) = refs[15 : 15 + count], refs[15 + count : 18 + count]
    at_ref = 18 + count
    acc, x_buf, y_buf, up_buf, down_buf, b_buf = [refs[at_ref + k * count : at_ref + (k + 1) * count] for k in range(6)]
    (
        act, slope, seed, shrink_w, second, expand_w, partial, other, resid, mixed, attend_w, grad_own, grad_mixed, probs,
        dkeys, dvalues, row_own, send_own, sum_recv, n_recv, stage, ring_buf, line_buf,
        load, resid_l, probs_l, x_s, x_r, y_s, y_r, u_s, u_r, n_s, n_r, f_s, f_r, small_s, small_r,
        part_s, part_r, sum_s, sum_r, one_s, one_r, give_s, give_r,
    ) = refs[at_ref + 6 * count :]
    d, s, z, y, x, c = own_place()
    twin = flip(s, 1)
    length, width = seed.shape
    hidden, half_width = act.shape[1], width // 2
    pairs = half_width // (2 * HD)
    normed, grad_pre, branch = second, slope, partial
    triple = slope.at[:, pl.ds(0, 3 * half_width)]
    grad_triple = act.at[:, pl.ds(0, 3 * half_width)]
    triple_w = expand_w.at[:, pl.ds(0, 3 * half_width)]

    sources = [
        (act_in, act), (seed_in, seed), (shrink_in, shrink_w), (slope_in, slope), (expand_in, expand_w),
        (second_in, second), (mixed_in, mixed), (attend_in, attend_w),
        (normed_in, normed), (triple_in, triple), (triple_w_in, triple_w),
    ]
    loads = [pltpu.make_async_copy(source, target, load.at[k]) for k, (source, target) in enumerate(sources)]
    row_loads = [
        pltpu.make_async_copy(
            row_in.at[pl.ds(pl.multiple_of((2 * h + c) * quarter, 16), quarter), :], row_own.at[h], load.at[len(sources) + h]
        )
        for h in range(2)
    ]

    def resid_load(i):
        return pltpu.make_async_copy(resid_in.at[pl.ds(i * quarter, quarter), :], resid.at[i % 2], resid_l.at[i % 2])

    def probs_load(k):
        return pltpu.make_async_copy(probs_in.at[k // 2, k % 2], probs.at[k % 2], probs_l.at[k % 2])

    for copy in loads[:8]:
        copy.start()
    resid_load(0).start()
    resid_load(1).start()
    for copy in row_loads:
        copy.start()
    probs_load(0).start()
    probs_load(1).start()

    def turned(offset):
        s_to = s
        for bit in (1, 2):
            s_to = flip(s_to, bit) if offset & bit else s_to
        return (flip(d, 1) if offset & 4 else d), s_to

    def along(offset):
        d_to = d
        for k in range(depth.bit_length() - 1):
            d_to = flip(d_to, 2 << k) if offset >> k & 1 else d_to
        return d_to, s

    barrier = pltpu.get_barrier_semaphore()
    ring, line = range(1, 8), range(1, depth)
    for to in [turned(offset) for offset in ring] + [along(offset) for offset in line]:
        pl.semaphore_signal(barrier, inc=1, device_id=to, device_id_type=MESH)
    pl.semaphore_wait(barrier, len(ring) + len(line))

    small_sum[...] = jnp.zeros_like(small_sum)


    def owners(g, core):
        return range(depth) if kinds[g] != "shards" else range(core * (depth // 2), (core + 1) * (depth // 2))

    def first_layer(g):
        return 0 if kinds[g] != "shards" else c * (depth // 2)

    def span(g, units, n):
        m = rows[g] // 3
        return pl.ds(pl.multiple_of(units * m, 16), n * m)

    def add(g, window, extra):
        acc[g][window] = acc[g][window] + extra

    def over_x(g, own):
        column = y if own else 1 - y
        return remote(
            acc[g].at[:, column, span(g, 2 * (1 - x), 1), :], x_buf[g].at[:, column],
            x_s.at[g, int(own)], x_r.at[g, int(own)], d, flip(s, 2),
        )

    def over_y(g):
        return remote(acc[g].at[:, 1 - y, span(g, x, 2), :], y_buf[g], y_s.at[g], y_r.at[g], flip(d, 1), s)

    def along_z(g, upward, hop, layers):
        first = layers[0] - owners(g, layers[0] // (depth // 2))[0] if kinds[g] == "shards" else layers[0]
        places = slice(first, first + len(layers))
        source = acc[g].at[places, y, span(g, x, 2), :]
        if upward:
            return remote(source, up_buf[g].at[places], u_s.at[g, hop], u_r.at[g, hop], d + 2, s), places
        return remote(source, down_buf[g].at[places], n_s.at[g, hop], n_r.at[g, hop], d - 2, s), places

    def stage_a(g, own):
        over_x(g, own).start()

    def stage_c(g, own):
        over_x(g, own).wait_recv()
        column = y if own else 1 - y
        add(g, (slice(None), column, span(g, 2 * x, 1), slice(None)), x_buf[g][:, column])
        if not own:
            over_y(g).start()

    def stage_d(g):
        over_y(g).wait_recv()
        add(g, (slice(None), y, span(g, x, 2), slice(None)), y_buf[g][...])

    def hop_cases(g, hop):
        cases = []
        for core in range(2) if kinds[g] == "shards" else (None,):
            whole = list(owners(g, core or 0))
            mine = True if core is None else c == core
            got, sent = [k for k in whole if k >= hop > 0], [k for k in whole if k > hop]
            cases.append(((z == hop) & mine, True, got, sent))
            got, sent = [k for k in whole if k < depth - hop and hop], [k for k in whole if k < depth - 1 - hop]
            cases.append(((z == depth - 1 - hop) & mine, False, got, sent))
        return [case for case in cases if case[2] or case[3]]

    def stage_e(g, hop):
        for condition, upward, got, sent in hop_cases(g, hop):

            def run():
                if got:
                    copy, places = along_z(g, upward, hop - 1, got)
                    copy.wait_recv()
                    arrived = (up_buf if upward else down_buf)[g][places]
                    add(g, (places, y, span(g, x, 2), slice(None)), arrived)
                if sent:
                    along_z(g, upward, hop, sent)[0].start()

            pl.when(condition)(run)

    def drain_e(g, hop):
        for condition, upward, _, sent in hop_cases(g, hop):
            if sent:
                pl.when(condition)(lambda: along_z(g, upward, hop, sent)[0].wait_send())

    def own_layer(g):
        return z - first_layer(g)

    def ours(g, action):
        if kinds[g] != "shards":
            action()
        else:
            pl.when((z >= first_layer(g)) & (z < first_layer(g) + depth // 2))(action)

    def out_rows(g, units, n):
        return outs[g].at[c, span(g, units, n), :] if kinds[g] != "shards" else outs[g].at[span(g, units, n), :]

    def final_share(g):
        source = acc[g].at[own_layer(g), y, span(g, 2 * x, 1), :]
        return remote(source, out_rows(g, 2 * x, 1), f_s.at[g, 0], f_r.at[g, 0], d, flip(s, 2))

    def final_swap(g):
        source = acc[g].at[own_layer(g), y, span(g, 1, 1), :]
        return remote(source, b_buf[g], f_s.at[g, 1], f_r.at[g, 1], d, flip(s, 2))

    def final_core(g):
        view = out_rows(g, 0, 3)
        return remote(view, view, f_s.at[g, 2], f_r.at[g, 2], d, twin)

    def finish_one(g):
        def run():
            final_share(g).start()
            final_swap(g).start()
            out_rows(g, 2 * x, 1)[...] = acc[g][own_layer(g), y, span(g, 2 * x, 1), :]

        ours(g, run)

    def finish_two(g):
        def run():
            final_swap(g).wait_recv()
            out_rows(g, 1, 1)[...] = acc[g][own_layer(g), y, span(g, 1, 1), :] + b_buf[g][...]
            final_share(g).wait_recv()
            final_core(g).start()

        ours(g, run)

    ring_place = y * 4 + s

    def ring_copy(t, offset):
        target = turned(offset)
        return remote(
            ring_buf.at[t, ring_place], ring_buf.at[t, ring_place], small_s.at[t, offset], small_r.at[t, offset], *target
        )

    def line_copy(t, offset):
        target = along(offset)
        return remote(
            line_buf.at[t, z], line_buf.at[t, z], small_s.at[t, 7 + offset], small_r.at[t, 7 + offset], *target
        )

    def small_begin(t):
        ring_buf[t, ring_place] = small_sum[t]
        for offset in ring:
            ring_copy(t, offset).start()

    def small_pass(t):
        for offset in ring:
            ring_copy(t, offset).wait()
        total = ring_buf[t, 0]
        for k in range(1, 8):
            total = total + ring_buf[t, k]
        line_buf[t, z] = total
        for offset in line:
            line_copy(t, offset).start()

    def small_end(t):
        for offset in line:
            line_copy(t, offset).wait()
        total = line_buf[t, 0]
        for k in line:
            total = total + line_buf[t, k]
        small_sum[t] = total


    def tile(i, n=quarter):
        return slice(i * n, (i + 1) * n)

    def own_tile(h):
        return pl.ds(pl.multiple_of((2 * h + c) * quarter, 16), quarter)

    def twin_tile(h):
        return pl.ds(pl.multiple_of((2 * h + 1 - c) * quarter, 16), quarter)

    def vector(index):
        return small_vector(small_full, sizes, index, range(dp))

    def sums(row_at, values, columns=slice(None)):
        block, at = row_at
        small_sum[block, at : at + 1, columns] += jnp.sum(values, axis=0, keepdims=True)

    def shrink_grad(k):
        if k == 0:
            loads[0].wait()
            loads[1].wait()
        grad = product_across(act[:, tile(k, rows[0])], seed[...]).astype(BF16)
        for g in range(2):
            acc[g][k // 2, k % 2] = grad[:, tile(g, width // 2)]

    def sum_copy(h):
        return remote(send_own.at[h], sum_recv.at[h], sum_s.at[h], sum_r.at[h], d, twin)

    def result_partial(h):
        send_own[h] = product(act[twin_tile(h), :], shrink_w[...]).astype(BF16)
        sum_copy(h).start()

    def grad_pre_tile(i):
        if i == 0:
            loads[2].wait()
            loads[3].wait()
        for k in range(hidden // 256):
            columns = tile(k, 256)
            value = product_back(seed[tile(i)], shrink_w[columns, :]) * slope[tile(i), columns].astype(F32)
            low_value = value.astype(BF16)
            grad_pre[tile(i), columns] = low_value
            total = jnp.sum(low_value.astype(F32), axis=0, keepdims=True)
            spot = (
                0, pl.ds(EXPAND_ROW + (hidden // width) * c + k * 256 // width, 1),
                slice(k * 256 % width, k * 256 % width + 256),
            )
            small_sum[spot] = small_sum[spot] + total
        sums(SHRINK_ROW, 0.5 * seed[tile(i)].astype(F32))

    def part_copy(i):
        return remote(partial.at[tile(i)], other.at[tile(i)], part_s.at[i], part_r.at[i], d, twin)

    def n_two_tile(i):
        if i == 0:
            loads[4].wait()
        partial[tile(i)] = product_back(grad_pre[tile(i)], expand_w[...]).astype(BF16)
        part_copy(i).start()

    shard_rows = rows[2]

    def by_owner(g, k, grad):
        acc[g][k * (depth // 2) : (k + 1) * (depth // 2)] = grad.astype(BF16).reshape(depth // 2, 2, shard_rows, -1)

    def expand_grad(g, k):
        if g == 2 and k == 0:
            loads[5].wait()
        by_owner(g, k, product_across(second[:, tile(k, half_width)], grad_pre[:, tile(g - 2, hidden // 2)]))

    def later_loads():
        for copy in loads[8:]:
            copy.start()

    def back_norm(n, values, gain, index, scale):
        center = values - jnp.mean(values, axis=-1, keepdims=True)
        r = lax.rsqrt(jnp.mean(center * center, axis=-1, keepdims=True) + EPSILON)
        hat = center * r
        sums(index, scale * n * hat)
        sums((index[0], index[1] + 1), scale * n)
        e = n * gain
        return r * (e - jnp.mean(e, axis=-1, keepdims=True) - hat * jnp.mean(e * hat, axis=-1, keepdims=True))

    def resid_tile(i):
        resid_load(i).wait()
        part_copy(i).wait()
        n = partial[tile(i)].astype(F32) + other[tile(i)].astype(F32)
        grad = seed[tile(i)].astype(F32) + back_norm(n, resid[i % 2], vector(4), SECOND_ROW, 0.5)
        low_grad = grad.astype(BF16)
        branch[tile(i)] = low_grad
        sums(ATTEND_ROW, 0.5 * low_grad.astype(F32))

        @pl.when(c == i % 2)
        def _():
            h = i // 2
            grad_own[h] = grad
            sum_copy(h).wait_recv()
            value = resid[i % 2] + product(act[tile(i)], shrink_w[...]) + sum_recv[h].astype(F32) + vector(7)
            stage[h] = value.astype(BF16)

        if i + 2 < 4:
            resid_load(i + 2).start()

    def give_copy(t):
        return remote(stage.at[1 - x], (result_out, tokens_out)[t].at[x], give_s.at[t], give_r.at[t], d, flip(s, 2))

    def give_back(t):
        (result_out, tokens_out)[t][x] = stage[x]
        give_copy(t).start()

    def attend_grad(k):
        if k == 0:
            loads[6].wait()
        columns = pl.ds(pl.multiple_of(c * half_width, 128), half_width)
        by_owner(4, k, product_across(mixed[:, tile(k, half_width)], branch[:, columns]))

    def mixed_tile(i):
        if i == 0:
            loads[7].wait()
        rows_c = pl.ds(pl.multiple_of(c * half_width, 16), half_width)
        grad_mixed[tile(i)] = product_back(branch[tile(i)], attend_w[rows_c, :]).astype(BF16)

    def attend_back_step(k, part):
        p, head = k // 2, k % 2
        if part == 3:
            probs_load(k).wait()
        if k == 0 and part == 3:
            loads[9].wait()
        columns = [tile(3 * p + n, 2 * HD) for n in range(3)]
        grad_query = attend_back_block(
            head, part, quarter, triple[tile(part), columns[0]], triple.at[:, columns[1]], triple.at[:, columns[2]],
            grad_mixed[tile(part), 2 * HD * p : 2 * HD * (p + 1)],
            probs[k % 2, part_start(part, quarter) : part_start(part + 1, quarter)], dkeys, dvalues,
            part == 3 and head == 0,
        )
        if head:
            grad_query = jnp.where(head_mask(), grad_triple[tile(part), columns[0]], grad_query)
            place_q = pl.ds(pl.multiple_of(c * half_width + 2 * HD * p, 128), 2 * HD)
            sums(TRIPLE_ROW, grad_query.astype(F32), place_q)
        grad_triple[tile(part), columns[0]] = grad_query
        if part == 0:
            if k + 2 < 2 * pairs:
                probs_load(k + 2).start()
            if head:
                grad_triple[:, columns[1]] = dkeys[...].astype(BF16)
                low_values = dvalues[...].astype(BF16)
                grad_triple[:, columns[2]] = low_values
                sums((TRIPLE_ROW[0], TRIPLE_ROW[1] + 1), low_values.astype(F32), place_q)

    def triple_grad(p, k):
        if p == 0 and k == 0:
            loads[8].wait()
        columns = tile(p, 6 * HD)
        by_owner(5 + p, k, product_across(normed[:, tile(k, half_width)], grad_triple[:, columns]))

    def one_copy(h):
        return remote(send_own.at[h], n_recv.at[h], one_s.at[h], one_r.at[h], d, twin)

    def n_one_partial(h):
        if h == 0:
            loads[10].wait()
        sum_copy(h).wait_send()
        send_own[h] = product_back(grad_triple[twin_tile(h), :], triple_w[...]).astype(BF16)
        one_copy(h).start()

    def first_tile(h):
        if h == 0:
            give_copy(0).wait_send()
        row_loads[h].wait()
        n = product_back(grad_triple[own_tile(h), :], triple_w[...])
        one_copy(h).wait_recv()
        n = n + n_recv[h].astype(F32)
        grad = grad_own[h] + back_norm(n, row_own[h].astype(F32), vector(0), FIRST_ROW, 1.0)
        stage[h] = grad.astype(BF16)


    plan = Plan()
    clock = [2.0]

    def compute(micros, action, *args):
        plan.add(clock[0], action, *args)
        clock[0] += micros

    made = []

    def group_made():
        made.append(clock[0] - 0.01)

    for k in range(hidden // rows[0]):
        compute(0.8, shrink_grad, k)
    group_made()
    group_made()
    for i in range(4):
        compute(0.9, grad_pre_tile, i)
    for i in range(4):
        compute(0.8, n_two_tile, i)
    for h in range(2):
        compute(0.8, result_partial, h)
    for g in (2, 3):
        for k in range(2):
            compute(0.8, expand_grad, g, k)
        group_made()
    compute(0.0, later_loads)
    for i in range(4):
        compute(1.5, resid_tile, i)
    compute(0.2, give_back, 0)
    for k in range(2):
        compute(0.5, attend_grad, k)
    group_made()
    for i in range(4):
        compute(0.3, mixed_tile, i)
    plan.add(clock[0], small_begin, 0)
    plan.add(clock[0] + 4.0, small_pass, 0)
    plan.add(clock[0] + 8.0, small_end, 0)
    for k in range(2 * pairs):
        for part in reversed(range(4)):
            compute(0.25 * (part + 1), attend_back_step, k, part)
        if k % 2:
            for n in range(2):
                compute(0.5, triple_grad, k // 2, n)
            group_made()
    for h in range(2):
        compute(0.6, n_one_partial, h)
    compute(1.0, lambda: None)
    for h in range(2):
        compute(1.8, first_tile, h)
    compute(0.2, give_back, 1)
    compute(3.0, small_begin, 1)
    compute(3.0, small_pass, 1)
    compute(0.1, small_end, 1)

    done, started = 0.0, 0.0
    for g in range(count):
        layers, _, group_rows, columns = acc[g].shape
        unit = layers * group_rows * columns * 2 / 50e3 / 3
        done = max(done, made[g])
        for own in (False, True):
            plan.add(max(started, made[g]), stage_a, g, own)
            started = done
            done += unit
            plan.add(done + 1.5, stage_c, g, own)
        at = done + 2.0 + max(0.0, unit - 1.0)
        plan.add(at, stage_d, g)
        for hop in range(depth):
            plan.add(at + 0.1, stage_e, g, hop)
            at += 2 * unit / layers * max(1, depth - 1 - hop) + 1.5
        plan.add(at, finish_one, g)
        plan.add(at + 2 * unit / layers + 2.0, finish_two, g)
    plan.run()

    for g in range(count):

        def drain():
            final_share(g).wait_send()
            final_swap(g).wait_send()
            if kinds[g] == "shards":
                final_core(g).wait_send()

        ours(g, drain)
        if kinds[g] == "shards":
            away = (z < first_layer(g)) | (z >= first_layer(g) + depth // 2)
            pl.when(away)(lambda: final_core(g).wait_recv())
        else:
            final_core(g).wait()
        over_x(g, False).wait_send()
        over_x(g, True).wait_send()
        over_y(g).wait_send()
        for hop in range(depth - 1):
            drain_e(g, hop)
    for h in range(2):
        one_copy(h).wait_send()
    give_copy(0).wait_recv()
    give_copy(1).wait()


def back(dp, sizes, weights, small_full, row, seed, normed, triple, probs, mixed, resid, second, act, slope):
    triple_w, attend_w, expand_w, shrink_w = weights
    length, width = row.shape
    quarter, hidden = length // 4, act.shape[1]
    pairs = width // (4 * HD)
    kinds = ["shards"] * 2 + ["cols"] * (3 + pairs)
    shapes = [(hidden, width // 2)] * 2 + [(width, hidden // 2)] * 2 + [(width, width // 2)] + [(width, 6 * HD)] * pairs
    owners = [dp // 2 if kind == "shards" else dp for kind in kinds]
    rows = [m[0] // n for m, n in zip(shapes, owners)]
    count, depth = len(rows), dp // 2
    dma = pltpu.SemaphoreType.DMA
    any_space = pl.BlockSpec(memory_space=pl.ANY)
    vmem = pl.BlockSpec(memory_space=pltpu.VMEM)

    def buffers(part, *columns):
        return [
            pltpu.VMEM((n // 2, *columns, r // 3 * part, m[1]), BF16) for n, r, m in zip(owners, rows, shapes)
        ]

    halves = (2, quarter, width)
    working = [
        (act.shape, BF16), (act.shape, BF16), (row.shape, BF16), (shrink_w.shape, BF16), (row.shape, BF16),
        (expand_w.shape, BF16), (row.shape, BF16), (row.shape, BF16), (halves, F32), (row.shape, BF16),
        (attend_w.shape, BF16), (halves, F32), ((length, width // 2), BF16), ((2, *probs.shape[2:]), BF16),
        ((length, 2 * HD), F32), ((length, 2 * HD), F32), (halves, BF16), (halves, BF16), (halves, BF16), (halves, BF16),
        (halves, BF16), ((2, 8, 8, width), F32), ((2, depth, 8, width), F32),
    ]
    return pl.pallas_call(
        functools.partial(back_kernel, dp, kinds, rows, quarter, sizes),
        out_shape=[
            jax.ShapeDtypeStruct((r, m[1]) if kind == "shards" else (2, r, m[1]), BF16)
            for r, m, kind in zip(rows, shapes, kinds)
        ]
        + [jax.ShapeDtypeStruct((2, 8, width), F32)]
        + [jax.ShapeDtypeStruct(halves, BF16)] * 2,
        in_specs=[any_space] * 4 + [vmem] + [any_space] * 10,
        out_specs=[vmem] * (count + 3),
        scratch_shapes=buffers(3, 2)
        + buffers(1, 2)
        + buffers(2)
        + buffers(2)
        + buffers(2)
        + [pltpu.VMEM((r // 3, m[1]), BF16) for r, m in zip(rows, shapes)]
        + [pltpu.VMEM(*item) for item in working]
        + [dma((13,)), dma((2,)), dma((2,))]
        + [dma((count, 2))] * 2
        + [dma((count,))] * 2
        + [dma((count, depth))] * 4
        + [dma((count, 3))] * 2
        + [dma((2, 7 + depth))] * 2
        + [dma((4,))] * 2
        + [dma((2,))] * 6,
        compiler_params=pltpu.CompilerParams(
            collective_id=2, has_side_effects=True, vmem_limit_bytes=60 * MIB
        ),
        name="back_and_fold",
    )(shrink_w, expand_w, attend_w, triple_w, small_full, row, seed, normed, triple, probs, mixed, resid, second, act, slope)


def write_kernel(dp, sizes, *refs):
    shrinks, expands, attend = refs[:2], refs[2:4], refs[4]
    at_ref = len(refs) - 14 - 3
    triples, (small, result, tokens_grad) = refs[5:at_ref], refs[at_ref : at_ref + 3]
    (
        result_out, tokens_out, gain_one, shift_one, triple_out, bias_triple, attend_out, bias_attend, gain_two, shift_two,
        expand_out, bias_expand, shrink_out, bias_shrink,
    ) = refs[at_ref + 3 :]
    d = lax.axis_index("dp")
    width = small.shape[2]
    result_out[...] = result[...]
    tokens_out[...] = tokens_grad[...]
    half = width // 2
    for k, source in enumerate(shrinks):
        shrink_out[:, k * half : (k + 1) * half] = source[...].astype(F32)
    for core in range(2):
        attend_out[:, core * half : (core + 1) * half] = attend[core].astype(F32)
        for k, source in enumerate(expands):
            n = source.shape[2]
            expand_out[:, (2 * core + k) * n : (2 * core + k + 1) * n] = source[core].astype(F32)
        for p, source in enumerate(triples):
            for t in range(3):
                at = t * width + core * (width // 2) + 2 * HD * p
                triple_out[:, at : at + 2 * HD] = source[core, :, 2 * HD * t : 2 * HD * (t + 1)].astype(F32)
    rows = (FIRST_ROW, (1, 1), TRIPLE_ROW, ATTEND_ROW, SECOND_ROW, (0, 2), (0, EXPAND_ROW), SHRINK_ROW)
    targets = (gain_one, shift_one, bias_triple, bias_attend, gain_two, shift_two, bias_expand, bias_shrink)
    for (block, at), size, target in zip(rows, sizes, targets):
        lines = size * dp // width
        whole = jnp.concatenate([small[block, at + k : at + k + 1, :] for k in range(lines)], axis=1)
        target[...] = pltpu.roll(whole, whole.shape[1] - size * d, 1)[0, 0:size]


def write(dp, sizes, sums, small, result, tokens_grad):
    shrink, expand, attend = [sums[k].shape for k in (0, 2, 4)]
    width = attend[2] * 2
    vmem = pl.BlockSpec(memory_space=pltpu.VMEM)
    halves = [jax.ShapeDtypeStruct(result.shape, BF16)] * 2
    whole = [(expand[1], 3 * width), (attend[1], width), (expand[1], 4 * expand[2]), (shrink[0], 2 * shrink[1])]
    triple_f, attend_f, expand_f, shrink_f = [jax.ShapeDtypeStruct(shape, F32) for shape in whole]
    v = [jax.ShapeDtypeStruct((size,), F32) for size in sizes]
    return pl.pallas_call(
        functools.partial(write_kernel, dp, sizes),
        out_shape=(
            *halves, v[0], v[1], triple_f, v[2], attend_f, v[3], v[4], v[5], expand_f, v[6], shrink_f, v[7],
        ),
        in_specs=[vmem] * (len(sums) + 3),
        out_specs=(vmem,) * 14,
        compiler_params=pltpu.CompilerParams(vmem_limit_bytes=60 * MIB),
        name="write_outputs",
    )(*sums, small, result, tokens_grad)


def head_mask():
    return lax.broadcasted_iota(jnp.int32, (1, 2 * HD), 1) < HD


def part_start(part, quarter):
    return quarter * (part * (part + 1) // 2)


def attend_block(part, quarter, total, query, k_ref, v_ref, probs_ref):
    first = head_mask()
    length = quarter * (part + 1)
    key_pos = lax.broadcasted_iota(jnp.int32, (length, 1), 0)
    key_pos = jnp.where(key_pos < total, key_pos, 1 << 20)
    allowed = key_pos <= lax.broadcasted_iota(jnp.int32, (1, quarter), 1) + part * quarter
    query = query * jnp.asarray(HD**-0.5, BF16)
    sums = []
    for head in range(2):
        mask = first if head == 0 else ~first
        scores = product_back(k_ref[:length], jnp.where(mask, query, jnp.zeros_like(query)))
        scores = jnp.where(allowed, scores, NEG_FILL)
        exponent = jnp.exp(scores - jnp.max(scores, axis=0, keepdims=True))
        probs = (exponent * (1.0 / jnp.sum(exponent, axis=0, keepdims=True))).astype(BF16)
        probs_ref[head, part_start(part, quarter) : part_start(part + 1, quarter)] = probs
        sums.append(product_across(probs, v_ref[:length]))
    return jnp.where(first, sums[0], sums[1]).astype(BF16)


def attend_kernel(quarter, total, q_ref, k_ref, v_ref, mixed_ref, probs_ref):
    for part in range(4):
        rows = slice(part * quarter, (part + 1) * quarter)
        mixed_ref[rows] = attend_block(part, quarter, total[0], q_ref[rows], k_ref, v_ref, probs_ref.at[0])


def attend(triple, total):
    tokens, width = triple.shape[0], triple.shape[1] // 3
    quarter = tokens // 4
    pairs = width // (2 * HD)
    kept = part_start(4, quarter)

    def block(shift):
        return pl.BlockSpec((tokens, 2 * HD), lambda p, _: (0, p + shift))

    return pl.pallas_call(
        functools.partial(attend_kernel, quarter),
        grid_spec=pltpu.PrefetchScalarGridSpec(
            num_scalar_prefetch=1,
            grid=(pairs,),
            in_specs=[block(0), block(pairs), block(2 * pairs)],
            out_specs=[block(0), pl.BlockSpec((1, 2, kept, quarter), lambda p, _: (p, 0, 0, 0))],
        ),
        out_shape=[
            jax.ShapeDtypeStruct((tokens, width), BF16),
            jax.ShapeDtypeStruct((pairs, 2, kept, quarter), BF16),
        ],
        compiler_params=pltpu.CompilerParams(vmem_limit_bytes=50 * MIB),
        name="attend",
    )(total, triple, triple, triple)


def attend_back_block(head, part, quarter, query, k_ref, v_ref, grad, probs, dkeys, dvalues, fresh):
    length = quarter * (part + 1)
    mask = head_mask() if head == 0 else ~head_mask()
    own_query = jnp.where(mask, query * jnp.asarray(HD**-0.5, BF16), jnp.zeros_like(query))
    own_grad = jnp.where(mask, grad, jnp.zeros_like(grad))
    wide = probs.astype(F32)
    grad_probs = product_back(v_ref[:length], own_grad)
    delta = jnp.sum(wide * grad_probs, axis=0, keepdims=True)
    grad_scores = (wide * (grad_probs - delta)).astype(BF16)
    dv = product(probs, own_grad)
    dk = product(grad_scores, own_query)
    if fresh:
        dvalues[:length] = dv
        dkeys[:length] = dk
    else:
        dvalues[:length] += dv
        dkeys[:length] += dk
    return (product_across(grad_scores, k_ref[:length]) * HD**-0.5).astype(BF16)


def attend_back_kernel(quarter, q_ref, k_ref, v_ref, g_ref, probs_ref, dq_ref, dk_ref, dv_ref, dkeys, dvalues):
    for part in reversed(range(4)):
        rows = slice(part * quarter, (part + 1) * quarter)
        kept = slice(part_start(part, quarter), part_start(part + 1, quarter))
        dq = [
            attend_back_block(
                head, part, quarter, q_ref[rows], k_ref, v_ref, g_ref[rows], probs_ref[0, head, kept], dkeys, dvalues,
                part == 3 and head == 0,
            )
            for head in range(2)
        ]
        dq_ref[rows] = jnp.where(head_mask(), dq[0], dq[1])
    dk_ref[...] = dkeys[...].astype(BF16)
    dv_ref[...] = dvalues[...].astype(BF16)


def attend_back(triple, grad, probs):
    tokens, width = triple.shape[0], triple.shape[1] // 3
    quarter = tokens // 4
    pairs = width // (2 * HD)

    def block(shift):
        return pl.BlockSpec((tokens, 2 * HD), lambda p: (0, p + shift))

    return pl.pallas_call(
        functools.partial(attend_back_kernel, quarter),
        grid=(pairs,),
        in_specs=[block(0), block(pairs), block(2 * pairs), block(0)]
        + [pl.BlockSpec((1, 2, part_start(4, quarter), quarter), lambda p: (p, 0, 0, 0))],
        out_specs=[block(0)] * 3,
        out_shape=[jax.ShapeDtypeStruct((tokens, width), BF16)] * 3,
        scratch_shapes=[pltpu.VMEM((tokens, 2 * HD), F32)] * 2,
        compiler_params=pltpu.CompilerParams(vmem_limit_bytes=50 * MIB),
        name="attend_back",
    )(triple, triple, triple, grad, probs)


def take(array, index, size, axis):
    return lax.dynamic_slice_in_dim(array, index * size, size, axis)


def gather_plain(matrices, small, tokens, core, upper):
    triple, attend_full, expand, shrink = [
        lax.all_gather(m.astype(BF16), "dp", axis=0, tiled=True) for m in matrices
    ]
    width = triple.shape[0]
    thirds = triple.reshape(width, 3, width)
    row = lax.all_gather(tokens, "seq", axis=1, tiled=True)
    return (
        take(thirds, core, width // 2, 2).reshape(width, -1),
        attend_full,
        take(expand, core, expand.shape[1] // 2, 1),
        take(shrink, core, shrink.shape[0] // 2, 0),
        lax.all_gather(small, "dp", axis=0),
        jnp.where(upper, row[1], row[0]),
    )


def fold_plain(grads, small, core):
    def by_core(array):
        empty = jnp.zeros_like(array)
        return jnp.stack([jnp.where(core == 0, array, empty), jnp.where(core == 1, array, empty)], axis=1)

    shrink, *others = grads
    wide = jnp.swapaxes(by_core(shrink), 0, 1).reshape(-1, shrink.shape[1])
    arrays = [wide] + [by_core(m) for m in others]
    sums = [lax.psum(lax.psum_scatter(m, "dp", scatter_dimension=0, tiled=True), "seq") for m in arrays]
    sums = [sums[0]] + [jnp.swapaxes(m, 0, 1) for m in sums[1:]]
    return sums, lax.psum(lax.psum_scatter(small, "dp", scatter_dimension=0, tiled=True), "seq").reshape(-1)


def outputs(result, tokens_grad, sums, small_out):
    width = result.shape[-1]
    shrink_sum, expand_sum, attend_sum, triple_sum = [member.astype(F32) for member in sums]
    triple_sum = triple_sum.reshape(2, -1, 3, width // 2).transpose(1, 2, 0, 3).reshape(-1, 3 * width)
    expand_sum, attend_sum = [m.transpose(1, 0, 2).reshape(m.shape[1], -1) for m in (expand_sum, attend_sum)]
    return (
        result,
        tokens_grad,
        small_out[0],
        small_out[1],
        triple_sum,
        small_out[2],
        attend_sum,
        small_out[3],
        small_out[4],
        small_out[5],
        expand_sum,
        small_out[6],
        shrink_sum,
        small_out[7],
    )


def body(
    dp,
    tokens,
    lengths,
    first_gain,
    first_shift,
    triple_weight,
    triple_bias,
    attend_weight,
    attend_bias,
    second_gain,
    second_shift,
    expand_weight,
    expand_bias,
    shrink_weight,
    shrink_bias,
    upstream,
):
    row_count, quarter, width = tokens.shape
    matrices = (triple_weight, attend_weight, expand_weight, shrink_weight)
    vectors = (first_gain, first_shift, triple_bias, attend_bias, second_gain, second_shift, expand_bias, shrink_bias)
    sizes = [member.shape[0] for member in vectors]
    by_kernel = dp & (dp - 1) == 0 and dp > 2 and all(m.shape[0] % 48 == 0 for m in matrices)
    by_kernel = by_kernel and small_rows(sizes)[1] <= 16 and width == matrices[0].shape[0] * dp
    by_kernel = by_kernel and sizes[2] * dp == 2 * width and (width // 2) % sizes[2] == 0
    place = lax.axis_index("seq")
    upper, core = place // 2 == 1, place % 2

    totals = lengths[:, 0] + lengths[:, 1]
    total = jnp.where(upper, totals[1], totals[0]).reshape(1)

    across = [(k, (k + 2) % 4) for k in range(4)]
    twin = [(k, k + 1 - 2 * (k % 2)) for k in range(4)]

    def halves(partial):
        view = partial.reshape(2, 2, quarter, width)
        mine = jnp.where(core == 0, view[:, 0], view[:, 1])
        theirs = jnp.where(core == 0, view[:, 1], view[:, 0]).astype(BF16)
        return mine + lax.ppermute(theirs, "seq", twin).astype(F32)

    def own_half(array):
        view = array.reshape(2, 2, quarter, width)
        return jnp.where(core == 0, view[:, 0], view[:, 1])

    def give_back(array):
        mine = jnp.where(upper, array[1], array[0])
        theirs = lax.ppermute(jnp.where(upper, array[0], array[1]), "seq", across)
        return jnp.stack([jnp.where(upper, theirs, mine), jnp.where(upper, mine, theirs)])

    def of_core(vector):
        return take(vector, core, vector.shape[0] // 2, 0)

    def spread_out(part):
        empty = jnp.zeros_like(part)
        return jnp.concatenate([jnp.where(core == 0, part, empty), jnp.where(core == 1, part, empty)])

    def whole_row(array):
        mine = jnp.where(upper, array[1], array[0])
        theirs = lax.ppermute(jnp.where(upper, array[0], array[1]), "seq", across)
        pair = jnp.stack([jnp.where(upper, theirs, mine), jnp.where(upper, mine, theirs)])
        others = lax.ppermute(pair, "seq", twin)
        return jnp.stack(
            [jnp.where(core == 0, pair, others), jnp.where(core == 0, others, pair)], axis=1
        ).reshape(-1, width)

    if by_kernel:
        *weights, small_full, row, seed_low, normed, triple, probs, mixed, resid, second, act, slope = spread(
            dp, matrices, vectors, tokens, upstream, lengths
        )
        *sums, small_sum, result, tokens_grad = back(
            dp, sizes, weights, small_full, row, seed_low, normed, triple, probs, mixed, resid, second, act, slope
        )
        return write(dp, sizes, sums, small_sum, result, tokens_grad)
    small = jnp.concatenate(vectors)
    *weights, small_full, row = gather_plain(matrices, small, tokens, core, upper)
    floats, at = [], 0
    for size in sizes:
        floats.append(small_full[:, at : at + size].reshape(-1).astype(BF16).astype(F32))
        at += size
    gain_one, shift_one, bias_triple, bias_attend, gain_two, shift_two, bias_expand, bias_shrink = floats
    triple_low, attend_low, expand_low, shrink_low = weights
    seed_low = whole_row(upstream)
    flat_tokens = row.astype(F32)
    seed = seed_low.astype(F32)

    bias_core = jnp.concatenate(
        [of_core(bias_triple[:width]), jnp.zeros((width // 2,), F32), of_core(bias_triple[width:])]
    )
    normed_low = layer_norm(flat_tokens, gain_one, shift_one).astype(BF16)
    triple = (product(normed_low, triple_low) + bias_core).astype(BF16)
    mixed_core, probs = attend(triple, total)
    mixed_other = lax.ppermute(mixed_core, "seq", twin)
    mixed_low = jnp.concatenate(
        [jnp.where(core == 0, mixed_core, mixed_other), jnp.where(core == 0, mixed_other, mixed_core)], axis=1
    )
    resid = flat_tokens + product(mixed_low, attend_low) + bias_attend
    normed_two_low = layer_norm(resid, gain_two, shift_two).astype(BF16)
    activated, gelu_pull = jax.vjp(gelu_tanh, product(normed_two_low, expand_low) + of_core(bias_expand))
    act_low, slope = activated.astype(BF16), gelu_pull(jnp.ones_like(activated))[0]
    _, second_pull = jax.vjp(layer_norm, resid, gain_two, shift_two)

    grad_pre = (product_back(seed_low, shrink_low) * slope.astype(F32)).astype(BF16)
    partial = product_back(grad_pre, expand_low).astype(BF16)
    other_partial = lax.ppermute(partial, "seq", twin)
    shrink_grad = product_across(act_low, seed_low)
    expand_grad = product_across(normed_two_low, grad_pre)
    result = own_half(resid) + halves(product(act_low, shrink_low)) + bias_shrink
    result = give_back(result.astype(BF16))
    shrink_bias_grad = 0.5 * jnp.sum(seed, axis=0)
    expand_bias_grad = spread_out(jnp.sum(grad_pre.astype(F32), axis=0))
    resid_part, second_gain_grad, second_shift_grad = second_pull(partial.astype(F32) + other_partial.astype(F32))
    grad_resid = seed + resid_part
    grad_branch = grad_resid.astype(BF16)
    attend_grad = product_across(mixed_low, take(grad_branch, core, width // 2, 1))
    attend_bias_grad = 0.5 * jnp.sum(grad_branch.astype(F32), axis=0)
    grad_mixed = product_back(grad_branch, take(attend_low, core, width // 2, 0)).astype(BF16)

    grad_triple = jnp.concatenate(attend_back(triple, grad_mixed, probs), axis=1)
    n_one = halves(product_back(grad_triple, triple_low))
    triple_grad = product_across(normed_low, grad_triple)
    triple_sums = jnp.sum(grad_triple.astype(F32), axis=0)
    triple_bias_grad = jnp.concatenate([spread_out(triple_sums[: width // 2]), spread_out(triple_sums[width:])])
    _, first_pull = jax.vjp(layer_norm, own_half(flat_tokens), gain_one, shift_one)
    flat_grad, first_gain_grad, first_shift_grad = first_pull(n_one)
    tokens_grad = give_back((own_half(grad_resid) + flat_grad).astype(BF16))

    big = [member.astype(BF16) for member in (shrink_grad, expand_grad, attend_grad, triple_grad)]
    small_grads = (
        first_gain_grad, first_shift_grad, triple_bias_grad, attend_bias_grad,
        0.5 * second_gain_grad, 0.5 * second_shift_grad, expand_bias_grad, shrink_bias_grad,
    )
    flat_small = jnp.concatenate([g.reshape(dp, -1) for g in small_grads], axis=1)
    sums, own_small = fold_plain(big, flat_small, core)
    small_out, at = [], 0
    for size in sizes:
        small_out.append(own_small[at : at + size])
        at += size
    return outputs(result, tokens_grad, sums, small_out)


def solution(mesh):
    return jax.shard_map(
        functools.partial(body, mesh.shape["dp"]),
        mesh=mesh,
        in_specs=(
            P("dp", "seq", None),
            P("dp", None),
            P("dp"),
            P("dp"),
            P("dp", None),
            P("dp"),
            P("dp", None),
            P("dp"),
            P("dp"),
            P("dp"),
            P("dp", None),
            P("dp"),
            P("dp", None),
            P("dp"),
            P("dp", "seq", None),
        ),
        out_specs=(
            P("dp", "seq", None),
            P("dp", "seq", None),
            P("dp"),
            P("dp"),
            P("dp", None),
            P("dp"),
            P("dp", None),
            P("dp"),
            P("dp"),
            P("dp"),
            P("dp", None),
            P("dp"),
            P("dp", None),
            P("dp"),
        ),
        check_vma=False,
    )
```

```python
import functools

import jax
import jax.numpy as jnp
from jax import lax
from jax.experimental import pallas as pl
from jax.experimental.pallas import tpu as pltpu
from jax.sharding import PartitionSpec as P

H = 12
HD = 64

EPSILON = 1e-05
NEG_FILL = -1e30
MESH = pl.DeviceIdType.MESH
MIB = 1024 * 1024
BF16 = jnp.bfloat16
F32 = jnp.float32


def layer_norm(values, norm_gain, norm_shift):
    center = values - jnp.mean(values, axis=-1, keepdims=True)
    spread = jnp.mean(center * center, axis=-1, keepdims=True)
    return center * lax.rsqrt(spread + EPSILON) * norm_gain + norm_shift


def gelu_tanh(values):
    inside = 0.7978845608028654 * (values + 0.044715 * values * values * values)
    return 0.5 * values * (1.0 + jnp.tanh(inside))


def product(operand, other):
    return jnp.dot(operand, other, preferred_element_type=F32)


def product_across(operand, other):
    return lax.dot_general(operand, other, (((0,), (0,)), ((), ())), preferred_element_type=F32)


def product_back(operand, other):
    return lax.dot_general(operand, other, (((1,), (1,)), ((), ())), preferred_element_type=F32)


def own_place():
    d, s = lax.axis_index("dp"), lax.axis_index("seq")
    return d, s, d // 2, d % 2, s // 2, s % 2


def flip(index, step):
    return index + step * (1 - 2 * ((index // step) % 2))


def remote(src, dst, send, recv, d, s):
    return pltpu.make_async_remote_copy(
        src_ref=src, dst_ref=dst, send_sem=send, recv_sem=recv, device_id=(d, s), device_id_type=MESH
    )


def turned(offset):
    d, s = lax.axis_index("dp"), lax.axis_index("seq")
    for bit in (1, 2):
        s = flip(s, bit) if offset & bit else s
    return (flip(d, 1) if offset & 4 else d), s


def along(depth, offset):
    d, s = lax.axis_index("dp"), lax.axis_index("seq")
    for k in range(depth.bit_length() - 1):
        d = flip(d, 2 << k) if offset >> k & 1 else d
    return d, s


def greet(depth, around):
    barrier = pltpu.get_barrier_semaphore()
    partners = [turned(offset) for offset in around] + [along(depth, offset) for offset in range(1, depth)]
    for partner in partners:
        pl.semaphore_signal(barrier, inc=1, device_id=partner, device_id_type=MESH)
    pl.semaphore_wait(barrier, len(partners))


def doubling_steps(count):
    return [1 << k for k in range(count.bit_length() - 1)]


class Plan:
    def __init__(self):
        self.steps = []

    def add(self, at, action, *args):
        self.steps.append((at, len(self.steps), action, args))

    def run(self):
        for _, _, action, args in sorted(self.steps, key=lambda step: step[:2]):
            action(*args)


def small_rows(sizes):
    firsts, at = [], 0
    for size in sizes:
        firsts.append(at)
        at += -(-size // 128)
    return firsts, at


def join_rows(pieces):
    lane = lax.broadcasted_iota(jnp.int32, (1, 128), 1)
    blocks = []
    for b in range(sum(n for _, n in pieces) // 128):
        block, start = jnp.zeros((1, 128), F32), -128 * b
        for piece, n in pieces:
            if start < 128 and start + n > 0:
                turned = piece if start % 128 == 0 else pltpu.roll(piece, start % 128, 1)
                block = jnp.where((lane >= start) & (lane < start + n), turned, block)
            start += n
        blocks.append(block)
    return jnp.concatenate(blocks, axis=1)


def small_vector(ref, sizes, index, shards):
    first, size = small_rows(sizes)[0][index], sizes[index]
    return join_rows(
        [
            (ref[pl.ds(at * 16 + first + k, 1), :].astype(BF16).astype(F32), min(128, size - 128 * k))
            for at in shards
            for k in range(-(-size // 128))
        ]
    )


class Links:
    def __init__(self, **free):
        self.free = free

    def send(self, link, ready, micros):
        start = max(ready, self.free[link])
        self.free[link] = start + micros
        return start, start + micros + 1.5


def spread_kernel(dp, kinds, rows, edges, groups, quarter, sizes, *refs):
    count = len(rows)
    depth, half = dp // 2, dp // 2
    shard, vectors = refs[:count], refs[count : count + len(sizes)]
    at_ref = count + len(sizes)
    tokens, upstream, lengths = refs[at_ref : at_ref + 3]
    at_ref += 3
    weights_out = refs[at_ref : at_ref + count]
    at_ref += count
    (
        small_full, row, seed, normed_out, triple_out, probs_out, mixed_out, hat_out, rdev_out, base_out, second_out,
        act_out, slope_out, grad_out,
    ) = refs[at_ref : at_ref + 14]
    at_ref += 14
    wide, gathered = refs[at_ref : at_ref + count], refs[at_ref + count : at_ref + 2 * count]
    (
        row_v, seed_v, normed, triple, probs, mixed, hat, rdev, base, second, act, slope, grad,
        load, local, up_s, down_s, z_r, y_s, y_r, x_s, x_r, ca_s, cb_s, ca_r, cb_r, small_s, small_r, tok_l, tok_s, tok_r,
        weight_l, row_l, out_l, probs_l, mixed_s, mixed_r,
    ) = refs[at_ref + 2 * count :]
    low = gathered[3]
    full = [*gathered[:3], weights_out[3]]
    d, s, z, y, x, c = own_place()
    steps = doubling_steps(dp)

    def tile(i, n=quarter):
        return slice(i * n, (i + 1) * n)

    def when(condition, action):
        if condition is True:
            action()
        else:
            pl.when(condition)(action)

    def active(a, at):
        return True if kinds[a] != "shards" else at // half == c

    def pieces(a):
        if kinds[a] != "cols":
            return [(slice(None), slice(None))]
        n = wide[a].shape[1]
        if a:
            return [(pl.ds(pl.multiple_of(c * n, 128), n), slice(None))]
        n, wide_pair = n // 3, 2 * HD
        return [
            (pl.ds(pl.multiple_of((2 * t + c) * n + wide_pair * p, 128), wide_pair), tile(3 * p + t, wide_pair))
            for p in range(n // wide_pair)
            for t in range(3)
        ]

    def fetches(a):
        return [
            pltpu.make_async_copy(shard[a].at[:, source], wide[a].at[:, target], load.at[a, t])
            for t, (source, target) in enumerate(pieces(a))
        ]

    for a in range(count):

        def fetch():
            for copy in fetches(a):
                copy.start()

        when(active(a, d), fetch)

    greet(depth, (1, 2, 4))

    def columns(g):
        a, part, parts = groups[g]
        n = full[a].shape[1] // parts
        if kinds[a] == "share":
            return pl.ds(pl.multiple_of(c * (n // 2), 128), n // 2)
        return tile(part, n)

    def window(g, at, offset, n):
        a = groups[g][0]
        place = at if kinds[a] != "shards" else at % half
        return full[a].at[pl.ds(pl.multiple_of(place * rows[a] + offset, 16), n), columns(g)]

    def body_rows(g):
        a = groups[g][0]
        return x * edges[a], rows[a] - edges[a]

    def edge_rows(g, plane):
        a = groups[g][0]
        return plane * (rows[a] - edges[a]), edges[a]

    def own_piece(g):
        if kinds[groups[g][0]] != "shards":
            return window(g, d, *body_rows(g))
        first, n = body_rows(g)
        return low.at[pl.ds(pl.multiple_of(first, 16), n), columns(g)]

    def up(g, at, own=False):
        view = window(g, at, *body_rows(g))
        return remote(own_piece(g) if own else view, view, up_s.at[g, at], z_r.at[g, at], d + 2, s)

    def down(g, at, own=False):
        view = window(g, at, *body_rows(g))
        return remote(own_piece(g) if own else view, view, down_s.at[g, at], z_r.at[g, at], d - 2, s)

    def over_y(g, at, own=False):
        view = window(g, at, *body_rows(g))
        source = own_piece(g) if own else view
        return remote(source, view, y_s.at[g, at], y_r.at[g, at], flip(d, 1), s)

    def over_x(g, at, plane):
        view = window(g, at, *edge_rows(g, plane))
        return remote(view, view, x_s.at[g, at], x_r.at[g, at], d, flip(s, 2))

    def core_a(g, at):
        view = window(g, at, *body_rows(g))
        return remote(view, view, ca_s.at[at], ca_r.at[at], d, flip(s, 1))

    def core_b(g, at):
        view = window(g, at, *edge_rows(g, 1 - x))
        return remote(view, view, cb_s.at[at], cb_r.at[at], d, flip(s, 1))

    def small_copy(k):
        size = 16 << k
        view = small_full.at[pl.ds(pl.multiple_of((d // (1 << k)) * size, 16), size), :]
        return remote(view, view, small_s.at[k], small_r.at[k], flip(d, 1 << k), s)

    own_shrink = pltpu.make_async_copy(
        low, full[3].at[pl.ds(pl.multiple_of((d % half) * rows[3], 16), rows[3]), :], local.at[0]
    )

    def spot(array, index):
        return array.at[pl.ds(pl.multiple_of(index * quarter, 16), quarter), :]

    def row_copies(t, source, target):
        mine, theirs = spot(target, 2 * x + c), spot(target, 2 * (1 - x) + c)
        return (
            pltpu.make_async_copy(source.at[x], mine, tok_l.at[t]),
            remote(source.at[1 - x], mine, tok_s.at[t, 0], tok_r.at[t, 0], d, flip(s, 2)),
            remote(source.at[x], mine, tok_s.at[t, 1], tok_r.at[t, 1], d, flip(s, 1)),
            remote(theirs, theirs, tok_s.at[t, 2], tok_r.at[t, 2], d, flip(s, 1)),
        )

    moves = [row_copies(0, tokens, row), row_copies(1, upstream, seed)]
    row_loads = [pltpu.make_async_copy(row, row_v, row_l.at[0]), pltpu.make_async_copy(seed, seed_v, row_l.at[1])]

    small_full[pl.ds(pl.multiple_of(d * 16, 16), 16), :] = jnp.zeros((16, 128), F32)
    for ref, size, first_row in zip(vectors, sizes, small_rows(sizes)[0]):
        for k in range(-(-size // 128)):
            n = min(128, size - 128 * k)
            small_full[pl.ds(d * 16 + first_row + k, 1), 0:n] = ref[128 * k : 128 * k + n].reshape(1, n)

    def row_begin(t):
        for copy in moves[t][:3]:
            copy.start()

    def row_pass(t):
        moves[t][1].wait_recv()
        moves[t][3].start()

    def row_ready(t):
        own, _, to_core, passed = moves[t]
        own.wait()
        to_core.wait_recv()
        passed.wait_recv()
        row_loads[t].start()

    def cast(a):
        for copy in fetches(a):
            copy.wait()
        if kinds[a] == "shards":
            low[...] = wide[a][...].astype(BF16)
            own_shrink.start()
        else:
            full[a][pl.ds(pl.multiple_of(d * rows[a], 16), rows[a]), :] = wide[a][...].astype(BF16)

    def begin(g):
        pl.when(z < depth - 1)(lambda: up(g, d, True).start())
        pl.when(z > 0)(lambda: down(g, d, True).start())
        over_y(g, d, True).start()

    def small_step(k):
        if k:
            small_copy(k - 1).wait()
        if k < len(steps):
            small_copy(k).start()

    def around(g, hops, base, action):
        a = groups[g][0]
        if hops == 0:
            when(active(a, base), lambda: action(base))
        else:
            pl.when((z >= hops) & active(a, base - 2 * hops))(lambda: action(base - 2 * hops))
            pl.when((z + hops < depth) & active(a, base + 2 * hops))(lambda: action(base + 2 * hops))

    def zs(g, hops, action):
        around(g, hops, d, action)

    def ys(g, hops, action):
        around(g, hops, flip(d, 1), action)

    def share(g, copy, at):
        if kinds[groups[g][0]] == "share":
            copy(g, at).start()

    def z_arrival(g, hops):
        def action(at):
            up(g, at).wait_recv()
            pl.when((at < d) & (z < depth - 1))(lambda: up(g, at).start())
            pl.when((at > d) & (z > 0))(lambda: down(g, at).start())
            over_y(g, at).start()
            share(g, core_a, at)

        zs(g, hops, action)

    def y_arrival(g, offset):
        def action(at):
            over_y(g, at).wait_recv()
            share(g, core_a, at)

        ys(g, offset, action)

    def x_send(g, offset, which):
        which(g, offset, lambda at: over_x(g, at, x).start())

    def x_arrival(g, offset, which):
        def action(at):
            over_x(g, at, 1 - x).wait_recv()
            share(g, core_b, at)

        which(g, offset, action)


    width, pairs = row.shape[1], triple.shape[1] // (6 * HD)
    half_width = width // 2
    triple_w, attend_w, expand_w = full[:3]
    total = lengths[x, 0] + lengths[x, 1]

    def vector(index, shards=range(dp)):
        return small_vector(small_full, sizes, index, shards)

    weight_copies = [pltpu.make_async_copy(full[a], weights_out[a], weight_l.at[a]) for a in range(3)]

    def weight_ready(a):
        if kinds[a] == "share":
            g = [group[0] for group in groups].index(a)

            def passed_on(at):
                core_a(g, at).wait_recv()
                core_b(g, at).wait_recv()

            for offset in range(depth):
                if offset:
                    zs(g, offset, passed_on)
                ys(g, offset, passed_on)
        weight_copies[a].start()

    def norm_tile(i):
        if i == 0:
            row_loads[0].wait()
        values = row_v[tile(i)].astype(F32)
        center = values - jnp.mean(values, axis=-1, keepdims=True)
        r = lax.rsqrt(jnp.mean(center * center, axis=-1, keepdims=True) + EPSILON)
        normed[tile(i)] = (center * r * vector(0) + vector(1)).astype(BF16)

    def triple_tile(i):
        n = half_width // sizes[2]
        ends = [vector(2, [first + c * n + k for k in range(n)]) for first in (0, dp // 2)]
        wide_pair = 2 * HD
        bias = jnp.concatenate(
            [
                part[:, tile(p, wide_pair)]
                for p in range(pairs)
                for part in (ends[0], jnp.zeros((1, half_width), F32), ends[1])
            ],
            axis=1,
        )
        triple[tile(i)] = (product(normed[tile(i)], triple_w[...]) + bias).astype(BF16)

    def probs_copy(p):
        return pltpu.make_async_copy(probs.at[p % 2], probs_out.at[p], probs_l.at[p % 2])

    def mixed_window(p, core):
        return pl.ds(pl.multiple_of(core * half_width + 2 * HD * p, 2 * HD), 2 * HD)

    def mixed_copy(p):
        view = mixed.at[:, mixed_window(p, c)]
        return remote(view, view, mixed_s.at[p], mixed_r.at[p], d, flip(s, 1))

    def attend_part(p, part, head):
        if p > 1 and part == 0 and head == 0:
            probs_copy(p - 2).wait()
        cut = [tile(3 * p + k, 2 * HD) for k in range(3)]
        values = attend_block(
            head, part, quarter, total, triple[tile(part), cut[0]], triple.at[:, cut[1]], triple.at[:, cut[2]],
            probs.at[p % 2],
        )
        spot_of = (tile(part), mixed_window(p, c))
        mixed[spot_of] = jnp.where(head_mask(), mixed[spot_of], values) if head else values
        if part == 3 and head == 1:
            probs_copy(p).start()
            mixed_copy(p).start()

    outs = (
        (normed, normed_out), (triple, triple_out), (mixed, mixed_out), (hat, hat_out), (rdev, rdev_out), (base, base_out),
        (second, second_out), (act, act_out), (slope, slope_out), (grad, grad_out),
    )
    out_copies = [
        pltpu.make_async_copy(source, target, out_l.at[k]) for k, (source, target) in enumerate(outs)
    ]

    def mixed_ready():
        out_copies[0].start()
        out_copies[1].start()
        for p in range(pairs):
            mixed_copy(p).wait()
        out_copies[2].start()

    def resid_tile(i):
        values = row_v[tile(i)].astype(F32) + product(mixed[tile(i)], attend_w[...]) + vector(3)
        center = values - jnp.mean(values, axis=-1, keepdims=True)
        r = lax.rsqrt(jnp.mean(center * center, axis=-1, keepdims=True) + EPSILON)
        hat_of = center * r
        hat[tile(i)] = hat_of.astype(BF16)
        rdev[tile(i)] = jnp.broadcast_to(r, (quarter, 128))
        second[tile(i)] = (hat_of * vector(4) + vector(5)).astype(BF16)

        @pl.when(c == i % 2)
        def _():
            base[i // 2] = values + vector(7)

    def expand_tile(i, k):
        if i == 0 and k == 0:
            for copy in out_copies[3:7]:
                copy.start()
        part = tile(k, 256)
        value = product(second[tile(i)], expand_w[:, part]) + vector(6, [c * half + n for n in range(half)])[:, part]
        square = value * value
        bend = jnp.tanh(0.7978845608028654 * value * (1.0 + 0.044715 * square))
        raised = 0.5 * (1.0 + bend)
        act[tile(i), part] = (value * raised).astype(BF16)
        inner = 0.7978845608028654 + (3 * 0.7978845608028654 * 0.044715) * square
        slope[tile(i), part] = (raised + 0.5 * value * (1.0 - bend * bend) * inner).astype(BF16)

    def shrink_grad(k):
        if k == 0:
            out_copies[7].start()
            out_copies[8].start()
            row_loads[1].wait()
        value = product_across(act[:, tile(k, rows[3])], seed_v[...]).astype(BF16)
        for part in range(2):
            grad[part, k // 2, k % 2] = value[:, tile(part, half_width)]


    plan = Plan()
    links = Links(z=0.0, y=0.0, x=8.0)
    for k in range(len(steps) + 1):
        plan.add(2.5 * k, small_step, k)
    plan.add(-1.0, row_begin, 0)
    plan.add(9.5, row_pass, 0)
    plan.add(12.0, row_ready, 0)
    ready = [0.0] * count
    begins = y_done = 0.0
    for g, (a, part, parts) in enumerate(groups):
        rate = 90e3 if kinds[a] == "shards" else 45e3
        n = full[a].shape[1] // parts // (2 if kinds[a] == "share" else 1)
        body, edge = [2 * n * m / rate for m in (rows[a] - edges[a], edges[a])]
        if part == 0:
            plan.add(begins - 0.1, when, active(a, d), functools.partial(cast, a))
        plan.add(begins, when, active(a, d), functools.partial(begin, g))
        x_queue = []
        for offset in range(depth):
            if offset:
                _, arrival = links.send("z", arrival, body)
                plan.add(arrival, z_arrival, g, offset)
                x_queue.append((arrival + 0.1, offset, zs))
            else:
                arrival = begins
            _, over = links.send("y", arrival, body)
            plan.add(over + 0.3, y_arrival, g, offset)
            x_queue.append((over + 0.4, offset, ys))
        for at, offset, which in sorted(x_queue, key=lambda entry: entry[0]):
            _, arrival = links.send("x", at, edge)
            plan.add(at, x_send, g, offset, which)
            plan.add(arrival + 0.5, x_arrival, g, offset, which)
            ready[a] = max(ready[a], arrival + 0.6)
        y_done += body * depth
        begins = max(begins + 0.5, y_done - 10.0)
    for a in range(3):
        ready[a] += 2.0 if kinds[a] == "share" else 0.0
        plan.add(ready[a], weight_ready, a)
    upstream_at = ready[0] + 2.0
    plan.add(upstream_at, row_begin, 1)
    plan.add(upstream_at + 14.0, row_pass, 1)
    plan.add(upstream_at + 18.0, row_ready, 1)

    clock = [13.0]

    def compute(micros, action, *args):
        plan.add(clock[0], action, *args)
        clock[0] += micros

    for i in range(4):
        compute(1.2, norm_tile, i)
    clock[0] = max(clock[0], ready[0] + 0.1)
    for i in range(4):
        compute(1.0, triple_tile, i)
    for p in range(pairs):
        for part in range(4):
            for head in range(2):
                compute(0.2 * (part + 1), attend_part, p, part, head)
    clock[0] = max(clock[0] + 2.0, ready[1] + 0.1)
    compute(0.0, mixed_ready)
    for i in range(4):
        compute(1.6, resid_tile, i)
    clock[0] = max(clock[0], ready[2] + 0.1)
    for i in range(4):
        for k in range(expand_w.shape[1] // 256):
            compute(0.35, expand_tile, i, k)
    clock[0] = max(clock[0], upstream_at + 18.5)
    for k in range(act.shape[1] // rows[3]):
        compute(1.0, shrink_grad, k)
    plan.run()

    out_copies[9].start()
    for copy in out_copies + weight_copies:
        copy.wait()
    for p in range(max(pairs - 2, 0), pairs):
        probs_copy(p).wait()
    for move_of in moves:
        for copy in move_of[1:]:
            copy.wait_send()
    pl.when(active(3, d))(lambda: own_shrink.wait())

    for g in range(len(groups)):

        def sent():
            pl.when(z < depth - 1)(lambda: up(g, d, True).wait_send())
            pl.when(z > 0)(lambda: down(g, d, True).wait_send())
            over_y(g, d, True).wait_send()

        when(active(groups[g][0], d), sent)

        def passed(at, own_column):
            if own_column:
                over_y(g, at).wait_send()
                pl.when((at < d) & (z < depth - 1))(lambda: up(g, at).wait_send())
                pl.when((at > d) & (z > 0))(lambda: down(g, at).wait_send())
            over_x(g, at, x).wait_send()
            if kinds[groups[g][0]] == "share":
                core_a(g, at).wait_send()
                core_b(g, at).wait_send()

        for offset in range(depth):
            if offset:
                zs(g, offset, functools.partial(passed, own_column=True))
            ys(g, offset, functools.partial(passed, own_column=False))


def spread(dp, shards, vectors, tokens, upstream, lengths):
    kinds = ["cols", "share", "cols", "shards"]
    groups = [(0, 0, 1), (1, 0, 1), (2, 0, 2), (2, 1, 2), (3, 0, 2), (3, 1, 2)]
    rows = [member.shape[0] for member in shards]
    edges = [m // 6 if kind == "shards" else m // 3 for m, kind in zip(rows, kinds)]
    count = len(rows)
    quarter, width = tokens.shape[1:]
    length = 4 * quarter
    dma = pltpu.SemaphoreType.DMA
    any_space = pl.BlockSpec(memory_space=pl.ANY)
    vmem = pl.BlockSpec(memory_space=pltpu.VMEM)
    held = [(m.shape[0], m.shape[1] // 2 if kind == "cols" else m.shape[1]) for m, kind in zip(shards, kinds)]
    whole = [(dp * r // 2 if kind == "shards" else dp * r, n) for (r, n), kind in zip(held, kinds)]
    kept = part_start(4, quarter)
    pairs = width // (4 * HD)
    hidden = whole[2][1]
    states = [
        ((length, width), BF16), ((length, 3 * width // 2), BF16), ((pairs, 2, kept, quarter), BF16),
        ((length, width), BF16), ((length, width), BF16), ((length, 128), F32), ((2, quarter, width), F32),
        ((length, width), BF16), ((length, hidden), BF16), ((length, hidden), BF16),
        ((2, dp // 4, 2, rows[3], width // 2), BF16),
    ]
    slots = [(shape if k != 2 else (2, *shape[1:]), kind) for k, (shape, kind) in enumerate(states)]
    return pl.pallas_call(
        functools.partial(spread_kernel, dp, kinds, rows, edges, groups, quarter, [v.shape[0] for v in vectors]),
        out_shape=[jax.ShapeDtypeStruct(shape, BF16) for shape in whole]
        + [jax.ShapeDtypeStruct((dp * 16, 128), F32)]
        + [jax.ShapeDtypeStruct((length, width), BF16)] * 2
        + [jax.ShapeDtypeStruct(*state) for state in states],
        in_specs=[any_space] * count
        + [vmem] * len(vectors)
        + [any_space] * 2
        + [pl.BlockSpec(memory_space=pltpu.SMEM)],
        out_specs=[any_space] * count + [vmem] + [any_space] * (2 + len(states)),
        scratch_shapes=[pltpu.VMEM(shape, F32) for shape in held]
        + [pltpu.VMEM(shape, BF16) for shape in [*whole[:3], held[3]]]
        + [pltpu.VMEM((length, width), BF16)] * 2
        + [pltpu.VMEM(*slot) for slot in slots]
        + [dma((count, 3 * pairs)), dma((1,))]
        + [dma((len(groups), dp))] * 7
        + [dma((dp,))] * 4
        + [dma((len(doubling_steps(dp)),))] * 2
        + [dma((2,)), dma((2, 3)), dma((2, 3))]
        + [dma((3,)), dma((2,)), dma((len(states) - 1,)), dma((2,)), dma((pairs,)), dma((pairs,))],
        compiler_params=pltpu.CompilerParams(
            collective_id=1, has_side_effects=True, vmem_limit_bytes=60 * MIB
        ),
        name="spread_weights",
    )(*shards, *vectors, tokens, upstream, lengths)


ATTEND_ROW, SECOND_ROW, EXPAND_ROW, SHRINK_ROW = (0, 0), (0, 1), 3, (0, 7)
FIRST_ROW, TRIPLE_ROW = (1, 0), (1, 2)


def back_kernel(dp, kinds, rows, edges, quarter, sizes, *refs):
    count = len(rows)
    depth, half = dp // 2, dp // 2
    (
        triple_w_in, attend_in, expand_in, shrink_in, small_full, row_in, seed_in, normed_in, triple_in, probs_in, mixed_in,
        hat_in, rdev_in, base_in, second_in, act_in, slope_in, grad_in,
    ) = refs[:18]
    outs, (small_sum, result_out, tokens_out) = refs[18 : 18 + count], refs[18 + count : 21 + count]
    at_ref = 21 + count
    acc, x_buf, y_buf, up_buf, down_buf, b_buf = [refs[at_ref + k * count : at_ref + (k + 1) * count] for k in range(6)]
    z_buf = refs[at_ref + 6 * count]
    at_ref += 1
    (
        act, slope, seed, shrink_w, second, expand_w, partial, other, rdev, base, mixed, attend_w, grad_own, grad_mixed,
        probs, dkeys, dvalues, row_own, send_own, sum_recv, n_recv, stage, ring_buf, line_buf,
        load, probs_l, x_s, x_r, y_s, y_r, u_s, u_r, n_s, n_r, z_s, z_r, f_s, f_r, small_s, small_r,
        part_s, part_r, sum_s, sum_r, one_s, one_r, give_s, give_r,
    ) = refs[at_ref + 6 * count :]
    d, s, z, y, x, c = own_place()
    twin = flip(s, 1)
    length, width = seed.shape
    hidden, half_width = act.shape[1], width // 2
    pairs = half_width // (2 * HD)
    normed, grad_pre, branch = second, slope, partial
    triple = slope.at[:, pl.ds(0, 3 * half_width)]
    grad_triple = act.at[:, pl.ds(0, 3 * half_width)]
    triple_w = expand_w.at[:, pl.ds(0, 3 * half_width)]
    hat = shrink_w.at[pl.ds(0, length), :]

    sources = [
        (grad_in.at[0], acc[0]), (grad_in.at[1], acc[1]), (seed_in, seed), (shrink_in, shrink_w), (slope_in, slope),
        (expand_in, expand_w), (act_in, act), (second_in, second), (base_in, base), (rdev_in, rdev), (mixed_in, mixed),
        (attend_in, attend_w), (hat_in, hat), (normed_in, normed), (triple_in, triple), (triple_w_in, triple_w),
    ]
    (
        grad_l0, grad_l1, seed_l, shrink_l, slope_l, expand_l, act_l, second_l, base_l, rdev_l, mixed_l, attend_l, hat_l,
        normed_l, triple_l, triple_w_l,
    ) = range(len(sources))
    loads = [pltpu.make_async_copy(source, target, load.at[k]) for k, (source, target) in enumerate(sources)]
    row_loads = [
        pltpu.make_async_copy(
            row_in.at[pl.ds(pl.multiple_of((2 * h + c) * quarter, 16), quarter), :], row_own.at[h], load.at[len(sources) + h]
        )
        for h in range(2)
    ]

    def probs_load(k):
        return pltpu.make_async_copy(probs_in.at[k // 2, k % 2], probs.at[k % 2], probs_l.at[k % 2])

    for copy in loads[:hat_l]:
        copy.start()
    for copy in row_loads:
        copy.start()
    probs_load(0).start()
    probs_load(1).start()

    ring, line = range(1, 8), range(1, depth)
    greet(depth, ring)

    small_sum[...] = jnp.zeros_like(small_sum)


    def first_layer(g):
        return 0 if kinds[g] != "shards" else c * (depth // 2)

    def body(g):
        return pl.ds(pl.multiple_of(x * edges[g], 16), rows[g] - edges[g])

    def edge(g, plane):
        return pl.ds(pl.multiple_of(plane * (rows[g] - edges[g]), 16), edges[g])

    def middle(g):
        return pl.ds(edges[g], rows[g] - 2 * edges[g])

    def add(g, window, extra):
        acc[g][window] = acc[g][window] + extra

    def over_x(g, own):
        column = y if own else 1 - y

        return remote(
            acc[g].at[:, column, edge(g, 1 - x), :], x_buf[g].at[:, column],
            x_s.at[g, int(own)], x_r.at[g, int(own)], d, flip(s, 2),
        )

    def over_y(g):
        return remote(acc[g].at[:, 1 - y, body(g), :], y_buf[g], y_s.at[g], y_r.at[g], flip(d, 1), s)

    def straight(g):
        return g == count - 1

    def over_z(g, offset):
        to = along(depth, offset)
        source = acc[g].at[to[0] // 2, y, body(g), :]
        return remote(source, z_buf.at[offset - 1], z_s.at[offset - 1], z_r.at[offset - 1], *to)

    def along_z(g, upward, hop, layers):
        first = layers[0] if kinds[g] != "shards" else layers[0] % (depth // 2)
        places = slice(first, first + len(layers))
        source = acc[g].at[places, y, body(g), :]
        if upward:
            return remote(source, up_buf[g].at[places], u_s.at[g, hop], u_r.at[g, hop], d + 2, s), places
        return remote(source, down_buf[g].at[places], n_s.at[g, hop], n_r.at[g, hop], d - 2, s), places

    def hop_cases(g, hop):
        cases = []
        for core in range(2) if kinds[g] == "shards" else (None,):
            whole = range(depth) if core is None else range(core * (depth // 2), (core + 1) * (depth // 2))
            mine = True if core is None else c == core
            got, sent = [k for k in whole if k >= hop > 0], [k for k in whole if k > hop]
            cases.append(((z == hop) & mine, True, got, sent))
            got, sent = [k for k in whole if k < depth - hop and hop], [k for k in whole if k < depth - 1 - hop]
            cases.append(((z == depth - 1 - hop) & mine, False, got, sent))
        return [case for case in cases if case[2] or case[3]]

    def stage_a(g, own):
        if g < 2 and not own:
            loads[(grad_l0, grad_l1)[g]].wait()
        over_x(g, own).start()

    def stage_c(g, own):
        over_x(g, own).wait_recv()
        column = y if own else 1 - y
        add(g, (slice(None), column, edge(g, x), slice(None)), x_buf[g][:, column])
        if not own:
            over_y(g).start()

    def stage_d(g):
        over_y(g).wait_recv()
        add(g, (slice(None), y, body(g), slice(None)), y_buf[g][...])

    def stage_e(g, hop):
        if straight(g):
            for offset in line if hop == 0 else ():
                over_z(g, offset).start()
            return
        for condition, upward, got, sent in hop_cases(g, hop):

            def run():
                if got:
                    copy, places = along_z(g, upward, hop - 1, got)
                    copy.wait_recv()
                    add(g, (places, y, body(g), slice(None)), (up_buf if upward else down_buf)[g][places])
                if sent:
                    along_z(g, upward, hop, sent)[0].start()

            pl.when(condition)(run)

    def drain_e(g, hop):
        if straight(g):
            for offset in line if hop == 0 else ():
                over_z(g, offset).wait_send()
            return
        for condition, upward, _, sent in hop_cases(g, hop):
            if sent:
                pl.when(condition)(lambda: along_z(g, upward, hop, sent)[0].wait_send())

    def own_layer(g):
        return z - first_layer(g)

    def ours(g, action):
        if kinds[g] != "shards":
            action()
        else:
            pl.when((z >= first_layer(g)) & (z < first_layer(g) + depth // 2))(action)

    def out_rows(g, window):
        return outs[g].at[c, window, :] if kinds[g] != "shards" else outs[g].at[window, :]

    def final_share(g):
        source = acc[g].at[own_layer(g), y, edge(g, x), :]
        return remote(source, out_rows(g, edge(g, x)), f_s.at[g, 0], f_r.at[g, 0], d, flip(s, 2))

    def final_swap(g):
        source = acc[g].at[own_layer(g), y, middle(g), :]
        return remote(source, b_buf[g], f_s.at[g, 1], f_r.at[g, 1], d, flip(s, 2))

    def final_core(g):
        view = out_rows(g, pl.ds(0, rows[g]))
        return remote(view, view, f_s.at[g, 2], f_r.at[g, 2], d, twin)

    def finish_one(g):
        def run():
            if straight(g):
                for offset in line:
                    over_z(g, offset).wait_recv()
                window = (own_layer(g), y, body(g), slice(None))
                total = acc[g][window].astype(F32)
                for offset in line:
                    total = total + z_buf[offset - 1].astype(F32)
                acc[g][window] = total.astype(BF16)
            final_share(g).start()
            final_swap(g).start()
            out_rows(g, edge(g, x))[...] = acc[g][own_layer(g), y, edge(g, x), :]

        ours(g, run)

    def finish_two(g):
        def run():
            final_swap(g).wait_recv()
            out_rows(g, middle(g))[...] = acc[g][own_layer(g), y, middle(g), :] + b_buf[g][...]
            final_share(g).wait_recv()
            final_core(g).start()

        ours(g, run)

    ring_place = y * 4 + s

    def ring_copy(t, offset):
        target = turned(offset)
        return remote(
            ring_buf.at[t, ring_place], ring_buf.at[t, ring_place], small_s.at[t, offset], small_r.at[t, offset], *target
        )

    def line_copy(t, offset):
        target = along(depth, offset)
        return remote(
            line_buf.at[t, z], line_buf.at[t, z], small_s.at[t, 7 + offset], small_r.at[t, 7 + offset], *target
        )

    def small_begin(t):
        ring_buf[t, ring_place] = small_sum[t]
        for offset in ring:
            ring_copy(t, offset).start()

    def small_pass(t):
        for offset in ring:
            ring_copy(t, offset).wait()
        total = ring_buf[t, 0]
        for k in range(1, 8):
            total = total + ring_buf[t, k]
        line_buf[t, z] = total
        for offset in line:
            line_copy(t, offset).start()

    def small_end(t):
        for offset in line:
            line_copy(t, offset).wait()
        total = line_buf[t, 0]
        for k in line:
            total = total + line_buf[t, k]
        small_sum[t] = total


    def tile(i, n=quarter):
        return slice(i * n, (i + 1) * n)

    def own_tile(h):
        return pl.ds(pl.multiple_of((2 * h + c) * quarter, 16), quarter)

    def twin_tile(h):
        return pl.ds(pl.multiple_of((2 * h + 1 - c) * quarter, 16), quarter)

    def vector(index):
        return small_vector(small_full, sizes, index, range(dp))

    def sums(row_at, values, columns=slice(None)):
        block, at = row_at
        small_sum[block, at : at + 1, columns] += jnp.sum(values, axis=0, keepdims=True)

    def sum_copy(h):
        return remote(send_own.at[h], sum_recv.at[h], sum_s.at[h], sum_r.at[h], d, twin)

    def result_own(h):
        if h == 0:
            loads[base_l].wait()
        base[h] = base[h] + product(act[own_tile(h), :], shrink_w[...])

    def result_end(h):
        sum_copy(h).wait_recv()
        stage[h] = (base[h] + sum_recv[h].astype(F32)).astype(BF16)

    def result_partial(h):
        if h == 0:
            loads[act_l].wait()
        send_own[h] = product(act[twin_tile(h), :], shrink_w[...]).astype(BF16)
        sum_copy(h).start()

    def grad_pre_tile(i):
        if i == 0:
            for k in (seed_l, shrink_l, slope_l):
                loads[k].wait()
        for k in range(hidden // 256):
            columns = tile(k, 256)
            value = product_back(seed[tile(i)], shrink_w[columns, :]) * slope[tile(i), columns].astype(F32)
            low_value = value.astype(BF16)
            grad_pre[tile(i), columns] = low_value
            total = jnp.sum(low_value.astype(F32), axis=0, keepdims=True)
            spot = (
                0, pl.ds(EXPAND_ROW + (hidden // width) * c + k * 256 // width, 1),
                slice(k * 256 % width, k * 256 % width + 256),
            )
            small_sum[spot] = small_sum[spot] + total
        sums(SHRINK_ROW, 0.5 * seed[tile(i)].astype(F32))

    def part_copy(i):
        return remote(partial.at[tile(i)], other.at[tile(i)], part_s.at[i], part_r.at[i], d, twin)

    def n_two_tile(i):
        if i == 0:
            loads[expand_l].wait()
        partial[tile(i)] = product_back(grad_pre[tile(i)], expand_w[...]).astype(BF16)
        part_copy(i).start()

    shard_rows = rows[2]

    def by_owner(g, k, grad):
        acc[g][k * (depth // 2) : (k + 1) * (depth // 2)] = grad.astype(BF16).reshape(depth // 2, 2, shard_rows, -1)

    def expand_grad(g, k):
        if g == 2 and k == 0:
            loads[second_l].wait()
        by_owner(g, k, product_across(second[:, tile(k, half_width)], grad_pre[:, tile(g - 2, hidden // 2)]))

    def later_loads():
        for copy in loads[normed_l:]:
            copy.start()

    def back_norm(n, hat_of, r, gain, index, scale):
        sums(index, scale * n * hat_of)
        sums((index[0], index[1] + 1), scale * n)
        e = n * gain
        return r * (e - jnp.mean(e, axis=-1, keepdims=True) - hat_of * jnp.mean(e * hat_of, axis=-1, keepdims=True))

    def resid_tile(i):
        if i == 0:
            loads[hat_l].wait()
            loads[rdev_l].wait()
        part_copy(i).wait()
        n = partial[tile(i)].astype(F32) + other[tile(i)].astype(F32)
        grad = back_norm(n, hat[tile(i)].astype(F32), rdev[tile(i), 0:1], vector(4), SECOND_ROW, 0.5)
        grad = seed[tile(i)].astype(F32) + grad
        low_grad = grad.astype(BF16)
        branch[tile(i)] = low_grad
        sums(ATTEND_ROW, 0.5 * low_grad.astype(F32))

        @pl.when(c == i % 2)
        def _():
            grad_own[i // 2] = grad

    def give_copy(t):
        return remote(stage.at[1 - x], (result_out, tokens_out)[t].at[x], give_s.at[t], give_r.at[t], d, flip(s, 2))

    def give_back(t):
        (result_out, tokens_out)[t][x] = stage[x]
        give_copy(t).start()

    def attend_grad(k):
        if k == 0:
            loads[mixed_l].wait()
        columns = pl.ds(pl.multiple_of(c * half_width, 128), half_width)
        by_owner(4, k, product_across(mixed[:, tile(k, half_width)], branch[:, columns]))

    def mixed_tile(i):
        if i == 0:
            loads[attend_l].wait()
        rows_c = pl.ds(pl.multiple_of(c * half_width, 16), half_width)
        grad_mixed[tile(i)] = product_back(branch[tile(i)], attend_w[rows_c, :]).astype(BF16)

    def attend_back_step(k, part):
        p, head = k // 2, k % 2
        if part == 3:
            probs_load(k).wait()
        if k == 0 and part == 3:
            loads[triple_l].wait()
        columns = [tile(3 * p + n, 2 * HD) for n in range(3)]
        grad_query = attend_back_block(
            head, part, quarter, triple[tile(part), columns[0]], triple.at[:, columns[1]], triple.at[:, columns[2]],
            grad_mixed[tile(part), 2 * HD * p : 2 * HD * (p + 1)],
            probs[k % 2, part_start(part, quarter) : part_start(part + 1, quarter)], dkeys, dvalues,
            part == 3 and head == 0,
        )
        if head:
            grad_query = jnp.where(head_mask(), grad_triple[tile(part), columns[0]], grad_query)
            place_q = pl.ds(pl.multiple_of(c * half_width + 2 * HD * p, 128), 2 * HD)
            sums(TRIPLE_ROW, grad_query.astype(F32), place_q)
        grad_triple[tile(part), columns[0]] = grad_query
        if part == 0:
            if k + 2 < 2 * pairs:
                probs_load(k + 2).start()
            if head:
                grad_triple[:, columns[1]] = dkeys[...].astype(BF16)
                low_values = dvalues[...].astype(BF16)
                grad_triple[:, columns[2]] = low_values
                sums((TRIPLE_ROW[0], TRIPLE_ROW[1] + 1), low_values.astype(F32), place_q)

    def triple_grad(p, k):
        if p == 0 and k == 0:
            loads[normed_l].wait()
        columns = tile(p, 6 * HD)
        by_owner(5 + p, k, product_across(normed[:, tile(k, half_width)], grad_triple[:, columns]))

    def one_copy(h):
        return remote(send_own.at[h], n_recv.at[h], one_s.at[h], one_r.at[h], d, twin)

    def n_one_partial(h):
        if h == 0:
            loads[triple_w_l].wait()
        sum_copy(h).wait_send()
        send_own[h] = product_back(grad_triple[twin_tile(h), :], triple_w[...]).astype(BF16)
        one_copy(h).start()

    def first_tile(h):
        if h == 0:
            give_copy(0).wait_send()
        row_loads[h].wait()
        n = product_back(grad_triple[own_tile(h), :], triple_w[...])
        one_copy(h).wait_recv()
        n = n + n_recv[h].astype(F32)
        values = row_own[h].astype(F32)
        center = values - jnp.mean(values, axis=-1, keepdims=True)
        r = lax.rsqrt(jnp.mean(center * center, axis=-1, keepdims=True) + EPSILON)
        grad = grad_own[h] + back_norm(n, center * r, r, vector(0), FIRST_ROW, 1.0)
        stage[h] = grad.astype(BF16)


    plan = Plan()
    clock = [2.0]

    def compute(micros, action, *args):
        plan.add(clock[0], action, *args)
        clock[0] += 1.5 * micros

    made = []

    def group_made():
        made.append(clock[0] - 0.01)

    group_made()
    group_made()
    for i in range(4):
        compute(1.4, grad_pre_tile, i)
    for i in range(4):
        compute(0.9, n_two_tile, i)
    for h in range(2):
        compute(0.8, result_partial, h)
    for h in range(2):
        compute(0.8, result_own, h)
    compute(0.0, loads[hat_l].start)
    for g in (2, 3):
        for k in range(2):
            compute(1.0, expand_grad, g, k)
        group_made()
    compute(0.0, later_loads)
    for i in range(4):
        compute(2.0, resid_tile, i)
    for k in range(2):
        compute(0.6, attend_grad, k)
    group_made()
    for i in range(4):
        compute(0.3, mixed_tile, i)
    for h in range(2):
        compute(0.3, result_end, h)
    compute(0.2, give_back, 0)
    plan.add(clock[0], small_begin, 0)
    plan.add(clock[0] + 4.0, small_pass, 0)
    plan.add(clock[0] + 8.0, small_end, 0)
    for k in range(2 * pairs):
        for part in reversed(range(4)):
            compute(0.25 * (part + 1), attend_back_step, k, part)
        if k % 2:
            for n in range(2):
                compute(0.5, triple_grad, k // 2, n)
            group_made()
    for h in range(2):
        compute(0.6, n_one_partial, h)
    compute(1.0, lambda: None)
    for h in range(2):
        compute(1.8, first_tile, h)
    compute(0.2, give_back, 1)
    compute(3.0, small_begin, 1)
    compute(3.0, small_pass, 1)
    compute(0.1, small_end, 1)

    links = Links(x=0.0, y=0.0, z=0.0)
    before = [0.0]
    for g in range(count):
        layers, _, _, columns = acc[g].shape
        unit = layers * columns * 2 / 40e3
        slack = 8.0 if g < count - 1 else 0.0
        kept = rows[g] - edges[g]
        for own in (False, True):
            start, arrival = links.send("x", made[g], edges[g] * unit)
            plan.add(max(before[-1], made[g]), stage_a, g, own)
            before.append(start)
            plan.add(arrival, stage_c, g, own)
            if not own:
                _, over = links.send("y", arrival, kept * unit)
        at = max(arrival, over) + 0.5 + 0.2 * slack
        plan.add(at, stage_d, g)
        piece = kept * unit / layers
        if straight(g):
            plan.add(at + 0.1, stage_e, g, 0)
            _, at = links.send("z", at + 0.1, kept * unit)
        else:
            for hop in range(depth):
                plan.add(at + 0.1, stage_e, g, hop)
                if hop < depth - 1:
                    _, at = links.send("z", at + 0.1, piece * (depth - 1 - hop) * layers / depth)
                    at += 0.1 * slack
        plan.add(at + 0.5 + slack, finish_one, g)
        plan.add(at + 0.5 + kept * unit / layers + 1.5 + 2 * slack, finish_two, g)
    plan.run()

    for g in range(count):

        def drain():
            final_share(g).wait_send()
            final_swap(g).wait_send()
            if kinds[g] == "shards":
                final_core(g).wait_send()

        ours(g, drain)
        if kinds[g] == "shards":
            away = (z < first_layer(g)) | (z >= first_layer(g) + depth // 2)
            pl.when(away)(lambda: final_core(g).wait_recv())
        else:
            final_core(g).wait()
        over_x(g, False).wait_send()
        over_x(g, True).wait_send()
        over_y(g).wait_send()
        for hop in range(depth):
            drain_e(g, hop)
    for h in range(2):
        one_copy(h).wait_send()
    give_copy(0).wait_recv()
    give_copy(1).wait()


def back(dp, sizes, *kept):
    _, attend_w, expand_w, shrink_w, _, row, _, _, _, probs, _, _, rdev, base, _, act, _, _ = kept
    length, width = row.shape
    quarter, hidden = length // 4, act.shape[1]
    pairs = width // (4 * HD)
    kinds = ["shards"] * 2 + ["cols"] * (3 + pairs)
    shapes = [(hidden, width // 2)] * 2 + [(width, hidden // 2)] * 2 + [(width, width // 2)] + [(width, 6 * HD)] * pairs
    owners = [dp // 2 if kind == "shards" else dp for kind in kinds]
    rows = [m[0] // n for m, n in zip(shapes, owners)]
    count, depth = len(rows), dp // 2
    dma = pltpu.SemaphoreType.DMA
    any_space = pl.BlockSpec(memory_space=pl.ANY)
    vmem = pl.BlockSpec(memory_space=pltpu.VMEM)

    edges = [r * 5 // 24 if kind == "shards" else r // 6 for r, kind in zip(rows, kinds)]

    def buffers(size, *columns):
        return [pltpu.VMEM((n // 2, *columns, k, m[1]), BF16) for n, k, m in zip(owners, size, shapes)]

    kept_rows = [r - e for r, e in zip(rows, edges)]
    halves = (2, quarter, width)
    working = [
        (act.shape, BF16), (act.shape, BF16), (row.shape, BF16), (shrink_w.shape, BF16), (row.shape, BF16),
        (expand_w.shape, BF16), (row.shape, BF16), (row.shape, BF16), (rdev.shape, F32), (base.shape, F32), (row.shape, BF16),
        (attend_w.shape, BF16), (halves, F32), ((length, width // 2), BF16), ((2, *probs.shape[2:]), BF16),
        ((length, 2 * HD), F32), ((length, 2 * HD), F32), (halves, BF16), (halves, BF16), (halves, BF16), (halves, BF16),
        (halves, BF16), ((2, 8, 8, width), F32), ((2, depth, 8, width), F32),
    ]
    return pl.pallas_call(
        functools.partial(back_kernel, dp, kinds, rows, edges, quarter, sizes),
        out_shape=[
            jax.ShapeDtypeStruct((r, m[1]) if kind == "shards" else (2, r, m[1]), BF16)
            for r, m, kind in zip(rows, shapes, kinds)
        ]
        + [jax.ShapeDtypeStruct((2, 8, width), F32)]
        + [jax.ShapeDtypeStruct(halves, BF16)] * 2,
        in_specs=[any_space] * 4 + [vmem] + [any_space] * 13,
        out_specs=[vmem] * (count + 3),
        scratch_shapes=buffers(rows, 2)
        + buffers(edges, 2)
        + buffers(kept_rows)
        + buffers(kept_rows)
        + buffers(kept_rows)
        + [pltpu.VMEM((r - e, m[1]), BF16) for r, e, m in zip(kept_rows, edges, shapes)]
        + [pltpu.VMEM((depth - 1, kept_rows[-1], shapes[-1][1]), BF16)]
        + [pltpu.VMEM(*item) for item in working]
        + [dma((18,)), dma((2,))]
        + [dma((count, 2))] * 2
        + [dma((count,))] * 2
        + [dma((count, depth))] * 4
        + [dma((depth - 1,))] * 2
        + [dma((count, 3))] * 2
        + [dma((2, 7 + depth))] * 2
        + [dma((4,))] * 2
        + [dma((2,))] * 6,
        compiler_params=pltpu.CompilerParams(
            collective_id=2, has_side_effects=True, vmem_limit_bytes=60 * MIB
        ),
        name="back_and_fold",
    )(*kept)


def write_kernel(dp, sizes, *refs):
    shrinks, expands, attend = refs[:2], refs[2:4], refs[4]
    at_ref = len(refs) - 14 - 3
    triples, (small, result, tokens_grad) = refs[5:at_ref], refs[at_ref : at_ref + 3]
    (
        result_out, tokens_out, gain_one, shift_one, triple_out, bias_triple, attend_out, bias_attend, gain_two, shift_two,
        expand_out, bias_expand, shrink_out, bias_shrink,
    ) = refs[at_ref + 3 :]
    d = lax.axis_index("dp")
    width = small.shape[2]
    result_out[...] = result[...]
    tokens_out[...] = tokens_grad[...]
    half = width // 2
    for k, source in enumerate(shrinks):
        shrink_out[:, k * half : (k + 1) * half] = source[...].astype(F32)
    for core in range(2):
        attend_out[:, core * half : (core + 1) * half] = attend[core].astype(F32)
        for k, source in enumerate(expands):
            n = source.shape[2]
            expand_out[:, (2 * core + k) * n : (2 * core + k + 1) * n] = source[core].astype(F32)
        for p, source in enumerate(triples):
            for t in range(3):
                at = t * width + core * (width // 2) + 2 * HD * p
                triple_out[:, at : at + 2 * HD] = source[core, :, 2 * HD * t : 2 * HD * (t + 1)].astype(F32)
    rows = (FIRST_ROW, (1, 1), TRIPLE_ROW, ATTEND_ROW, SECOND_ROW, (0, 2), (0, EXPAND_ROW), SHRINK_ROW)
    targets = (gain_one, shift_one, bias_triple, bias_attend, gain_two, shift_two, bias_expand, bias_shrink)
    for (block, at), size, target in zip(rows, sizes, targets):
        lines = size * dp // width
        whole = jnp.concatenate([small[block, at + k : at + k + 1, :] for k in range(lines)], axis=1)
        target[...] = pltpu.roll(whole, whole.shape[1] - size * d, 1)[0, 0:size]


def write(dp, sizes, sums, small, result, tokens_grad):
    shrink, expand, attend = [sums[k].shape for k in (0, 2, 4)]
    width = attend[2] * 2
    vmem = pl.BlockSpec(memory_space=pltpu.VMEM)
    halves = [jax.ShapeDtypeStruct(result.shape, BF16)] * 2
    whole = [(expand[1], 3 * width), (attend[1], width), (expand[1], 4 * expand[2]), (shrink[0], 2 * shrink[1])]
    triple_f, attend_f, expand_f, shrink_f = [jax.ShapeDtypeStruct(shape, F32) for shape in whole]
    v = [jax.ShapeDtypeStruct((size,), F32) for size in sizes]
    return pl.pallas_call(
        functools.partial(write_kernel, dp, sizes),
        out_shape=(
            *halves, v[0], v[1], triple_f, v[2], attend_f, v[3], v[4], v[5], expand_f, v[6], shrink_f, v[7],
        ),
        in_specs=[vmem] * (len(sums) + 3),
        out_specs=(vmem,) * 14,
        compiler_params=pltpu.CompilerParams(vmem_limit_bytes=60 * MIB),
        name="write_outputs",
    )(*sums, small, result, tokens_grad)


def head_mask():
    return lax.broadcasted_iota(jnp.int32, (1, 2 * HD), 1) < HD


def part_start(part, quarter):
    return quarter * (part * (part + 1) // 2)


def attend_block(head, part, quarter, total, query, k_ref, v_ref, probs_ref):
    length = quarter * (part + 1)
    key_pos = lax.broadcasted_iota(jnp.int32, (length, 1), 0)
    key_pos = jnp.where(key_pos < total, key_pos, 1 << 20)
    allowed = key_pos <= lax.broadcasted_iota(jnp.int32, (1, quarter), 1) + part * quarter
    mask = head_mask() if head == 0 else ~head_mask()
    query = jnp.where(mask, query * jnp.asarray(HD**-0.5, BF16), jnp.zeros_like(query))
    scores = jnp.where(allowed, product_back(k_ref[:length], query), NEG_FILL)
    exponent = jnp.exp(scores - jnp.max(scores, axis=0, keepdims=True))
    probs = (exponent * (1.0 / jnp.sum(exponent, axis=0, keepdims=True))).astype(BF16)
    probs_ref[head, part_start(part, quarter) : part_start(part + 1, quarter)] = probs
    return product_across(probs, v_ref[:length]).astype(BF16)


def attend_kernel(quarter, total, q_ref, k_ref, v_ref, mixed_ref, probs_ref):
    for part in range(4):
        rows = slice(part * quarter, (part + 1) * quarter)
        mixed = [
            attend_block(head, part, quarter, total[0], q_ref[rows], k_ref, v_ref, probs_ref.at[0]) for head in range(2)
        ]
        mixed_ref[rows] = jnp.where(head_mask(), *mixed)


def attend(triple, total):
    tokens, width = triple.shape[0], triple.shape[1] // 3
    quarter = tokens // 4
    pairs = width // (2 * HD)
    kept = part_start(4, quarter)

    def block(shift):
        return pl.BlockSpec((tokens, 2 * HD), lambda p, _: (0, p + shift))

    return pl.pallas_call(
        functools.partial(attend_kernel, quarter),
        grid_spec=pltpu.PrefetchScalarGridSpec(
            num_scalar_prefetch=1,
            grid=(pairs,),
            in_specs=[block(0), block(pairs), block(2 * pairs)],
            out_specs=[block(0), pl.BlockSpec((1, 2, kept, quarter), lambda p, _: (p, 0, 0, 0))],
        ),
        out_shape=[
            jax.ShapeDtypeStruct((tokens, width), BF16),
            jax.ShapeDtypeStruct((pairs, 2, kept, quarter), BF16),
        ],
        compiler_params=pltpu.CompilerParams(vmem_limit_bytes=50 * MIB),
        name="attend",
    )(total, triple, triple, triple)


def attend_back_block(head, part, quarter, query, k_ref, v_ref, grad, probs, dkeys, dvalues, fresh):
    length = quarter * (part + 1)
    mask = head_mask() if head == 0 else ~head_mask()
    own_query = jnp.where(mask, query * jnp.asarray(HD**-0.5, BF16), jnp.zeros_like(query))
    own_grad = jnp.where(mask, grad, jnp.zeros_like(grad))
    wide = probs.astype(F32)
    grad_probs = product_back(v_ref[:length], own_grad)
    delta = jnp.sum(wide * grad_probs, axis=0, keepdims=True)
    grad_scores = (wide * (grad_probs - delta)).astype(BF16)
    dv = product(probs, own_grad)
    dk = product(grad_scores, own_query)
    if fresh:
        dvalues[:length] = dv
        dkeys[:length] = dk
    else:
        dvalues[:length] += dv
        dkeys[:length] += dk
    return (product_across(grad_scores, k_ref[:length]) * HD**-0.5).astype(BF16)


def attend_back_kernel(quarter, q_ref, k_ref, v_ref, g_ref, probs_ref, dq_ref, dk_ref, dv_ref, dkeys, dvalues):
    for part in reversed(range(4)):
        rows = slice(part * quarter, (part + 1) * quarter)
        kept = slice(part_start(part, quarter), part_start(part + 1, quarter))
        dq = [
            attend_back_block(
                head, part, quarter, q_ref[rows], k_ref, v_ref, g_ref[rows], probs_ref[0, head, kept], dkeys, dvalues,
                part == 3 and head == 0,
            )
            for head in range(2)
        ]
        dq_ref[rows] = jnp.where(head_mask(), dq[0], dq[1])
    dk_ref[...] = dkeys[...].astype(BF16)
    dv_ref[...] = dvalues[...].astype(BF16)


def attend_back(triple, grad, probs):
    tokens, width = triple.shape[0], triple.shape[1] // 3
    quarter = tokens // 4
    pairs = width // (2 * HD)

    def block(shift):
        return pl.BlockSpec((tokens, 2 * HD), lambda p: (0, p + shift))

    return pl.pallas_call(
        functools.partial(attend_back_kernel, quarter),
        grid=(pairs,),
        in_specs=[block(0), block(pairs), block(2 * pairs), block(0)]
        + [pl.BlockSpec((1, 2, part_start(4, quarter), quarter), lambda p: (p, 0, 0, 0))],
        out_specs=[block(0)] * 3,
        out_shape=[jax.ShapeDtypeStruct((tokens, width), BF16)] * 3,
        scratch_shapes=[pltpu.VMEM((tokens, 2 * HD), F32)] * 2,
        compiler_params=pltpu.CompilerParams(vmem_limit_bytes=50 * MIB),
        name="attend_back",
    )(triple, triple, triple, grad, probs)


def take(array, index, size, axis):
    return lax.dynamic_slice_in_dim(array, index * size, size, axis)


def gather_plain(matrices, small, tokens, core, upper):
    triple, attend_full, expand, shrink = [
        lax.all_gather(m.astype(BF16), "dp", axis=0, tiled=True) for m in matrices
    ]
    width = triple.shape[0]
    thirds = triple.reshape(width, 3, width)
    row = lax.all_gather(tokens, "seq", axis=1, tiled=True)
    return (
        take(thirds, core, width // 2, 2).reshape(width, -1),
        attend_full,
        take(expand, core, expand.shape[1] // 2, 1),
        take(shrink, core, shrink.shape[0] // 2, 0),
        lax.all_gather(small, "dp", axis=0),
        jnp.where(upper, row[1], row[0]),
    )


def fold_plain(grads, small, core):
    def by_core(array):
        empty = jnp.zeros_like(array)
        return jnp.stack([jnp.where(core == 0, array, empty), jnp.where(core == 1, array, empty)], axis=1)

    shrink, *others = grads
    wide = jnp.swapaxes(by_core(shrink), 0, 1).reshape(-1, shrink.shape[1])
    arrays = [wide] + [by_core(m) for m in others]
    sums = [lax.psum(lax.psum_scatter(m, "dp", scatter_dimension=0, tiled=True), "seq") for m in arrays]
    sums = [sums[0]] + [jnp.swapaxes(m, 0, 1) for m in sums[1:]]
    return sums, lax.psum(lax.psum_scatter(small, "dp", scatter_dimension=0, tiled=True), "seq").reshape(-1)


def outputs(result, tokens_grad, sums, small_out):
    width = result.shape[-1]
    shrink_sum, expand_sum, attend_sum, triple_sum = [member.astype(F32) for member in sums]
    triple_sum = triple_sum.reshape(2, -1, 3, width // 2).transpose(1, 2, 0, 3).reshape(-1, 3 * width)
    expand_sum, attend_sum = [m.transpose(1, 0, 2).reshape(m.shape[1], -1) for m in (expand_sum, attend_sum)]
    return (
        result,
        tokens_grad,
        small_out[0],
        small_out[1],
        triple_sum,
        small_out[2],
        attend_sum,
        small_out[3],
        small_out[4],
        small_out[5],
        expand_sum,
        small_out[6],
        shrink_sum,
        small_out[7],
    )


def body(
    dp,
    tokens,
    lengths,
    first_gain,
    first_shift,
    triple_weight,
    triple_bias,
    attend_weight,
    attend_bias,
    second_gain,
    second_shift,
    expand_weight,
    expand_bias,
    shrink_weight,
    shrink_bias,
    upstream,
):
    row_count, quarter, width = tokens.shape
    matrices = (triple_weight, attend_weight, expand_weight, shrink_weight)
    vectors = (first_gain, first_shift, triple_bias, attend_bias, second_gain, second_shift, expand_bias, shrink_bias)
    sizes = [member.shape[0] for member in vectors]
    by_kernel = dp & (dp - 1) == 0 and dp > 2 and all(m.shape[0] % 96 == 0 for m in matrices)
    by_kernel = by_kernel and matrices[3].shape[0] * 5 % (24 * 16) == 0
    by_kernel = by_kernel and small_rows(sizes)[1] <= 16 and width == matrices[0].shape[0] * dp
    by_kernel = by_kernel and sizes[2] * dp == 2 * width and (width // 2) % sizes[2] == 0
    place = lax.axis_index("seq")
    upper, core = place // 2 == 1, place % 2

    totals = lengths[:, 0] + lengths[:, 1]
    total = jnp.where(upper, totals[1], totals[0]).reshape(1)

    across = [(k, (k + 2) % 4) for k in range(4)]
    twin = [(k, k + 1 - 2 * (k % 2)) for k in range(4)]

    def halves(partial):
        view = partial.reshape(2, 2, quarter, width)
        mine = jnp.where(core == 0, view[:, 0], view[:, 1])
        theirs = jnp.where(core == 0, view[:, 1], view[:, 0]).astype(BF16)
        return mine + lax.ppermute(theirs, "seq", twin).astype(F32)

    def own_half(array):
        view = array.reshape(2, 2, quarter, width)
        return jnp.where(core == 0, view[:, 0], view[:, 1])

    def give_back(array):
        mine = jnp.where(upper, array[1], array[0])
        theirs = lax.ppermute(jnp.where(upper, array[0], array[1]), "seq", across)
        return jnp.stack([jnp.where(upper, theirs, mine), jnp.where(upper, mine, theirs)])

    def of_core(vector):
        return take(vector, core, vector.shape[0] // 2, 0)

    def spread_out(part):
        empty = jnp.zeros_like(part)
        return jnp.concatenate([jnp.where(core == 0, part, empty), jnp.where(core == 1, part, empty)])

    def whole_row(array):
        mine = jnp.where(upper, array[1], array[0])
        theirs = lax.ppermute(jnp.where(upper, array[0], array[1]), "seq", across)
        pair = jnp.stack([jnp.where(upper, theirs, mine), jnp.where(upper, mine, theirs)])
        others = lax.ppermute(pair, "seq", twin)
        return jnp.stack(
            [jnp.where(core == 0, pair, others), jnp.where(core == 0, others, pair)], axis=1
        ).reshape(-1, width)

    if by_kernel:
        kept = spread(dp, matrices, vectors, tokens, upstream, lengths)
        *sums, small_sum, result, tokens_grad = back(dp, sizes, *kept)
        return write(dp, sizes, sums, small_sum, result, tokens_grad)
    small = jnp.concatenate(vectors)
    *weights, small_full, row = gather_plain(matrices, small, tokens, core, upper)
    floats, at = [], 0
    for size in sizes:
        floats.append(small_full[:, at : at + size].reshape(-1).astype(BF16).astype(F32))
        at += size
    gain_one, shift_one, bias_triple, bias_attend, gain_two, shift_two, bias_expand, bias_shrink = floats
    triple_low, attend_low, expand_low, shrink_low = weights
    seed_low = whole_row(upstream)
    flat_tokens = row.astype(F32)
    seed = seed_low.astype(F32)

    bias_core = jnp.concatenate(
        [of_core(bias_triple[:width]), jnp.zeros((width // 2,), F32), of_core(bias_triple[width:])]
    )
    normed_low = layer_norm(flat_tokens, gain_one, shift_one).astype(BF16)
    triple = (product(normed_low, triple_low) + bias_core).astype(BF16)
    mixed_core, probs = attend(triple, total)
    mixed_other = lax.ppermute(mixed_core, "seq", twin)
    mixed_low = jnp.concatenate(
        [jnp.where(core == 0, mixed_core, mixed_other), jnp.where(core == 0, mixed_other, mixed_core)], axis=1
    )
    resid = flat_tokens + product(mixed_low, attend_low) + bias_attend
    normed_two_low = layer_norm(resid, gain_two, shift_two).astype(BF16)
    activated, gelu_pull = jax.vjp(gelu_tanh, product(normed_two_low, expand_low) + of_core(bias_expand))
    act_low, slope = activated.astype(BF16), gelu_pull(jnp.ones_like(activated))[0]
    _, second_pull = jax.vjp(layer_norm, resid, gain_two, shift_two)

    grad_pre = (product_back(seed_low, shrink_low) * slope.astype(F32)).astype(BF16)
    partial = product_back(grad_pre, expand_low).astype(BF16)
    other_partial = lax.ppermute(partial, "seq", twin)
    shrink_grad = product_across(act_low, seed_low)
    expand_grad = product_across(normed_two_low, grad_pre)
    result = own_half(resid) + halves(product(act_low, shrink_low)) + bias_shrink
    result = give_back(result.astype(BF16))
    shrink_bias_grad = 0.5 * jnp.sum(seed, axis=0)
    expand_bias_grad = spread_out(jnp.sum(grad_pre.astype(F32), axis=0))
    resid_part, second_gain_grad, second_shift_grad = second_pull(partial.astype(F32) + other_partial.astype(F32))
    grad_resid = seed + resid_part
    grad_branch = grad_resid.astype(BF16)
    attend_grad = product_across(mixed_low, take(grad_branch, core, width // 2, 1))
    attend_bias_grad = 0.5 * jnp.sum(grad_branch.astype(F32), axis=0)
    grad_mixed = product_back(grad_branch, take(attend_low, core, width // 2, 0)).astype(BF16)

    grad_triple = jnp.concatenate(attend_back(triple, grad_mixed, probs), axis=1)
    n_one = halves(product_back(grad_triple, triple_low))
    triple_grad = product_across(normed_low, grad_triple)
    triple_sums = jnp.sum(grad_triple.astype(F32), axis=0)
    triple_bias_grad = jnp.concatenate([spread_out(triple_sums[: width // 2]), spread_out(triple_sums[width:])])
    _, first_pull = jax.vjp(layer_norm, own_half(flat_tokens), gain_one, shift_one)
    flat_grad, first_gain_grad, first_shift_grad = first_pull(n_one)
    tokens_grad = give_back((own_half(grad_resid) + flat_grad).astype(BF16))

    big = [member.astype(BF16) for member in (shrink_grad, expand_grad, attend_grad, triple_grad)]
    small_grads = (
        first_gain_grad, first_shift_grad, triple_bias_grad, attend_bias_grad,
        0.5 * second_gain_grad, 0.5 * second_shift_grad, expand_bias_grad, shrink_bias_grad,
    )
    flat_small = jnp.concatenate([g.reshape(dp, -1) for g in small_grads], axis=1)
    sums, own_small = fold_plain(big, flat_small, core)
    small_out, at = [], 0
    for size in sizes:
        small_out.append(own_small[at : at + size])
        at += size
    return outputs(result, tokens_grad, sums, small_out)


def solution(mesh):
    return jax.shard_map(
        functools.partial(body, mesh.shape["dp"]),
        mesh=mesh,
        in_specs=(
            P("dp", "seq", None),
            P("dp", None),
            P("dp"),
            P("dp"),
            P("dp", None),
            P("dp"),
            P("dp", None),
            P("dp"),
            P("dp"),
            P("dp"),
            P("dp", None),
            P("dp"),
            P("dp", None),
            P("dp"),
            P("dp", "seq", None),
        ),
        out_specs=(
            P("dp", "seq", None),
            P("dp", "seq", None),
            P("dp"),
            P("dp"),
            P("dp", None),
            P("dp"),
            P("dp", None),
            P("dp"),
            P("dp"),
            P("dp"),
            P("dp", None),
            P("dp"),
            P("dp", None),
            P("dp"),
        ),
        check_vma=False,
    )
```

```python
import functools

import jax
import jax.numpy as jnp
from jax import lax
from jax.experimental import pallas as pl
from jax.experimental.pallas import tpu as pltpu
from jax.sharding import PartitionSpec as P

H = 12
HD = 64

EPSILON = 1e-05
NEG_FILL = -1e30
MESH = pl.DeviceIdType.MESH
MIB = 1024 * 1024
BF16 = jnp.bfloat16
F32 = jnp.float32


def layer_norm(values, norm_gain, norm_shift):
    center = values - jnp.mean(values, axis=-1, keepdims=True)
    spread = jnp.mean(center * center, axis=-1, keepdims=True)
    return center * lax.rsqrt(spread + EPSILON) * norm_gain + norm_shift


def gelu_tanh(values):
    inside = 0.7978845608028654 * (values + 0.044715 * values * values * values)
    return 0.5 * values * (1.0 + jnp.tanh(inside))


def product(operand, other):
    return jnp.dot(operand, other, preferred_element_type=F32)


def product_across(operand, other):
    return lax.dot_general(operand, other, (((0,), (0,)), ((), ())), preferred_element_type=F32)


def product_back(operand, other):
    return lax.dot_general(operand, other, (((1,), (1,)), ((), ())), preferred_element_type=F32)


def own_place():
    d, s = lax.axis_index("dp"), lax.axis_index("seq")
    return d, s, d // 2, d % 2, s // 2, s % 2


def flip(index, step):
    return index + step * (1 - 2 * ((index // step) % 2))


def remote(src, dst, send, recv, d, s):
    return pltpu.make_async_remote_copy(
        src_ref=src, dst_ref=dst, send_sem=send, recv_sem=recv, device_id=(d, s), device_id_type=MESH
    )


def turned(offset):
    d, s = lax.axis_index("dp"), lax.axis_index("seq")
    for bit in (1, 2):
        s = flip(s, bit) if offset & bit else s
    return (flip(d, 1) if offset & 4 else d), s


def along(depth, offset):
    d, s = lax.axis_index("dp"), lax.axis_index("seq")
    for k in range(depth.bit_length() - 1):
        d = flip(d, 2 << k) if offset >> k & 1 else d
    return d, s


def line_order(depth):
    return sorted(range(1, depth), key=lambda offset: (offset < depth // 2, offset))


def greet(depth, around):
    barrier = pltpu.get_barrier_semaphore()
    partners = [turned(offset) for offset in around] + [along(depth, offset) for offset in range(1, depth)]
    for partner in partners:
        pl.semaphore_signal(barrier, inc=1, device_id=partner, device_id_type=MESH)
    pl.semaphore_wait(barrier, len(partners))


def doubling_steps(count):
    return [1 << k for k in range(count.bit_length() - 1)]


class Plan:
    def __init__(self):
        self.steps = []

    def add(self, at, action, *args):
        self.steps.append((at, len(self.steps), action, args))

    def run(self):
        for _, _, action, args in sorted(self.steps, key=lambda step: step[:2]):
            action(*args)


def small_rows(sizes):
    firsts, at = [], 0
    for size in sizes:
        firsts.append(at)
        at += -(-size // 128)
    return firsts, at


def join_rows(pieces):
    lane = lax.broadcasted_iota(jnp.int32, (1, 128), 1)
    blocks = []
    for b in range(sum(n for _, n in pieces) // 128):
        block, start = jnp.zeros((1, 128), F32), -128 * b
        for piece, n in pieces:
            if start < 128 and start + n > 0:
                turned = piece if start % 128 == 0 else pltpu.roll(piece, start % 128, 1)
                block = jnp.where((lane >= start) & (lane < start + n), turned, block)
            start += n
        blocks.append(block)
    return jnp.concatenate(blocks, axis=1)


def small_vector(ref, sizes, index, shards):
    first, size = small_rows(sizes)[0][index], sizes[index]
    return join_rows(
        [
            (ref[pl.ds(at * 16 + first + k, 1), :].astype(BF16).astype(F32), min(128, size - 128 * k))
            for at in shards
            for k in range(-(-size // 128))
        ]
    )


class Links:
    def __init__(self, **free):
        self.free = free

    def send(self, link, ready, micros):
        start = max(ready, self.free[link])
        self.free[link] = start + micros
        return start, start + micros + 1.5


def spread_kernel(dp, kinds, rows, edges, groups, quarter, sizes, *refs):
    count = len(rows)
    depth, half = dp // 2, dp // 2
    shard, vectors = refs[:count], refs[count : count + len(sizes)]
    at_ref = count + len(sizes)
    tokens, upstream, lengths = refs[at_ref : at_ref + 3]
    at_ref += 3
    weights_out = refs[at_ref : at_ref + count]
    at_ref += count
    (
        small_full, row, seed, normed_out, triple_out, probs_out, mixed_out, hat_out, rdev_out, base_out, second_out,
        act_out, slope_out, grad_out,
    ) = refs[at_ref : at_ref + 14]
    at_ref += 14
    wide, gathered = refs[at_ref : at_ref + count], refs[at_ref + count : at_ref + 2 * count]
    (
        row_v, seed_v, normed, triple, probs, mixed, hat, rdev, base, second, act, slope, grad,
        load, local, z_s, z_r, y_s, y_r, x_s, x_r, ca_s, cb_s, ca_r, cb_r, small_s, small_r, tok_l, tok_s, tok_r,
        weight_l, row_l, out_l, probs_l, mixed_s, mixed_r,
    ) = refs[at_ref + 2 * count :]
    low = gathered[3]
    full = [*gathered[:3], weights_out[3]]
    d, s, z, y, x, c = own_place()
    steps = doubling_steps(dp)
    line = line_order(depth)

    def tile(i, n=quarter):
        return slice(i * n, (i + 1) * n)

    def when(condition, action):
        if condition is True:
            action()
        else:
            pl.when(condition)(action)

    def active(a, at):
        return True if kinds[a] != "shards" else at // half == c

    def pieces(a):
        if kinds[a] != "cols":
            return [(slice(None), slice(None))]
        n = wide[a].shape[1]
        if a:
            return [(pl.ds(pl.multiple_of(c * n, 128), n), slice(None))]
        n, wide_pair = n // 3, 2 * HD
        return [
            (pl.ds(pl.multiple_of((2 * t + c) * n + wide_pair * p, 128), wide_pair), tile(3 * p + t, wide_pair))
            for p in range(n // wide_pair)
            for t in range(3)
        ]

    def fetches(a):
        return [
            pltpu.make_async_copy(shard[a].at[:, source], wide[a].at[:, target], load.at[a, t])
            for t, (source, target) in enumerate(pieces(a))
        ]

    for a in range(count):

        def fetch():
            for copy in fetches(a):
                copy.start()

        when(active(a, d), fetch)

    greet(depth, (1, 2, 4))

    def columns(g):
        a, part, parts = groups[g]
        n = full[a].shape[1] // parts
        if kinds[a] == "share":
            return pl.ds(pl.multiple_of(c * (n // 2), 128), n // 2)
        return tile(part, n)

    def window(g, at, offset, n):
        a = groups[g][0]
        place = at if kinds[a] != "shards" else at % half
        return full[a].at[pl.ds(pl.multiple_of(place * rows[a] + offset, 16), n), columns(g)]

    def body_rows(g):
        a = groups[g][0]
        return x * edges[a], rows[a] - edges[a]

    def edge_rows(g, plane):
        a = groups[g][0]
        return plane * (rows[a] - edges[a]), edges[a]

    def own_piece(g):
        if kinds[groups[g][0]] != "shards":
            return window(g, d, *body_rows(g))
        first, n = body_rows(g)
        return low.at[pl.ds(pl.multiple_of(first, 16), n), columns(g)]

    def over_z(g, at, offset, own=False):
        view = window(g, at, *body_rows(g))
        source = own_piece(g) if own else view
        return remote(source, view, z_s.at[g, offset - 1], z_r.at[g, offset - 1], *along(depth, offset))

    def over_y(g, at, own=False):
        view = window(g, at, *body_rows(g))
        source = own_piece(g) if own else view
        return remote(source, view, y_s.at[g, at], y_r.at[g, at], flip(d, 1), s)

    def over_x(g, at, plane):
        view = window(g, at, *edge_rows(g, plane))
        return remote(view, view, x_s.at[g, at], x_r.at[g, at], d, flip(s, 2))

    def core_a(g, at):
        view = window(g, at, *body_rows(g))
        return remote(view, view, ca_s.at[at], ca_r.at[at], d, flip(s, 1))

    def core_b(g, at):
        view = window(g, at, *edge_rows(g, 1 - x))
        return remote(view, view, cb_s.at[at], cb_r.at[at], d, flip(s, 1))

    def small_copy(k):
        size = 16 << k
        view = small_full.at[pl.ds(pl.multiple_of((d // (1 << k)) * size, 16), size), :]
        return remote(view, view, small_s.at[k], small_r.at[k], flip(d, 1 << k), s)

    own_shrink = pltpu.make_async_copy(
        low, full[3].at[pl.ds(pl.multiple_of((d % half) * rows[3], 16), rows[3]), :], local.at[0]
    )

    def spot(array, index):
        return array.at[pl.ds(pl.multiple_of(index * quarter, 16), quarter), :]

    def row_copies(t, source, target):
        mine, theirs = spot(target, 2 * x + c), spot(target, 2 * (1 - x) + c)
        return (
            pltpu.make_async_copy(source.at[x], mine, tok_l.at[t]),
            remote(source.at[1 - x], mine, tok_s.at[t, 0], tok_r.at[t, 0], d, flip(s, 2)),
            remote(source.at[x], mine, tok_s.at[t, 1], tok_r.at[t, 1], d, flip(s, 1)),
            remote(theirs, theirs, tok_s.at[t, 2], tok_r.at[t, 2], d, flip(s, 1)),
        )

    moves = [row_copies(0, tokens, row), row_copies(1, upstream, seed)]
    row_loads = [pltpu.make_async_copy(row, row_v, row_l.at[0]), pltpu.make_async_copy(seed, seed_v, row_l.at[1])]

    small_full[pl.ds(pl.multiple_of(d * 16, 16), 16), :] = jnp.zeros((16, 128), F32)
    for ref, size, first_row in zip(vectors, sizes, small_rows(sizes)[0]):
        for k in range(-(-size // 128)):
            n = min(128, size - 128 * k)
            small_full[pl.ds(d * 16 + first_row + k, 1), 0:n] = ref[128 * k : 128 * k + n].reshape(1, n)

    def row_begin(t):
        for copy in moves[t][:3]:
            copy.start()

    def row_pass(t):
        moves[t][1].wait_recv()
        moves[t][3].start()

    def row_ready(t):
        own, _, to_core, passed = moves[t]
        own.wait()
        to_core.wait_recv()
        passed.wait_recv()
        row_loads[t].start()

    def cast(a):
        for copy in fetches(a):
            copy.wait()
        if kinds[a] == "shards":
            low[...] = wide[a][...].astype(BF16)
            own_shrink.start()
        else:
            full[a][pl.ds(pl.multiple_of(d * rows[a], 16), rows[a]), :] = wide[a][...].astype(BF16)

    def begin(g):
        for offset in line:
            over_z(g, d, offset, True).start()
        over_y(g, d, True).start()

    def small_step(k):
        if k:
            small_copy(k - 1).wait()
        if k < len(steps):
            small_copy(k).start()

    def zs(g, offset, action):
        at = along(depth, offset)[0]
        when(active(groups[g][0], at), lambda: action(at))

    def ys(g, offset, action):
        at = flip(along(depth, offset)[0], 1)
        when(active(groups[g][0], at), lambda: action(at))

    def share(g, copy, at):
        if kinds[groups[g][0]] == "share":
            copy(g, at).start()

    def z_arrival(g, offset):
        def action(at):
            over_z(g, at, offset).wait_recv()
            over_y(g, at).start()
            share(g, core_a, at)

        zs(g, offset, action)

    def y_arrival(g, offset):
        def action(at):
            over_y(g, at).wait_recv()
            share(g, core_a, at)

        ys(g, offset, action)

    def x_send(g, offset, which):
        which(g, offset, lambda at: over_x(g, at, x).start())

    def x_arrival(g, offset, which):
        def action(at):
            over_x(g, at, 1 - x).wait_recv()
            share(g, core_b, at)

        which(g, offset, action)


    width, pairs = row.shape[1], triple.shape[1] // (6 * HD)
    half_width = width // 2
    triple_w, attend_w, expand_w = full[:3]
    total = lengths[x, 0] + lengths[x, 1]

    def vector(index, shards=range(dp)):
        return small_vector(small_full, sizes, index, shards)

    weight_copies = [pltpu.make_async_copy(full[a], weights_out[a], weight_l.at[a]) for a in range(3)]

    def weight_ready(a):
        if kinds[a] == "share":
            g = [group[0] for group in groups].index(a)

            def passed_on(at):
                core_a(g, at).wait_recv()
                core_b(g, at).wait_recv()

            for offset in range(depth):
                if offset:
                    zs(g, offset, passed_on)
                ys(g, offset, passed_on)
        weight_copies[a].start()

    def norm_tile(i):
        if i == 0:
            row_loads[0].wait()
        values = row_v[tile(i)].astype(F32)
        center = values - jnp.mean(values, axis=-1, keepdims=True)
        r = lax.rsqrt(jnp.mean(center * center, axis=-1, keepdims=True) + EPSILON)
        normed[tile(i)] = (center * r * vector(0) + vector(1)).astype(BF16)

    def triple_tile(i):
        n = half_width // sizes[2]
        ends = [vector(2, [first + c * n + k for k in range(n)]) for first in (0, dp // 2)]
        wide_pair = 2 * HD
        bias = jnp.concatenate(
            [
                part[:, tile(p, wide_pair)]
                for p in range(pairs)
                for part in (ends[0], jnp.zeros((1, half_width), F32), ends[1])
            ],
            axis=1,
        )
        triple[tile(i)] = (product(normed[tile(i)], triple_w[...]) + bias).astype(BF16)

    def probs_copy(p):
        return pltpu.make_async_copy(probs.at[p % 2], probs_out.at[p], probs_l.at[p % 2])

    def mixed_window(p, core):
        return pl.ds(pl.multiple_of(core * half_width + 2 * HD * p, 2 * HD), 2 * HD)

    def mixed_copy(p):
        view = mixed.at[:, mixed_window(p, c)]
        return remote(view, view, mixed_s.at[p], mixed_r.at[p], d, flip(s, 1))

    def attend_part(p, part, head):
        if p > 1 and part == 0 and head == 0:
            probs_copy(p - 2).wait()
        cut = [tile(3 * p + k, 2 * HD) for k in range(3)]
        values = attend_block(
            head, part, quarter, total, triple[tile(part), cut[0]], triple.at[:, cut[1]], triple.at[:, cut[2]],
            probs.at[p % 2],
        )
        spot_of = (tile(part), mixed_window(p, c))
        mixed[spot_of] = jnp.where(head_mask(), mixed[spot_of], values) if head else values
        if part == 3 and head == 1:
            probs_copy(p).start()
            mixed_copy(p).start()

    outs = (
        (normed, normed_out), (triple, triple_out), (mixed, mixed_out), (hat, hat_out), (rdev, rdev_out), (base, base_out),
        (second, second_out), (act, act_out), (slope, slope_out), (grad, grad_out),
    )
    out_copies = [
        pltpu.make_async_copy(source, target, out_l.at[k]) for k, (source, target) in enumerate(outs)
    ]

    def mixed_ready():
        out_copies[0].start()
        out_copies[1].start()
        for p in range(pairs):
            mixed_copy(p).wait()
        out_copies[2].start()

    def resid_tile(i):
        values = row_v[tile(i)].astype(F32) + product(mixed[tile(i)], attend_w[...]) + vector(3)
        center = values - jnp.mean(values, axis=-1, keepdims=True)
        r = lax.rsqrt(jnp.mean(center * center, axis=-1, keepdims=True) + EPSILON)
        hat_of = center * r
        hat[tile(i)] = hat_of.astype(BF16)
        rdev[tile(i)] = jnp.broadcast_to(r, (quarter, 128))
        second[tile(i)] = (hat_of * vector(4) + vector(5)).astype(BF16)

        @pl.when(c == i % 2)
        def _():
            base[i // 2] = values + vector(7)

    def expand_tile(i, k):
        if i == 0 and k == 0:
            for copy in out_copies[3:7]:
                copy.start()
        part = tile(k, 256)
        value = product(second[tile(i)], expand_w[:, part]) + vector(6, [c * half + n for n in range(half)])[:, part]
        square = value * value
        bend = jnp.tanh(0.7978845608028654 * value * (1.0 + 0.044715 * square))
        raised = 0.5 * (1.0 + bend)
        act[tile(i), part] = (value * raised).astype(BF16)
        inner = 0.7978845608028654 + (3 * 0.7978845608028654 * 0.044715) * square
        slope[tile(i), part] = (raised + 0.5 * value * (1.0 - bend * bend) * inner).astype(BF16)

    def shrink_grad(k):
        if k == 0:
            out_copies[7].start()
            out_copies[8].start()
            row_loads[1].wait()
        grad[tile(k, rows[3]), :] = product_across(act[:, tile(k, rows[3])], seed_v[...]).astype(BF16)


    plan = Plan()
    links = Links(z=0.0, y=0.0, x=8.0)
    for k in range(len(steps) + 1):
        plan.add(2.5 * k, small_step, k)
    plan.add(-1.0, row_begin, 0)
    plan.add(9.5, row_pass, 0)
    plan.add(12.0, row_ready, 0)
    ready = [0.0] * count
    begins = line_done = 0.0
    for g, (a, part, parts) in enumerate(groups):
        rate = 90e3 if kinds[a] == "shards" else 45e3
        n = full[a].shape[1] // parts // (2 if kinds[a] == "share" else 1)
        body, edge = [2 * n * m / rate for m in (rows[a] - edges[a], edges[a])]
        if part == 0:
            plan.add(begins - 0.1, when, active(a, d), functools.partial(cast, a))
        plan.add(begins, when, active(a, d), functools.partial(begin, g))
        y_done, x_queue = [], []
        for offset in (0, *line):
            if offset:
                _, arrival = links.send("z", begins, body * depth / (depth - 1))
                plan.add(arrival, z_arrival, g, offset)
                x_queue.append((arrival + 0.1, offset, zs))
            else:
                arrival = begins
            _, over = links.send("y", arrival, body)
            plan.add(over + 0.3, y_arrival, g, offset)
            x_queue.append((over + 0.4, offset, ys))
        for at, offset, which in sorted(x_queue, key=lambda entry: entry[0]):
            _, arrival = links.send("x", at, edge)
            plan.add(at, x_send, g, offset, which)
            plan.add(arrival + 0.5, x_arrival, g, offset, which)
            ready[a] = max(ready[a], arrival + 0.6)
        line_done += body * depth / (depth - 1) * len(line)
        begins = max(begins + 0.5, line_done - 8.0)
    for a in range(3):
        ready[a] += 2.0 if kinds[a] == "share" else 0.0
        plan.add(ready[a], weight_ready, a)
    upstream_at = ready[0] + 2.0
    plan.add(upstream_at, row_begin, 1)
    plan.add(upstream_at + 14.0, row_pass, 1)
    plan.add(upstream_at + 18.0, row_ready, 1)

    clock = [13.0]

    def compute(micros, action, *args):
        plan.add(clock[0], action, *args)
        clock[0] += micros

    for i in range(4):
        compute(1.2, norm_tile, i)
    clock[0] = max(clock[0], ready[0] + 0.1)
    for i in range(4):
        compute(1.0, triple_tile, i)
    for p in range(pairs):
        for part in range(4):
            for head in range(2):
                compute(0.2 * (part + 1), attend_part, p, part, head)
    clock[0] = max(clock[0] + 2.0, ready[1] + 0.1)
    compute(0.0, mixed_ready)
    for i in range(4):
        compute(1.6, resid_tile, i)
    clock[0] = max(clock[0], ready[2] + 0.1)
    for i in range(4):
        for k in range(expand_w.shape[1] // 256):
            compute(0.35, expand_tile, i, k)
    clock[0] = max(clock[0], upstream_at + 18.5)
    for k in range(act.shape[1] // rows[3]):
        compute(1.0, shrink_grad, k)
    plan.run()

    out_copies[9].start()
    for copy in out_copies + weight_copies:
        copy.wait()
    for p in range(max(pairs - 2, 0), pairs):
        probs_copy(p).wait()
    for move_of in moves:
        for copy in move_of[1:]:
            copy.wait_send()
    pl.when(active(3, d))(lambda: own_shrink.wait())

    for g in range(len(groups)):

        def sent():
            for offset in line:
                over_z(g, d, offset, True).wait_send()
            over_y(g, d, True).wait_send()

        when(active(groups[g][0], d), sent)

        def passed(at, own_column):
            if own_column:
                over_y(g, at).wait_send()
            over_x(g, at, x).wait_send()
            if kinds[groups[g][0]] == "share":
                core_a(g, at).wait_send()
                core_b(g, at).wait_send()

        for offset in range(depth):
            if offset:
                zs(g, offset, functools.partial(passed, own_column=True))
            ys(g, offset, functools.partial(passed, own_column=False))


def spread(dp, shards, vectors, tokens, upstream, lengths):
    kinds = ["cols", "share", "cols", "shards"]
    groups = [(0, 0, 1), (1, 0, 1), (2, 0, 2), (3, 0, 2), (2, 1, 2), (3, 1, 2)]
    rows = [member.shape[0] for member in shards]
    edges = [m // 3 for m in rows]
    count = len(rows)
    quarter, width = tokens.shape[1:]
    length = 4 * quarter
    dma = pltpu.SemaphoreType.DMA
    any_space = pl.BlockSpec(memory_space=pl.ANY)
    vmem = pl.BlockSpec(memory_space=pltpu.VMEM)
    held = [(m.shape[0], m.shape[1] // 2 if kind == "cols" else m.shape[1]) for m, kind in zip(shards, kinds)]
    whole = [(dp * r // 2 if kind == "shards" else dp * r, n) for (r, n), kind in zip(held, kinds)]
    kept = part_start(4, quarter)
    pairs = width // (4 * HD)
    hidden = whole[2][1]
    states = [
        ((length, width), BF16), ((length, 3 * width // 2), BF16), ((pairs, 2, kept, quarter), BF16),
        ((length, width), BF16), ((length, width), BF16), ((length, 128), F32), ((2, quarter, width), F32),
        ((length, width), BF16), ((length, hidden), BF16), ((length, hidden), BF16),
        (whole[3], BF16),
    ]
    slots = [(shape if k != 2 else (2, *shape[1:]), kind) for k, (shape, kind) in enumerate(states)]
    return pl.pallas_call(
        functools.partial(spread_kernel, dp, kinds, rows, edges, groups, quarter, [v.shape[0] for v in vectors]),
        out_shape=[jax.ShapeDtypeStruct(shape, BF16) for shape in whole]
        + [jax.ShapeDtypeStruct((dp * 16, 128), F32)]
        + [jax.ShapeDtypeStruct((length, width), BF16)] * 2
        + [jax.ShapeDtypeStruct(*state) for state in states],
        in_specs=[any_space] * count
        + [vmem] * len(vectors)
        + [any_space] * 2
        + [pl.BlockSpec(memory_space=pltpu.SMEM)],
        out_specs=[any_space] * count + [vmem] + [any_space] * (2 + len(states)),
        scratch_shapes=[pltpu.VMEM(shape, F32) for shape in held]
        + [pltpu.VMEM(shape, BF16) for shape in [*whole[:3], held[3]]]
        + [pltpu.VMEM((length, width), BF16)] * 2
        + [pltpu.VMEM(*slot) for slot in slots]
        + [dma((count, 3 * pairs)), dma((1,))]
        + [dma((len(groups), dp // 2))] * 2
        + [dma((len(groups), dp))] * 4
        + [dma((dp,))] * 4
        + [dma((len(doubling_steps(dp)),))] * 2
        + [dma((2,)), dma((2, 3)), dma((2, 3))]
        + [dma((3,)), dma((2,)), dma((len(states) - 1,)), dma((2,)), dma((pairs,)), dma((pairs,))],
        compiler_params=pltpu.CompilerParams(
            collective_id=1, has_side_effects=True, vmem_limit_bytes=60 * MIB
        ),
        name="spread_weights",
    )(*shards, *vectors, tokens, upstream, lengths)


ATTEND_ROW, SECOND_ROW, EXPAND_ROW, SHRINK_ROW = (0, 0), (0, 1), 3, (0, 7)
FIRST_ROW, TRIPLE_ROW = (1, 0), (1, 2)


def back_kernel(dp, kinds, rows, quarter, sizes, *refs):
    count = len(rows)
    depth, half = dp // 2, dp // 2
    (
        triple_w_in, attend_in, expand_in, shrink_in, small_full, row_in, seed_in, normed_in, triple_in, probs_in, mixed_in,
        hat_in, rdev_in, base_in, second_in, act_in, slope_in, grad_in,
    ) = refs[:18]
    outs, (small_sum, result_out, tokens_out) = refs[18 : 18 + count], refs[18 + count : 21 + count]
    at_ref = 21 + count
    acc, x_buf, y_buf, z_buf, b_buf = [refs[at_ref + k * count : at_ref + (k + 1) * count] for k in range(5)]
    (
        act, slope, seed, shrink_w, second, expand_w, partial, other, rdev, base, mixed, attend_w, grad_own, grad_mixed,
        probs, dkeys, dvalues, row_own, send_own, sum_recv, n_recv, stage, ring_buf, line_buf,
        load, probs_l, x_s, x_r, y_s, y_r, u_s, u_r, n_s, n_r, f_s, f_r, small_s, small_r,
        part_s, part_r, sum_s, sum_r, one_s, one_r, give_s, give_r,
    ) = refs[at_ref + 5 * count :]
    d, s, z, y, x, c = own_place()
    twin = flip(s, 1)
    length, width = seed.shape
    hidden, half_width = act.shape[1], width // 2
    pairs = half_width // (2 * HD)
    normed, grad_pre, branch = second, slope, partial
    triple = slope.at[:, pl.ds(0, 3 * half_width)]
    grad_triple = act.at[:, pl.ds(0, 3 * half_width)]
    triple_w = expand_w.at[:, pl.ds(0, 3 * half_width)]
    hat = shrink_w.at[pl.ds(0, length), :]

    sources = [
        (grad_in, acc[0]), (seed_in, seed), (shrink_in, shrink_w), (slope_in, slope),
        (expand_in, expand_w), (act_in, act), (second_in, second), (base_in, base), (rdev_in, rdev), (mixed_in, mixed),
        (attend_in, attend_w), (hat_in, hat), (normed_in, normed), (triple_in, triple), (triple_w_in, triple_w),
    ]
    (
        grad_l, seed_l, shrink_l, slope_l, expand_l, act_l, second_l, base_l, rdev_l, mixed_l, attend_l, hat_l,
        normed_l, triple_l, triple_w_l,
    ) = range(len(sources))
    loads = [pltpu.make_async_copy(source, target, load.at[k]) for k, (source, target) in enumerate(sources)]
    row_loads = [
        pltpu.make_async_copy(
            row_in.at[pl.ds(pl.multiple_of((2 * h + c) * quarter, 16), quarter), :], row_own.at[h], load.at[len(sources) + h]
        )
        for h in range(2)
    ]

    def probs_load(k):
        return pltpu.make_async_copy(probs_in.at[k // 2, k % 2], probs.at[k % 2], probs_l.at[k % 2])

    for copy in loads[:expand_l]:
        copy.start()

    ring, line = range(1, 8), range(1, depth)
    greet(depth, ring)

    for copy in loads[expand_l:hat_l] + row_loads + [probs_load(0), probs_load(1)]:
        copy.start()

    small_sum[...] = jnp.zeros_like(small_sum)


    def layers(g):
        return depth if kinds[g] != "shards" else depth // 2

    def first_layer(g):
        return 0 if kinds[g] != "shards" else c * (depth // 2)

    def layer(g, n):
        if kinds[g] != "shards":
            return sorted(range(depth), key=lambda k: -abs(2 * k - depth + 1))[n]
        return n + c * (depth // 2 - 1 - 2 * n)

    def of(j, own):
        return 2 * j + (y if own else 1 - y)

    def place(g, at, units, n):
        m = rows[g] // 3
        return pl.ds(pl.multiple_of(at * rows[g] + units * m, 16), n * m)

    def span(g, units, n):
        return place(g, 0, units, n)

    def add(g, window, extra):
        acc[g][window, :] = acc[g][window, :] + extra

    def over_x(g, at):
        return remote(
            acc[g].at[place(g, at, 2 * (1 - x), 1), :], x_buf[g].at[at], x_s.at[g, at], x_r.at[g, at], d, flip(s, 2)
        )

    def over_y(g, j):
        source = acc[g].at[place(g, of(j, False), x, 2), :]
        return remote(source, y_buf[g].at[j], y_s.at[g, j], y_r.at[g, j], flip(d, 1), s)

    def up(g, j):
        source = acc[g].at[place(g, of(j, True), x, 2), :]
        return remote(source, z_buf[g].at[j], u_s.at[g, j], u_r.at[g, j], d + 2, s)

    def down_slot(g, j, at_z):
        return jnp.where(j + first_layer(g) == at_z, layers(g), j)

    def down(g, j):
        source = acc[g].at[place(g, of(j, True), x, 2), :]
        return remote(source, z_buf[g].at[down_slot(g, j, z - 1)], n_s.at[g, j], n_r.at[g, j], d - 2, s)

    def stage_a(g, n, own):
        if g == 0 and n == 0 and not own:
            loads[grad_l].wait()
        over_x(g, of(layer(g, n), own)).start()

    def stage_c(g, n, own):
        j = layer(g, n)
        at = of(j, own)
        over_x(g, at).wait_recv()
        add(g, place(g, at, 2 * x, 1), x_buf[g][at])
        if not own:
            over_y(g, j).start()

    def stage_d(g, n):
        j = layer(g, n)
        over_y(g, j).wait_recv()
        add(g, place(g, of(j, True), x, 2), y_buf[g][j])

    def stage_e(g, n, hop):
        j = layer(g, n)
        k = j + first_layer(g)
        window = place(g, of(j, True), x, 2)

        @pl.when((z == hop) & (k > hop))
        def _():
            if hop:
                up(g, j).wait_recv()
                add(g, window, z_buf[g][j])
            up(g, j).start()

        @pl.when((z == depth - 1 - hop) & (k < depth - 1 - hop))
        def _():
            if hop:
                down(g, j).wait_recv()
                add(g, window, z_buf[g][down_slot(g, j, z)])
            down(g, j).start()

    def own_layer(g):
        return z - first_layer(g)

    def ours(g, action):
        if kinds[g] != "shards":
            action()
        else:
            pl.when((z >= first_layer(g)) & (z < first_layer(g) + layers(g)))(action)

    def out_rows(g, units, n):
        return outs[g].at[c, span(g, units, n), :] if kinds[g] != "shards" else outs[g].at[span(g, units, n), :]

    def final_share(g):
        source = acc[g].at[place(g, of(own_layer(g), True), 2 * x, 1), :]
        return remote(source, out_rows(g, 2 * x, 1), f_s.at[g, 0], f_r.at[g, 0], d, flip(s, 2))

    def final_swap(g):
        source = acc[g].at[place(g, of(own_layer(g), True), 1, 1), :]
        return remote(source, b_buf[g], f_s.at[g, 1], f_r.at[g, 1], d, flip(s, 2))

    def final_core(g):
        view = out_rows(g, 0, 3)
        return remote(view, view, f_s.at[g, 2], f_r.at[g, 2], d, twin)

    def finish_one(g):
        def run():
            j = own_layer(g)
            at = of(j, True)
            window = place(g, at, x, 2)

            @pl.when(z > 0)
            def _():
                up(g, j).wait_recv()
                add(g, window, z_buf[g][j])

            @pl.when(z < depth - 1)
            def _():
                down(g, j).wait_recv()
                add(g, window, z_buf[g][layers(g)])

            final_share(g).start()
            final_swap(g).start()
            out_rows(g, 2 * x, 1)[...] = acc[g][place(g, at, 2 * x, 1), :]

        ours(g, run)

    def finish_two(g):
        def run():
            final_swap(g).wait_recv()
            out_rows(g, 1, 1)[...] = acc[g][place(g, of(own_layer(g), True), 1, 1), :] + b_buf[g][...]
            final_share(g).wait_recv()
            final_core(g).start()

        ours(g, run)

    ring_place = y * 4 + s

    def ring_copy(t, offset):
        target = turned(offset)
        return remote(
            ring_buf.at[t, ring_place], ring_buf.at[t, ring_place], small_s.at[t, offset], small_r.at[t, offset], *target
        )

    def line_copy(t, offset):
        target = along(depth, offset)
        return remote(
            line_buf.at[t, z], line_buf.at[t, z], small_s.at[t, 7 + offset], small_r.at[t, 7 + offset], *target
        )

    def small_begin(t):
        ring_buf[t, ring_place] = small_sum[t]
        for offset in ring:
            ring_copy(t, offset).start()

    def small_pass(t):
        for offset in ring:
            ring_copy(t, offset).wait()
        total = ring_buf[t, 0]
        for k in range(1, 8):
            total = total + ring_buf[t, k]
        line_buf[t, z] = total
        for offset in line:
            line_copy(t, offset).start()

    def small_end(t):
        for offset in line:
            line_copy(t, offset).wait()
        total = line_buf[t, 0]
        for k in range(1, depth):
            total = total + line_buf[t, k]
        small_sum[t] = total


    def tile(i, n=quarter):
        return slice(i * n, (i + 1) * n)

    def own_tile(h):
        return pl.ds(pl.multiple_of((2 * h + c) * quarter, 16), quarter)

    def twin_tile(h):
        return pl.ds(pl.multiple_of((2 * h + 1 - c) * quarter, 16), quarter)

    def vector(index):
        return small_vector(small_full, sizes, index, range(dp))

    def sums(row_at, values, columns=slice(None)):
        block, at = row_at
        small_sum[block, at : at + 1, columns] += jnp.sum(values, axis=0, keepdims=True)

    def sum_copy(h):
        return remote(send_own.at[h], sum_recv.at[h], sum_s.at[h], sum_r.at[h], d, twin)

    def result_own(h):
        if h == 0:
            loads[base_l].wait()
        base[h] = base[h] + product(act[own_tile(h), :], shrink_w[...])

    def result_end(h):
        sum_copy(h).wait_recv()
        stage[h] = (base[h] + sum_recv[h].astype(F32)).astype(BF16)

    def result_partial(h):
        if h == 0:
            loads[act_l].wait()
        send_own[h] = product(act[twin_tile(h), :], shrink_w[...]).astype(BF16)
        sum_copy(h).start()

    def grad_pre_tile(i):
        if i == 0:
            for k in (seed_l, shrink_l, slope_l):
                loads[k].wait()
        for k in range(hidden // 256):
            columns = tile(k, 256)
            value = product_back(seed[tile(i)], shrink_w[columns, :]) * slope[tile(i), columns].astype(F32)
            low_value = value.astype(BF16)
            grad_pre[tile(i), columns] = low_value
            total = jnp.sum(low_value.astype(F32), axis=0, keepdims=True)
            spot = (
                0, pl.ds(EXPAND_ROW + (hidden // width) * c + k * 256 // width, 1),
                slice(k * 256 % width, k * 256 % width + 256),
            )
            small_sum[spot] = small_sum[spot] + total
        sums(SHRINK_ROW, 0.5 * seed[tile(i)].astype(F32))

    def part_copy(i):
        return remote(partial.at[tile(i)], other.at[tile(i)], part_s.at[i], part_r.at[i], d, twin)

    def n_two_tile(i):
        if i == 0:
            loads[expand_l].wait()
        partial[tile(i)] = product_back(grad_pre[tile(i)], expand_w[...]).astype(BF16)
        part_copy(i).start()

    def expand_grad(k):
        if k == 0:
            loads[second_l].wait()
        acc[1][tile(k, 256), :] = product_across(second[:, tile(k, 256)], grad_pre[...]).astype(BF16)

    def later_loads():
        for copy in loads[normed_l:]:
            copy.start()

    def back_norm(n, hat_of, r, gain, index, scale):
        sums(index, scale * n * hat_of)
        sums((index[0], index[1] + 1), scale * n)
        e = n * gain
        return r * (e - jnp.mean(e, axis=-1, keepdims=True) - hat_of * jnp.mean(e * hat_of, axis=-1, keepdims=True))

    def resid_tile(i):
        if i == 0:
            loads[hat_l].wait()
            loads[rdev_l].wait()
        part_copy(i).wait()
        n = partial[tile(i)].astype(F32) + other[tile(i)].astype(F32)
        grad = back_norm(n, hat[tile(i)].astype(F32), rdev[tile(i), 0:1], vector(4), SECOND_ROW, 0.5)
        grad = seed[tile(i)].astype(F32) + grad
        low_grad = grad.astype(BF16)
        branch[tile(i)] = low_grad
        sums(ATTEND_ROW, 0.5 * low_grad.astype(F32))

        @pl.when(c == i % 2)
        def _():
            grad_own[i // 2] = grad

    def give_copy(t):
        return remote(stage.at[1 - x], (result_out, tokens_out)[t].at[x], give_s.at[t], give_r.at[t], d, flip(s, 2))

    def give_back(t):
        (result_out, tokens_out)[t][x] = stage[x]
        give_copy(t).start()

    def attend_grad(k):
        if k == 0:
            loads[mixed_l].wait()
        columns = pl.ds(pl.multiple_of(c * half_width, 128), half_width)
        acc[2][tile(k, half_width), :] = product_across(mixed[:, tile(k, half_width)], branch[:, columns]).astype(BF16)

    def mixed_tile(i):
        if i == 0:
            loads[attend_l].wait()
        rows_c = pl.ds(pl.multiple_of(c * half_width, 16), half_width)
        grad_mixed[tile(i)] = product_back(branch[tile(i)], attend_w[rows_c, :]).astype(BF16)

    def attend_back_step(k, part):
        p, head = k // 2, k % 2
        if part == 3:
            probs_load(k).wait()
        if k == 0 and part == 3:
            loads[triple_l].wait()
        columns = [tile(3 * p + n, 2 * HD) for n in range(3)]
        grad_query = attend_back_block(
            head, part, quarter, triple[tile(part), columns[0]], triple.at[:, columns[1]], triple.at[:, columns[2]],
            grad_mixed[tile(part), 2 * HD * p : 2 * HD * (p + 1)],
            probs[k % 2, part_start(part, quarter) : part_start(part + 1, quarter)], dkeys, dvalues,
            part == 3 and head == 0,
        )
        if head:
            grad_query = jnp.where(head_mask(), grad_triple[tile(part), columns[0]], grad_query)
            place_q = pl.ds(pl.multiple_of(c * half_width + 2 * HD * p, 128), 2 * HD)
            sums(TRIPLE_ROW, grad_query.astype(F32), place_q)
        grad_triple[tile(part), columns[0]] = grad_query
        if part == 0:
            if k + 2 < 2 * pairs:
                probs_load(k + 2).start()
            if head:
                grad_triple[:, columns[1]] = dkeys[...].astype(BF16)
                low_values = dvalues[...].astype(BF16)
                grad_triple[:, columns[2]] = low_values
                sums((TRIPLE_ROW[0], TRIPLE_ROW[1] + 1), low_values.astype(F32), place_q)

    def triple_grad(p, k):
        if p == 0 and k == 0:
            loads[normed_l].wait()
        columns = tile(p, 6 * HD)
        acc[3][tile(k, half_width), columns] = product_across(normed[:, tile(k, half_width)], grad_triple[:, columns]).astype(BF16)

    def one_copy(h):
        return remote(send_own.at[h], n_recv.at[h], one_s.at[h], one_r.at[h], d, twin)

    def n_one_partial(h):
        if h == 0:
            loads[triple_w_l].wait()
        sum_copy(h).wait_send()
        send_own[h] = product_back(grad_triple[twin_tile(h), :], triple_w[...]).astype(BF16)
        one_copy(h).start()

    def first_tile(h):
        if h == 0:
            give_copy(0).wait_send()
        row_loads[h].wait()
        n = product_back(grad_triple[own_tile(h), :], triple_w[...])
        one_copy(h).wait_recv()
        n = n + n_recv[h].astype(F32)
        values = row_own[h].astype(F32)
        center = values - jnp.mean(values, axis=-1, keepdims=True)
        r = lax.rsqrt(jnp.mean(center * center, axis=-1, keepdims=True) + EPSILON)
        grad = grad_own[h] + back_norm(n, center * r, r, vector(0), FIRST_ROW, 1.0)
        stage[h] = grad.astype(BF16)


    plan = Plan()
    clock = [2.0]

    def compute(micros, action, *args):
        plan.add(clock[0], action, *args)
        clock[0] += micros

    made = []

    def group_made():
        made.append(clock[0] - 0.01)

    group_made()
    for i in range(4):
        compute(1.4, grad_pre_tile, i)
    for i in range(4):
        compute(0.9, n_two_tile, i)
    for h in range(2):
        compute(0.8, result_partial, h)
    for h in range(2):
        compute(0.8, result_own, h)
    compute(0.0, loads[hat_l].start)
    for k in range(width // 256):
        compute(1.3, expand_grad, k)
    group_made()
    compute(0.0, later_loads)
    for i in range(4):
        compute(2.0, resid_tile, i)
    for k in range(2):
        compute(0.6, attend_grad, k)
    group_made()
    for i in range(4):
        compute(0.3, mixed_tile, i)
    for h in range(2):
        compute(0.3, result_end, h)
    compute(0.2, give_back, 0)
    plan.add(clock[0], small_begin, 0)
    plan.add(clock[0] + 4.0, small_pass, 0)
    plan.add(clock[0] + 8.0, small_end, 0)
    for k in range(2 * pairs):
        for part in reversed(range(4)):
            compute(0.25 * (part + 1), attend_back_step, k, part)
        if k % 2:
            for n in range(2):
                compute(0.5, triple_grad, k // 2, n)
    group_made()
    for h in range(2):
        compute(0.6, n_one_partial, h)
    compute(1.0, lambda: None)
    for h in range(2):
        compute(1.8, first_tile, h)
    compute(0.2, give_back, 1)
    compute(3.0, small_begin, 1)
    compute(3.0, small_pass, 1)
    compute(0.1, small_end, 1)

    done = 0.0
    for g in range(count):
        unit = rows[g] * acc[g].shape[1] * 2 / 50e3 / 3
        done = max(done, made[g])
        for own in (False, True):
            for n in range(layers(g)):
                plan.add(max(done - 4.0, made[g]), stage_a, g, n, own)
                done += unit
                plan.add(done + 1.5, stage_c, g, n, own)
                if own:
                    plan.add(done + 3.5, stage_d, g, n)
                    for hop in range(depth - 1):
                        plan.add(done + 4.0 + (2 * unit + 1.5) * hop, stage_e, g, n, hop)
        last = done + 4.0 + (2 * unit + 1.5) * (depth - 1)
        plan.add(last, finish_one, g)
        plan.add(last + unit + 2.0, finish_two, g)
    plan.run()

    for g in range(count):

        def drain():
            final_share(g).wait_send()
            final_swap(g).wait_send()
            if kinds[g] == "shards":
                final_core(g).wait_send()

        ours(g, drain)
        if kinds[g] == "shards":
            away = (z < first_layer(g)) | (z >= first_layer(g) + depth // 2)
            pl.when(away)(lambda: final_core(g).wait_recv())
        else:
            final_core(g).wait()
        for j in range(layers(g)):
            over_x(g, of(j, False)).wait_send()
            over_x(g, of(j, True)).wait_send()
            over_y(g, j).wait_send()
            pl.when(j + first_layer(g) > z)(lambda: up(g, j).wait_send())
            pl.when(j + first_layer(g) < z)(lambda: down(g, j).wait_send())
    for h in range(2):
        one_copy(h).wait_send()
    give_copy(0).wait_recv()
    give_copy(1).wait()


def back(dp, sizes, *kept):
    _, attend_w, expand_w, shrink_w, _, row, _, _, _, probs, _, _, rdev, base, _, act, _, _ = kept
    length, width = row.shape
    quarter, hidden = length // 4, act.shape[1]
    pairs = width // (4 * HD)
    kinds = ["shards"] + ["cols"] * 3
    shapes = [(hidden, width), (width, hidden), (width, width // 2), (width, 3 * width // 2)]
    owners = [dp // 2 if kind == "shards" else dp for kind in kinds]
    rows = [m[0] // n for m, n in zip(shapes, owners)]
    count, depth = len(rows), dp // 2
    dma = pltpu.SemaphoreType.DMA
    any_space = pl.BlockSpec(memory_space=pl.ANY)
    vmem = pl.BlockSpec(memory_space=pltpu.VMEM)

    def buffers(lead, part, extra=0):
        slots = [() if lead is None else (n // lead + extra,) for n in owners]
        return [pltpu.VMEM((*slot, r // 3 * part, m[1]), BF16) for slot, r, m in zip(slots, rows, shapes)]

    halves = (2, quarter, width)
    working = [
        (act.shape, BF16), (act.shape, BF16), (row.shape, BF16), (shrink_w.shape, BF16), (row.shape, BF16),
        (expand_w.shape, BF16), (row.shape, BF16), (row.shape, BF16), (rdev.shape, F32), (base.shape, F32), (row.shape, BF16),
        (attend_w.shape, BF16), (halves, F32), ((length, width // 2), BF16), ((2, *probs.shape[2:]), BF16),
        ((length, 2 * HD), F32), ((length, 2 * HD), F32), (halves, BF16), (halves, BF16), (halves, BF16), (halves, BF16),
        (halves, BF16), ((2, 8, 8, width), F32), ((2, depth, 8, width), F32),
    ]
    return pl.pallas_call(
        functools.partial(back_kernel, dp, kinds, rows, quarter, sizes),
        out_shape=[
            jax.ShapeDtypeStruct((r, m[1]) if kind == "shards" else (2, r, m[1]), BF16)
            for r, m, kind in zip(rows, shapes, kinds)
        ]
        + [jax.ShapeDtypeStruct((2, 8, width), F32)]
        + [jax.ShapeDtypeStruct(halves, BF16)] * 2,
        in_specs=[any_space] * 4 + [vmem] + [any_space] * 13,
        out_specs=[vmem] * (count + 3),
        scratch_shapes=[pltpu.VMEM(m, BF16) for m in shapes]
        + buffers(1, 1)
        + buffers(2, 2)
        + buffers(2, 2, 1)
        + buffers(None, 1)
        + [pltpu.VMEM(*item) for item in working]
        + [dma((18,)), dma((2,))]
        + [dma((count, dp))] * 2
        + [dma((count, depth))] * 6
        + [dma((count, 3))] * 2
        + [dma((2, 7 + depth))] * 2
        + [dma((4,))] * 2
        + [dma((2,))] * 6,
        compiler_params=pltpu.CompilerParams(
            collective_id=2, has_side_effects=True, vmem_limit_bytes=60 * MIB
        ),
        name="back_and_fold",
    )(*kept)


def write_kernel(dp, sizes, *refs):
    shrink, expand, attend, triple, small, result, tokens_grad = refs[:7]
    (
        result_out, tokens_out, gain_one, shift_one, triple_out, bias_triple, attend_out, bias_attend, gain_two, shift_two,
        expand_out, bias_expand, shrink_out, bias_shrink,
    ) = refs[7:]
    d = lax.axis_index("dp")
    width = small.shape[2]
    result_out[...] = result[...]
    tokens_out[...] = tokens_grad[...]
    half = width // 2
    shrink_out[...] = shrink[...].astype(F32)
    for core in range(2):
        for source, target in ((expand, expand_out), (attend, attend_out)):
            n = source.shape[2]
            target[:, core * n : (core + 1) * n] = source[core].astype(F32)
        for k in range(triple.shape[2] // (2 * HD)):
            at = k % 3 * width + core * half + k // 3 * 2 * HD
            triple_out[:, at : at + 2 * HD] = triple[core, :, k * 2 * HD : (k + 1) * 2 * HD].astype(F32)
    rows = (FIRST_ROW, (1, 1), TRIPLE_ROW, ATTEND_ROW, SECOND_ROW, (0, 2), (0, EXPAND_ROW), SHRINK_ROW)
    targets = (gain_one, shift_one, bias_triple, bias_attend, gain_two, shift_two, bias_expand, bias_shrink)
    for (block, at), size, target in zip(rows, sizes, targets):
        lines = size * dp // width
        whole = jnp.concatenate([small[block, at + k : at + k + 1, :] for k in range(lines)], axis=1)
        target[...] = pltpu.roll(whole, whole.shape[1] - size * d, 1)[0, 0:size]


def write(dp, sizes, sums, small, result, tokens_grad):
    shrink, expand, attend, _ = [member.shape for member in sums]
    width = attend[2] * 2
    vmem = pl.BlockSpec(memory_space=pltpu.VMEM)
    halves = [jax.ShapeDtypeStruct(result.shape, BF16)] * 2
    whole = [(expand[1], 3 * width), (attend[1], width), (expand[1], 2 * expand[2]), shrink]
    triple_f, attend_f, expand_f, shrink_f = [jax.ShapeDtypeStruct(shape, F32) for shape in whole]
    v = [jax.ShapeDtypeStruct((size,), F32) for size in sizes]
    return pl.pallas_call(
        functools.partial(write_kernel, dp, sizes),
        out_shape=(
            *halves, v[0], v[1], triple_f, v[2], attend_f, v[3], v[4], v[5], expand_f, v[6], shrink_f, v[7],
        ),
        in_specs=[vmem] * (len(sums) + 3),
        out_specs=(vmem,) * 14,
        compiler_params=pltpu.CompilerParams(vmem_limit_bytes=60 * MIB),
        name="write_outputs",
    )(*sums, small, result, tokens_grad)


def head_mask():
    return lax.broadcasted_iota(jnp.int32, (1, 2 * HD), 1) < HD


def part_start(part, quarter):
    return quarter * (part * (part + 1) // 2)


def attend_block(head, part, quarter, total, query, k_ref, v_ref, probs_ref):
    length = quarter * (part + 1)
    key_pos = lax.broadcasted_iota(jnp.int32, (length, 1), 0)
    key_pos = jnp.where(key_pos < total, key_pos, 1 << 20)
    allowed = key_pos <= lax.broadcasted_iota(jnp.int32, (1, quarter), 1) + part * quarter
    mask = head_mask() if head == 0 else ~head_mask()
    query = jnp.where(mask, query * jnp.asarray(HD**-0.5, BF16), jnp.zeros_like(query))
    scores = jnp.where(allowed, product_back(k_ref[:length], query), NEG_FILL)
    exponent = jnp.exp(scores - jnp.max(scores, axis=0, keepdims=True))
    probs = (exponent * (1.0 / jnp.sum(exponent, axis=0, keepdims=True))).astype(BF16)
    probs_ref[head, part_start(part, quarter) : part_start(part + 1, quarter)] = probs
    return product_across(probs, v_ref[:length]).astype(BF16)


def attend_kernel(quarter, total, q_ref, k_ref, v_ref, mixed_ref, probs_ref):
    for part in range(4):
        rows = slice(part * quarter, (part + 1) * quarter)
        mixed = [
            attend_block(head, part, quarter, total[0], q_ref[rows], k_ref, v_ref, probs_ref.at[0]) for head in range(2)
        ]
        mixed_ref[rows] = jnp.where(head_mask(), *mixed)


def attend(triple, total):
    tokens, width = triple.shape[0], triple.shape[1] // 3
    quarter = tokens // 4
    pairs = width // (2 * HD)
    kept = part_start(4, quarter)

    def block(shift):
        return pl.BlockSpec((tokens, 2 * HD), lambda p, _: (0, p + shift))

    return pl.pallas_call(
        functools.partial(attend_kernel, quarter),
        grid_spec=pltpu.PrefetchScalarGridSpec(
            num_scalar_prefetch=1,
            grid=(pairs,),
            in_specs=[block(0), block(pairs), block(2 * pairs)],
            out_specs=[block(0), pl.BlockSpec((1, 2, kept, quarter), lambda p, _: (p, 0, 0, 0))],
        ),
        out_shape=[
            jax.ShapeDtypeStruct((tokens, width), BF16),
            jax.ShapeDtypeStruct((pairs, 2, kept, quarter), BF16),
        ],
        compiler_params=pltpu.CompilerParams(vmem_limit_bytes=50 * MIB),
        name="attend",
    )(total, triple, triple, triple)


def attend_back_block(head, part, quarter, query, k_ref, v_ref, grad, probs, dkeys, dvalues, fresh):
    length = quarter * (part + 1)
    mask = head_mask() if head == 0 else ~head_mask()
    own_query = jnp.where(mask, query * jnp.asarray(HD**-0.5, BF16), jnp.zeros_like(query))
    own_grad = jnp.where(mask, grad, jnp.zeros_like(grad))
    wide = probs.astype(F32)
    grad_probs = product_back(v_ref[:length], own_grad)
    delta = jnp.sum(wide * grad_probs, axis=0, keepdims=True)
    grad_scores = (wide * (grad_probs - delta)).astype(BF16)
    dv = product(probs, own_grad)
    dk = product(grad_scores, own_query)
    if fresh:
        dvalues[:length] = dv
        dkeys[:length] = dk
    else:
        dvalues[:length] += dv
        dkeys[:length] += dk
    return (product_across(grad_scores, k_ref[:length]) * HD**-0.5).astype(BF16)


def attend_back_kernel(quarter, q_ref, k_ref, v_ref, g_ref, probs_ref, dq_ref, dk_ref, dv_ref, dkeys, dvalues):
    for part in reversed(range(4)):
        rows = slice(part * quarter, (part + 1) * quarter)
        kept = slice(part_start(part, quarter), part_start(part + 1, quarter))
        dq = [
            attend_back_block(
                head, part, quarter, q_ref[rows], k_ref, v_ref, g_ref[rows], probs_ref[0, head, kept], dkeys, dvalues,
                part == 3 and head == 0,
            )
            for head in range(2)
        ]
        dq_ref[rows] = jnp.where(head_mask(), dq[0], dq[1])
    dk_ref[...] = dkeys[...].astype(BF16)
    dv_ref[...] = dvalues[...].astype(BF16)


def attend_back(triple, grad, probs):
    tokens, width = triple.shape[0], triple.shape[1] // 3
    quarter = tokens // 4
    pairs = width // (2 * HD)

    def block(shift):
        return pl.BlockSpec((tokens, 2 * HD), lambda p: (0, p + shift))

    return pl.pallas_call(
        functools.partial(attend_back_kernel, quarter),
        grid=(pairs,),
        in_specs=[block(0), block(pairs), block(2 * pairs), block(0)]
        + [pl.BlockSpec((1, 2, part_start(4, quarter), quarter), lambda p: (p, 0, 0, 0))],
        out_specs=[block(0)] * 3,
        out_shape=[jax.ShapeDtypeStruct((tokens, width), BF16)] * 3,
        scratch_shapes=[pltpu.VMEM((tokens, 2 * HD), F32)] * 2,
        compiler_params=pltpu.CompilerParams(vmem_limit_bytes=50 * MIB),
        name="attend_back",
    )(triple, triple, triple, grad, probs)


def take(array, index, size, axis):
    return lax.dynamic_slice_in_dim(array, index * size, size, axis)


def gather_plain(matrices, small, tokens, core, upper):
    triple, attend_full, expand, shrink = [
        lax.all_gather(m.astype(BF16), "dp", axis=0, tiled=True) for m in matrices
    ]
    width = triple.shape[0]
    thirds = triple.reshape(width, 3, width)
    row = lax.all_gather(tokens, "seq", axis=1, tiled=True)
    return (
        take(thirds, core, width // 2, 2).reshape(width, -1),
        attend_full,
        take(expand, core, expand.shape[1] // 2, 1),
        take(shrink, core, shrink.shape[0] // 2, 0),
        lax.all_gather(small, "dp", axis=0),
        jnp.where(upper, row[1], row[0]),
    )


def fold_plain(grads, small, core):
    def by_core(array):
        empty = jnp.zeros_like(array)
        return jnp.stack([jnp.where(core == 0, array, empty), jnp.where(core == 1, array, empty)], axis=1)

    shrink, *others = grads
    wide = jnp.swapaxes(by_core(shrink), 0, 1).reshape(-1, shrink.shape[1])
    arrays = [wide] + [by_core(m) for m in others]
    sums = [lax.psum(lax.psum_scatter(m, "dp", scatter_dimension=0, tiled=True), "seq") for m in arrays]
    sums = [sums[0]] + [jnp.swapaxes(m, 0, 1) for m in sums[1:]]
    return sums, lax.psum(lax.psum_scatter(small, "dp", scatter_dimension=0, tiled=True), "seq").reshape(-1)


def outputs(result, tokens_grad, sums, small_out):
    width = result.shape[-1]
    shrink_sum, expand_sum, attend_sum, triple_sum = [member.astype(F32) for member in sums]
    triple_sum = triple_sum.reshape(2, -1, 3, width // 2).transpose(1, 2, 0, 3).reshape(-1, 3 * width)
    expand_sum, attend_sum = [m.transpose(1, 0, 2).reshape(m.shape[1], -1) for m in (expand_sum, attend_sum)]
    return (
        result,
        tokens_grad,
        small_out[0],
        small_out[1],
        triple_sum,
        small_out[2],
        attend_sum,
        small_out[3],
        small_out[4],
        small_out[5],
        expand_sum,
        small_out[6],
        shrink_sum,
        small_out[7],
    )


def body(
    dp,
    tokens,
    lengths,
    first_gain,
    first_shift,
    triple_weight,
    triple_bias,
    attend_weight,
    attend_bias,
    second_gain,
    second_shift,
    expand_weight,
    expand_bias,
    shrink_weight,
    shrink_bias,
    upstream,
):
    row_count, quarter, width = tokens.shape
    matrices = (triple_weight, attend_weight, expand_weight, shrink_weight)
    vectors = (first_gain, first_shift, triple_bias, attend_bias, second_gain, second_shift, expand_bias, shrink_bias)
    sizes = [member.shape[0] for member in vectors]
    by_kernel = dp & (dp - 1) == 0 and dp > 2 and all(m.shape[0] % 96 == 0 for m in matrices)
    by_kernel = by_kernel and matrices[0].shape[0] % 96 == 0
    by_kernel = by_kernel and small_rows(sizes)[1] <= 16 and width == matrices[0].shape[0] * dp
    by_kernel = by_kernel and sizes[2] * dp == 2 * width and (width // 2) % sizes[2] == 0
    place = lax.axis_index("seq")
    upper, core = place // 2 == 1, place % 2

    totals = lengths[:, 0] + lengths[:, 1]
    total = jnp.where(upper, totals[1], totals[0]).reshape(1)

    across = [(k, (k + 2) % 4) for k in range(4)]
    twin = [(k, k + 1 - 2 * (k % 2)) for k in range(4)]

    def halves(partial):
        view = partial.reshape(2, 2, quarter, width)
        mine = jnp.where(core == 0, view[:, 0], view[:, 1])
        theirs = jnp.where(core == 0, view[:, 1], view[:, 0]).astype(BF16)
        return mine + lax.ppermute(theirs, "seq", twin).astype(F32)

    def own_half(array):
        view = array.reshape(2, 2, quarter, width)
        return jnp.where(core == 0, view[:, 0], view[:, 1])

    def give_back(array):
        mine = jnp.where(upper, array[1], array[0])
        theirs = lax.ppermute(jnp.where(upper, array[0], array[1]), "seq", across)
        return jnp.stack([jnp.where(upper, theirs, mine), jnp.where(upper, mine, theirs)])

    def of_core(vector):
        return take(vector, core, vector.shape[0] // 2, 0)

    def spread_out(part):
        empty = jnp.zeros_like(part)
        return jnp.concatenate([jnp.where(core == 0, part, empty), jnp.where(core == 1, part, empty)])

    def whole_row(array):
        mine = jnp.where(upper, array[1], array[0])
        theirs = lax.ppermute(jnp.where(upper, array[0], array[1]), "seq", across)
        pair = jnp.stack([jnp.where(upper, theirs, mine), jnp.where(upper, mine, theirs)])
        others = lax.ppermute(pair, "seq", twin)
        return jnp.stack(
            [jnp.where(core == 0, pair, others), jnp.where(core == 0, others, pair)], axis=1
        ).reshape(-1, width)

    if by_kernel:
        kept = spread(dp, matrices, vectors, tokens, upstream, lengths)
        *sums, small_sum, result, tokens_grad = back(dp, sizes, *kept)
        return write(dp, sizes, sums, small_sum, result, tokens_grad)
    small = jnp.concatenate(vectors)
    *weights, small_full, row = gather_plain(matrices, small, tokens, core, upper)
    floats, at = [], 0
    for size in sizes:
        floats.append(small_full[:, at : at + size].reshape(-1).astype(BF16).astype(F32))
        at += size
    gain_one, shift_one, bias_triple, bias_attend, gain_two, shift_two, bias_expand, bias_shrink = floats
    triple_low, attend_low, expand_low, shrink_low = weights
    seed_low = whole_row(upstream)
    flat_tokens = row.astype(F32)
    seed = seed_low.astype(F32)

    bias_core = jnp.concatenate(
        [of_core(bias_triple[:width]), jnp.zeros((width // 2,), F32), of_core(bias_triple[width:])]
    )
    normed_low = layer_norm(flat_tokens, gain_one, shift_one).astype(BF16)
    triple = (product(normed_low, triple_low) + bias_core).astype(BF16)
    mixed_core, probs = attend(triple, total)
    mixed_other = lax.ppermute(mixed_core, "seq", twin)
    mixed_low = jnp.concatenate(
        [jnp.where(core == 0, mixed_core, mixed_other), jnp.where(core == 0, mixed_other, mixed_core)], axis=1
    )
    resid = flat_tokens + product(mixed_low, attend_low) + bias_attend
    normed_two_low = layer_norm(resid, gain_two, shift_two).astype(BF16)
    activated, gelu_pull = jax.vjp(gelu_tanh, product(normed_two_low, expand_low) + of_core(bias_expand))
    act_low, slope = activated.astype(BF16), gelu_pull(jnp.ones_like(activated))[0]
    _, second_pull = jax.vjp(layer_norm, resid, gain_two, shift_two)

    grad_pre = (product_back(seed_low, shrink_low) * slope.astype(F32)).astype(BF16)
    partial = product_back(grad_pre, expand_low).astype(BF16)
    other_partial = lax.ppermute(partial, "seq", twin)
    shrink_grad = product_across(act_low, seed_low)
    expand_grad = product_across(normed_two_low, grad_pre)
    result = own_half(resid) + halves(product(act_low, shrink_low)) + bias_shrink
    result = give_back(result.astype(BF16))
    shrink_bias_grad = 0.5 * jnp.sum(seed, axis=0)
    expand_bias_grad = spread_out(jnp.sum(grad_pre.astype(F32), axis=0))
    resid_part, second_gain_grad, second_shift_grad = second_pull(partial.astype(F32) + other_partial.astype(F32))
    grad_resid = seed + resid_part
    grad_branch = grad_resid.astype(BF16)
    attend_grad = product_across(mixed_low, take(grad_branch, core, width // 2, 1))
    attend_bias_grad = 0.5 * jnp.sum(grad_branch.astype(F32), axis=0)
    grad_mixed = product_back(grad_branch, take(attend_low, core, width // 2, 0)).astype(BF16)

    grad_triple = jnp.concatenate(attend_back(triple, grad_mixed, probs), axis=1)
    n_one = halves(product_back(grad_triple, triple_low))
    triple_grad = product_across(normed_low, grad_triple)
    triple_sums = jnp.sum(grad_triple.astype(F32), axis=0)
    triple_bias_grad = jnp.concatenate([spread_out(triple_sums[: width // 2]), spread_out(triple_sums[width:])])
    _, first_pull = jax.vjp(layer_norm, own_half(flat_tokens), gain_one, shift_one)
    flat_grad, first_gain_grad, first_shift_grad = first_pull(n_one)
    tokens_grad = give_back((own_half(grad_resid) + flat_grad).astype(BF16))

    big = [member.astype(BF16) for member in (shrink_grad, expand_grad, attend_grad, triple_grad)]
    small_grads = (
        first_gain_grad, first_shift_grad, triple_bias_grad, attend_bias_grad,
        0.5 * second_gain_grad, 0.5 * second_shift_grad, expand_bias_grad, shrink_bias_grad,
    )
    flat_small = jnp.concatenate([g.reshape(dp, -1) for g in small_grads], axis=1)
    sums, own_small = fold_plain(big, flat_small, core)
    small_out, at = [], 0
    for size in sizes:
        small_out.append(own_small[at : at + size])
        at += size
    return outputs(result, tokens_grad, sums, small_out)


def solution(mesh):
    return jax.shard_map(
        functools.partial(body, mesh.shape["dp"]),
        mesh=mesh,
        in_specs=(
            P("dp", "seq", None),
            P("dp", None),
            P("dp"),
            P("dp"),
            P("dp", None),
            P("dp"),
            P("dp", None),
            P("dp"),
            P("dp"),
            P("dp"),
            P("dp", None),
            P("dp"),
            P("dp", None),
            P("dp"),
            P("dp", "seq", None),
        ),
        out_specs=(
            P("dp", "seq", None),
            P("dp", "seq", None),
            P("dp"),
            P("dp"),
            P("dp", None),
            P("dp"),
            P("dp", None),
            P("dp"),
            P("dp"),
            P("dp"),
            P("dp", None),
            P("dp"),
            P("dp", None),
            P("dp"),
        ),
        check_vma=False,
    )
```
